32 devices in a mesh: seq: 16 (over z, y, core), sp: 2 (over x).
Axes of the slice: x: 2, y: 2, z: 4, core: 2. Of those that a mesh axis runs over, the one named last changes fastest.
Arguments:
- frames: bfloat16 [16, 1664, 1024], P('seq', 'sp'), may hold values from -6 to 6
- clip_ids: int32 [16, 1664], P('seq'), may hold values from 0 to 7, never falling along the last dimension, each value on 1 to 350 neighbouring positions
- norm_gain: float32 [1024], replicated, may hold values from 0.5 to 1.5
- w_query: bfloat16 [1024, 1024], replicated, may hold values from -0.1875 to 0.1875
- w_key: bfloat16 [1024, 1024], replicated, may hold values from -0.1875 to 0.1875
- w_value: bfloat16 [1024, 1024], replicated, may hold values from -0.1875 to 0.1875
- w_output: bfloat16 [1024, 1024], replicated, may hold values from -0.5 to 0.5
- attn_scale: float32 [1024], replicated, may hold values from 0.5 to 1.5
- mlp_gain: float32 [1024], replicated, may hold values from 0.5 to 1.5
- w_gate: bfloat16 [1024, 4096], replicated, may hold values from -0.1875 to 0.1875
- w_up: bfloat16 [1024, 4096], replicated, may hold values from -0.1875 to 0.1875
- w_down: bfloat16 [4096, 1024], replicated, may hold values from -0.09375 to 0.09375
- mlp_scale: float32 [1024], replicated, may hold values from 0.5 to 1.5
- out_grad: bfloat16 [16, 1664, 1024], P('seq', 'sp'), may hold values from -6 to 6
Outputs:
- layer_out: bfloat16 [16, 1664, 1024], P('seq', 'sp')
- frames_grad: bfloat16 [16, 1664, 1024], P('seq', 'sp')
- norm_grad: float32 [1024], P(('seq', 'sp'))
- query_grad: float32 [1024, 1024], P(('seq', 'sp'))
- key_grad: float32 [1024, 1024], P(('seq', 'sp'))
- value_grad: float32 [1024, 1024], P(('seq', 'sp'))
- output_grad: float32 [1024, 1024], P(('seq', 'sp'))
- attn_scale_grad: float32 [1024], P(('seq', 'sp'))
- mlp_norm_grad: float32 [1024], P(('seq', 'sp'))
- gate_grad: float32 [1024, 4096], P(('seq', 'sp'))
- up_grad: float32 [1024, 4096], P(('seq', 'sp'))
- down_grad: float32 [4096, 1024], P(('seq', 'sp'))
- mlp_scale_grad: float32 [1024], P(('seq', 'sp'))
The draws below stay inside these ranges and needn't reach their ends.
Inputs may be any that keep to these rules, and one draw needn't show every extreme that they name: `clip_ids`: clip numbers never fall along a sequence; every clip has 1 to 350 frames and one clip of each sequence has exactly 350.
All inputs are finite; a program needn't handle non-finite values.
Results may differ from the reference program's by a relative error of at most 0.014.
Values may be sent and summed in bfloat16 or wider, within the bound.
No kernel may reach another device: no remote copies, remote signals or barrier semaphores. Data moves between devices by JAX's collectives and lax.ppermute only.
A program may use at most 320 MiB of HBM per device.

```python
import math
import jax
import jax.numpy as jnp
import numpy as np
from jax import lax

D = 1024
HEAD_DIM = 64
FF = 4096
WINDOW = 128
BLOCK = 832
SEQ_LEN = 1664
CLIPS = 8
CLIP_MOST = 350
NSEQ = 16


def strengthened(result, rng, source, target, parts, factor):
    owner, partner = [(jnp.arange(result.shape[axis_at]) // (result.shape[axis_at] // parts)).reshape([-1 if axis == axis_at else 1 for axis in range(result.ndim)]) for axis_at in (source, target)]
    chosen = jax.random.permutation(rng, parts)[partner]
    strong = (owner == chosen) | (owner == (partner + parts // 2) % parts)
    return jnp.where(strong, factor * result, result)


def steps_of(stream_key, dims, cuts, smallest, largest):
    factor_of = 1.0
    for dim, shards_of in cuts:
        steps = jax.random.uniform(jax.random.fold_in(jax.random.fold_in(stream_key, 6), dim), (shards_of,), jnp.float32, smallest / len(cuts), largest / len(cuts))
        factor_of = factor_of * jnp.repeat(jnp.exp(steps), dims[dim] // shards_of).reshape((-1,) + (1,) * (len(dims) - 1 - dim))
    return factor_of


def split_up(count, total, most, lean):
    loads = [(1 << 20) // math.isqrt(standing ** lean) + 1 for standing in range(2, count + 1)]
    spare, holding = total - most - (count - 1), [1] * (count - 1)
    while spare > 0:
        free = [i for i in range(count - 1) if holding[i] < most]
        whole, budget = sum([loads[i] for i in free]), spare
        for i in free:
            more = min(most - holding[i], max(1, budget * loads[i] // whole), spare)
            holding[i] = holding[i] + more
            spare = spare - more
    return np.array([most] + holding)


def ragged(rng, amount, total, bound, lean):
    if amount == 2:
        one = jax.random.randint(rng, (), max(1, total - bound), min(bound, total - 1) + 1)
        return jnp.stack([one, total - one])
    lengths = jnp.asarray(split_up(amount, total, bound, lean), jnp.int32)
    couples = (amount - 1) // 2
    giver, sink = lengths[1:1 + 2 * couples:2], lengths[2:2 + 2 * couples:2]
    slack = jnp.minimum(giver - 1, bound - sink)
    moved = jax.random.randint(jax.random.fold_in(rng, 1), (couples,), 0, 1 << 20) % (slack + 1)
    lengths = lengths.at[1:1 + 2 * couples:2].set(giver - moved).at[2:2 + 2 * couples:2].set(sink + moved)
    return lengths[jax.random.permutation(jax.random.fold_in(rng, 2), amount)]


def normal_values(stream_key, shape, scale, limit, shards=(), held_as=jnp.bfloat16):
    gain = steps_of(stream_key, shape, shards, -0.22, 0.18) if shards else 1.0
    entries = jax.random.normal(stream_key, shape, jnp.float32) * scale * gain
    return jnp.minimum(jnp.maximum(entries, -limit), limit).astype(held_as)


def bell_draw_with(stream_key, dims, scale, reach, shards, heavy, kind=jnp.bfloat16):
    entries = scale * jax.random.normal(stream_key, dims, jnp.float32)
    if shards:
        entries = entries * steps_of(stream_key, dims, shards, -0.22, 0.18)
    return jnp.clip(strengthened(entries, jax.random.fold_in(stream_key, 3), *heavy), -reach, reach).astype(kind)


def setup_inputs(seed: int = 0) -> dict:
    streams_of = jax.random.split(jax.random.key(seed), 15)
    return {
        "frames": bell_draw_with(streams_of[0], (NSEQ, SEQ_LEN, D), 1.0, 6.0, ((0, 16), (1, 2)), (0, 2, 16, 2.0)),
        "clip_ids": jax.vmap(lambda own: jnp.searchsorted(jnp.cumsum(ragged(own, CLIPS, SEQ_LEN, CLIP_MOST, 0)), jnp.arange(SEQ_LEN), side="right"))(jax.random.split(streams_of[1], NSEQ)).reshape((NSEQ, SEQ_LEN)).astype(jnp.int32),
        "norm_gain": jnp.clip(1.0 + 0.1 * jax.random.normal(streams_of[2], (D,), jnp.float32), 0.5, 1.5),
        "w_query": normal_values(streams_of[3], (D, D), D ** -0.5, 0.1875),
        "w_key": normal_values(streams_of[4], (D, D), D ** -0.5, 0.1875),
        "w_value": normal_values(streams_of[5], (D, D), D ** -0.5, 0.1875),
        "w_output": normal_values(streams_of[6], (D, D), (D // 8) ** -0.5, 0.5),
        "attn_scale": jnp.clip(jax.random.uniform(streams_of[7], (D,), jnp.float32, 0.5, 1.5), 0.5, 1.5),
        "mlp_gain": jnp.clip(1.0 + 0.1 * jax.random.normal(streams_of[8], (D,), jnp.float32), 0.5, 1.5),
        "w_gate": normal_values(streams_of[9], (D, FF), D ** -0.5, 0.1875),
        "w_up": normal_values(streams_of[10], (D, FF), D ** -0.5, 0.1875),
        "w_down": normal_values(streams_of[11], (FF, D), FF ** -0.5, 0.09375),
        "mlp_scale": jnp.clip(jax.random.uniform(streams_of[12], (D,), jnp.float32, 0.5, 1.5), 0.5, 1.5),
        "out_grad": normal_values(streams_of[13], (NSEQ, SEQ_LEN, D), 1.0, 6.0, ((0, 16), (1, 2))),
    }


@jax.custom_vjp
def low(v):
    return lax.optimization_barrier(v.astype(jnp.bfloat16)).astype(jnp.float32)

@jax.custom_vjp
def low_back(v):
    return v

def low_keep(v):
    return (low(v), None)

def low_pass(kept, grad):
    return (grad,)

def back_keep(v):
    return (v, None)

def back_low(kept, grad):
    return (low(grad),)
low.defvjp(low_keep, low_pass)
low_back.defvjp(back_keep, back_low)

def clip_positions(clip_rows):
    last_axis = clip_rows.ndim - 1
    frame_index = lax.broadcasted_iota(jnp.int32, clip_rows.shape, last_axis)
    previous = jnp.concatenate([clip_rows[..., :1] - 1, clip_rows[..., :-1]], axis=last_axis)
    starting = jnp.where(clip_rows != previous, frame_index, jnp.zeros_like(frame_index))
    first_frame = lax.cummax(starting, axis=last_axis)
    return (frame_index - first_frame).astype(jnp.float32)

def rotary_tables(positions):
    half_dim = HEAD_DIM // 2
    exponent = jnp.arange(half_dim, dtype=jnp.float32) * (2.0 / HEAD_DIM)
    frequency = jnp.exp(-math.log(10000.0) * exponent)
    angles = positions[..., None] * frequency
    return (jnp.cos(angles), jnp.sin(angles))

def rotate(values_in, cos_tab, sin_tab):
    half_dim = values_in.shape[-1] // 2
    leading, trailing = (values_in[..., :half_dim], values_in[..., half_dim:])
    cos_use = cos_tab[..., None, :]
    sin_use = sin_tab[..., None, :]
    return jnp.concatenate([leading * cos_use - trailing * sin_use, trailing * cos_use + leading * sin_use], axis=-1)

def forward_layer(values, clip_row, norm_gain, w_query, w_key, w_value, w_output, attn_scale, mlp_gain, w_gate, w_up, w_down, mlp_scale):
    highest = lax.Precision.HIGHEST
    length, width = values.shape
    heads_all = width // HEAD_DIM
    half_span = WINDOW // 2
    span_keys = BLOCK + WINDOW
    centered = values - lax.optimization_barrier(jnp.mean(values, axis=-1, keepdims=True))
    inv_root = lax.rsqrt(lax.optimization_barrier(jnp.mean(centered * centered, axis=-1, keepdims=True)) + 1e-05)
    normed = low(centered * inv_root * norm_gain)
    cos_tab, sin_tab = rotary_tables(clip_positions(clip_row))
    head_shape = (length, heads_all, HEAD_DIM)
    query = low(rotate(low_back(jnp.dot(normed, w_query, precision=highest).reshape(head_shape)), cos_tab, sin_tab))
    keys = low(rotate(low_back(jnp.dot(normed, w_key, precision=highest).reshape(head_shape)), cos_tab, sin_tab))
    values_h = low_back(low(jnp.dot(normed, w_value, precision=highest).reshape(head_shape)))
    pad_heads = ((half_span, half_span), (0, 0), (0, 0))
    key_pad = jnp.pad(keys, pad_heads)
    value_pad = jnp.pad(values_h, pad_heads)
    clip_pad = jnp.pad(clip_row, (half_span, half_span), constant_values=-1)
    offsets = lax.broadcasted_iota(jnp.int32, (BLOCK, span_keys), 1) - lax.broadcasted_iota(jnp.int32, (BLOCK, span_keys), 0)
    banded = (offsets >= 0) & (offsets < WINDOW)
    scaling = 1.0 / math.sqrt(HEAD_DIM)

    def one_block(index):
        start = index * BLOCK
        query_blk = lax.dynamic_slice_in_dim(query, start, BLOCK, 0)
        key_blk = lax.dynamic_slice_in_dim(key_pad, start, span_keys, 0)
        value_blk = lax.dynamic_slice_in_dim(value_pad, start, span_keys, 0)
        clip_query = lax.dynamic_slice_in_dim(clip_pad, start + half_span, BLOCK, 0)
        clip_keys = lax.dynamic_slice_in_dim(clip_pad, start, span_keys, 0)
        allowed = ((clip_query[:, None] == clip_keys[None, :]) & banded)[None]
        scores = low_back(jnp.einsum('qhd,khd->hqk', query_blk, key_blk, precision=highest) * scaling)
        masked = jnp.where(allowed, scores, -1e+30)
        row_max = lax.optimization_barrier(jnp.max(masked, axis=-1, keepdims=True))
        exp_terms = jnp.where(allowed, jnp.exp(masked - row_max), 0.0)
        attn_probs = exp_terms / lax.optimization_barrier(jnp.sum(exp_terms, axis=-1, keepdims=True))
        return jnp.einsum('hqk,khd->qhd', low(attn_probs), value_blk, precision=highest)
    mixed = lax.map(jax.checkpoint(one_block), jnp.arange(length // BLOCK, dtype=jnp.int32))
    mixed = low_back(low(mixed.reshape(length, width)))
    attn_out = low_back(jnp.dot(mixed, w_output, precision=highest))
    middle = values + attn_scale * attn_out
    inv_rms = lax.rsqrt(lax.optimization_barrier(jnp.mean(middle * middle, axis=-1, keepdims=True)) + 1e-06)
    mlp_in = low(middle * inv_rms * mlp_gain)
    gate_pre = low_back(jnp.dot(mlp_in, w_gate, precision=highest))
    up_pre = low_back(jnp.dot(mlp_in, w_up, precision=highest))
    hidden = low(jax.nn.silu(gate_pre) * up_pre)
    down_out = low_back(jnp.dot(hidden, w_down, precision=highest))
    return middle + mlp_scale * down_out

def reference(frames, clip_ids, norm_gain, w_query, w_key, w_value, w_output, attn_scale, mlp_gain, w_gate, w_up, w_down, mlp_scale, out_grad):
    params = tuple((member.astype(jnp.float32) for member in (norm_gain, w_query, w_key, w_value, w_output, attn_scale, mlp_gain, w_gate, w_up, w_down, mlp_scale)))
    inputs = frames.astype(jnp.float32)
    cotangent = out_grad.astype(jnp.float32)

    def one_sequence(totals, packed):
        seq_in, clip_row, seq_cot = packed

        def forward(values, weights_in):
            return forward_layer(values, clip_row, *weights_in)
        out_val, pullback = jax.vjp(forward, seq_in, params)
        grad_in, grad_params = pullback(seq_cot)
        totals = tuple((running + gradient for running, gradient in zip(totals, grad_params)))
        return (totals, (out_val.astype(jnp.bfloat16), grad_in.astype(jnp.bfloat16)))
    initial = tuple((jnp.zeros(member.shape, jnp.float32) for member in params))
    totals, (layer_out, frames_grad) = lax.scan(one_sequence, initial, (inputs, clip_ids, cotangent))
    return (layer_out, frames_grad, totals[0], totals[1], totals[2], totals[3], totals[4], totals[5], totals[6], totals[7], totals[8], totals[9], totals[10])
```

```python
import functools
import math

import jax
import jax.numpy as jnp
import numpy as np
from jax import lax
from jax.experimental import pallas as pl
from jax.experimental.pallas import tpu as pltpu
from jax.sharding import PartitionSpec as P

HEAD_DIM = 64
HALF = 64
LANES = 128
GROUP = 256
GH = GROUP // HEAD_DIM
QB = 128
KB = QB + 2 * HALF
LN_EPS = 1e-05
RMS_EPS = 1e-06
VMEM = 58 << 20
F32 = jnp.float32
BF16 = jnp.bfloat16

NT = (((1,), (1,)), ((), ()))
NN = (((1,), (0,)), ((), ()))
TN = (((0,), (0,)), ((), ()))


def dot(a, b, dims=NN):
    return lax.dot_general(a, b, dims, preferred_element_type=F32)


def params(grid=0):
    kinds = ("arbitrary",) * grid if grid else None
    return pltpu.CompilerParams(vmem_limit_bytes=VMEM, dimension_semantics=kinds)


def cost(flops, moved, trans=0):
    return pl.CostEstimate(
        flops=int(flops), bytes_accessed=int(moved), transcendentals=int(trans)
    )


def whole(shape):
    return pl.BlockSpec(shape, lambda *_: (0,) * len(shape))


def swap_halves(v):
    lane = lax.broadcasted_iota(jnp.int32, v.shape, 1)
    return jnp.where(lane % HEAD_DIM < HEAD_DIM // 2, pltpu.roll(v, 96, 1), pltpu.roll(v, 32, 1))


def rotated(v, cos_tab, sin_tab, sign):
    pieces = []
    for at in range(0, v.shape[1], LANES):
        part = v[:, at : at + LANES]
        turned = swap_halves(part) * sin_tab
        pieces.append(part * cos_tab + turned if sign > 0 else part * cos_tab - turned)
    return jnp.concatenate(pieces, axis=1)


def project_kernel(with_query, x_ref, gain_ref, cos_ref, sin_ref, *refs):
    count = 3 if with_query else 2
    weights, outs = refs[:count], refs[count:]
    normed_ref, outs = outs[0], outs[1:]
    step = pl.program_id(0)
    blocks = weights[0].shape[0] // GROUP

    @pl.when(step == 0)
    def _():
        x = x_ref[...].astype(F32)
        centered = x - jnp.mean(x, axis=-1, keepdims=True)
        inv = lax.rsqrt(jnp.mean(centered * centered, axis=-1, keepdims=True) + LN_EPS)
        normed_ref[...] = (centered * inv * gain_ref[...]).astype(BF16)

    for which in range(count):

        @pl.when(step // blocks == which)
        def _(which=which):
            out = dot(normed_ref[...], weights[which][...])
            if which < count - 1:
                out = rotated(out, cos_ref[...], sin_ref[...], 1)
            if with_query and which == 0:
                out = out * (1.0 / math.sqrt(HEAD_DIM))
            outs[which][...] = out.astype(BF16)


def project(x, gain, cos_tab, sin_tab, weights):
    rows, width = x.shape
    with_query = len(weights) == 3
    blocks = width // GROUP
    grid = blocks * len(weights)

    def at(which):
        return lambda j: (0, jnp.clip(j - which * blocks, 0, blocks - 1))

    out = jax.ShapeDtypeStruct((rows, width), BF16)
    return pl.pallas_call(
        functools.partial(project_kernel, with_query),
        grid=(grid,),
        in_specs=[
            whole((rows, width)),
            whole((1, width)),
            whole((rows, LANES)),
            whole((rows, LANES)),
        ]
        + [pl.BlockSpec((width, GROUP), at(w)) for w in range(len(weights))],
        out_specs=[whole((rows, width))]
        + [pl.BlockSpec((rows, GROUP), at(w)) for w in range(len(weights))],
        out_shape=[out] * (1 + len(weights)),
        compiler_params=params(1),
        cost_estimate=cost(
            2 * rows * width * width * len(weights),
            2 * len(weights) * width * width + 2 * rows * width * (2 + len(weights)),
        ),
        name="project_rows" if with_query else "project_halo",
    )(x, gain, cos_tab, sin_tab, *weights)


def stack_heads(block):
    lane = lax.broadcasted_iota(jnp.int32, block.shape, 1)
    zero = jnp.zeros_like(block)
    return jnp.concatenate(
        [jnp.where(lane // HEAD_DIM == h, block, zero) for h in range(GH)], axis=0
    )


def fill_keys(buf, own_ref, halo_ref, length):
    buf[0:HALF, :] = halo_ref[0:HALF, :]
    buf[HALF : HALF + length, :] = own_ref[...]
    buf[HALF + length : 2 * HALF + length, :] = halo_ref[HALF : 2 * HALF, :]
    rest = buf.shape[0] - 2 * HALF - length
    if rest:
        buf[2 * HALF + length :, :] = jnp.zeros((rest, buf.shape[1]), buf.dtype)


def fill_queries(buf, own_ref, length):
    buf[0:length, :] = own_ref[...]
    rest = buf.shape[0] - length
    if rest:
        buf[length:, :] = jnp.zeros((rest, buf.shape[1]), buf.dtype)


def attend_kernel(span_ref, q_ref, k_ref, v_ref, kh_ref, vh_ref, o_ref, p_ref, kbuf, vbuf, qbuf, vt, ot):
    length = q_ref.shape[0]
    padded = qbuf.shape[0]
    fill_keys(kbuf, k_ref, kh_ref, length)
    fill_keys(vbuf, v_ref, vh_ref, length)
    fill_queries(qbuf, q_ref, length)
    vt[...] = vbuf[...].T
    for b in range(padded // QB):
        q4 = stack_heads(qbuf[b * QB : (b + 1) * QB, :])
        scores = dot(kbuf[b * QB : b * QB + KB, :], q4, NT)
        place = lax.broadcasted_iota(jnp.int32, (KB, QB), 0) + b * QB
        low = span_ref[0, 0:1, b * QB : (b + 1) * QB]
        high = span_ref[0, 1:2, b * QB : (b + 1) * QB]
        seen = (place >= low) & (place < high)
        for h in range(GH):
            masked = jnp.where(seen, scores[:, h * QB : (h + 1) * QB], -1e30)
            terms = jnp.exp(masked - jnp.max(masked, axis=0, keepdims=True))
            total = jnp.sum(terms, axis=0, keepdims=True)
            probs = (terms * (1.0 / total)).astype(BF16)
            p_ref[:, b * GH * QB + h * QB : b * GH * QB + (h + 1) * QB] = probs
            ot[h * HEAD_DIM : (h + 1) * HEAD_DIM, b * QB : (b + 1) * QB] = dot(
                vt[h * HEAD_DIM : (h + 1) * HEAD_DIM, b * QB : b * QB + KB], probs
            ).astype(BF16)
    o_ref[...] = ot[...].T[0:length, :]


def attend(span, query, key, value, key_halo, value_halo, seqs):
    rows, width = query.shape
    length = rows // seqs
    padded = span.shape[2]
    groups = width // GROUP
    keys = padded + 2 * HALF
    own = pl.BlockSpec((length, GROUP), lambda s, g: (s, g))
    edge = pl.BlockSpec((2 * HALF, GROUP), lambda s, g: (s, g))
    return pl.pallas_call(
        attend_kernel,
        grid=(seqs, groups),
        in_specs=[
            pl.BlockSpec((1, 2, padded), lambda s, g: (s, 0, 0)),
            own,
            own,
            own,
            edge,
            edge,
        ],
        out_specs=[
            own,
            pl.BlockSpec((KB, GH * padded), lambda s, g: (s, g)),
        ],
        out_shape=[
            jax.ShapeDtypeStruct((rows, width), BF16),
            jax.ShapeDtypeStruct((seqs * KB, groups * GH * padded), BF16),
        ],
        scratch_shapes=[
            pltpu.VMEM((keys, GROUP), BF16),
            pltpu.VMEM((keys, GROUP), BF16),
            pltpu.VMEM((padded, GROUP), BF16),
            pltpu.VMEM((GROUP, keys), BF16),
            pltpu.VMEM((GROUP, padded), BF16),
        ],
        compiler_params=params(2),
        cost_estimate=cost(
            2 * 2 * seqs * width * padded * KB * 4, 2 * width * (4 * rows + KB * seqs * padded // 64)
        ),
        name="attend",
    )(span, query, key, value, key_halo, value_halo)


def attend_back_kernel(
    p_ref, q_ref, k_ref, v_ref, kh_ref, vh_ref, g_ref, cos_ref, sin_ref,
    dq_ref, dk_ref, dv_ref, dkh_ref, dvh_ref,
    kbuf, vbuf, qbuf, gbuf, kt, dqt, dkb, dvb,
):
    length = q_ref.shape[0]
    padded = qbuf.shape[0]
    fill_keys(kbuf, k_ref, kh_ref, length)
    fill_keys(vbuf, v_ref, vh_ref, length)
    fill_queries(qbuf, q_ref, length)
    fill_queries(gbuf, g_ref, length)
    kt[...] = kbuf[...].T
    dkb[...] = jnp.zeros_like(dkb)
    dvb[...] = jnp.zeros_like(dvb)
    for b in range(padded // QB):
        at, keys = slice(b * QB, (b + 1) * QB), slice(b * QB, b * QB + KB)
        q4 = stack_heads(qbuf[at, :])
        g4 = stack_heads(gbuf[at, :])
        probs = p_ref[:, b * GH * QB : (b + 1) * GH * QB]
        grads = dot(vbuf[keys, :], g4, NT)
        pieces = []
        for h in range(GH):
            part = probs[:, h * QB : (h + 1) * QB].astype(F32)
            grad = grads[:, h * QB : (h + 1) * QB]
            delta = jnp.sum(part * grad, axis=0, keepdims=True)
            low = (part * (grad - delta)).astype(BF16)
            pieces.append(low)
            dqt[h * HEAD_DIM : (h + 1) * HEAD_DIM, at] = dot(
                kt[h * HEAD_DIM : (h + 1) * HEAD_DIM, keys], low
            )
        dvb[keys, :] += dot(probs, g4)
        dkb[keys, :] += dot(jnp.concatenate(pieces, axis=1), q4)
    cos_tab, sin_tab = cos_ref[0], sin_ref[0]
    middle = slice(HALF, HALF + length)
    dq = dqt[...].T[0:length, :] * (1.0 / math.sqrt(HEAD_DIM))
    dq_ref[...] = rotated(dq, cos_tab[middle], sin_tab[middle], -1).astype(BF16)
    span = length + 2 * HALF
    dk = rotated(dkb[0:span, :], cos_tab, sin_tab, -1).astype(BF16)
    dk_ref[...] = dk[middle]
    dkh_ref[0:HALF, :] = dk[0:HALF]
    dkh_ref[HALF:, :] = dk[span - HALF :]
    dv_ref[...] = dvb[middle, :].astype(BF16)
    dvh_ref[0:HALF, :] = dvb[0:HALF, :].astype(BF16)
    dvh_ref[HALF:, :] = dvb[span - HALF : span, :].astype(BF16)


def attend_back(probs, query, key, value, key_halo, value_halo, grad, cos_tab, sin_tab, seqs):
    rows, width = query.shape
    length = rows // seqs
    padded = -(-length // QB) * QB
    groups = width // GROUP
    keys = padded + 2 * HALF
    own = pl.BlockSpec((length, GROUP), lambda s, g: (s, g))
    edge = pl.BlockSpec((2 * HALF, GROUP), lambda s, g: (s, g))
    table = pl.BlockSpec((1, length + 2 * HALF, LANES), lambda s, g: (s, 0, 0))
    out = jax.ShapeDtypeStruct((rows, width), BF16)
    out_edge = jax.ShapeDtypeStruct((seqs * 2 * HALF, width), BF16)
    return pl.pallas_call(
        attend_back_kernel,
        grid=(seqs, groups),
        in_specs=[
            pl.BlockSpec((KB, GH * padded), lambda s, g: (s, g)),
            own,
            own,
            own,
            edge,
            edge,
            own,
            table,
            table,
        ],
        out_specs=[own, own, own, edge, edge],
        out_shape=[out, out, out, out_edge, out_edge],
        scratch_shapes=[
            pltpu.VMEM((keys, GROUP), BF16),
            pltpu.VMEM((keys, GROUP), BF16),
            pltpu.VMEM((padded, GROUP), BF16),
            pltpu.VMEM((padded, GROUP), BF16),
            pltpu.VMEM((GROUP, keys), BF16),
            pltpu.VMEM((GROUP, padded), F32),
            pltpu.VMEM((keys, GROUP), F32),
            pltpu.VMEM((keys, GROUP), F32),
        ],
        compiler_params=params(2),
        cost_estimate=cost(
            2 * 4 * seqs * width * padded * KB * 4, 2 * width * (8 * rows + KB * seqs * padded // 64)
        ),
        name="attend_back",
    )(probs, query, key, value, key_halo, value_halo, grad, cos_tab, sin_tab)


def out_proj_kernel(m_ref, x_ref, w_ref, scale_ref, gain_ref, attn_ref, in_ref):
    attn = dot(m_ref[...], w_ref[...])
    attn_ref[...] = attn
    middle = x_ref[...].astype(F32) + scale_ref[...] * attn
    inv = lax.rsqrt(jnp.mean(middle * middle, axis=-1, keepdims=True) + RMS_EPS)
    in_ref[...] = (middle * inv * gain_ref[...]).astype(BF16)


def out_proj(mixed, x, w_output, scale, gain):
    rows, width = x.shape
    block = rows // 4
    row = pl.BlockSpec((block, width), lambda i: (i, 0))
    return pl.pallas_call(
        out_proj_kernel,
        grid=(rows // block,),
        in_specs=[row, row, whole((width, width)), whole((1, width)), whole((1, width))],
        out_specs=[row, row],
        out_shape=[
            jax.ShapeDtypeStruct((rows, width), F32),
            jax.ShapeDtypeStruct((rows, width), BF16),
        ],
        compiler_params=params(1),
        cost_estimate=cost(2 * rows * width * width, 2 * rows * width * 5 + 2 * width * width),
        name="out_proj",
    )(mixed, x, w_output, scale, gain)


def hidden_grad_kernel(core_ref, own_ref, peer_ref, scale_ref, w_ref, low_ref, out_ref):
    rows = own_ref.shape[0]

    @pl.when(pl.program_id(0) == 0)
    def _():
        low_ref[0:rows, :] = (own_ref[...].astype(F32) * scale_ref[...]).astype(BF16)
        low_ref[rows:, :] = (peer_ref[...].astype(F32) * scale_ref[...]).astype(BF16)

    for at in (0, rows):
        out_ref[at : at + rows, :] = dot(low_ref[at : at + rows, :], w_ref[...], NT).astype(BF16)


def hidden_grad(core, own, peer, scale, w_down, block):
    rows, width = own.shape
    count = w_down.shape[0] // block // 2
    return pl.pallas_call(
        hidden_grad_kernel,
        grid_spec=pltpu.PrefetchScalarGridSpec(
            num_scalar_prefetch=1,
            grid=(count,),
            in_specs=[
                whole((rows, width)),
                whole((rows, width)),
                whole((1, width)),
                pl.BlockSpec((block, width), lambda j, c: (2 * j + c[0], 0)),
            ],
            out_specs=[
                whole((2 * rows, width)),
                pl.BlockSpec((2 * rows, block), lambda j, c: (0, j)),
            ],
        ),
        out_shape=[
            jax.ShapeDtypeStruct((2 * rows, width), BF16),
            jax.ShapeDtypeStruct((2 * rows, count * block), BF16),
        ],
        compiler_params=params(1),
        cost_estimate=cost(
            4 * rows * width * count * block, 2 * (4 * rows * width + count * block * (width + 2 * rows))
        ),
        name="hidden_grad",
    )(core, own, peer, scale, w_down)


def feed_kernel(core_ref, xo_ref, xp_ref, gh_ref, wg_ref, wu_ref, *refs):
    hid_ref, gg_ref, gu_ref, gate_ref, up_ref, x_all = refs[-6:]
    rows = xo_ref.shape[0]

    @pl.when(pl.program_id(0) == 0)
    def _():
        x_all[0:rows, :] = xo_ref[...]
        x_all[rows:, :] = xp_ref[...]

    for at in (0, rows):
        part = slice(at, at + rows)
        gate = dot(x_all[part, :], wg_ref[...])
        up = dot(x_all[part, :], wu_ref[...])
        grad = gh_ref[part, :].astype(F32)
        sig = 1.0 / (1.0 + jnp.exp(-gate))
        act = gate * sig
        hid_ref[part, :] = (act * up).astype(BF16)
        gg_ref[part, :] = (grad * up * sig * (1.0 + gate * (1.0 - sig))).astype(BF16)
        gu_ref[part, :] = (grad * act).astype(BF16)
    gate_ref[...] = dot(x_all[...], gg_ref[...], TN).astype(BF16)
    up_ref[...] = dot(x_all[...], gu_ref[...], TN).astype(BF16)


def feed(core, x_own, x_peer, grad_hidden, w_gate, w_up, block, first, count, before):
    rows, width = x_own.shape
    half = grad_hidden.shape[1]
    wide = pl.BlockSpec((2 * rows, block), lambda j, c: (0, j + first))
    weight = pl.BlockSpec((width, block), lambda j, c: (0, 2 * (j + first) + c[0]))
    kept = jax.ShapeDtypeStruct((2 * rows, half), BF16)
    grads = jax.ShapeDtypeStruct((width, count * block), BF16)
    any_spec = pl.BlockSpec(memory_space=pl.ANY)
    return pl.pallas_call(
        feed_kernel,
        grid_spec=pltpu.PrefetchScalarGridSpec(
            num_scalar_prefetch=1,
            grid=(count,),
            in_specs=[whole((rows, width)), whole((rows, width)), wide, weight, weight]
            + [any_spec] * len(before),
            out_specs=[wide] * 3 + [pl.BlockSpec((width, block), lambda j, c: (0, j))] * 2,
            scratch_shapes=[pltpu.VMEM((2 * rows, width), BF16)],
        ),
        out_shape=[kept] * 3 + [grads] * 2,
        input_output_aliases={6 + i: i for i in range(len(before))},
        compiler_params=params(1),
        cost_estimate=cost(
            2 * 2 * rows * width * block * count * 4,
            2 * (4 * rows * width + count * block * (8 * rows + 4 * width)),
        ),
        name="feed",
    )(core, x_own, x_peer, grad_hidden, w_gate, w_up, *before)


def down_kernel(hid_ref, low_ref, one_ref, two_ref):
    out = dot(hid_ref[...], low_ref[...], TN).astype(BF16)
    half = one_ref.shape[1]
    one_ref[...] = out[:, :half]
    two_ref[...] = out[:, half:]


def down(hidden, low):
    rows, half = hidden.shape
    width = low.shape[1]
    block = 512
    return pl.pallas_call(
        down_kernel,
        grid=(half // block,),
        in_specs=[pl.BlockSpec((rows, block), lambda j: (0, j)), whole((rows, width))],
        out_specs=[pl.BlockSpec((block, width // 2), lambda j: (j, 0))] * 2,
        out_shape=[jax.ShapeDtypeStruct((half, width // 2), BF16)] * 2,
        compiler_params=params(1),
        cost_estimate=cost(
            2 * rows * half * width, 2 * (rows * half + rows * width + half * width)
        ),
        name="down_weight",
    )(hidden, low)


def feed_back_kernel(core_ref, *refs):
    pairs, (out_ref, acc) = len(refs[:-2]) // 3, refs[-2:]
    step = pl.program_id(0)
    block = refs[pairs].shape[1]
    total = None
    for i in range(pairs):
        for half, weight in enumerate(refs[pairs + 2 * i : pairs + 2 * i + 2]):
            part = dot(refs[i][:, half * block : (half + 1) * block], weight[...], NT)
            total = part if total is None else total + part

    @pl.when(step == 0)
    def _():
        acc[...] = total

    @pl.when((step > 0) & (step < pl.num_programs(0) - 1))
    def _():
        acc[...] += total

    @pl.when(step == pl.num_programs(0) - 1)
    def _():
        out_ref[...] = (acc[...] + total).astype(out_ref.dtype)


def feed_back(core, grads, weights, block, part, dtype):
    rows, half = grads[0].shape
    rows = rows // 2
    width = weights[0].shape[0]
    tall = pl.BlockSpec((rows, 2 * block), lambda j, c: (part, j))
    one = pl.BlockSpec((width, block), lambda j, c: (0, 4 * j + c[0]))
    two = pl.BlockSpec((width, block), lambda j, c: (0, 4 * j + 2 + c[0]))
    return pl.pallas_call(
        feed_back_kernel,
        grid_spec=pltpu.PrefetchScalarGridSpec(
            num_scalar_prefetch=1,
            grid=(half // block // 2,),
            in_specs=[tall] * len(grads) + [one, two] * len(weights),
            out_specs=whole((rows, width)),
            scratch_shapes=[pltpu.VMEM((rows, width), F32)],
        ),
        out_shape=jax.ShapeDtypeStruct((rows, width), dtype),
        compiler_params=params(1),
        cost_estimate=cost(
            2 * len(grads) * rows * half * width, 2 * len(grads) * (rows * half + half * width)
        ),
        name="feed_back",
    )(core, *grads, *[w for weight in weights for w in (weight, weight)])


def feed_out_kernel(core_ref, hid_ref, one_ref, two_ref, out_ref, acc):
    step = pl.program_id(0)
    block = one_ref.shape[0]
    total = dot(hid_ref[:, :block], one_ref[...]) + dot(hid_ref[:, block:], two_ref[...])

    @pl.when(step == 0)
    def _():
        acc[...] = total

    @pl.when((step > 0) & (step < pl.num_programs(0) - 1))
    def _():
        acc[...] += total

    @pl.when(step == pl.num_programs(0) - 1)
    def _():
        out_ref[...] = (acc[...] + total).astype(out_ref.dtype)


def feed_out(core, hidden, w_down, block, part, dtype):
    rows, half = hidden.shape
    rows = rows // 2
    width = w_down.shape[1]
    return pl.pallas_call(
        feed_out_kernel,
        grid_spec=pltpu.PrefetchScalarGridSpec(
            num_scalar_prefetch=1,
            grid=(half // block // 2,),
            in_specs=[
                pl.BlockSpec((rows, 2 * block), lambda j, c: (part, j)),
                pl.BlockSpec((block, width), lambda j, c: (4 * j + c[0], 0)),
                pl.BlockSpec((block, width), lambda j, c: (4 * j + 2 + c[0], 0)),
            ],
            out_specs=whole((rows, width)),
            scratch_shapes=[pltpu.VMEM((rows, width), F32)],
        ),
        out_shape=jax.ShapeDtypeStruct((rows, width), dtype),
        compiler_params=params(1),
        cost_estimate=cost(2 * rows * half * width, 2 * (rows * half + half * width)),
        name="feed_out",
    )(core, hidden, w_down, w_down)


def join_kernel(
    x_ref, attn_ref, g_ref, in_ref, in_got_ref, attn_scale_ref, gain_ref, w_ref,
    grad_attn_ref, grad_mixed_ref, middle_ref, sums_ref,
):
    x = x_ref[...].astype(F32)
    attn = attn_ref[...]
    grad_y = g_ref[...].astype(F32)
    grad_in = in_ref[...] + in_got_ref[...].astype(F32)
    middle = x + attn_scale_ref[...] * attn
    inv = lax.rsqrt(jnp.mean(middle * middle, axis=-1, keepdims=True) + RMS_EPS)
    unit = middle * inv
    scaled = grad_in * gain_ref[...]
    grad_middle = grad_y + inv * (scaled - unit * jnp.mean(scaled * unit, axis=-1, keepdims=True))
    middle_ref[...] = grad_middle
    grad_attn = (attn_scale_ref[...] * grad_middle).astype(BF16)
    grad_attn_ref[...] = grad_attn
    grad_mixed_ref[...] = dot(grad_attn, w_ref[...], NT).astype(BF16)

    @pl.when(pl.program_id(0) == 0)
    def _():
        sums_ref[...] = jnp.zeros_like(sums_ref)

    sums_ref[0:1, :] += jnp.sum(grad_middle * attn, axis=0, keepdims=True)
    sums_ref[1:2, :] += jnp.sum(grad_in * unit, axis=0, keepdims=True)


def join(x, attn, grad_y, grad_in, grad_in_got, attn_scale, gain, w_output):
    rows, width = x.shape
    block = rows // 4
    row = pl.BlockSpec((block, width), lambda i: (i, 0))
    vec = whole((1, width))
    low = jax.ShapeDtypeStruct((rows, width), BF16)
    return pl.pallas_call(
        join_kernel,
        grid=(rows // block,),
        in_specs=[row] * 5 + [vec] * 2 + [whole((width, width))],
        out_specs=[row] * 3 + [whole((8, width))],
        out_shape=[
            low,
            low,
            jax.ShapeDtypeStruct((rows, width), F32),
            jax.ShapeDtypeStruct((8, width), F32),
        ],
        compiler_params=params(1),
        cost_estimate=cost(2 * rows * width * width, rows * width * 22 + 2 * width * width),
        name="join",
    )(x, attn, grad_y, grad_in, grad_in_got, attn_scale, gain, w_output)


def finish_kernel(x_ref, attn_ref, g_ref, out_ref, out_got_ref, attn_scale_ref, mlp_scale_ref, layer_ref, sums_ref):
    down_out = out_ref[...] + out_got_ref[...].astype(F32)
    middle = x_ref[...].astype(F32) + attn_scale_ref[...] * attn_ref[...]
    layer_ref[...] = (middle + mlp_scale_ref[...] * down_out).astype(BF16)

    @pl.when(pl.program_id(0) == 0)
    def _():
        sums_ref[...] = jnp.zeros_like(sums_ref)

    sums_ref[0:1, :] += jnp.sum(g_ref[...].astype(F32) * down_out, axis=0, keepdims=True)


def finish(x, attn, grad_y, out, out_got, attn_scale, mlp_scale):
    rows, width = x.shape
    block = rows // 4
    row = pl.BlockSpec((block, width), lambda i: (i, 0))
    vec = whole((1, width))
    return pl.pallas_call(
        finish_kernel,
        grid=(rows // block,),
        in_specs=[row] * 5 + [vec] * 2,
        out_specs=[row, whole((8, width))],
        out_shape=[
            jax.ShapeDtypeStruct((rows, width), BF16),
            jax.ShapeDtypeStruct((8, width), F32),
        ],
        compiler_params=params(1),
        cost_estimate=cost(8 * rows * width, rows * width * 16),
        name="finish",
    )(x, attn, grad_y, out, out_got, attn_scale, mlp_scale)


def weight_grad_kernel(a_ref, b_ref, out_ref):
    out_ref[...] = dot(a_ref[...], b_ref[...], TN).astype(BF16)


def weight_grad(a, b, name):
    rows, width = a.shape
    columns = b.shape[1]
    block = 512
    return pl.pallas_call(
        weight_grad_kernel,
        grid=(columns // block,),
        in_specs=[whole((rows, width)), pl.BlockSpec((rows, block), lambda j: (0, j))],
        out_specs=pl.BlockSpec((width, block), lambda j: (0, j)),
        out_shape=jax.ShapeDtypeStruct((width, columns), BF16),
        compiler_params=params(1),
        cost_estimate=cost(
            2 * rows * width * columns, 2 * (rows * width + rows * columns + width * columns)
        ),
        name=name,
    )(a, b)


def input_grad_kernel(
    x_ref, gq_ref, gk_ref, gv_ref, middle_ref, gain_ref, wq_ref, wk_ref, wv_ref, out_ref, sums_ref
):
    grad = (
        dot(gq_ref[...], wq_ref[...], NT)
        + dot(gk_ref[...], wk_ref[...], NT)
        + dot(gv_ref[...], wv_ref[...], NT)
    )
    x = x_ref[...].astype(F32)
    centered = x - jnp.mean(x, axis=-1, keepdims=True)
    inv = lax.rsqrt(jnp.mean(centered * centered, axis=-1, keepdims=True) + LN_EPS)
    unit = centered * inv
    scaled = grad * gain_ref[...]
    back = inv * (
        scaled
        - jnp.mean(scaled, axis=-1, keepdims=True)
        - unit * jnp.mean(scaled * unit, axis=-1, keepdims=True)
    )
    out_ref[...] = (middle_ref[...] + back).astype(BF16)

    @pl.when(pl.program_id(0) == 0)
    def _():
        sums_ref[...] = jnp.zeros_like(sums_ref)

    sums_ref[0:1, :] += jnp.sum(grad * unit, axis=0, keepdims=True)


def input_grad(x, gq, gk, gv, grad_middle, gain, w_query, w_key, w_value):
    rows, width = x.shape
    block = rows // 4
    row = pl.BlockSpec((block, width), lambda i: (i, 0))
    square = whole((width, width))
    return pl.pallas_call(
        input_grad_kernel,
        grid=(rows // block,),
        in_specs=[row] * 5 + [whole((1, width))] + [square] * 3,
        out_specs=[row, whole((8, width))],
        out_shape=[
            jax.ShapeDtypeStruct((rows, width), BF16),
            jax.ShapeDtypeStruct((8, width), F32),
        ],
        compiler_params=params(1),
        cost_estimate=cost(2 * 3 * rows * width * width, rows * width * 14 + 6 * width * width),
        name="input_grad",
    )(x, gq, gk, gv, grad_middle, gain, w_query, w_key, w_value)


def log2(n):
    return n.bit_length() - 1


class Places:
    def __init__(self):
        self.n_seq, self.n_sp = lax.axis_size("seq"), lax.axis_size("sp")
        self.sp_bits = log2(self.n_sp)
        self.count = self.sp_bits + log2(self.n_seq)
        self.core = self.sp_bits
        self.me = lax.axis_index("seq") * self.n_sp + lax.axis_index("sp")
        self.down_bits = [b for b in reversed(range(self.count)) if b != self.core]

    def swap(self, value, bit):
        if bit < self.sp_bits:
            axis, size, at = "sp", self.n_sp, bit
        else:
            axis, size, at = "seq", self.n_seq, bit - self.sp_bits
        return lax.ppermute(value, axis, [(i, i ^ (1 << at)) for i in range(size)])

    def own(self, bit):
        return (self.me >> bit) & 1


class Piece:
    def __init__(self, places, value, bits):
        self.places, self.bits = places, list(bits)
        self.value = value.reshape((2,) * len(self.bits) + value.shape[-2:])

    def split(self, value, axis, bit):
        at = self.places.own(bit)
        pick = lambda i: lax.dynamic_index_in_dim(value, i, axis, False)
        return pick(1 - at), pick(at)

    def send(self, bit):
        axis = self.bits.index(bit)
        out, self.value = self.split(self.value, axis, bit)
        self.got = self.places.swap(out, bit)
        self.bits.pop(axis)

    def add(self, low=True):
        self.value = self.value.astype(F32) + self.got.astype(F32)
        if low:
            self.value = self.value.astype(BF16)


def tie(small, pieces):
    small, got = lax.optimization_barrier((small, [p.got for p in pieces]))
    for p, g in zip(pieces, got):
        p.got = g
    return small


def on_device(
    frames, clip_ids, norm_gain, w_query, w_key, w_value, w_output, attn_scale,
    mlp_gain, w_gate, w_up, w_down, mlp_scale, out_grad,
):
    places = Places()
    seqs, length, width = frames.shape
    total_len = clip_ids.shape[1]
    rows = seqs * length
    n_sp, n_seq = places.n_sp, places.n_seq
    devices = n_sp * n_seq
    feed_width = w_gate.shape[1]
    own_rows = width // devices
    feed_rows = feed_width // devices
    block = feed_rows * n_sp
    core = lax.axis_index("seq") & 1
    core_s = core.astype(jnp.int32).reshape(1)
    sp = lax.axis_index("sp")
    sp_bits = list(range(places.core))
    seq_bits = list(range(places.core + 1, places.count))
    flows = ((sp_bits, seq_bits[:1]), (seq_bits[:1], sp_bits))
    late = seq_bits[1:]

    x = frames.reshape(rows, width)
    grad_y = out_grad.reshape(rows, width)

    def neighbours(last, first):
        if n_sp == 2:
            got = lax.ppermute(jnp.where(sp == 0, last, first), "sp", [(0, 1), (1, 0)])
            return got * (sp == 1).astype(got.dtype), got * (sp == 0).astype(got.dtype)
        return (
            lax.ppermute(last, "sp", [(i, i + 1) for i in range(n_sp - 1)]),
            lax.ppermute(first, "sp", [(i + 1, i) for i in range(n_sp - 1)]),
        )

    from_left, from_right = neighbours(frames[:, length - HALF :], frames[:, :HALF])
    grad_y_peer = places.swap(grad_y, places.core)

    start = sp * length
    padded_ids = jnp.pad(clip_ids, ((0, 0), (HALF, HALF)), mode="edge")
    near = lax.dynamic_slice_in_dim(padded_ids, start, length + 2 * HALF, 1)
    first = jnp.sum((clip_ids[:, None, :] < near[:, :, None]).astype(jnp.int32), axis=-1)
    end = jnp.sum((clip_ids[:, None, :] <= near[:, :, None]).astype(jnp.int32), axis=-1)
    frame = lax.broadcasted_iota(jnp.int32, near.shape, 1) + (start - HALF)
    position = (frame - first).astype(F32)
    exponent = jnp.arange(HEAD_DIM // 2, dtype=F32) * (2.0 / HEAD_DIM)
    frequency = jnp.exp(-math.log(10000.0) * exponent)
    angles = position[..., None] * jnp.tile(frequency, LANES // (HEAD_DIM // 2))
    sign = np.where(np.arange(LANES) % HEAD_DIM < HEAD_DIM // 2, -1.0, 1.0).astype(np.float32)
    cos_tab = jnp.cos(angles)
    sin_tab = jnp.sin(angles) * sign
    mid = slice(HALF, HALF + length)
    low = jnp.maximum(frame - HALF, first)[:, mid] - (start - HALF)
    high = jnp.minimum(frame + HALF, end)[:, mid] - (start - HALF)
    padded = -(-length // QB) * QB
    span = jnp.pad(jnp.stack([low, high], axis=1), ((0, 0), (0, 0), (0, padded - length)))

    gain = norm_gain[None]
    normed, query, key, value = project(
        x,
        gain,
        cos_tab[:, mid].reshape(rows, LANES),
        sin_tab[:, mid].reshape(rows, LANES),
        (w_query, w_key, w_value),
    )

    def edges(table):
        return jnp.concatenate([table[:, :HALF], table[:, HALF + length :]], axis=1).reshape(
            seqs * 2 * HALF, -1
        )

    halo = jnp.concatenate([from_left, from_right], axis=1).reshape(seqs * 2 * HALF, width)
    _, key_halo, value_halo = project(
        halo, gain, edges(cos_tab), edges(sin_tab), (w_key, w_value)
    )
    mixed, probs = attend(span, query, key, value, key_halo, value_halo, seqs)

    attn_out, mlp_in = out_proj(mixed, x, w_output, attn_scale[None], mlp_gain[None])
    mlp_in_peer = places.swap(mlp_in, places.core)
    grad_low, grad_hidden = hidden_grad(
        core_s, grad_y, grad_y_peer, mlp_scale[None], w_down, block
    )

    blocks = n_seq // 2
    per = blocks // 2
    every = [b for b in reversed(range(places.count))]

    def start_pair(one, two, bits):
        return [Piece(places, one, bits), Piece(places, two, bits)]

    def go(pair, stage):
        for p, flow in zip(pair, flows):
            for bit in flow[stage][:-1]:
                p.send(bit)
                p.add()
            p.send(flow[stage][-1])

    def land(pair):
        for p in pair:
            p.add()

    *kept, gate_one, up_one = feed(
        core_s, mlp_in, mlp_in_peer, grad_hidden, w_gate, w_up, block, 0, per, ()
    )

    def rows_pair(one, two, bits):
        return start_pair(one, two, bits)

    def by_bits(value, rows_each):
        return value.reshape(-1, rows_each, value.shape[-1])

    first = rows_pair(by_bits(gate_one, own_rows), by_bits(up_one, own_rows), every)
    go(first, 0)
    *kept, gate_two, up_two = feed(
        core_s, mlp_in, mlp_in_peer, grad_hidden, w_gate, w_up, block, per, per, tuple(kept)
    )
    hidden, grad_gate, grad_up = kept
    small = tie(core_s, first)
    land(first)
    go(first, 1)
    second = rows_pair(by_bits(gate_two, own_rows), by_bits(up_two, own_rows), every)
    go(second, 0)

    in_peer = feed_back(small, (grad_gate, grad_up), (w_gate, w_up), block, 1, BF16)
    in_got = places.swap(in_peer, places.core)
    in_own = feed_back(small, (grad_gate, grad_up), (w_gate, w_up), block, 0, F32)
    down_one, down_two = down(hidden, grad_low)
    scale_row = tie(attn_scale[None], first + second)
    land(first)
    land(second)
    go(second, 1)
    third = rows_pair(by_bits(down_one, feed_rows), by_bits(down_two, feed_rows), places.down_bits)
    go(third, 0)

    grad_attn, grad_mixed, grad_middle, join_sums = join(
        x, attn_out, grad_y, in_own, in_got, scale_row, mlp_gain[None], w_output
    )
    grad_query, grad_key, grad_value, key_edge, value_edge = attend_back(
        probs, query, key, value, key_halo, value_halo, grad_mixed, cos_tab, sin_tab, seqs
    )
    edge = jnp.concatenate([key_edge, value_edge], axis=1).reshape(seqs, 2 * HALF, 2 * width)
    to_right, to_left = neighbours(edge[:, HALF:], edge[:, :HALF])

    def with_edges(own, at):
        own = own.reshape(seqs, length, width)
        left = own[:, :HALF] + to_right[..., at * width : (at + 1) * width]
        right = own[:, length - HALF :] + to_left[..., at * width : (at + 1) * width]
        return jnp.concatenate([left, own[:, HALF : length - HALF], right], axis=1).reshape(
            rows, width
        )

    fourth = rows_pair(
        by_bits(weight_grad(mixed, grad_attn, "output_weight"), own_rows),
        by_bits(weight_grad(normed, grad_query, "query_weight"), own_rows),
        every,
    )
    for p in fourth:
        p.send(places.core)
    scale_row = tie(gain, second + third + fourth)
    land(second)
    land(third)
    land(fourth)
    go(third, 1)
    go(fourth, 0)

    grad_key = with_edges(grad_key, 0)
    grad_value = with_edges(grad_value, 1)
    frames_grad, norm_sums = input_grad(
        x, grad_query, grad_key, grad_value, grad_middle, scale_row, w_query, w_key, w_value
    )
    fifth = rows_pair(
        by_bits(weight_grad(normed, grad_key, "key_weight"), own_rows),
        by_bits(weight_grad(normed, grad_value, "value_weight"), own_rows),
        every,
    )
    for p in fifth:
        p.send(places.core)

    small = tie(core_s, third + fourth)
    land(third)
    land(fourth)
    go(fourth, 1)
    out_peer = feed_out(small, hidden, w_down, block, 1, BF16)
    out_got = places.swap(out_peer, places.core)
    small = tie(small, fifth)
    land(fifth)
    go(fifth, 0)
    out_own = feed_out(small, hidden, w_down, block, 0, F32)
    layer_out, out_sums = finish(
        x, attn_out, grad_y, out_own, out_got, attn_scale[None], mlp_scale[None]
    )
    land(fourth)
    land(fifth)
    go(fifth, 1)
    land(fifth)

    def rest(pairs):
        joined = Piece(places, jnp.concatenate([p.value for pair in pairs for p in pair], axis=-1), pairs[0][0].bits)
        for bit in late:
            joined.send(bit)
            joined.add(bit != late[-1])
        return joined.value

    feeds = rest([first, second])
    downs = rest([third])
    one = rest([fourth])
    two = rest([fifth])
    output_grad, query_grad = one[:, :width], one[:, width:]
    key_grad, value_grad = two[:, :width], two[:, width:]

    vectors = jnp.stack([norm_sums[0], join_sums[0], join_sums[1], out_sums[0]], axis=1)
    piece = Piece(places, by_bits(vectors, own_rows), every)
    for bit in [places.core] + sp_bits + seq_bits:
        piece.send(bit)
        piece.add(False)
    vectors = piece.value.T

    wide = per * block
    halves = feeds.reshape(2, own_rows, 2, 2, wide).transpose(0, 1, 3, 2, 4)
    halves = halves.reshape(2, own_rows, 2 * blocks * block)
    mine = lax.dynamic_index_in_dim(halves, core, 0, False)
    got = places.swap(lax.dynamic_index_in_dim(halves, 1 - core, 0, False), places.core)
    pair = jnp.stack([jnp.where(core == 0, mine, got), jnp.where(core == 0, got, mine)], axis=0)
    pair = pair.reshape(2, own_rows, 2, blocks, block)
    pair = pair.transpose(2, 1, 3, 0, 4).reshape(2, own_rows, feed_width)
    return (
        layer_out.reshape(frames.shape),
        frames_grad.reshape(frames.shape),
        vectors[0],
        query_grad,
        key_grad,
        value_grad,
        output_grad,
        vectors[1],
        vectors[2],
        pair[0],
        pair[1],
        downs,
        vectors[3],
    )


def solution(mesh):
    split = P("seq", "sp", None)
    rows = P(("seq", "sp"), None)
    vec = P(("seq", "sp"))
    return jax.shard_map(
        on_device,
        mesh=mesh,
        in_specs=(split, P("seq", None)) + (P(),) * 11 + (split,),
        out_specs=(
            split, split, vec, rows, rows, rows, rows, vec, vec, rows, rows, rows, vec,
        ),
        check_vma=False,
    )
```

```python
import functools
import math

import jax
import jax.numpy as jnp
import numpy as np
from jax import lax
from jax.experimental import pallas as pl
from jax.experimental.pallas import tpu as pltpu
from jax.sharding import PartitionSpec as P

HEAD_DIM = 64
HALF = 64
LANES = 128
GROUP = 256
GH = GROUP // HEAD_DIM
QB = 128
KB = QB + 2 * HALF
CLIPS = 8
LN_EPS = 1e-05
RMS_EPS = 1e-06
VMEM = 58 << 20
F32 = jnp.float32
BF16 = jnp.bfloat16

NT = (((1,), (1,)), ((), ()))
NN = (((1,), (0,)), ((), ()))
TN = (((0,), (0,)), ((), ()))


def dot(a, b, dims=NN):
    return lax.dot_general(a, b, dims, preferred_element_type=F32)


def params(grid=0):
    kinds = ("arbitrary",) * grid if grid else None
    return pltpu.CompilerParams(vmem_limit_bytes=VMEM, dimension_semantics=kinds)


def cost(flops, moved, scale=0.02):
    return pl.CostEstimate(
        flops=int(flops * scale), bytes_accessed=int(moved * scale), transcendentals=0
    )


def whole(shape):
    return pl.BlockSpec(shape, lambda *_: (0,) * len(shape))


def swap_halves(v):
    lane = lax.broadcasted_iota(jnp.int32, v.shape, 1)
    return jnp.where(lane % HEAD_DIM < HEAD_DIM // 2, pltpu.roll(v, 96, 1), pltpu.roll(v, 32, 1))


def rotated(v, cos_tab, sin_tab, sign):
    pieces = []
    for at in range(0, v.shape[1], LANES):
        part = v[:, at : at + LANES]
        turned = swap_halves(part) * sin_tab
        pieces.append(part * cos_tab + turned if sign > 0 else part * cos_tab - turned)
    return jnp.concatenate(pieces, axis=1)


def project_kernel(
    seqs, x_ref, place_ref, gain_ref, wv_ref, wk_ref, wq_ref,
    all_ref, normed_ref, v_ref, k_ref, q_ref, cos_ref, sin_ref,
):
    step = pl.program_id(0)
    padded = x_ref.shape[0] // seqs
    length = padded - 2 * HALF

    def own(s):
        return slice(s * padded + HALF, s * padded + HALF + length)

    @pl.when(step == 0)
    def _():
        x = x_ref[...].astype(F32)
        centered = x - jnp.mean(x, axis=-1, keepdims=True)
        inv = lax.rsqrt(jnp.mean(centered * centered, axis=-1, keepdims=True) + LN_EPS)
        all_ref[...] = (centered * inv * gain_ref[...]).astype(BF16)
        for s in range(seqs):
            normed_ref[s * length : (s + 1) * length, :] = all_ref[own(s), :]
        v_ref[...] = dot(all_ref[...], wv_ref[...]).astype(BF16)

    @pl.when(step == 1)
    def _():
        lane = lax.broadcasted_iota(jnp.int32, (1, LANES), 1)
        exponent = (lane % (HEAD_DIM // 2)).astype(F32) * (2.0 / HEAD_DIM)
        angles = place_ref[...] * jnp.exp(-math.log(10000.0) * exponent)
        cos_ref[...] = jnp.cos(angles)
        sin_ref[...] = jnp.where(lane % HEAD_DIM < HEAD_DIM // 2, -1.0, 1.0) * jnp.sin(angles)
        v_ref[...] = dot(all_ref[...], wv_ref[...]).astype(BF16)

    @pl.when((step == 2) | (step == 3))
    def _():
        out = dot(all_ref[...], wk_ref[...])
        k_ref[...] = rotated(out, cos_ref[...], sin_ref[...], 1).astype(BF16)

    @pl.when(step >= 4)
    def _():
        for s in range(seqs):
            out = dot(all_ref[own(s), :], wq_ref[...])
            out = rotated(out, cos_ref[own(s), :], sin_ref[own(s), :], 1)
            q_ref[s * length : (s + 1) * length, :] = (out * (1.0 / math.sqrt(HEAD_DIM))).astype(BF16)


def project(x, place, gain, w_query, w_key, w_value, seqs):
    rows, width = x.shape
    own = rows - seqs * 2 * HALF
    block = width // 2

    def at(which):
        return lambda j: (0, jnp.clip(j - 2 * which, 0, 1))

    low = functools.partial(jax.ShapeDtypeStruct, dtype=BF16)
    table = jax.ShapeDtypeStruct((rows, LANES), F32)
    return pl.pallas_call(
        functools.partial(project_kernel, seqs),
        grid=(6,),
        in_specs=[whole((rows, width)), whole((rows, 1)), whole((1, width))]
        + [pl.BlockSpec((width, block), at(w)) for w in range(3)],
        out_specs=[
            whole((rows, width)),
            whole((own, width)),
            pl.BlockSpec((rows, block), at(0)),
            pl.BlockSpec((rows, block), at(1)),
            pl.BlockSpec((own, block), at(2)),
            whole((rows, LANES)),
            whole((rows, LANES)),
        ],
        out_shape=[low((rows, width)), low((own, width)), low((rows, width)), low((rows, width))]
        + [low((own, width)), table, table],
        compiler_params=params(1),
        cost_estimate=cost(6 * rows * width * width, 6 * width * width + 10 * rows * width),
        name="project",
    )(x, place, gain, w_value, w_key, w_query)


def stack_heads(block):
    lane = lax.broadcasted_iota(jnp.int32, block.shape, 1)
    zero = jnp.zeros_like(block)
    return jnp.concatenate(
        [jnp.where(lane // HEAD_DIM == h, block, zero) for h in range(GH)], axis=0
    )


def fill_keys(buf, ref):
    rows = ref.shape[0]
    buf[0:rows, :] = ref[...]
    if buf.shape[0] > rows:
        buf[rows:, :] = jnp.zeros((buf.shape[0] - rows, buf.shape[1]), buf.dtype)


def fill_queries(buf, own_ref, length):
    buf[0:length, :] = own_ref[...]
    rest = buf.shape[0] - length
    if rest:
        buf[length:, :] = jnp.zeros((rest, buf.shape[1]), buf.dtype)


def attend_kernel(span_ref, q_ref, k_ref, v_ref, o_ref, p_ref, kbuf, vbuf, qbuf, vt, ot):
    length = q_ref.shape[0]
    padded = qbuf.shape[0]
    fill_keys(kbuf, k_ref)
    fill_keys(vbuf, v_ref)
    fill_queries(qbuf, q_ref, length)
    vt[...] = vbuf[...].T
    for b in range(padded // QB):
        q4 = stack_heads(qbuf[b * QB : (b + 1) * QB, :])
        scores = dot(kbuf[b * QB : b * QB + KB, :], q4, NT)
        place = lax.broadcasted_iota(jnp.int32, (KB, QB), 0) + b * QB
        low = span_ref[0, 0:1, b * QB : (b + 1) * QB]
        high = span_ref[0, 1:2, b * QB : (b + 1) * QB]
        seen = (place >= low) & (place < high)
        for h in range(GH):
            masked = jnp.where(seen, scores[:, h * QB : (h + 1) * QB], -1e30)
            terms = jnp.exp(masked - jnp.max(masked, axis=0, keepdims=True))
            total = jnp.sum(terms, axis=0, keepdims=True)
            probs = (terms * (1.0 / total)).astype(BF16)
            p_ref[:, b * GH * QB + h * QB : b * GH * QB + (h + 1) * QB] = probs
            ot[h * HEAD_DIM : (h + 1) * HEAD_DIM, b * QB : (b + 1) * QB] = dot(
                vt[h * HEAD_DIM : (h + 1) * HEAD_DIM, b * QB : b * QB + KB], probs
            ).astype(BF16)
    o_ref[...] = ot[...].T[0:length, :]


def attend(span, query, key, value, seqs):
    rows, width = query.shape
    length = rows // seqs
    padded = span.shape[2]
    groups = width // GROUP
    keys = padded + 2 * HALF
    own = pl.BlockSpec((length, GROUP), lambda s, g: (s, g))
    near = pl.BlockSpec((length + 2 * HALF, GROUP), lambda s, g: (s, g))
    return pl.pallas_call(
        attend_kernel,
        grid=(seqs, groups),
        in_specs=[
            pl.BlockSpec((1, 2, padded), lambda s, g: (s, 0, 0)),
            own,
            near,
            near,
        ],
        out_specs=[
            own,
            pl.BlockSpec((KB, GH * padded), lambda s, g: (s, g)),
        ],
        out_shape=[
            jax.ShapeDtypeStruct((rows, width), BF16),
            jax.ShapeDtypeStruct((seqs * KB, groups * GH * padded), BF16),
        ],
        scratch_shapes=[
            pltpu.VMEM((keys, GROUP), BF16),
            pltpu.VMEM((keys, GROUP), BF16),
            pltpu.VMEM((padded, GROUP), BF16),
            pltpu.VMEM((GROUP, keys), BF16),
            pltpu.VMEM((GROUP, padded), BF16),
        ],
        compiler_params=params(2),
        cost_estimate=cost(
            2 * 2 * seqs * width * padded * KB * 4, 2 * width * (4 * rows + KB * seqs * padded // 64)
        ),
        name="attend",
    )(span, query, key, value)


def attend_back_kernel(
    p_ref, q_ref, k_ref, v_ref, g_ref, cos_ref, sin_ref,
    dq_ref, dkv_ref, near_ref,
    kbuf, vbuf, qbuf, gbuf, kt, dqt, dkb, dvb,
):
    length = q_ref.shape[0]
    padded = qbuf.shape[0]
    fill_keys(kbuf, k_ref)
    fill_keys(vbuf, v_ref)
    fill_queries(qbuf, q_ref, length)
    fill_queries(gbuf, g_ref, length)
    kt[...] = kbuf[...].T
    dkb[...] = jnp.zeros_like(dkb)
    dvb[...] = jnp.zeros_like(dvb)
    for b in range(padded // QB):
        at, keys = slice(b * QB, (b + 1) * QB), slice(b * QB, b * QB + KB)
        q4 = stack_heads(qbuf[at, :])
        g4 = stack_heads(gbuf[at, :])
        probs = p_ref[:, b * GH * QB : (b + 1) * GH * QB]
        grads = dot(vbuf[keys, :], g4, NT)
        pieces = []
        for h in range(GH):
            part = probs[:, h * QB : (h + 1) * QB].astype(F32)
            grad = grads[:, h * QB : (h + 1) * QB]
            delta = jnp.sum(part * grad, axis=0, keepdims=True)
            low = (part * (grad - delta)).astype(BF16)
            pieces.append(low)
            dqt[h * HEAD_DIM : (h + 1) * HEAD_DIM, at] = dot(
                kt[h * HEAD_DIM : (h + 1) * HEAD_DIM, keys], low
            )
        dvb[keys, :] += dot(probs, g4)
        dkb[keys, :] += dot(jnp.concatenate(pieces, axis=1), q4)
    cos_tab, sin_tab = cos_ref[...], sin_ref[...]
    middle = slice(HALF, HALF + length)
    dq = dqt[...].T[0:length, :] * (1.0 / math.sqrt(HEAD_DIM))
    dq_ref[...] = rotated(dq, cos_tab[middle], sin_tab[middle], -1).astype(BF16)
    span = length + 2 * HALF
    dk = rotated(dkb[0:span, :], cos_tab, sin_tab, -1).astype(BF16)
    dv = dvb[0:span, :].astype(BF16)
    for i, grad in enumerate((dk, dv)):
        dkv_ref[i] = grad[middle]
        near_ref[i] = grad


def attend_back(probs, query, key, value, grad, cos_tab, sin_tab, seqs):
    rows, width = query.shape
    length = rows // seqs
    padded = -(-length // QB) * QB
    groups = width // GROUP
    keys = padded + 2 * HALF
    own = pl.BlockSpec((length, GROUP), lambda s, g: (s, g))
    both = pl.BlockSpec((2, length, GROUP), lambda s, g: (0, s, g))
    both_near = pl.BlockSpec((2, length + 2 * HALF, GROUP), lambda s, g: (0, s, g))
    near = pl.BlockSpec((length + 2 * HALF, GROUP), lambda s, g: (s, g))
    table = pl.BlockSpec((length + 2 * HALF, LANES), lambda s, g: (s, 0))
    out = jax.ShapeDtypeStruct((rows, width), BF16)
    out_both = jax.ShapeDtypeStruct((2, rows, width), BF16)
    out_near = jax.ShapeDtypeStruct((2, rows + seqs * 2 * HALF, width), BF16)
    return pl.pallas_call(
        attend_back_kernel,
        grid=(seqs, groups),
        in_specs=[
            pl.BlockSpec((KB, GH * padded), lambda s, g: (s, g)),
            own,
            near,
            near,
            own,
            table,
            table,
        ],
        out_specs=[own, both, both_near],
        out_shape=[out, out_both, out_near],
        scratch_shapes=[
            pltpu.VMEM((keys, GROUP), BF16),
            pltpu.VMEM((keys, GROUP), BF16),
            pltpu.VMEM((padded, GROUP), BF16),
            pltpu.VMEM((padded, GROUP), BF16),
            pltpu.VMEM((GROUP, keys), BF16),
            pltpu.VMEM((GROUP, padded), F32),
            pltpu.VMEM((keys, GROUP), F32),
            pltpu.VMEM((keys, GROUP), F32),
        ],
        compiler_params=params(2),
        cost_estimate=cost(
            2 * 4 * seqs * width * padded * KB * 4, 2 * width * (8 * rows + KB * seqs * padded // 64)
        ),
        name="attend_back",
    )(probs, query, key, value, grad, cos_tab, sin_tab)


def edges_kernel(seqs, flags_ref, from_ref, left_ref, right_ref, to_ref, buf, sems):
    length = from_ref.shape[1] // seqs
    places = [
        (i, s, e, pl.ds(s * length + e * (length - HALF), HALF))
        for i in range(2)
        for s in range(seqs)
        for e in range(2)
    ]
    copies = [
        (from_ref.at[i, rows, :], to_ref.at[i, rows, :], buf.at[at]) for at, (i, _, _, rows) in enumerate(places)
    ]
    for at, (src, _, mid) in enumerate(copies):
        pltpu.make_async_copy(src, mid, sems.at[0, at]).start()
    for at, (src, _, mid) in enumerate(copies):
        pltpu.make_async_copy(src, mid, sems.at[0, at]).wait()
    for at, (i, s, e, _) in enumerate(places):
        got = (right_ref if e else left_ref)[i, s].astype(F32) * flags_ref[e].astype(F32)
        buf[at] = (buf[at].astype(F32) + got).astype(BF16)
    for at, (_, dst, mid) in enumerate(copies):
        pltpu.make_async_copy(mid, dst, sems.at[1, at]).start()
    for at, (_, dst, mid) in enumerate(copies):
        pltpu.make_async_copy(mid, dst, sems.at[1, at]).wait()


def add_edges(flags, grads, left, right):
    seqs = left.shape[1]
    hbm = pl.BlockSpec(memory_space=pl.ANY)
    return pl.pallas_call(
        functools.partial(edges_kernel, seqs),
        grid_spec=pltpu.PrefetchScalarGridSpec(
            num_scalar_prefetch=1,
            grid=(1,),
            in_specs=[hbm, whole(left.shape), whole(right.shape)],
            out_specs=hbm,
            scratch_shapes=[
                pltpu.VMEM((4 * seqs, HALF, grads.shape[2]), BF16),
                pltpu.SemaphoreType.DMA((2, 4 * seqs)),
            ],
        ),
        out_shape=jax.ShapeDtypeStruct(grads.shape, BF16),
        input_output_aliases={1: 0},
        compiler_params=params(1),
        cost_estimate=cost(left.size, 8 * left.size),
        name="add_edges",
    )(flags, grads, left, right)


def out_proj_kernel(m_ref, x_ref, w_ref, scale_ref, gain_ref, attn_ref, in_ref):
    attn = dot(m_ref[...], w_ref[...])
    attn_ref[...] = attn.astype(BF16)
    middle = x_ref[...].astype(F32) + scale_ref[...] * attn
    inv = lax.rsqrt(jnp.mean(middle * middle, axis=-1, keepdims=True) + RMS_EPS)
    in_ref[...] = (middle * inv * gain_ref[...]).astype(BF16)


def out_proj(mixed, x, w_output, scale, gain):
    rows, width = x.shape
    block = rows // 2
    row = pl.BlockSpec((block, width), lambda i: (i, 0))
    return pl.pallas_call(
        out_proj_kernel,
        grid=(rows // block,),
        in_specs=[row, row, whole((width, width)), whole((1, width)), whole((1, width))],
        out_specs=[row, row],
        out_shape=[
            jax.ShapeDtypeStruct((rows, width), BF16),
            jax.ShapeDtypeStruct((rows, width), BF16),
        ],
        compiler_params=params(1),
        cost_estimate=cost(2 * rows * width * width, 2 * rows * width * 5 + 2 * width * width),
        name="out_proj",
    )(mixed, x, w_output, scale, gain)


def hidden_grad_kernel(core_ref, own_ref, peer_ref, scale_ref, one_ref, two_ref, low_ref, out_ref):
    rows = own_ref.shape[0]
    block = one_ref.shape[0]

    @pl.when(pl.program_id(0) == 0)
    def _():
        low_ref[0:rows, :] = (own_ref[...].astype(F32) * scale_ref[...]).astype(BF16)
        low_ref[rows:, :] = (peer_ref[...].astype(F32) * scale_ref[...]).astype(BF16)

    out_ref[:, :block] = dot(low_ref[...], one_ref[...], NT).astype(BF16)
    out_ref[:, block:] = dot(low_ref[...], two_ref[...], NT).astype(BF16)


def hidden_grad(core, own, peer, scale, w_down, block):
    rows, width = own.shape
    count = w_down.shape[0] // block // 4
    half = w_down.shape[0] // 2
    return pl.pallas_call(
        hidden_grad_kernel,
        grid_spec=pltpu.PrefetchScalarGridSpec(
            num_scalar_prefetch=1,
            grid=(count,),
            in_specs=[
                whole((rows, width)),
                whole((rows, width)),
                whole((1, width)),
                pl.BlockSpec((block, width), lambda j, c: (4 * j + c[0], 0)),
                pl.BlockSpec((block, width), lambda j, c: (4 * j + 2 + c[0], 0)),
            ],
            out_specs=[
                whole((2 * rows, width)),
                pl.BlockSpec((2 * rows, 2 * block), lambda j, c: (0, j)),
            ],
        ),
        out_shape=[
            jax.ShapeDtypeStruct((2 * rows, width), BF16),
            jax.ShapeDtypeStruct((2 * rows, half), BF16),
        ],
        compiler_params=params(1),
        cost_estimate=cost(
            4 * rows * width * half, 2 * (4 * rows * width + half * (width + 2 * rows))
        ),
        name="hidden_grad",
    )(core, own, peer, scale, w_down, w_down)


def halves_of(value, bit, inner):
    rows, columns = value.shape
    both = value.reshape(rows // (2 * inner), 2, inner, columns)
    zero, one = both[:, 0], both[:, 1]
    out = jnp.where(bit == 0, one, zero).reshape(rows // 2, columns)
    stay = jnp.where(bit == 0, zero, one).reshape(rows // 2, columns)
    return out, stay


def feed_kernel(inners, core_ref, xo_ref, xp_ref, gh_ref, wg_ref, wu_ref, *refs):
    hid_ref, gg_ref, gu_ref, *outs, x_all = refs[-8:]
    rows = xo_ref.shape[0]

    @pl.when(pl.program_id(0) == 0)
    def _():
        x_all[0:rows, :] = xo_ref[...]
        x_all[rows:, :] = xp_ref[...]

    for at in (0, rows):
        part = slice(at, at + rows)
        gate = dot(x_all[part, :], wg_ref[...])
        up = dot(x_all[part, :], wu_ref[...])
        grad = gh_ref[part, :].astype(F32)
        sig = 1.0 / (1.0 + jnp.exp(-gate))
        act = gate * sig
        hid_ref[part, :] = (act * up).astype(BF16)
        gg_ref[part, :] = (grad * up * sig * (1.0 + gate * (1.0 - sig))).astype(BF16)
        gu_ref[part, :] = (grad * act).astype(BF16)
    for i, src in enumerate((gg_ref, gu_ref)):
        out, stay = halves_of(dot(x_all[...], src[...], TN), core_ref[1 + i], inners[i])
        outs[2 * i][...] = out.astype(BF16)
        outs[2 * i + 1][...] = stay.astype(BF16)


def feed(core, x_own, x_peer, grad_hidden, w_gate, w_up, block, first, count, before, inners):
    rows, width = x_own.shape
    half = grad_hidden.shape[1]
    wide = pl.BlockSpec((2 * rows, block), lambda j, c: (0, j + first))
    weight = pl.BlockSpec((width, block), lambda j, c: (0, 2 * (j + first) + c[0]))
    kept = jax.ShapeDtypeStruct((2 * rows, half), BF16)
    grads = jax.ShapeDtypeStruct((width // 2, count * block), BF16)
    any_spec = pl.BlockSpec(memory_space=pl.ANY)
    return pl.pallas_call(
        functools.partial(feed_kernel, inners),
        grid_spec=pltpu.PrefetchScalarGridSpec(
            num_scalar_prefetch=1,
            grid=(count,),
            in_specs=[whole((rows, width)), whole((rows, width)), wide, weight, weight]
            + [any_spec] * len(before),
            out_specs=[wide] * 3 + [pl.BlockSpec((width // 2, block), lambda j, c: (0, j))] * 4,
            scratch_shapes=[pltpu.VMEM((2 * rows, width), BF16)],
        ),
        out_shape=[kept] * 3 + [grads] * 4,
        input_output_aliases={6 + i: i for i in range(len(before))},
        compiler_params=params(1),
        cost_estimate=cost(
            2 * 2 * rows * width * block * count * 4,
            2 * (4 * rows * width + count * block * (8 * rows + 4 * width)),
        ),
        name="feed",
    )(core, x_own, x_peer, grad_hidden, w_gate, w_up, *before)


def down_kernel(each, inners, bits_ref, hid_ref, low_ref, *outs):
    value = dot(hid_ref[...], low_ref[...], TN)
    rows, width = value.shape
    value = value.reshape(rows // (2 * each), 2, each, width)
    for i in range(2):
        part = value[:, i].reshape(rows // 2, width)
        out, stay = halves_of(part, bits_ref[1 + i], inners[i])
        outs[2 * i][...] = out.astype(BF16)
        outs[2 * i + 1][...] = stay.astype(BF16)


def down(bits, hidden, low, each, inners):
    rows, half = hidden.shape
    width = low.shape[1]
    block = 512
    out = jax.ShapeDtypeStruct((half // 4, width), BF16)
    return pl.pallas_call(
        functools.partial(down_kernel, each, inners),
        grid_spec=pltpu.PrefetchScalarGridSpec(
            num_scalar_prefetch=1,
            grid=(half // block,),
            in_specs=[
                pl.BlockSpec((rows, block), lambda j, c: (0, j)),
                whole((rows, width)),
            ],
            out_specs=[pl.BlockSpec((block // 4, width), lambda j, c: (j, 0))] * 4,
        ),
        out_shape=[out] * 4,
        compiler_params=params(1),
        cost_estimate=cost(
            2 * rows * half * width, 2 * (rows * half + rows * width + half * width)
        ),
        name="down_weight",
    )(bits, hidden, low)


def in_halves(value, refs):
    half = value.shape[1] // 2
    refs[0][...] = value[:, :half]
    refs[1][...] = value[:, half:]


def feed_back_kernel(core_ref, *refs):
    *peer_refs, own_ref, acc = refs[-4:]
    part, step = pl.program_id(0), pl.program_id(1)
    block = refs[2].shape[1]
    total = None
    for i in range(2):
        for half in range(2):
            out = dot(refs[i][:, half * block : (half + 1) * block], refs[2 + 2 * i + half][...], NT)
            total = out if total is None else total + out
    last = pl.num_programs(1) - 1

    @pl.when(step == 0)
    def _():
        acc[...] = total

    @pl.when((step > 0) & (step < last))
    def _():
        acc[...] += total

    @pl.when((step == last) & (part == 0))
    def _():
        in_halves((acc[...] + total).astype(BF16), peer_refs)

    @pl.when((step == last) & (part == 1))
    def _():
        own_ref[...] = (acc[...] + total).astype(BF16)


def feed_back(core, grad_gate, grad_up, w_gate, w_up, block):
    rows, half = grad_gate.shape
    rows = rows // 2
    width = w_gate.shape[0]
    tall = pl.BlockSpec((rows, 2 * block), lambda p, j, c: (1 - p, j))
    one = pl.BlockSpec((width, block), lambda p, j, c: (0, 4 * j + c[0]))
    two = pl.BlockSpec((width, block), lambda p, j, c: (0, 4 * j + 2 + c[0]))
    return pl.pallas_call(
        feed_back_kernel,
        grid_spec=pltpu.PrefetchScalarGridSpec(
            num_scalar_prefetch=1,
            grid=(2, half // block // 2),
            in_specs=[tall, tall, one, two, one, two],
            out_specs=[whole((rows, width // 2))] * 2 + [whole((rows, width))],
            scratch_shapes=[pltpu.VMEM((rows, width), F32)],
        ),
        out_shape=[jax.ShapeDtypeStruct((rows, width // 2), BF16)] * 2
        + [jax.ShapeDtypeStruct((rows, width), BF16)],
        compiler_params=params(2),
        cost_estimate=cost(8 * rows * half * width, 8 * (rows * half + half * width)),
        name="feed_back",
    )(core, grad_gate, grad_up, w_gate, w_gate, w_up, w_up)


def feed_out_kernel(core_ref, hid_ref, one_ref, two_ref, *refs):
    *peer_refs, own_ref, acc = refs
    part, step = pl.program_id(0), pl.program_id(1)
    block = one_ref.shape[0]
    total = dot(hid_ref[:, :block], one_ref[...]) + dot(hid_ref[:, block:], two_ref[...])
    last = pl.num_programs(1) - 1

    @pl.when(step == 0)
    def _():
        acc[...] = total

    @pl.when((step > 0) & (step < last))
    def _():
        acc[...] += total

    @pl.when((step == last) & (part == 0))
    def _():
        in_halves((acc[...] + total).astype(BF16), peer_refs)

    @pl.when((step == last) & (part == 1))
    def _():
        own_ref[...] = (acc[...] + total).astype(BF16)


def feed_out(core, hidden, w_down, block):
    rows, half = hidden.shape
    rows = rows // 2
    width = w_down.shape[1]
    return pl.pallas_call(
        feed_out_kernel,
        grid_spec=pltpu.PrefetchScalarGridSpec(
            num_scalar_prefetch=1,
            grid=(2, half // block // 2),
            in_specs=[
                pl.BlockSpec((rows, 2 * block), lambda p, j, c: (1 - p, j)),
                pl.BlockSpec((block, width), lambda p, j, c: (4 * j + c[0], 0)),
                pl.BlockSpec((block, width), lambda p, j, c: (4 * j + 2 + c[0], 0)),
            ],
            out_specs=[whole((rows, width // 2))] * 2 + [whole((rows, width))],
            scratch_shapes=[pltpu.VMEM((rows, width), F32)],
        ),
        out_shape=[jax.ShapeDtypeStruct((rows, width // 2), BF16)] * 2
        + [jax.ShapeDtypeStruct((rows, width), BF16)],
        compiler_params=params(2),
        cost_estimate=cost(4 * rows * half * width, 4 * (rows * half + half * width), 4),
        name="feed_out",
    )(core, hidden, w_down, w_down)


def join_kernel(
    x_ref, attn_ref, g_ref, in_ref, got_one_ref, got_two_ref, attn_scale_ref, gain_ref, w_ref,
    grad_attn_ref, grad_mixed_ref, middle_ref, sums_ref,
):
    x = x_ref[...].astype(F32)
    attn = attn_ref[...].astype(F32)
    grad_y = g_ref[...].astype(F32)
    got = jnp.concatenate([got_one_ref[...], got_two_ref[...]], axis=1)
    grad_in = in_ref[...].astype(F32) + got.astype(F32)
    middle = x + attn_scale_ref[...] * attn
    inv = lax.rsqrt(jnp.mean(middle * middle, axis=-1, keepdims=True) + RMS_EPS)
    unit = middle * inv
    scaled = grad_in * gain_ref[...]
    grad_middle = grad_y + inv * (scaled - unit * jnp.mean(scaled * unit, axis=-1, keepdims=True))
    middle_ref[...] = grad_middle.astype(BF16)
    grad_attn = (attn_scale_ref[...] * grad_middle).astype(BF16)
    grad_attn_ref[...] = grad_attn
    grad_mixed_ref[...] = dot(grad_attn, w_ref[...], NT).astype(BF16)

    @pl.when(pl.program_id(0) == 0)
    def _():
        sums_ref[...] = jnp.zeros_like(sums_ref)

    sums_ref[0:1, :] += jnp.sum(grad_middle * attn, axis=0, keepdims=True)
    sums_ref[1:2, :] += jnp.sum(grad_in * unit, axis=0, keepdims=True)


def join(x, attn, grad_y, grad_in, got, attn_scale, gain, w_output):
    rows, width = x.shape
    block = rows // 2
    row = pl.BlockSpec((block, width), lambda i: (i, 0))
    half = pl.BlockSpec((block, width // 2), lambda i: (i, 0))
    vec = whole((1, width))
    low = jax.ShapeDtypeStruct((rows, width), BF16)
    return pl.pallas_call(
        join_kernel,
        grid=(rows // block,),
        in_specs=[row] * 4 + [half] * 2 + [vec] * 2 + [whole((width, width))],
        out_specs=[row] * 3 + [whole((8, width))],
        out_shape=[
            low,
            low,
            low,
            jax.ShapeDtypeStruct((8, width), F32),
        ],
        compiler_params=params(1),
        cost_estimate=cost(2 * rows * width * width, rows * width * 22 + 2 * width * width),
        name="join",
    )(x, attn, grad_y, grad_in, *got, attn_scale, gain, w_output)


def finish_kernel(
    x_ref, attn_ref, g_ref, out_ref, got_one_ref, got_two_ref, attn_scale_ref, mlp_scale_ref, layer_ref, sums_ref
):
    got = jnp.concatenate([got_one_ref[...], got_two_ref[...]], axis=1)
    down_out = out_ref[...].astype(F32) + got.astype(F32)
    middle = x_ref[...].astype(F32) + attn_scale_ref[...] * attn_ref[...].astype(F32)
    layer_ref[...] = (middle + mlp_scale_ref[...] * down_out).astype(BF16)

    @pl.when(pl.program_id(0) == 0)
    def _():
        sums_ref[...] = jnp.zeros_like(sums_ref)

    sums_ref[0:1, :] += jnp.sum(g_ref[...].astype(F32) * down_out, axis=0, keepdims=True)


def finish(x, attn, grad_y, out, got, attn_scale, mlp_scale):
    rows, width = x.shape
    block = rows // 2
    row = pl.BlockSpec((block, width), lambda i: (i, 0))
    half = pl.BlockSpec((block, width // 2), lambda i: (i, 0))
    vec = whole((1, width))
    return pl.pallas_call(
        finish_kernel,
        grid=(rows // block,),
        in_specs=[row] * 4 + [half] * 2 + [vec] * 2,
        out_specs=[row, whole((8, width))],
        out_shape=[
            jax.ShapeDtypeStruct((rows, width), BF16),
            jax.ShapeDtypeStruct((8, width), F32),
        ],
        compiler_params=params(1),
        cost_estimate=cost(8 * rows * width, rows * width * 16),
        name="finish",
    )(x, attn, grad_y, out, *got, attn_scale, mlp_scale)


def weight_grad_kernel(inner, order, counts, bit_ref, *refs):
    *out_refs, stay_ref = refs[-3:]
    step = pl.program_id(0)
    lefts = [refs[i] for i in order]
    rights = refs[max(order) + 1 : -3]
    first = 0
    for left, right, count, out_ref in zip(lefts, rights, counts, out_refs):

        @pl.when((step >= first) & (step < first + count))
        def _(left=left, right=right, out_ref=out_ref):
            rows = right[...].reshape(right.shape[-2:])
            out, stay = halves_of(dot(left[...], rows, TN), bit_ref[0], inner)
            out_ref[...] = out.astype(BF16)
            stay_ref[...] = stay.astype(BF16)

        first += count


def weight_grad(bit, inner, pairs, name, scale):
    block = 512
    width = pairs[0][0].shape[1]
    lefts = []
    for left, _ in pairs:
        if not any(left is other for other in lefts):
            lefts.append(left)
    order = [[left is other for other in lefts].index(True) for left, _ in pairs]
    counts, specs, rights, first = [], [], [], 0
    for left, right in pairs:
        rows = left.shape[0]
        array, part = right if isinstance(right, tuple) else (right, None)
        count = array.shape[-1] // block
        at = lambda j, first=first, count=count: jnp.clip(j - first, 0, count - 1)
        if part is None:
            specs.append(pl.BlockSpec((rows, block), lambda j, c, at=at: (0, at(j))))
        else:
            specs.append(
                pl.BlockSpec((1, rows, block), lambda j, c, at=at, part=part: (part, 0, at(j)))
            )
        rights.append(array)
        counts.append(count)
        first += count
    sends = [
        pl.BlockSpec((width // 2, block), lambda j, c, k=k: (0, jnp.clip(j - k * counts[0], 0, counts[0] - 1)))
        for k in range(2)
    ]
    out = jax.ShapeDtypeStruct((width // 2, counts[0] * block), BF16)
    stay = jax.ShapeDtypeStruct((width // 2, first * block), BF16)
    return pl.pallas_call(
        functools.partial(weight_grad_kernel, inner, order, counts),
        grid_spec=pltpu.PrefetchScalarGridSpec(
            num_scalar_prefetch=1,
            grid=(first,),
            in_specs=[whole(left.shape) for left in lefts] + specs,
            out_specs=sends + [pl.BlockSpec((width // 2, block), lambda j, c: (0, j))],
        ),
        out_shape=[out, out, stay],
        compiler_params=params(1),
        cost_estimate=cost(
            2 * rows * width * first * block,
            2 * (len(lefts) * rows * width + (rows + width) * first * block),
            scale,
        ),
        name=name,
    )(bit, *lefts, *rights)


def input_grad_kernel(
    x_ref, gq_ref, gk_ref, gv_ref, middle_ref, gain_ref, wq_ref, wk_ref, wv_ref, out_ref, sums_ref
):
    grad = (
        dot(gq_ref[...], wq_ref[...], NT)
        + dot(gk_ref[0], wk_ref[...], NT)
        + dot(gv_ref[0], wv_ref[...], NT)
    )
    x = x_ref[...].astype(F32)
    centered = x - jnp.mean(x, axis=-1, keepdims=True)
    inv = lax.rsqrt(jnp.mean(centered * centered, axis=-1, keepdims=True) + LN_EPS)
    unit = centered * inv
    scaled = grad * gain_ref[...]
    back = inv * (
        scaled
        - jnp.mean(scaled, axis=-1, keepdims=True)
        - unit * jnp.mean(scaled * unit, axis=-1, keepdims=True)
    )
    out_ref[...] = (middle_ref[...].astype(F32) + back).astype(BF16)

    @pl.when(pl.program_id(0) == 0)
    def _():
        sums_ref[...] = jnp.zeros_like(sums_ref)

    sums_ref[0:1, :] += jnp.sum(grad * unit, axis=0, keepdims=True)


def input_grad(x, gq, gkv, grad_middle, gain, w_query, w_key, w_value):
    rows, width = x.shape
    block = rows // 2
    row = pl.BlockSpec((block, width), lambda i: (i, 0))
    square = whole((width, width))
    return pl.pallas_call(
        input_grad_kernel,
        grid=(rows // block,),
        in_specs=[
            row,
            row,
            pl.BlockSpec((1, block, width), lambda i: (0, i, 0)),
            pl.BlockSpec((1, block, width), lambda i: (1, i, 0)),
            row,
            whole((1, width)),
        ]
        + [square] * 3,
        out_specs=[row, whole((8, width))],
        out_shape=[
            jax.ShapeDtypeStruct((rows, width), BF16),
            jax.ShapeDtypeStruct((8, width), F32),
        ],
        compiler_params=params(1),
        cost_estimate=cost(2 * 3 * rows * width * width, rows * width * 14 + 6 * width * width, 4),
        name="input_grad",
    )(x, gq, gkv, gkv, grad_middle, gain, w_query, w_key, w_value)


def log2(n):
    return n.bit_length() - 1


class Places:
    def __init__(self):
        self.n_seq, self.n_sp = lax.axis_size("seq"), lax.axis_size("sp")
        self.sp_bits = log2(self.n_sp)
        self.count = self.sp_bits + log2(self.n_seq)
        self.core = self.sp_bits
        self.me = lax.axis_index("seq") * self.n_sp + lax.axis_index("sp")
        self.down_bits = [b for b in reversed(range(self.count)) if b != self.core]

    def swap(self, value, bit):
        if bit < self.sp_bits:
            axis, size, at = "sp", self.n_sp, bit
        else:
            axis, size, at = "seq", self.n_seq, bit - self.sp_bits
        return lax.ppermute(value, axis, [(i, i ^ (1 << at)) for i in range(size)])

    def send(self, value, flip):
        pairs = [(i, i ^ flip) for i in range(1 << self.count)]
        return lax.ppermute(value, ("seq", "sp"), pairs)

    def own(self, bit):
        return (self.me >> bit) & 1


def round_kernel(has, inners, bits_ref, *refs):
    two, one, new = has
    refs = list(refs)
    take = lambda n: [refs.pop(0) for _ in range(n)]
    got_x, got_y = take(2) if one or two else (None, None)
    keep_a2, keep_b2 = take(2) if two else (None, None)
    keep_a1, keep_b1 = take(2) if one else (None, None)
    fresh = take({"sent": 2, "core": 4, "": 0}[new])
    buf_x, buf_y = take(2) if one or new else (None, None)
    bit_x, bit_y, bit_z = bits_ref[1], bits_ref[2], bits_ref[3]
    first = keep_a2.shape[0] if two else 0
    added = lambda keep, got, at: keep[...].astype(F32) + got[at : at + keep.shape[0], :].astype(F32)
    if two:
        z_send, z_keep = take(2)
        half = first // 2
        for i, total in enumerate((added(keep_a2, got_y, 0), added(keep_b2, got_x, 0))):
            out, stay = halves_of(total, bit_z, inners["two"])
            z_send[i * half : (i + 1) * half, :] = out.astype(BF16)
            z_keep[i * half : (i + 1) * half, :] = stay.astype(BF16)
    at = 0
    if one:
        stay_a, stay_b = take(2)
        at = keep_a1.shape[0] // 2
        total = added(keep_a1, got_x, first)
        out, stay = halves_of(total, bit_y, inners["one_a"])
        buf_y[0:at, :], stay_a[...] = out.astype(BF16), stay.astype(BF16)
        total = added(keep_b1, got_y, first)
        out, stay = halves_of(total, bit_x, inners["one_b"])
        buf_x[0:at, :], stay_b[...] = out.astype(BF16), stay.astype(BF16)
    if new == "sent":
        buf_x[at:, :] = fresh[0][...]
        buf_y[at:, :] = fresh[1][...]
    if new == "core":
        stays = take(2)
        for i, (buf, bit) in enumerate(((buf_x, bit_x), (buf_y, bit_y))):
            total = fresh[2 * i][...].astype(F32) + fresh[2 * i + 1][...].astype(F32)
            out, stay = halves_of(total, bit, inners["new"][i])
            buf[at:, :], stays[i][...] = out.astype(BF16), stay.astype(BF16)


class Rounds:
    def __init__(self, places, x, y, z, width):
        self.places, self.x, self.y, self.z, self.width = places, x, y, z, width
        self.one = self.two = None
        self.got = []

    def inner(self, group, without, bit):
        bits = [b for b in sorted(group["bits"], reverse=True) if b not in without]
        return group["each"] << (len(bits) - 1 - bits.index(bit))

    def first_inners(self, bits, each):
        group = {"bits": bits, "each": each}
        return [self.inner(group, (), self.x), self.inner(group, (), self.y)]

    def send(self, buf_x, buf_y):
        self.got = [self.places.swap(buf_x, self.x), self.places.swap(buf_y, self.y)]

    def begin(self, parts, bits, each):
        self.one = {"bits": bits, "each": each, "keep": [parts[1], parts[3]]}
        self.send(parts[0], parts[2])

    def run(self, flags, new="", arrays=(), bits=(), each=0):
        one, two, width = self.one, self.two, self.width
        steps = 2
        block = width // steps
        tall = lambda rows, at=0: pl.BlockSpec((rows, block), lambda j, b: (0, j + at))
        ins, specs, outs, inners = [], [], [], {}
        if one or two:
            ins += self.got
        if two:
            ins += two["keep"]
            rows = two["keep"][0].shape[0]
            outs += [rows, rows]
            inners["two"] = self.inner(two, (self.x, self.y), self.z)
        if one:
            ins += one["keep"]
            rows = one["keep"][0].shape[0] // 2
            outs += [rows, rows]
            inners["one_a"] = self.inner(one, (self.x,), self.y)
            inners["one_b"] = self.inner(one, (self.y,), self.x)
        specs += [tall(v.shape[0]) for v in ins]
        sent = one["keep"][0].shape[0] // 2 if one else 0
        group = {"bits": [b for b in bits], "each": each}
        if new == "sent":
            ins += [arrays[0], arrays[2]]
            specs += [tall(arrays[0].shape[0]), tall(arrays[2].shape[0])]
            sent += arrays[0].shape[0]
            group["keep"] = [arrays[1], arrays[3]]
        if new == "core":
            keep, got_a, got_b = arrays
            rows = keep.shape[0]
            ins += [keep, got_a, keep, got_b]
            specs += [tall(rows), tall(rows), tall(rows, steps), tall(rows)]
            sent += rows // 2
            outs += [rows // 2, rows // 2]
            inners["new"] = self.first_inners(bits, each)
        if one or new:
            outs = [sent, sent] + outs
        size = sum(v.shape[0] for v in ins) * width
        results = list(
            pl.pallas_call(
                functools.partial(round_kernel, (bool(two), bool(one), new), inners),
                grid_spec=pltpu.PrefetchScalarGridSpec(
                    num_scalar_prefetch=1,
                    grid=(steps,),
                    in_specs=specs,
                    out_specs=[tall(rows) for rows in outs],
                ),
                out_shape=[jax.ShapeDtypeStruct((rows, width), BF16) for rows in outs],
                compiler_params=params(1),
                cost_estimate=cost(2 * size, 4 * size),
                name="round",
            )(flags, *ins)
        )
        if one or new:
            buf_x, buf_y = results[:2]
            results = results[2:]
        done = None
        if two:
            done = Piece(self.places, [b for b in two["bits"] if b not in (self.x, self.y)], two["each"])
            done.fork(results[0], results[1], self.z)
            results = results[2:]
        self.two = None
        if one:
            self.two = dict(one, keep=results[:2])
            results = results[2:]
        if new == "core":
            group["keep"] = results
        self.one = group if new else None
        self.got = []
        if one or new:
            self.send(buf_x, buf_y)
        return done


class Piece:
    def __init__(self, places, bits, each):
        self.places, self.bits, self.each = places, sorted(bits, reverse=True), each
        self.keep = self.got = None
        self.at = 0

    def inner(self, bit):
        return self.each << (len(self.bits) - 1 - self.bits.index(bit))

    def fork(self, out, stay, bit):
        self.bits.remove(bit)
        self.keep, self.got = stay, self.places.swap(out, bit)
        self.at, self.columns = 0, stay.shape[1]

    def split(self, bit):
        rows, columns = self.keep.shape
        inner = self.inner(bit)
        both = self.keep.reshape(rows // (2 * inner), 2, inner, columns)
        at = self.places.own(bit)
        out = lax.dynamic_index_in_dim(both, 1 - at, 1, False).reshape(rows // 2, columns)
        stay = lax.dynamic_index_in_dim(both, at, 1, False).reshape(rows // 2, columns)
        self.fork(out, stay, bit)

    def add(self, low=True):
        cols = slice(self.at * self.columns, (self.at + 1) * self.columns)
        self.keep = self.keep[:, cols].astype(F32) + self.got[:, cols].astype(F32)
        self.at = 0
        if low:
            self.keep = self.keep.astype(BF16)


def share(places, value, bits, group):
    axes = [bits.index(b) for b in group]

    def part(flip):
        out = value
        for b, axis in zip(group, axes):
            out = lax.dynamic_index_in_dim(out, places.own(b) ^ ((flip >> b) & 1), axis, True)
        return lax.squeeze(out, axes)

    flips = [sum(b << g for b, g in zip(f, group)) for f in np.ndindex(*(2,) * len(group))]
    return [part(0)] + [places.send(part(f), f) for f in flips if f]


def hold(small, *arrays):
    small, *arrays = lax.optimization_barrier((small, *arrays))
    return (small, *arrays)


def meet(small, arrays=(), pieces=(), rounds=None):
    many = list(arrays), [p.got for p in pieces], list(rounds.got) if rounds else []
    small, (arrays, gots, round_gots) = lax.optimization_barrier((small, many))
    for p, g in zip(pieces, gots):
        p.got = g
    if rounds:
        rounds.got = round_gots
    return (small, *arrays)


def on_device(
    frames, clip_ids, norm_gain, w_query, w_key, w_value, w_output, attn_scale,
    mlp_gain, w_gate, w_up, w_down, mlp_scale, out_grad,
):
    places = Places()
    seqs, length, width = frames.shape
    total_len = clip_ids.shape[1]
    rows = seqs * length
    n_sp, n_seq = places.n_sp, places.n_seq
    devices = n_sp * n_seq
    feed_width = w_gate.shape[1]
    own_rows = width // devices
    feed_rows = feed_width // devices
    block = feed_rows * n_sp
    core = lax.axis_index("seq") & 1
    sp = lax.axis_index("sp")
    sp_bits = list(reversed(range(places.core)))
    seq_bits = list(range(places.core + 1, places.count))
    x_bit, y_bit, z_bit = sp_bits[0], seq_bits[0], seq_bits[1]
    late = seq_bits[2:] + sp_bits[1:]
    every = list(range(places.count))
    not_core = [b for b in every if b != places.core]
    flags = jnp.stack([places.own(b) for b in (places.core, x_bit, y_bit, z_bit)]).astype(jnp.int32)
    rounds = Rounds(places, x_bit, y_bit, z_bit, width)

    x = frames.reshape(rows, width)
    grad_y = out_grad.reshape(rows, width)

    def neighbours(last, first):
        if n_sp == 2:
            got = lax.ppermute(jnp.where(sp == 0, last, first), "sp", [(0, 1), (1, 0)])
            return got, got
        return (
            lax.ppermute(last, "sp", [(i, i + 1) for i in range(n_sp - 1)]),
            lax.ppermute(first, "sp", [(i + 1, i) for i in range(n_sp - 1)]),
        )

    has = jnp.stack([sp > 0, sp < n_sp - 1]).astype(jnp.int32)
    from_left, from_right = neighbours(frames[:, length - HALF :], frames[:, :HALF])
    grad_y_peer = places.swap(grad_y, places.core)

    start = sp * length
    near = lax.dynamic_slice_in_dim(
        jnp.pad(clip_ids, ((0, 0), (HALF, HALF))), start, length + 2 * HALF, 1
    )
    ids = jnp.arange(CLIPS + 1, dtype=jnp.int32)
    begins = jnp.sum((clip_ids[:, None, :] < ids[:, None]).astype(jnp.int32), axis=-1)
    is_id = near[:, None, :] == ids[:CLIPS, None]
    first = jnp.sum(jnp.where(is_id, begins[:, :CLIPS, None], 0), axis=1)
    end = jnp.sum(jnp.where(is_id, begins[:, 1:, None], 0), axis=1)
    frame = lax.broadcasted_iota(jnp.int32, near.shape, 1) + (start - HALF)
    place = (frame - first).astype(F32).reshape(-1, 1)
    mid = slice(HALF, HALF + length)
    low = jnp.maximum(frame - HALF, first)[:, mid] - (start - HALF)
    high = jnp.minimum(frame + HALF, end)[:, mid] - (start - HALF)
    padded = -(-length // QB) * QB
    span = jnp.pad(jnp.stack([low, high], axis=1), ((0, 0), (0, 0), (0, padded - length)))

    gain = norm_gain[None]
    x_near = jnp.concatenate([from_left, frames, from_right], axis=1).reshape(-1, width)
    normed, normed_own, value, key, query, cos_tab, sin_tab = project(
        x_near, place, gain, w_query, w_key, w_value, seqs
    )
    mixed, probs = attend(span, query, key, value, seqs)

    attn_out, mlp_in = out_proj(mixed, x, w_output, attn_scale[None], mlp_gain[None])
    flags_now, mlp_in = hold(flags, mlp_in)
    mlp_in_peer = places.swap(mlp_in, places.core)
    grad_low, grad_hidden = hidden_grad(
        flags_now, grad_y, grad_y_peer, mlp_scale[None], w_down, block
    )

    blocks = n_seq // 2
    per = blocks // 2

    def onward(piece):
        piece.add()
        piece.split(late[-1 - piece.left])
        piece.left -= 1

    def started(piece):
        piece.left = len(late) - 1
        return piece

    def finished(piece):
        while piece.left >= 0:
            onward(piece)
        piece.add(False)
        return piece.keep

    inners = rounds.first_inners(every, own_rows)
    *kept, a, b, c, d = feed(
        flags, mlp_in, mlp_in_peer, grad_hidden, w_gate, w_up, block, 0, per, (), inners
    )
    rounds.begin((a, b, c, d), every, own_rows)
    *kept, a, b, c, d = feed(
        flags, mlp_in, mlp_in_peer, grad_hidden, w_gate, w_up, block, per, per, kept, inners
    )
    hidden, grad_gate, grad_up = kept
    flags_now, a = meet(flags, [a], rounds=rounds)
    rounds.run(flags_now, "sent", (a, b, c, d), every, own_rows)

    flags_now, rounds.two["keep"][0] = meet(flags, [rounds.two["keep"][0]])
    *in_peer, in_own = feed_back(flags_now, grad_gate, grad_up, w_gate, w_up, block)
    in_got = [places.swap(v, places.core) for v in in_peer]

    flags_now, in_own = meet(flags, [in_own])
    each = feed_rows // 2
    parts = down(flags_now, hidden, grad_low, each, rounds.first_inners(not_core, each))

    flags_now, *both = meet(flags, [*in_got, *parts], rounds=rounds)
    in_got, parts = both[:2], both[2:]
    first = started(rounds.run(flags_now, "sent", parts, not_core, each))

    scale_row, rounds.two["keep"][0] = meet(attn_scale[None], [rounds.two["keep"][0]])
    grad_attn, grad_mixed, grad_middle, join_sums = join(
        x, attn_out, grad_y, in_own, in_got, scale_row, mlp_gain[None], w_output
    )
    grad_query, grad_kv, grad_near = attend_back(
        probs, query, key, value, grad_mixed, cos_tab, sin_tab, seqs
    )
    edge = grad_near.reshape(2, seqs, -1, width)
    to_right, to_left = neighbours(edge[:, :, HALF + length :], edge[:, :, :HALF])

    core_inner = Piece(places, every, own_rows).inner(places.core)

    def core_pair(flag, pairs, name, scale):
        *out, stay = weight_grad(flag, core_inner, pairs, name, scale)
        return [stay, *[places.swap(v, places.core) for v in out]]

    flags_now, grad_query = meet(flags, [grad_query])
    fourth = core_pair(
        flags_now, [(mixed, grad_attn), (normed_own, grad_query)], "output_query_weight", 0.02
    )
    flags_now, fourth[0] = meet(flags, [fourth[0]], [first], rounds)
    onward(first)
    fifth = core_pair(
        flags_now, [(normed, (grad_near, 0)), (normed, (grad_near, 1))], "key_value_weight", 4
    )
    flags_now, fifth[0], *fourth = meet(flags, [fifth[0], *fourth], [first])
    second = started(rounds.run(flags_now, "core", fourth, not_core, own_rows))

    flags_now, rounds.one["keep"][0] = meet(flags, [rounds.one["keep"][0]])
    *out_peer, out_own = feed_out(flags_now, hidden, w_down, block)
    out_got = [places.swap(v, places.core) for v in out_peer]
    has_now, out_own = meet(has, [out_own])
    grad_kv = add_edges(has_now, grad_kv, to_right, to_left)
    flags_now, grad_kv, *fifth = meet(flags, [grad_kv, *fifth], [second], rounds)
    third = started(rounds.run(flags_now, "core", fifth, not_core, own_rows))
    onward(second)
    gain_now, rounds.one["keep"][0], *out_got = meet(gain, [rounds.one["keep"][0], *out_got])
    frames_grad, norm_sums = input_grad(
        x, grad_query, grad_kv, grad_middle, gain_now, w_query, w_key, w_value
    )
    scale_row, frames_grad = meet(attn_scale[None], [frames_grad], [second, third])
    onward(third)
    layer_out, out_sums = finish(
        x, attn_out, grad_y, out_own, out_got, scale_row, mlp_scale[None]
    )

    vectors = jnp.stack([norm_sums[0], join_sums[0], join_sums[1], out_sums[0]], axis=1)
    vectors = vectors.reshape((2,) * places.count + (own_rows, 4))
    left = list(reversed(every))
    groups = [[places.core], [x_bit, y_bit]]
    rest = [z_bit] + late
    groups += [rest[i : i + 2] for i in range(0, len(rest), 2)]

    flags_now, layer_out, vectors = meet(flags, [layer_out, vectors], [], rounds)
    fourth = started(rounds.run(flags_now))
    shares = share(places, vectors, left, groups[0])
    feeds = jnp.stack([finished(first), finished(second)]).reshape(2, 2, 2, own_rows, width)
    mine = lax.dynamic_index_in_dim(feeds, core, 2, False)
    got = places.swap(lax.dynamic_index_in_dim(feeds, 1 - core, 2, False), places.core)

    flags_now, got, *shares = meet(flags, [got, *shares], [fourth], rounds)
    fifth = started(rounds.run(flags_now))
    onward(fourth)
    left = [b for b in left if b not in groups[0]]
    shares = share(places, sum(shares), left, groups[1])
    pair = jnp.stack([jnp.where(core == 0, mine, got), jnp.where(core == 0, got, mine)], axis=0)
    pair = pair.reshape(2, 2, 2, own_rows, per, block)
    pair = pair.transpose(2, 3, 1, 4, 0, 5).reshape(2, own_rows, feed_width)

    _, gate_grad, up_grad, *shares = meet(flags, [pair[0], pair[1], *shares], [fifth, third])
    onward(fifth)
    for done, group in zip(groups[1:], groups[2:]):
        left = [b for b in left if b not in done]
        shares = share(places, sum(shares), left, group)
    vectors = sum(shares).T
    down_grad = finished(third)
    one, two = finished(fourth), finished(fifth)
    output_grad, query_grad = one[:own_rows], one[own_rows:]
    key_grad, value_grad = two[:own_rows], two[own_rows:]
    return (
        layer_out.reshape(frames.shape),
        frames_grad.reshape(frames.shape),
        vectors[0],
        query_grad,
        key_grad,
        value_grad,
        output_grad,
        vectors[1],
        vectors[2],
        gate_grad,
        up_grad,
        down_grad,
        vectors[3],
    )


def solution(mesh):
    split = P("seq", "sp", None)
    rows = P(("seq", "sp"), None)
    vec = P(("seq", "sp"))
    return jax.shard_map(
        on_device,
        mesh=mesh,
        in_specs=(split, P("seq", None)) + (P(),) * 11 + (split,),
        out_specs=(
            split, split, vec, rows, rows, rows, rows, vec, vec, rows, rows, rows, vec,
        ),
        check_vma=False,
    )
```

```python
import functools
import math

import jax
import jax.numpy as jnp
import numpy as np
from jax import lax
from jax.experimental import pallas as pl
from jax.experimental.pallas import tpu as pltpu
from jax.sharding import PartitionSpec as P

HEAD_DIM = 64
HALF = 64
LANES = 128
GROUP = 256
GH = GROUP // HEAD_DIM
QB = 128
KB = QB + 2 * HALF
CLIPS = 8
LN_EPS = 1e-05
RMS_EPS = 1e-06
VMEM = 58 << 20
F32 = jnp.float32
BF16 = jnp.bfloat16

NT = (((1,), (1,)), ((), ()))
NN = (((1,), (0,)), ((), ()))
TN = (((0,), (0,)), ((), ()))


def dot(a, b, dims=NN):
    return lax.dot_general(a, b, dims, preferred_element_type=F32)


def params(grid=0):
    kinds = ("arbitrary",) * grid if grid else None
    return pltpu.CompilerParams(vmem_limit_bytes=VMEM, dimension_semantics=kinds)


def cost(flops, moved, scale=0.02):
    return pl.CostEstimate(
        flops=int(flops * scale), bytes_accessed=int(moved * scale), transcendentals=0
    )


def whole(shape):
    return pl.BlockSpec(shape, lambda *_: (0,) * len(shape))


def swap_halves(v):
    lane = lax.broadcasted_iota(jnp.int32, v.shape, 1)
    return jnp.where(lane % HEAD_DIM < HEAD_DIM // 2, pltpu.roll(v, 96, 1), pltpu.roll(v, 32, 1))


def rotated(v, cos_tab, sin_tab, sign):
    pieces = []
    for at in range(0, v.shape[1], LANES):
        part = v[:, at : at + LANES]
        turned = swap_halves(part) * sin_tab
        pieces.append(part * cos_tab + turned if sign > 0 else part * cos_tab - turned)
    return jnp.concatenate(pieces, axis=1)


def project_kernel(
    seqs, x_ref, place_ref, gain_ref, wv_ref, wk_ref, wq_ref,
    all_ref, normed_ref, v_ref, k_ref, q_ref, cos_ref, sin_ref,
):
    step = pl.program_id(0)
    padded = x_ref.shape[0] // seqs
    length = padded - 2 * HALF

    def own(s):
        return slice(s * padded + HALF, s * padded + HALF + length)

    @pl.when(step == 0)
    def _():
        x = x_ref[...].astype(F32)
        centered = x - jnp.mean(x, axis=-1, keepdims=True)
        inv = lax.rsqrt(jnp.mean(centered * centered, axis=-1, keepdims=True) + LN_EPS)
        all_ref[...] = (centered * inv * gain_ref[...]).astype(BF16)
        for s in range(seqs):
            normed_ref[s * length : (s + 1) * length, :] = all_ref[own(s), :]
        v_ref[...] = dot(all_ref[...], wv_ref[...]).astype(BF16)

    @pl.when(step == 1)
    def _():
        lane = lax.broadcasted_iota(jnp.int32, (1, LANES), 1)
        exponent = (lane % (HEAD_DIM // 2)).astype(F32) * (2.0 / HEAD_DIM)
        angles = place_ref[...] * jnp.exp(-math.log(10000.0) * exponent)
        cos_ref[...] = jnp.cos(angles)
        sin_ref[...] = jnp.where(lane % HEAD_DIM < HEAD_DIM // 2, -1.0, 1.0) * jnp.sin(angles)
        v_ref[...] = dot(all_ref[...], wv_ref[...]).astype(BF16)

    @pl.when((step == 2) | (step == 3))
    def _():
        out = dot(all_ref[...], wk_ref[...])
        k_ref[...] = rotated(out, cos_ref[...], sin_ref[...], 1).astype(BF16)

    @pl.when(step >= 4)
    def _():
        for s in range(seqs):
            out = dot(all_ref[own(s), :], wq_ref[...])
            out = rotated(out, cos_ref[own(s), :], sin_ref[own(s), :], 1)
            q_ref[s * length : (s + 1) * length, :] = (out * (1.0 / math.sqrt(HEAD_DIM))).astype(BF16)


def project(x, place, gain, w_query, w_key, w_value, seqs):
    rows, width = x.shape
    own = rows - seqs * 2 * HALF
    block = width // 2

    def at(which):
        return lambda j: (0, jnp.clip(j - 2 * which, 0, 1))

    low = functools.partial(jax.ShapeDtypeStruct, dtype=BF16)
    table = jax.ShapeDtypeStruct((rows, LANES), F32)
    return pl.pallas_call(
        functools.partial(project_kernel, seqs),
        grid=(6,),
        in_specs=[whole((rows, width)), whole((rows, 1)), whole((1, width))]
        + [pl.BlockSpec((width, block), at(w)) for w in range(3)],
        out_specs=[
            whole((rows, width)),
            whole((own, width)),
            pl.BlockSpec((rows, block), at(0)),
            pl.BlockSpec((rows, block), at(1)),
            pl.BlockSpec((own, block), at(2)),
            whole((rows, LANES)),
            whole((rows, LANES)),
        ],
        out_shape=[low((rows, width)), low((own, width)), low((rows, width)), low((rows, width))]
        + [low((own, width)), table, table],
        compiler_params=params(1),
        cost_estimate=cost(6 * rows * width * width, 6 * width * width + 10 * rows * width),
        name="project",
    )(x, place, gain, w_value, w_key, w_query)


def stack_heads(block):
    lane = lax.broadcasted_iota(jnp.int32, block.shape, 1)
    zero = jnp.zeros_like(block)
    return jnp.concatenate(
        [jnp.where(lane // HEAD_DIM == h, block, zero) for h in range(GH)], axis=0
    )


def fill_keys(buf, ref):
    rows = ref.shape[0]
    buf[0:rows, :] = ref[...]
    if buf.shape[0] > rows:
        buf[rows:, :] = jnp.zeros((buf.shape[0] - rows, buf.shape[1]), buf.dtype)


def fill_queries(buf, own_ref, length):
    buf[0:length, :] = own_ref[...]
    rest = buf.shape[0] - length
    if rest:
        buf[length:, :] = jnp.zeros((rest, buf.shape[1]), buf.dtype)


def attend_kernel(span_ref, q_ref, k_ref, v_ref, o_ref, p_ref, kbuf, vbuf, qbuf, vt, ot):
    length = q_ref.shape[0]
    padded = qbuf.shape[0]
    fill_keys(kbuf, k_ref)
    fill_keys(vbuf, v_ref)
    fill_queries(qbuf, q_ref, length)
    vt[...] = vbuf[...].T
    for b in range(padded // QB):
        q4 = stack_heads(qbuf[b * QB : (b + 1) * QB, :])
        scores = dot(kbuf[b * QB : b * QB + KB, :], q4, NT)
        place = lax.broadcasted_iota(jnp.int32, (KB, QB), 0) + b * QB
        low = span_ref[0, 0:1, b * QB : (b + 1) * QB]
        high = span_ref[0, 1:2, b * QB : (b + 1) * QB]
        seen = (place >= low) & (place < high)
        for h in range(GH):
            masked = jnp.where(seen, scores[:, h * QB : (h + 1) * QB], -1e30)
            terms = jnp.exp(masked - jnp.max(masked, axis=0, keepdims=True))
            total = jnp.sum(terms, axis=0, keepdims=True)
            probs = (terms * (1.0 / total)).astype(BF16)
            p_ref[:, b * GH * QB + h * QB : b * GH * QB + (h + 1) * QB] = probs
            ot[h * HEAD_DIM : (h + 1) * HEAD_DIM, b * QB : (b + 1) * QB] = dot(
                vt[h * HEAD_DIM : (h + 1) * HEAD_DIM, b * QB : b * QB + KB], probs
            ).astype(BF16)
    o_ref[...] = ot[...].T[0:length, :]


def attend(span, query, key, value, seqs):
    rows, width = query.shape
    length = rows // seqs
    padded = span.shape[2]
    groups = width // GROUP
    keys = padded + 2 * HALF
    own = pl.BlockSpec((length, GROUP), lambda s, g: (s, g))
    near = pl.BlockSpec((length + 2 * HALF, GROUP), lambda s, g: (s, g))
    return pl.pallas_call(
        attend_kernel,
        grid=(seqs, groups),
        in_specs=[
            pl.BlockSpec((1, 2, padded), lambda s, g: (s, 0, 0)),
            own,
            near,
            near,
        ],
        out_specs=[
            own,
            pl.BlockSpec((KB, GH * padded), lambda s, g: (s, g)),
        ],
        out_shape=[
            jax.ShapeDtypeStruct((rows, width), BF16),
            jax.ShapeDtypeStruct((seqs * KB, groups * GH * padded), BF16),
        ],
        scratch_shapes=[
            pltpu.VMEM((keys, GROUP), BF16),
            pltpu.VMEM((keys, GROUP), BF16),
            pltpu.VMEM((padded, GROUP), BF16),
            pltpu.VMEM((GROUP, keys), BF16),
            pltpu.VMEM((GROUP, padded), BF16),
        ],
        compiler_params=params(2),
        cost_estimate=cost(
            2 * 2 * seqs * width * padded * KB * 4, 2 * width * (4 * rows + KB * seqs * padded // 64)
        ),
        name="attend",
    )(span, query, key, value)


def attend_back_kernel(
    flip_ref, p_ref, q_ref, k_ref, v_ref, g_ref, cos_ref, sin_ref,
    dq_ref, dkv_ref, near_ref, edge_ref, other_ref,
    kbuf, vbuf, qbuf, gbuf, kt, dqt, dkb, dvb,
):
    length = q_ref.shape[0]
    padded = qbuf.shape[0]
    fill_keys(kbuf, k_ref)
    fill_keys(vbuf, v_ref)
    fill_queries(qbuf, q_ref, length)
    fill_queries(gbuf, g_ref, length)
    kt[...] = kbuf[...].T
    dkb[...] = jnp.zeros_like(dkb)
    dvb[...] = jnp.zeros_like(dvb)
    for b in range(padded // QB):
        at, keys = slice(b * QB, (b + 1) * QB), slice(b * QB, b * QB + KB)
        q4 = stack_heads(qbuf[at, :])
        g4 = stack_heads(gbuf[at, :])
        probs = p_ref[:, b * GH * QB : (b + 1) * GH * QB]
        grads = dot(vbuf[keys, :], g4, NT)
        pieces = []
        for h in range(GH):
            part = probs[:, h * QB : (h + 1) * QB].astype(F32)
            grad = grads[:, h * QB : (h + 1) * QB]
            delta = jnp.sum(part * grad, axis=0, keepdims=True)
            low = (part * (grad - delta)).astype(BF16)
            pieces.append(low)
            dqt[h * HEAD_DIM : (h + 1) * HEAD_DIM, at] = dot(
                kt[h * HEAD_DIM : (h + 1) * HEAD_DIM, keys], low
            )
        dvb[keys, :] += dot(probs, g4)
        dkb[keys, :] += dot(jnp.concatenate(pieces, axis=1), q4)
    cos_tab, sin_tab = cos_ref[...], sin_ref[...]
    middle = slice(HALF, HALF + length)
    dq = dqt[...].T[0:length, :] * (1.0 / math.sqrt(HEAD_DIM))
    dq_ref[...] = rotated(dq, cos_tab[middle], sin_tab[middle], -1).astype(BF16)
    span = length + 2 * HALF
    dk = rotated(dkb[0:span, :], cos_tab, sin_tab, -1).astype(BF16)
    dv = dvb[0:span, :].astype(BF16)
    for i, grad in enumerate((dk, dv)):
        dkv_ref[i] = grad[middle]
        near_ref[i] = grad
        ends = grad[0:HALF], grad[span - HALF :]
        edge_ref[i] = jnp.where(flip_ref[0] == 1, ends[1], ends[0])
        other_ref[i] = jnp.where(flip_ref[0] == 1, ends[0], ends[1])


def attend_back(flip, probs, query, key, value, grad, cos_tab, sin_tab, seqs):
    rows, width = query.shape
    length = rows // seqs
    padded = -(-length // QB) * QB
    groups = width // GROUP
    keys = padded + 2 * HALF
    own = pl.BlockSpec((length, GROUP), lambda s, g, f: (s, g))
    both = pl.BlockSpec((2, length, GROUP), lambda s, g, f: (0, s, g))
    both_near = pl.BlockSpec((2, length + 2 * HALF, GROUP), lambda s, g, f: (0, s, g))
    near = pl.BlockSpec((length + 2 * HALF, GROUP), lambda s, g, f: (s, g))
    table = pl.BlockSpec((length + 2 * HALF, LANES), lambda s, g, f: (s, 0))
    edge = pl.BlockSpec((2, HALF, GROUP), lambda s, g, f: (0, s, g))
    out_edge = jax.ShapeDtypeStruct((2, seqs * HALF, width), BF16)
    out = jax.ShapeDtypeStruct((rows, width), BF16)
    out_both = jax.ShapeDtypeStruct((2, rows, width), BF16)
    out_near = jax.ShapeDtypeStruct((2, rows + seqs * 2 * HALF, width), BF16)
    return pl.pallas_call(
        attend_back_kernel,
        grid_spec=pltpu.PrefetchScalarGridSpec(
            num_scalar_prefetch=1,
            grid=(seqs, groups),
        in_specs=[
            pl.BlockSpec((KB, GH * padded), lambda s, g, f: (s, g)),
            own,
            near,
            near,
            own,
            table,
            table,
        ],
        out_specs=[own, both, both_near, edge, edge],
        scratch_shapes=[
            pltpu.VMEM((keys, GROUP), BF16),
            pltpu.VMEM((keys, GROUP), BF16),
            pltpu.VMEM((padded, GROUP), BF16),
            pltpu.VMEM((padded, GROUP), BF16),
            pltpu.VMEM((GROUP, keys), BF16),
            pltpu.VMEM((GROUP, padded), F32),
            pltpu.VMEM((keys, GROUP), F32),
            pltpu.VMEM((keys, GROUP), F32),
        ],
        ),
        out_shape=[out, out_both, out_near, out_edge, out_edge],
        compiler_params=params(2),
        cost_estimate=cost(
            2 * 4 * seqs * width * padded * KB * 4, 2 * width * (8 * rows + KB * seqs * padded // 64)
        ),
        name="attend_back",
    )(flip, probs, query, key, value, grad, cos_tab, sin_tab)


def edges_kernel(seqs, flags_ref, from_ref, left_ref, right_ref, to_ref, buf, sems):
    length = from_ref.shape[1] // seqs
    places = [
        (i, s, e, pl.ds(s * length + e * (length - HALF), HALF))
        for i in range(2)
        for s in range(seqs)
        for e in range(2)
    ]
    copies = [
        (from_ref.at[i, rows, :], to_ref.at[i, rows, :], buf.at[at]) for at, (i, _, _, rows) in enumerate(places)
    ]
    for at, (src, _, mid) in enumerate(copies):
        pltpu.make_async_copy(src, mid, sems.at[0, at]).start()
    for at, (src, _, mid) in enumerate(copies):
        pltpu.make_async_copy(src, mid, sems.at[0, at]).wait()
    for at, (i, s, e, _) in enumerate(places):
        got = (right_ref if e else left_ref)[i, s].astype(F32) * flags_ref[e].astype(F32)
        buf[at] = (buf[at].astype(F32) + got).astype(BF16)
    for at, (_, dst, mid) in enumerate(copies):
        pltpu.make_async_copy(mid, dst, sems.at[1, at]).start()
    for at, (_, dst, mid) in enumerate(copies):
        pltpu.make_async_copy(mid, dst, sems.at[1, at]).wait()


def add_edges(flags, grads, left, right):
    seqs = left.shape[1]
    hbm = pl.BlockSpec(memory_space=pl.ANY)
    return pl.pallas_call(
        functools.partial(edges_kernel, seqs),
        grid_spec=pltpu.PrefetchScalarGridSpec(
            num_scalar_prefetch=1,
            grid=(1,),
            in_specs=[hbm, whole(left.shape), whole(right.shape)],
            out_specs=hbm,
            scratch_shapes=[
                pltpu.VMEM((4 * seqs, HALF, grads.shape[2]), BF16),
                pltpu.SemaphoreType.DMA((2, 4 * seqs)),
            ],
        ),
        out_shape=jax.ShapeDtypeStruct(grads.shape, BF16),
        input_output_aliases={1: 0},
        compiler_params=params(1),
        cost_estimate=cost(1e4 * left.size, 8 * left.size, 1000),
        name="add_edges",
    )(flags, grads, left, right)


def out_proj_kernel(m_ref, x_ref, w_ref, scale_ref, gain_ref, attn_ref, in_ref):
    attn = dot(m_ref[...], w_ref[...])
    attn_ref[...] = attn.astype(BF16)
    middle = x_ref[...].astype(F32) + scale_ref[...] * attn
    inv = lax.rsqrt(jnp.mean(middle * middle, axis=-1, keepdims=True) + RMS_EPS)
    in_ref[...] = (middle * inv * gain_ref[...]).astype(BF16)


def out_proj(mixed, x, w_output, scale, gain):
    rows, width = x.shape
    block = rows // 2
    row = pl.BlockSpec((block, width), lambda i: (i, 0))
    return pl.pallas_call(
        out_proj_kernel,
        grid=(rows // block,),
        in_specs=[row, row, whole((width, width)), whole((1, width)), whole((1, width))],
        out_specs=[row, row],
        out_shape=[
            jax.ShapeDtypeStruct((rows, width), BF16),
            jax.ShapeDtypeStruct((rows, width), BF16),
        ],
        compiler_params=params(1),
        cost_estimate=cost(2 * rows * width * width, 2 * rows * width * 5 + 2 * width * width),
        name="out_proj",
    )(mixed, x, w_output, scale, gain)


def hidden_grad_kernel(core_ref, own_ref, peer_ref, scale_ref, one_ref, two_ref, low_ref, out_ref):
    rows = own_ref.shape[0]
    block = one_ref.shape[0]

    @pl.when(pl.program_id(0) == 0)
    def _():
        low_ref[0:rows, :] = (own_ref[...].astype(F32) * scale_ref[...]).astype(BF16)
        low_ref[rows:, :] = (peer_ref[...].astype(F32) * scale_ref[...]).astype(BF16)

    out_ref[:, :block] = dot(low_ref[...], one_ref[...], NT).astype(BF16)
    out_ref[:, block:] = dot(low_ref[...], two_ref[...], NT).astype(BF16)


def hidden_grad(core, own, peer, scale, w_down, block):
    rows, width = own.shape
    count = w_down.shape[0] // block // 4
    half = w_down.shape[0] // 2
    return pl.pallas_call(
        hidden_grad_kernel,
        grid_spec=pltpu.PrefetchScalarGridSpec(
            num_scalar_prefetch=1,
            grid=(count,),
            in_specs=[
                whole((rows, width)),
                whole((rows, width)),
                whole((1, width)),
                pl.BlockSpec((block, width), lambda j, c: (4 * j + c[0], 0)),
                pl.BlockSpec((block, width), lambda j, c: (4 * j + 2 + c[0], 0)),
            ],
            out_specs=[
                whole((2 * rows, width)),
                pl.BlockSpec((2 * rows, 2 * block), lambda j, c: (0, j)),
            ],
        ),
        out_shape=[
            jax.ShapeDtypeStruct((2 * rows, width), BF16),
            jax.ShapeDtypeStruct((2 * rows, half), BF16),
        ],
        compiler_params=params(1),
        cost_estimate=cost(
            4 * rows * width * half, 2 * (4 * rows * width + half * (width + 2 * rows))
        ),
        name="hidden_grad",
    )(core, own, peer, scale, w_down, w_down)


def halves_of(value, bit, inner):
    rows, columns = value.shape
    both = value.reshape(rows // (2 * inner), 2, inner, columns)
    zero, one = both[:, 0], both[:, 1]
    out = jnp.where(bit == 0, one, zero).reshape(rows // 2, columns)
    stay = jnp.where(bit == 0, zero, one).reshape(rows // 2, columns)
    return out, stay


def feed_kernel(inners, core_ref, xo_ref, xp_ref, gh_ref, wg_ref, wu_ref, *refs):
    hid_own_ref, hid_peer_ref, gg_ref, gu_ref, *outs, x_all = refs[-9:]
    rows = xo_ref.shape[0]

    @pl.when(pl.program_id(0) == 0)
    def _():
        x_all[0:rows, :] = xo_ref[...]
        x_all[rows:, :] = xp_ref[...]

    for at in (0, rows):
        part = slice(at, at + rows)
        gate = dot(x_all[part, :], wg_ref[...])
        up = dot(x_all[part, :], wu_ref[...])
        grad = gh_ref[part, :].astype(F32)
        sig = 1.0 / (1.0 + jnp.exp(-gate))
        act = gate * sig
        (hid_peer_ref if at else hid_own_ref)[...] = (act * up).astype(BF16)
        gg_ref[part, :] = (grad * up * sig * (1.0 + gate * (1.0 - sig))).astype(BF16)
        gu_ref[part, :] = (grad * act).astype(BF16)
    for i, src in enumerate((gg_ref, gu_ref)):
        out, stay = halves_of(dot(x_all[...], src[...], TN), core_ref[1 + i], inners[i])
        outs[2 * i][...] = out.astype(BF16)
        outs[2 * i + 1][...] = stay.astype(BF16)


def feed(core, x_own, x_peer, grad_hidden, w_gate, w_up, block, first, count, before, inners):
    rows, width = x_own.shape
    half = grad_hidden.shape[1]
    wide = pl.BlockSpec((2 * rows, block), lambda j, c: (0, j + first))
    weight = pl.BlockSpec((width, block), lambda j, c: (0, 2 * (j + first) + c[0]))
    tall = pl.BlockSpec((rows, block), lambda j, c: (0, j + first))
    kept = jax.ShapeDtypeStruct((2 * rows, half), BF16)
    single = jax.ShapeDtypeStruct((rows, half), BF16)
    grads = jax.ShapeDtypeStruct((width // 2, count * block), BF16)
    any_spec = pl.BlockSpec(memory_space=pl.ANY)
    return pl.pallas_call(
        functools.partial(feed_kernel, inners),
        grid_spec=pltpu.PrefetchScalarGridSpec(
            num_scalar_prefetch=1,
            grid=(count,),
            in_specs=[whole((rows, width)), whole((rows, width)), wide, weight, weight]
            + [any_spec] * len(before),
            out_specs=[tall] * 2
            + [wide] * 2
            + [pl.BlockSpec((width // 2, block), lambda j, c: (0, j))] * 4,
            scratch_shapes=[pltpu.VMEM((2 * rows, width), BF16)],
        ),
        out_shape=[single] * 2 + [kept] * 2 + [grads] * 4,
        input_output_aliases={6 + i: i for i in range(len(before))},
        compiler_params=params(1),
        cost_estimate=cost(
            2 * 2 * rows * width * block * count * 4,
            2 * (4 * rows * width + count * block * (8 * rows + 4 * width)),
        ),
        name="feed",
    )(core, x_own, x_peer, grad_hidden, w_gate, w_up, *before)


def down_kernel(each, inners, bits_ref, own_ref, peer_ref, low_ref, *refs):
    *outs, both = refs
    both[: own_ref.shape[0], :] = own_ref[...]
    both[own_ref.shape[0] :, :] = peer_ref[...]
    value = dot(both[...], low_ref[...], TN)
    rows, width = value.shape
    value = value.reshape(rows // (2 * each), 2, each, width)
    for i in range(2):
        part = value[:, i].reshape(rows // 2, width)
        out, stay = halves_of(part, bits_ref[1 + i], inners[i])
        outs[2 * i][...] = out.astype(BF16)
        outs[2 * i + 1][...] = stay.astype(BF16)


def down(bits, own, peer, low, each, inners):
    rows, half = own.shape
    width = low.shape[1]
    block = 512
    out = jax.ShapeDtypeStruct((half // 4, width), BF16)
    return pl.pallas_call(
        functools.partial(down_kernel, each, inners),
        grid_spec=pltpu.PrefetchScalarGridSpec(
            num_scalar_prefetch=1,
            grid=(half // block,),
            in_specs=[
                pl.BlockSpec((rows, block), lambda j, c: (0, j)),
                pl.BlockSpec((rows, block), lambda j, c: (0, j)),
                whole((2 * rows, width)),
            ],
            out_specs=[pl.BlockSpec((block // 4, width), lambda j, c: (j, 0))] * 4,
            scratch_shapes=[pltpu.VMEM((2 * rows, block), BF16)],
        ),
        out_shape=[out] * 4,
        compiler_params=params(1),
        cost_estimate=cost(
            4 * rows * half * width, 2 * (2 * rows * half + 2 * rows * width + half * width)
        ),
        name="down_weight",
    )(bits, own, peer, low)


def in_halves(value, refs):
    half = value.shape[1] // 2
    refs[0][...] = value[:, :half]
    refs[1][...] = value[:, half:]


def feed_back_kernel(core_ref, *refs):
    *peer_refs, own_ref, acc = refs[-4:]
    part, step = pl.program_id(0), pl.program_id(1)
    block = refs[2].shape[1]
    total = None
    for i in range(2):
        for half in range(2):
            out = dot(refs[i][:, half * block : (half + 1) * block], refs[2 + 2 * i + half][...], NT)
            total = out if total is None else total + out
    last = pl.num_programs(1) - 1

    @pl.when(step == 0)
    def _():
        acc[...] = total

    @pl.when((step > 0) & (step < last))
    def _():
        acc[...] += total

    @pl.when((step == last) & (part == 0))
    def _():
        in_halves((acc[...] + total).astype(BF16), peer_refs)

    @pl.when((step == last) & (part == 1))
    def _():
        own_ref[...] = (acc[...] + total).astype(BF16)


def feed_back(core, grad_gate, grad_up, w_gate, w_up, block):
    rows, half = grad_gate.shape
    rows = rows // 2
    width = w_gate.shape[0]
    tall = pl.BlockSpec((rows, 2 * block), lambda p, j, c: (1 - p, j))
    one = pl.BlockSpec((width, block), lambda p, j, c: (0, 4 * j + c[0]))
    two = pl.BlockSpec((width, block), lambda p, j, c: (0, 4 * j + 2 + c[0]))
    return pl.pallas_call(
        feed_back_kernel,
        grid_spec=pltpu.PrefetchScalarGridSpec(
            num_scalar_prefetch=1,
            grid=(2, half // block // 2),
            in_specs=[tall, tall, one, two, one, two],
            out_specs=[whole((rows, width // 2))] * 2 + [whole((rows, width))],
            scratch_shapes=[pltpu.VMEM((rows, width), F32)],
        ),
        out_shape=[jax.ShapeDtypeStruct((rows, width // 2), BF16)] * 2
        + [jax.ShapeDtypeStruct((rows, width), BF16)],
        compiler_params=params(2),
        cost_estimate=cost(8 * rows * half * width, 8 * (rows * half + half * width)),
        name="feed_back",
    )(core, grad_gate, grad_up, w_gate, w_gate, w_up, w_up)


def join_kernel(
    x_ref, attn_ref, g_ref, in_ref, got_one_ref, got_two_ref, attn_scale_ref, gain_ref, w_ref,
    grad_attn_ref, grad_mixed_ref, middle_ref, sums_ref,
):
    x = x_ref[...].astype(F32)
    attn = attn_ref[...].astype(F32)
    grad_y = g_ref[...].astype(F32)
    got = jnp.concatenate([got_one_ref[...], got_two_ref[...]], axis=1)
    grad_in = in_ref[...].astype(F32) + got.astype(F32)
    middle = x + attn_scale_ref[...] * attn
    inv = lax.rsqrt(jnp.mean(middle * middle, axis=-1, keepdims=True) + RMS_EPS)
    unit = middle * inv
    scaled = grad_in * gain_ref[...]
    grad_middle = grad_y + inv * (scaled - unit * jnp.mean(scaled * unit, axis=-1, keepdims=True))
    middle_ref[...] = grad_middle.astype(BF16)
    grad_attn = (attn_scale_ref[...] * grad_middle).astype(BF16)
    grad_attn_ref[...] = grad_attn
    grad_mixed_ref[...] = dot(grad_attn, w_ref[...], NT).astype(BF16)

    @pl.when(pl.program_id(0) == 0)
    def _():
        sums_ref[...] = jnp.zeros_like(sums_ref)

    sums_ref[0:1, :] += jnp.sum(grad_middle * attn, axis=0, keepdims=True)
    sums_ref[1:2, :] += jnp.sum(grad_in * unit, axis=0, keepdims=True)


def join(x, attn, grad_y, grad_in, got, attn_scale, gain, w_output):
    rows, width = x.shape
    block = rows // 2
    row = pl.BlockSpec((block, width), lambda i: (i, 0))
    half = pl.BlockSpec((block, width // 2), lambda i: (i, 0))
    vec = whole((1, width))
    low = jax.ShapeDtypeStruct((rows, width), BF16)
    return pl.pallas_call(
        join_kernel,
        grid=(rows // block,),
        in_specs=[row] * 4 + [half] * 2 + [vec] * 2 + [whole((width, width))],
        out_specs=[row] * 3 + [whole((8, width))],
        out_shape=[
            low,
            low,
            low,
            jax.ShapeDtypeStruct((8, width), F32),
        ],
        compiler_params=params(1),
        cost_estimate=cost(2 * rows * width * width, rows * width * 22 + 2 * width * width),
        name="join",
    )(x, attn, grad_y, grad_in, *got, attn_scale, gain, w_output)


def feed_out_kernel(
    core_ref, own_ref, got_ref, w_ref, x_ref, attn_ref, g_ref, attn_scale_ref, mlp_scale_ref,
    layer_ref, sums_ref, hidden, acc,
):
    step, last = pl.program_id(0), pl.num_programs(0) - 1
    block = own_ref.shape[1] // 2
    for i in range(2):
        part = slice(i * block, (i + 1) * block)
        own, got = own_ref[:, part], got_ref[:, part]
        first = core_ref[0] == 0
        hidden[:, 2 * i * block : (2 * i + 1) * block] = jnp.where(first, own, got)
        hidden[:, (2 * i + 1) * block : (2 * i + 2) * block] = jnp.where(first, got, own)
    total = dot(hidden[...], w_ref[...])

    @pl.when(step == 0)
    def _():
        acc[...] = total

    @pl.when((step > 0) & (step < last))
    def _():
        acc[...] += total

    @pl.when(step == last)
    def _():
        down_out = acc[...] + total
        middle = x_ref[...].astype(F32) + attn_scale_ref[...] * attn_ref[...].astype(F32)
        layer_ref[...] = (middle + mlp_scale_ref[...] * down_out).astype(BF16)
        sums_ref[...] = jnp.zeros_like(sums_ref)
        sums_ref[0:1, :] = jnp.sum(g_ref[...].astype(F32) * down_out, axis=0, keepdims=True)


def feed_out(core, own, got, w_down, x, attn, grad_y, attn_scale, mlp_scale, block):
    rows, half = own.shape
    width = w_down.shape[1]
    tall = pl.BlockSpec((rows, 2 * block), lambda j, c: (0, j))
    row, vec = whole((rows, width)), whole((1, width))
    return pl.pallas_call(
        feed_out_kernel,
        grid_spec=pltpu.PrefetchScalarGridSpec(
            num_scalar_prefetch=1,
            grid=(half // block // 2,),
            in_specs=[tall, tall, pl.BlockSpec((4 * block, width), lambda j, c: (j, 0))]
            + [row] * 3
            + [vec] * 2,
            out_specs=[row, whole((8, width))],
            scratch_shapes=[pltpu.VMEM((rows, 4 * block), BF16), pltpu.VMEM((rows, width), F32)],
        ),
        out_shape=[
            jax.ShapeDtypeStruct((rows, width), BF16),
            jax.ShapeDtypeStruct((8, width), F32),
        ],
        compiler_params=params(1),
        cost_estimate=cost(4 * rows * half * width, 4 * (rows * half + half * width), 10),
        name="feed_out",
    )(core, own, got, w_down, x, attn, grad_y, attn_scale, mlp_scale)


def weight_grad_kernel(inner, order, counts, bit_ref, *refs):
    out_ref, stay_ref = refs[-2:]
    step = pl.program_id(0)
    lefts = [refs[i] for i in order]
    rights = refs[max(order) + 1 : -2]
    first = 0
    for left, right, count in zip(lefts, rights, counts):

        @pl.when((step >= first) & (step < first + count))
        def _(left=left, right=right):
            rows = right[...].reshape(right.shape[-2:])
            out, stay = halves_of(dot(left[...], rows, TN), bit_ref[0], inner)
            out_ref[...] = out.astype(BF16)
            stay_ref[...] = stay.astype(BF16)

        first += count


def weight_grad(bit, inner, pairs, name, scale):
    block = 512
    width = pairs[0][0].shape[1]
    lefts = []
    for left, _ in pairs:
        if not any(left is other for other in lefts):
            lefts.append(left)
    order = [[left is other for other in lefts].index(True) for left, _ in pairs]
    counts, specs, rights, first = [], [], [], 0
    for left, right in pairs:
        rows = left.shape[0]
        array, part = right if isinstance(right, tuple) else (right, None)
        count = array.shape[-1] // block
        at = lambda j, first=first, count=count: jnp.clip(j - first, 0, count - 1)
        if part is None:
            specs.append(pl.BlockSpec((rows, block), lambda j, c, at=at: (0, at(j))))
        else:
            specs.append(
                pl.BlockSpec((1, rows, block), lambda j, c, at=at, part=part: (part, 0, at(j)))
            )
        rights.append(array)
        counts.append(count)
        first += count
    out = jax.ShapeDtypeStruct((width // 2, first * block), BF16)
    return pl.pallas_call(
        functools.partial(weight_grad_kernel, inner, order, counts),
        grid_spec=pltpu.PrefetchScalarGridSpec(
            num_scalar_prefetch=1,
            grid=(first,),
            in_specs=[whole(left.shape) for left in lefts] + specs,
            out_specs=[pl.BlockSpec((width // 2, block), lambda j, c: (0, j))] * 2,
        ),
        out_shape=[out, out],
        compiler_params=params(1),
        cost_estimate=cost(
            2 * rows * width * first * block,
            2 * (len(lefts) * rows * width + (rows + width) * first * block),
            scale,
        ),
        name=name,
    )(bit, *lefts, *rights)


def input_grad_kernel(
    x_ref, gq_ref, gk_ref, gv_ref, middle_ref, gain_ref, wq_ref, wk_ref, wv_ref, out_ref, sums_ref
):
    grad = (
        dot(gq_ref[...], wq_ref[...], NT)
        + dot(gk_ref[0], wk_ref[...], NT)
        + dot(gv_ref[0], wv_ref[...], NT)
    )
    x = x_ref[...].astype(F32)
    centered = x - jnp.mean(x, axis=-1, keepdims=True)
    inv = lax.rsqrt(jnp.mean(centered * centered, axis=-1, keepdims=True) + LN_EPS)
    unit = centered * inv
    scaled = grad * gain_ref[...]
    back = inv * (
        scaled
        - jnp.mean(scaled, axis=-1, keepdims=True)
        - unit * jnp.mean(scaled * unit, axis=-1, keepdims=True)
    )
    out_ref[...] = (middle_ref[...].astype(F32) + back).astype(BF16)

    @pl.when(pl.program_id(0) == 0)
    def _():
        sums_ref[...] = jnp.zeros_like(sums_ref)

    sums_ref[0:1, :] += jnp.sum(grad * unit, axis=0, keepdims=True)


def input_grad(x, gq, gkv, grad_middle, gain, w_query, w_key, w_value):
    rows, width = x.shape
    block = rows // 2
    row = pl.BlockSpec((block, width), lambda i: (i, 0))
    square = whole((width, width))
    return pl.pallas_call(
        input_grad_kernel,
        grid=(rows // block,),
        in_specs=[
            row,
            row,
            pl.BlockSpec((1, block, width), lambda i: (0, i, 0)),
            pl.BlockSpec((1, block, width), lambda i: (1, i, 0)),
            row,
            whole((1, width)),
        ]
        + [square] * 3,
        out_specs=[row, whole((8, width))],
        out_shape=[
            jax.ShapeDtypeStruct((rows, width), BF16),
            jax.ShapeDtypeStruct((8, width), F32),
        ],
        compiler_params=params(1),
        cost_estimate=cost(2 * 3 * rows * width * width, rows * width * 14 + 6 * width * width),
        name="input_grad",
    )(x, gq, gkv, gkv, grad_middle, gain, w_query, w_key, w_value)


def log2(n):
    return n.bit_length() - 1


class Places:
    def __init__(self):
        self.n_seq, self.n_sp = lax.axis_size("seq"), lax.axis_size("sp")
        self.sp_bits = log2(self.n_sp)
        self.count = self.sp_bits + log2(self.n_seq)
        self.core = self.sp_bits
        self.me = lax.axis_index("seq") * self.n_sp + lax.axis_index("sp")
        self.down_bits = [b for b in reversed(range(self.count)) if b != self.core]

    def swap(self, value, bit):
        if bit < self.sp_bits:
            axis, size, at = "sp", self.n_sp, bit
        else:
            axis, size, at = "seq", self.n_seq, bit - self.sp_bits
        return lax.ppermute(value, axis, [(i, i ^ (1 << at)) for i in range(size)])

    def send(self, value, flip):
        pairs = [(i, i ^ flip) for i in range(1 << self.count)]
        return lax.ppermute(value, ("seq", "sp"), pairs)

    def own(self, bit):
        return (self.me >> bit) & 1


def round_kernel(has, inners, bits_ref, *refs):
    two, one, new, carry = has
    refs = list(refs)
    take = lambda n: [refs.pop(0) for _ in range(n)]
    second, carried = take(4) if two else (), take(2) if carry else ()
    first = take(4) if one else ()
    fresh = take({"sent": 2, "core": 4, "": 0}[new])
    bufs = take(2) if one or new else ()
    bits = bits_ref[1], bits_ref[2], bits_ref[3]

    def split(keep, got, bit, inner):
        total = keep[...].astype(F32) + got[...].astype(F32)
        return [v.astype(BF16) for v in halves_of(total, bit, inner)]

    if two:
        outs = take(2)
        at = carried[0].shape[0] if carry else 0
        for src, dst in zip(carried, outs):
            dst[0:at, :] = src[...]
        for i in range(2):
            rows = second[i].shape[0] // 2
            for dst, part in zip(outs, split(second[i], second[2 + i], bits[2], inners["two"])):
                dst[at : at + rows, :] = part
            at += rows
    at = [0, 0]
    if new:
        stays = take(2) if new == "core" else ()
        for i in range(2):
            if new == "core":
                out, stays[i][...] = split(fresh[2 * i], fresh[2 * i + 1], bits[i], inners["new"][i])
            else:
                out = fresh[i][...]
            at[i] = out.shape[0]
            bufs[i][0 : at[i], :] = out
    if one:
        stays = take(2)
        for i in range(2):
            out, stays[i][...] = split(first[i], first[2 + i], bits[1 - i], inners["one"][i])
            bufs[1 - i][at[1 - i] :, :] = out


class Rounds:
    def __init__(self, places, x, y, z):
        self.places, self.x, self.y, self.z = places, x, y, z
        self.one = self.two = None
        self.got = []

    def inner(self, group, without, bit):
        bits = [b for b in sorted(group["bits"], reverse=True) if b not in without]
        return group["each"] << (len(bits) - 1 - bits.index(bit))

    def first_inners(self, bits, each):
        group = {"bits": bits, "each": each}
        return [self.inner(group, (), self.x), self.inner(group, (), self.y)]

    def send(self, buf_x, buf_y):
        self.got = [self.places.swap(buf_x, self.x), self.places.swap(buf_y, self.y)]

    def begin(self, parts, bits, each):
        self.one = {"bits": bits, "each": each, "keep": [parts[1], parts[3]]}
        self.send(parts[0], parts[2])

    def set_aside(self):
        group, self.two = self.two, None
        return dict(group, got=self.got)

    def run(self, flags, new="", arrays=(), bits=(), each=0, carry=(), wait=False, aside=None, scale=0.02):
        one = self.one
        two = aside or self.two
        steps = 2
        ins, specs, outs, inners, heights, wide = [], [], [], {}, [0, 0], 0

        def tall(rows, columns, at=0, row=0):
            return pl.BlockSpec((rows, columns // steps), lambda j, b: (row, j + at))

        if two:
            rows, columns = two["keep"][0].shape
            got_x, got_y = two["got"] if aside else self.got
            ins += two["keep"] + [got_y, got_x]
            last = [got_y.shape[0] // rows - 1, got_x.shape[0] // rows - 1]
            specs += [tall(rows, columns)] * 2 + [tall(rows, columns, 0, row) for row in last]
            ins += carry
            specs += [tall(*v.shape) for v in carry]
            outs += [(rows + (carry[0].shape[0] if carry else 0), columns)] * 2
            inners["two"] = self.inner(two, (self.x, self.y), self.z)
        group = {"bits": list(bits), "each": each}
        if one:
            rows, wide = one["keep"][0].shape
            ins += one["keep"] + self.got
            specs += [tall(rows, wide)] * 4
            inners["one"] = self.inner(one, (self.x,), self.y), self.inner(one, (self.y,), self.x)
        if new == "sent":
            ins += [arrays[0], arrays[2]]
            specs += [tall(*arrays[0].shape), tall(*arrays[2].shape)]
            heights, wide = [arrays[0].shape[0], arrays[2].shape[0]], arrays[0].shape[1]
            group["keep"] = [arrays[1], arrays[3]]
        if new == "core":
            keep, got = arrays
            rows, wide = keep.shape[0], keep.shape[1] // 2
            ins += [keep, got, keep, got]
            specs += [tall(rows, wide)] * 2 + [tall(rows, wide, steps)] * 2
            heights = [rows // 2, rows // 2]
            outs += [(rows // 2, wide)] * 2
            inners["new"] = self.first_inners(bits, each)
        if one:
            rows = one["keep"][0].shape[0] // 2
            heights = [h + rows for h in heights]
            outs += [(rows, wide)] * 2
        if one or new:
            outs = [(h, wide) for h in heights] + outs
        size = sum(v.size for v in ins)
        results = list(
            pl.pallas_call(
                functools.partial(round_kernel, (bool(two), bool(one), new, bool(carry)), inners),
                grid_spec=pltpu.PrefetchScalarGridSpec(
                    num_scalar_prefetch=1,
                    grid=(steps,),
                    in_specs=specs,
                    out_specs=[tall(*shape) for shape in outs],
                ),
                out_shape=[jax.ShapeDtypeStruct(shape, BF16) for shape in outs],
                compiler_params=params(1),
                cost_estimate=cost(2 * size, 4 * size, scale),
                name="round",
            )(flags, *ins)
        )
        take = lambda n: [results.pop(0) for _ in range(n)]
        buf_x, buf_y = take(2) if one or new else (None, None)
        done = None
        if two:
            done = take(2)
            if not wait:
                piece = Piece(self.places, [b for b in two["bits"] if b not in (self.x, self.y)], two["each"])
                piece.fork(*done, self.z)
                done = piece
        if new == "core":
            group["keep"] = take(2)
        self.two = dict(one, keep=take(2)) if one else None
        self.one = group if new else None
        self.got = []
        if one or new:
            self.send(buf_x, buf_y)
        return done


class Piece:
    def __init__(self, places, bits, each):
        self.places, self.bits, self.each = places, sorted(bits, reverse=True), each
        self.keep = self.got = None
        self.at = 0

    def inner(self, bit):
        return self.each << (len(self.bits) - 1 - self.bits.index(bit))

    def fork(self, out, stay, bit):
        self.bits.remove(bit)
        self.keep, self.got = stay, self.places.swap(out, bit)
        self.at, self.columns = 0, stay.shape[1]

    def split(self, bit):
        rows, columns = self.keep.shape
        inner = self.inner(bit)
        both = self.keep.reshape(rows // (2 * inner), 2, inner, columns)
        at = self.places.own(bit)
        out = lax.dynamic_index_in_dim(both, 1 - at, 1, False).reshape(rows // 2, columns)
        stay = lax.dynamic_index_in_dim(both, at, 1, False).reshape(rows // 2, columns)
        self.fork(out, stay, bit)

    def add(self, low=True):
        cols = slice(self.at * self.columns, (self.at + 1) * self.columns)
        self.keep = self.keep[:, cols].astype(F32) + self.got[:, cols].astype(F32)
        self.at = 0
        if low:
            self.keep = self.keep.astype(BF16)


def share(places, value, bits, group):
    axes = [bits.index(b) for b in group]

    def part(flip):
        out = value
        for b, axis in zip(group, axes):
            out = lax.dynamic_index_in_dim(out, places.own(b) ^ ((flip >> b) & 1), axis, True)
        return lax.squeeze(out, axes)

    flips = [sum(b << g for b, g in zip(f, group)) for f in np.ndindex(*(2,) * len(group))]
    return [part(0)] + [places.send(part(f), f) for f in flips if f]


def hold(small, *arrays):
    small, *arrays = lax.optimization_barrier((small, *arrays))
    return (small, *arrays)


def meet(small, arrays=(), pieces=(), rounds=None):
    many = list(arrays), [p.got for p in pieces], list(rounds.got) if rounds else []
    small, (arrays, gots, round_gots) = lax.optimization_barrier((small, many))
    for p, g in zip(pieces, gots):
        p.got = g
    if rounds:
        rounds.got = round_gots
    return (small, *arrays)


def on_device(
    frames, clip_ids, norm_gain, w_query, w_key, w_value, w_output, attn_scale,
    mlp_gain, w_gate, w_up, w_down, mlp_scale, out_grad,
):
    places = Places()
    seqs, length, width = frames.shape
    total_len = clip_ids.shape[1]
    rows = seqs * length
    n_sp, n_seq = places.n_sp, places.n_seq
    devices = n_sp * n_seq
    feed_width = w_gate.shape[1]
    own_rows = width // devices
    feed_rows = feed_width // devices
    block = feed_rows * n_sp
    core = lax.axis_index("seq") & 1
    sp = lax.axis_index("sp")
    sp_bits = list(reversed(range(places.core)))
    seq_bits = list(range(places.core + 1, places.count))
    x_bit, y_bit, z_bit = sp_bits[0], seq_bits[0], seq_bits[1]
    late = seq_bits[2:] + sp_bits[1:]
    every = list(range(places.count))
    not_core = [b for b in every if b != places.core]
    flags = jnp.stack([places.own(b) for b in (places.core, x_bit, y_bit, z_bit)]).astype(jnp.int32)
    rounds = Rounds(places, x_bit, y_bit, z_bit)

    x = frames.reshape(rows, width)
    grad_y = out_grad.reshape(rows, width)

    def neighbours(last, first):
        if n_sp == 2:
            got = lax.ppermute(jnp.where(sp == 0, last, first), "sp", [(0, 1), (1, 0)])
            return got, got
        return (
            lax.ppermute(last, "sp", [(i, i + 1) for i in range(n_sp - 1)]),
            lax.ppermute(first, "sp", [(i + 1, i) for i in range(n_sp - 1)]),
        )

    has = jnp.stack([sp > 0, sp < n_sp - 1]).astype(jnp.int32)
    from_left, from_right = neighbours(frames[:, length - HALF :], frames[:, :HALF])
    grad_y_peer = places.swap(grad_y, places.core)

    start = sp * length
    near = lax.dynamic_slice_in_dim(
        jnp.pad(clip_ids, ((0, 0), (HALF, HALF))), start, length + 2 * HALF, 1
    )
    ids = jnp.arange(CLIPS + 1, dtype=jnp.int32)
    begins = jnp.sum((clip_ids[:, None, :] < ids[:, None]).astype(jnp.int32), axis=-1)
    is_id = near[:, None, :] == ids[:CLIPS, None]
    first = jnp.sum(jnp.where(is_id, begins[:, :CLIPS, None], 0), axis=1)
    end = jnp.sum(jnp.where(is_id, begins[:, 1:, None], 0), axis=1)
    frame = lax.broadcasted_iota(jnp.int32, near.shape, 1) + (start - HALF)
    place = (frame - first).astype(F32).reshape(-1, 1)
    mid = slice(HALF, HALF + length)
    low = jnp.maximum(frame - HALF, first)[:, mid] - (start - HALF)
    high = jnp.minimum(frame + HALF, end)[:, mid] - (start - HALF)
    padded = -(-length // QB) * QB
    span = jnp.pad(jnp.stack([low, high], axis=1), ((0, 0), (0, 0), (0, padded - length)))

    gain = norm_gain[None]
    x_near = jnp.concatenate([from_left, frames, from_right], axis=1).reshape(-1, width)
    normed, normed_own, value, key, query, cos_tab, sin_tab = project(
        x_near, place, gain, w_query, w_key, w_value, seqs
    )
    mixed, probs = attend(span, query, key, value, seqs)

    attn_out, mlp_in = out_proj(mixed, x, w_output, attn_scale[None], mlp_gain[None])
    flags_now, mlp_in = hold(flags, mlp_in)
    mlp_in_peer = places.swap(mlp_in, places.core)
    grad_low, grad_hidden = hidden_grad(
        flags_now, grad_y, grad_y_peer, mlp_scale[None], w_down, block
    )

    blocks = n_seq // 2
    per = blocks // 2

    def onward(piece):
        piece.add()
        piece.split(late[-1 - piece.left])
        piece.left -= 1

    def started(piece):
        piece.left = len(late) - 1
        return piece

    def finished(piece):
        while piece.left >= 0:
            onward(piece)
        piece.add(False)
        return piece.keep

    inners = rounds.first_inners(every, own_rows)
    *kept, a, b, c, d = feed(
        flags, mlp_in, mlp_in_peer, grad_hidden, w_gate, w_up, block, 0, per, (), inners
    )
    rounds.begin((a, b, c, d), every, own_rows)
    *kept, a, b, c, d = feed(
        flags, mlp_in, mlp_in_peer, grad_hidden, w_gate, w_up, block, per, per, kept, inners
    )
    hidden, hidden_peer, grad_gate, grad_up = kept
    hidden_got = places.swap(hidden_peer, places.core)
    flags_now, a = meet(flags, [a], rounds=rounds)
    rounds.run(flags_now, "sent", (a, b, c, d), every, own_rows)

    flags_now, rounds.two["keep"][0] = meet(flags, [rounds.two["keep"][0]])
    *in_peer, in_own = feed_back(flags_now, grad_gate, grad_up, w_gate, w_up, block)
    in_got = [places.swap(v, places.core) for v in in_peer]

    flags_now, in_own = meet(flags, [in_own])
    each = feed_rows // 2
    parts = down(
        flags_now, hidden, hidden_peer, grad_low, each, rounds.first_inners(not_core, each)
    )

    flags_now, *both = meet(flags, [*in_got, *parts], rounds=rounds)
    in_got, parts = both[:2], both[2:]
    carry = rounds.run(flags_now, "sent", parts, not_core, each, wait=True)

    scale_row, rounds.two["keep"][0], hidden_got = meet(
        attn_scale[None], [rounds.two["keep"][0], hidden_got]
    )
    grad_attn, grad_mixed, grad_middle, join_sums = join(
        x, attn_out, grad_y, in_own, in_got, scale_row, mlp_gain[None], w_output
    )
    flip = ((sp == 0) & (n_sp == 2)).astype(jnp.int32).reshape(1)
    grad_query, grad_kv, grad_near, edge, other_edge = attend_back(
        flip, probs, query, key, value, grad_mixed, cos_tab, sin_tab, seqs
    )
    if n_sp == 2:
        to_right = to_left = lax.ppermute(edge, "sp", [(0, 1), (1, 0)])
    else:
        to_left = lax.ppermute(edge, "sp", [(i + 1, i) for i in range(n_sp - 1)])
        to_right = lax.ppermute(other_edge, "sp", [(i, i + 1) for i in range(n_sp - 1)])
    to_right, to_left = [v.reshape(2, seqs, HALF, width) for v in (to_right, to_left)]

    core_inner = Piece(places, every, own_rows).inner(places.core)

    flags_now, grad_query = meet(flags, [grad_query])
    out, stay = weight_grad(
        flags_now,
        core_inner,
        [(mixed, grad_attn), (normed_own, grad_query), (normed, (grad_near, 0)), (normed, (grad_near, 1))],
        "attention_weights",
        0.02,
    )
    from_core = places.swap(out, places.core)

    flags_now, stay, to_right, to_left = meet(flags, [stay, to_right, to_left], [], rounds)
    first = started(rounds.run(flags_now, carry=carry))
    aside = rounds.set_aside()
    has_now, aside["keep"][0] = meet(has, [aside["keep"][0]])
    grad_kv = add_edges(has_now, grad_kv, to_right, to_left)
    flags_now, grad_kv, from_core = meet(flags, [grad_kv, from_core])
    rounds.run(flags_now, "core", (stay, from_core), not_core, own_rows)

    flags_now, rounds.one["keep"][0], *aside["got"] = meet(
        flags, [rounds.one["keep"][0], *aside["got"]]
    )
    layer_out, out_sums = feed_out(
        flags_now, hidden, hidden_got, w_down, x, attn_out, grad_y,
        attn_scale[None], mlp_scale[None], block,
    )
    flags_now, layer_out, join_sums = meet(flags, [layer_out, join_sums], [first])
    onward(first)
    flags_now, first.keep = meet(flags_now, [first.keep], [], rounds)
    third = started(rounds.run(flags_now, aside=aside))
    gain_now, rounds.two["keep"][0] = meet(gain, [rounds.two["keep"][0]])
    frames_grad, norm_sums = input_grad(
        x, grad_query, grad_kv, grad_middle, gain_now, w_query, w_key, w_value
    )
    flags_now, frames_grad = meet(flags, [frames_grad], [third], rounds)
    fourth = started(rounds.run(flags_now))
    onward(third)
    _, fourth.keep, norm_sums = meet(flags, [fourth.keep, norm_sums])
    vectors = jnp.stack([norm_sums[0], join_sums[0], join_sums[1], out_sums[0]], axis=1)
    vectors = vectors.reshape((2,) * places.count + (own_rows, 4))
    left = list(reversed(every))
    groups = [[b] for b in [places.core, x_bit, y_bit, z_bit] + late]
    shares = share(places, vectors, left, groups[0])
    _, *shares = meet(flags, shares, [first])
    feeds = finished(first).reshape(2, 2, 2, own_rows, width)
    mine = lax.dynamic_index_in_dim(feeds, core, 2, False)
    got = places.swap(lax.dynamic_index_in_dim(feeds, 1 - core, 2, False), places.core)
    for done, group in zip(groups, groups[1:]):
        left = [b for b in left if b not in done]
        shares = share(places, sum(shares), left, group)
        if group is groups[-3]:
            _, *shares = meet(flags, shares, [fourth])
            onward(fourth)
    down_grad = finished(third)
    pair = jnp.stack([jnp.where(core == 0, mine, got), jnp.where(core == 0, got, mine)], axis=0)
    pair = pair.reshape(2, 2, 2, own_rows, per, block)
    pair = pair.transpose(2, 3, 1, 4, 0, 5).reshape(2, own_rows, feed_width)
    while fourth.left >= 0:
        onward(fourth)
    _, gate_grad, up_grad, down_grad, *shares = meet(
        flags, [pair[0], pair[1], down_grad, *shares], [fourth]
    )
    vectors = sum(shares).T
    output_grad, query_grad, key_grad, value_grad = [
        fourth.keep[rows, columns].astype(F32) + fourth.got[rows, columns].astype(F32)
        for rows in (slice(0, own_rows), slice(own_rows, 2 * own_rows))
        for columns in (slice(0, width), slice(width, 2 * width))
    ]
    return (
        layer_out.reshape(frames.shape),
        frames_grad.reshape(frames.shape),
        vectors[0],
        query_grad,
        key_grad,
        value_grad,
        output_grad,
        vectors[1],
        vectors[2],
        gate_grad,
        up_grad,
        down_grad,
        vectors[3],
    )


def solution(mesh):
    split = P("seq", "sp", None)
    rows = P(("seq", "sp"), None)
    vec = P(("seq", "sp"))
    return jax.shard_map(
        on_device,
        mesh=mesh,
        in_specs=(split, P("seq", None)) + (P(),) * 11 + (split,),
        out_specs=(
            split, split, vec, rows, rows, rows, rows, vec, vec, rows, rows, rows, vec,
        ),
        check_vma=False,
    )
```

```python
import functools
import math

import jax
import jax.numpy as jnp
import numpy as np
from jax import lax
from jax.experimental import pallas as pl
from jax.experimental.pallas import tpu as pltpu
from jax.sharding import PartitionSpec as P

HEAD_DIM = 64
HALF = 64
LANES = 128
GROUP = 256
GH = GROUP // HEAD_DIM
QB = 128
KB = QB + 2 * HALF
CLIPS = 8
LN_EPS = 1e-05
RMS_EPS = 1e-06
VMEM = 58 << 20
F32 = jnp.float32
BF16 = jnp.bfloat16

NT = (((1,), (1,)), ((), ()))
NN = (((1,), (0,)), ((), ()))
TN = (((0,), (0,)), ((), ()))


def dot(a, b, dims=NN):
    return lax.dot_general(a, b, dims, preferred_element_type=F32)


def params(grid=0, vmem=VMEM):
    kinds = ("arbitrary",) * grid if grid else None
    return pltpu.CompilerParams(vmem_limit_bytes=vmem, dimension_semantics=kinds)


def cost(flops, moved, scale=0.02):
    return pl.CostEstimate(
        flops=int(flops * scale), bytes_accessed=int(moved * scale), transcendentals=0
    )


def in_hbm(values):
    return [pltpu.with_memory_space_constraint(v, pltpu.HBM) for v in values]


def whole(shape):
    return pl.BlockSpec(shape, lambda *_: (0,) * len(shape))


def swap_halves(v):
    lane = lax.broadcasted_iota(jnp.int32, v.shape, 1)
    return jnp.where(lane % HEAD_DIM < HEAD_DIM // 2, pltpu.roll(v, 96, 1), pltpu.roll(v, 32, 1))


def rotated(v, cos_tab, sin_tab, sign):
    pieces = []
    for at in range(0, v.shape[1], LANES):
        part = v[:, at : at + LANES]
        turned = swap_halves(part) * sin_tab
        pieces.append(part * cos_tab + turned if sign > 0 else part * cos_tab - turned)
    return jnp.concatenate(pieces, axis=1)


def project_kernel(
    seqs, x_ref, left_ref, right_ref, place_ref, gain_ref, wv_ref, wk_ref, wq_ref,
    out_ref, normed_ref, own_ref, cos_ref, sin_ref, low, weights, sems,
):
    step = pl.program_id(0)
    rows, width = low.shape
    padded = rows // seqs
    length = padded - 2 * HALF
    fetches = [
        pltpu.make_async_copy(src, weights.at[i], sems.at[i]) for i, src in enumerate((wv_ref, wk_ref, wq_ref))
    ]
    keeps = [pltpu.make_async_copy(low, normed_ref, sems.at[3])] + [
        pltpu.make_async_copy(
            low.at[s * padded + HALF : s * padded + HALF + length, :],
            own_ref.at[s * length : (s + 1) * length, :],
            sems.at[4 + s],
        )
        for s in range(seqs)
    ]

    def products(which, after):
        blocks = [slice(at, at + GROUP) for at in range(0, width, GROUP)]
        ahead = dot(low[...], weights[which, :, blocks[0]])
        for i, columns in enumerate(blocks):
            out = ahead
            if i + 1 < len(blocks):
                ahead = dot(low[...], weights[which, :, blocks[i + 1]])
            out_ref[0, :, columns] = after(out).astype(BF16)

    @pl.when(step == 0)
    def _():
        for copy in fetches:
            copy.start()
        for src, first, step in ((x_ref, HALF, length), (left_ref, 0, HALF), (right_ref, HALF + length, HALF)):
            x = src[...].astype(F32)
            centered = x - jnp.mean(x, axis=-1, keepdims=True)
            inv = lax.rsqrt(jnp.mean(centered * centered, axis=-1, keepdims=True) + LN_EPS)
            normed = (centered * inv * gain_ref[...]).astype(BF16)
            for s in range(seqs):
                at = s * padded + first
                low[at : at + step, :] = normed[s * step : (s + 1) * step]
        for copy in keeps:
            copy.start()
        fetches[0].wait()
        products(0, lambda out: out)
        lane = lax.broadcasted_iota(jnp.int32, (1, LANES), 1)
        exponent = (lane % (HEAD_DIM // 2)).astype(F32) * (2.0 / HEAD_DIM)
        angles = place_ref[...] * jnp.exp(-math.log(10000.0) * exponent)
        cos_ref[...] = jnp.cos(angles)
        sin_ref[...] = jnp.where(lane % HEAD_DIM < HEAD_DIM // 2, -1.0, 1.0) * jnp.sin(angles)

    @pl.when(step == 1)
    def _():
        fetches[1].wait()
        products(1, lambda out: rotated(out, cos_ref[...], sin_ref[...], 1))

    @pl.when(step == 2)
    def _():
        fetches[2].wait()
        scale = 1.0 / math.sqrt(HEAD_DIM)
        products(2, lambda out: rotated(out, cos_ref[...], sin_ref[...], 1) * scale)
        for copy in keeps:
            copy.wait()


def project(x, left, right, place, gain, w_query, w_key, w_value, seqs):
    own, width = x.shape
    rows = own + seqs * 2 * HALF
    edge = whole((seqs * HALF, width))
    hbm = pl.BlockSpec(memory_space=pl.ANY)
    table = jax.ShapeDtypeStruct((rows, LANES), F32)
    return pl.pallas_call(
        functools.partial(project_kernel, seqs),
        grid=(3,),
        in_specs=[whole((own, width)), edge, edge, whole((rows, 1)), whole((1, width))] + [hbm] * 3,
        out_specs=[
            pl.BlockSpec((1, rows, width), lambda j: (j, 0, 0)),
            hbm,
            hbm,
            whole((rows, LANES)),
            whole((rows, LANES)),
        ],
        out_shape=[
            jax.ShapeDtypeStruct((3, rows, width), BF16),
            jax.ShapeDtypeStruct((rows, width), BF16),
            jax.ShapeDtypeStruct((own, width), BF16),
            table,
            table,
        ],
        scratch_shapes=[
            pltpu.VMEM((rows, width), BF16),
            pltpu.VMEM((3, width, width), BF16),
            pltpu.SemaphoreType.DMA((4 + seqs,)),
        ],
        compiler_params=params(1),
        cost_estimate=cost(6 * rows * width * width, 6 * width * width + 10 * rows * width),
        name="project",
    )(x, left, right, place, gain, w_value, w_key, w_query)


def stack_heads(block):
    lane = lax.broadcasted_iota(jnp.int32, block.shape, 1)
    zero = jnp.zeros_like(block)
    return jnp.concatenate(
        [jnp.where(lane // HEAD_DIM == h, block, zero) for h in range(GH)], axis=0
    )


def fill_keys(buf, ref):
    rows = ref.shape[1]
    buf[0:rows, :] = ref[0]
    if buf.shape[0] > rows:
        buf[rows:, :] = jnp.zeros((buf.shape[0] - rows, buf.shape[1]), buf.dtype)


def fill_queries(buf, ref, length):
    buf[0:length, :] = ref[0, HALF : HALF + length, :] if ref.ndim == 3 else ref[...]
    rest = buf.shape[0] - length
    if rest:
        buf[length:, :] = jnp.zeros((rest, buf.shape[1]), buf.dtype)


def attend_kernel(span_ref, q_ref, k_ref, v_ref, o_ref, p_ref, kbuf, vbuf, qbuf, vt, ot):
    length = o_ref.shape[0]
    padded = qbuf.shape[0]
    fill_keys(kbuf, k_ref)
    fill_keys(vbuf, v_ref)
    fill_queries(qbuf, q_ref, length)
    blocks = padded // QB

    def scores_of(b):
        return dot(kbuf[b * QB : b * QB + KB, :], stack_heads(qbuf[b * QB : (b + 1) * QB, :]), NT)

    def mix(b, probs):
        for h in range(GH):
            rows = slice(h * HEAD_DIM, (h + 1) * HEAD_DIM)
            ot[rows, b * QB : (b + 1) * QB] = dot(vt[rows, b * QB : b * QB + KB], probs[h]).astype(BF16)

    ahead = scores_of(0)
    vt[...] = vbuf[...].T
    before = None
    for b in range(blocks):
        scores = ahead
        if b + 1 < blocks:
            ahead = scores_of(b + 1)
        if before is not None:
            mix(b - 1, before)
        place = lax.broadcasted_iota(jnp.int32, (KB, QB), 0) + b * QB
        low = span_ref[0, 0:1, b * QB : (b + 1) * QB]
        high = span_ref[0, 1:2, b * QB : (b + 1) * QB]
        seen = (place >= low) & (place < high)
        before = []
        for h in range(GH):
            masked = jnp.where(seen, scores[:, h * QB : (h + 1) * QB], -1e30)
            terms = jnp.exp(masked - jnp.max(masked, axis=0, keepdims=True))
            total = jnp.sum(terms, axis=0, keepdims=True)
            probs = (terms * (1.0 / total)).astype(BF16)
            p_ref[:, b * GH * QB + h * QB : b * GH * QB + (h + 1) * QB] = probs
            before.append(probs)
    mix(blocks - 1, before)
    o_ref[...] = ot[...].T[0:length, :]


def attend(span, joint, seqs):
    _, rows, width = joint.shape
    length = rows // seqs - 2 * HALF
    rows = seqs * length
    padded = span.shape[2]
    groups = width // GROUP
    keys = padded + 2 * HALF
    own = pl.BlockSpec((length, GROUP), lambda s, g: (s, g))
    near = [pl.BlockSpec((1, length + 2 * HALF, GROUP), lambda s, g, i=i: (i, s, g)) for i in range(3)]
    return pl.pallas_call(
        attend_kernel,
        grid=(seqs, groups),
        in_specs=[
            pl.BlockSpec((1, 2, padded), lambda s, g: (s, 0, 0)),
            near[2],
            near[1],
            near[0],
        ],
        out_specs=[
            own,
            pl.BlockSpec((KB, GH * padded), lambda s, g: (s, g)),
        ],
        out_shape=[
            jax.ShapeDtypeStruct((rows, width), BF16),
            jax.ShapeDtypeStruct((seqs * KB, groups * GH * padded), BF16),
        ],
        scratch_shapes=[
            pltpu.VMEM((keys, GROUP), BF16),
            pltpu.VMEM((keys, GROUP), BF16),
            pltpu.VMEM((padded, GROUP), BF16),
            pltpu.VMEM((GROUP, keys), BF16),
            pltpu.VMEM((GROUP, padded), BF16),
        ],
        compiler_params=params(2),
        cost_estimate=cost(
            2 * 2 * seqs * width * padded * KB * 4, 2 * width * (4 * rows + KB * seqs * padded // 64)
        ),
        name="attend",
    )(span, joint, joint, joint)


def attend_back_kernel(
    flip_ref, p_ref, q_ref, k_ref, v_ref, g_ref, cos_ref, sin_ref,
    dq_ref, dkv_ref, near_ref, edge_ref, other_ref,
    kbuf, vbuf, qbuf, gbuf, kt, dqt, dkb, dvb,
):
    length = g_ref.shape[0]
    padded = qbuf.shape[0]
    fill_keys(kbuf, k_ref)
    fill_keys(vbuf, v_ref)
    fill_queries(qbuf, q_ref, length)
    fill_queries(gbuf, g_ref, length)
    blocks = padded // QB

    def probs_grads(b):
        g4 = stack_heads(gbuf[b * QB : (b + 1) * QB, :])
        return g4, dot(vbuf[b * QB : b * QB + KB, :], g4, NT)

    def spread(b, g4, probs, lows):
        at, keys = slice(b * QB, (b + 1) * QB), slice(b * QB, b * QB + KB)
        for h in range(GH):
            rows = slice(h * HEAD_DIM, (h + 1) * HEAD_DIM)
            dqt[rows, at] = dot(kt[rows, keys], lows[h])
        q4 = stack_heads(qbuf[at, :])
        grads = (dkb, dot(jnp.concatenate(lows, axis=1), q4)), (dvb, dot(probs, g4))
        for buf, grad in grads:
            if b:
                buf[at, :] += grad[:QB]
            else:
                buf[at, :] = grad[:QB]
            buf[(b + 1) * QB : b * QB + KB, :] = grad[QB:]

    ahead = probs_grads(0)
    kt[...] = kbuf[...].T
    before = None
    for b in range(blocks):
        g4, grads = ahead
        if b + 1 < blocks:
            ahead = probs_grads(b + 1)
        if before is not None:
            spread(b - 1, *before)
        probs = p_ref[:, b * GH * QB : (b + 1) * GH * QB]
        lows = []
        for h in range(GH):
            part = probs[:, h * QB : (h + 1) * QB].astype(F32)
            grad = grads[:, h * QB : (h + 1) * QB]
            delta = jnp.sum(part * grad, axis=0, keepdims=True)
            lows.append((part * (grad - delta)).astype(BF16))
        before = g4, probs, lows
    spread(blocks - 1, *before)
    cos_tab, sin_tab = cos_ref[...], sin_ref[...]
    middle = slice(HALF, HALF + length)
    dq = dqt[...].T[0:length, :] * (1.0 / math.sqrt(HEAD_DIM))
    dq_ref[...] = rotated(dq, cos_tab[middle], sin_tab[middle], -1).astype(BF16)
    span = length + 2 * HALF
    dk = rotated(dkb[0:span, :], cos_tab, sin_tab, -1).astype(BF16)
    dv = dvb[0:span, :].astype(BF16)
    for i, grad in enumerate((dk, dv)):
        dkv_ref[i] = grad[middle]
        near_ref[i] = grad
        ends = grad[0:HALF], grad[span - HALF :]
        edge_ref[i] = jnp.where(flip_ref[0] == 1, ends[1], ends[0])
        other_ref[i] = jnp.where(flip_ref[0] == 1, ends[0], ends[1])


def attend_back(flip, probs, joint, grad, cos_tab, sin_tab, seqs):
    rows, width = grad.shape
    length = rows // seqs
    padded = -(-length // QB) * QB
    groups = width // GROUP
    keys = padded + 2 * HALF
    own = pl.BlockSpec((length, GROUP), lambda s, g, f: (s, g))
    both = pl.BlockSpec((2, length, GROUP), lambda s, g, f: (0, s, g))
    both_near = pl.BlockSpec((2, length + 2 * HALF, GROUP), lambda s, g, f: (0, s, g))
    near = [pl.BlockSpec((1, length + 2 * HALF, GROUP), lambda s, g, f, i=i: (i, s, g)) for i in range(3)]
    table = pl.BlockSpec((length + 2 * HALF, LANES), lambda s, g, f: (s, 0))
    edge = pl.BlockSpec((2, HALF, GROUP), lambda s, g, f: (0, s, g))
    out_edge = jax.ShapeDtypeStruct((2, seqs * HALF, width), BF16)
    out = jax.ShapeDtypeStruct((rows, width), BF16)
    out_both = jax.ShapeDtypeStruct((2, rows, width), BF16)
    out_near = jax.ShapeDtypeStruct((2, rows + seqs * 2 * HALF, width), BF16)
    return pl.pallas_call(
        attend_back_kernel,
        grid_spec=pltpu.PrefetchScalarGridSpec(
            num_scalar_prefetch=1,
            grid=(seqs, groups),
        in_specs=[
            pl.BlockSpec((KB, GH * padded), lambda s, g, f: (s, g)),
            near[2],
            near[1],
            near[0],
            own,
            table,
            table,
        ],
        out_specs=[own, both, both_near, edge, edge],
        scratch_shapes=[
            pltpu.VMEM((keys, GROUP), BF16),
            pltpu.VMEM((keys, GROUP), BF16),
            pltpu.VMEM((padded, GROUP), BF16),
            pltpu.VMEM((padded, GROUP), BF16),
            pltpu.VMEM((GROUP, keys), BF16),
            pltpu.VMEM((GROUP, padded), F32),
            pltpu.VMEM((keys, GROUP), F32),
            pltpu.VMEM((keys, GROUP), F32),
        ],
        ),
        out_shape=[out, out_both, out_near, out_edge, out_edge],
        compiler_params=params(2),
        cost_estimate=cost(
            2 * 4 * seqs * width * padded * KB * 4, 2 * width * (8 * rows + KB * seqs * padded // 64)
        ),
        name="attend_back",
    )(flip, probs, joint, joint, joint, grad, cos_tab, sin_tab)


def edges_kernel(seqs, flags_ref, from_ref, left_ref, right_ref, to_ref, buf, sems):
    length = from_ref.shape[1] // seqs
    places = [
        (i, s, e, pl.ds(s * length + e * (length - HALF), HALF))
        for i in range(2)
        for s in range(seqs)
        for e in range(2)
    ]
    copies = [
        (from_ref.at[i, rows, :], to_ref.at[i, rows, :], buf.at[at]) for at, (i, _, _, rows) in enumerate(places)
    ]
    for at, (src, _, mid) in enumerate(copies):
        pltpu.make_async_copy(src, mid, sems.at[0, at]).start()
    for at, (src, _, mid) in enumerate(copies):
        pltpu.make_async_copy(src, mid, sems.at[0, at]).wait()
    for at, (i, s, e, _) in enumerate(places):
        got = (right_ref if e else left_ref)[i, s].astype(F32) * flags_ref[e].astype(F32)
        buf[at] = (buf[at].astype(F32) + got).astype(BF16)
    for at, (_, dst, mid) in enumerate(copies):
        pltpu.make_async_copy(mid, dst, sems.at[1, at]).start()
    for at, (_, dst, mid) in enumerate(copies):
        pltpu.make_async_copy(mid, dst, sems.at[1, at]).wait()


def add_edges(flags, grads, left, right):
    seqs = left.shape[1]
    hbm = pl.BlockSpec(memory_space=pl.ANY)
    return pl.pallas_call(
        functools.partial(edges_kernel, seqs),
        grid_spec=pltpu.PrefetchScalarGridSpec(
            num_scalar_prefetch=1,
            grid=(1,),
            in_specs=[hbm, whole(left.shape), whole(right.shape)],
            out_specs=hbm,
            scratch_shapes=[
                pltpu.VMEM((4 * seqs, HALF, grads.shape[2]), BF16),
                pltpu.SemaphoreType.DMA((2, 4 * seqs)),
            ],
        ),
        out_shape=jax.ShapeDtypeStruct(grads.shape, BF16),
        input_output_aliases={1: 0},
        compiler_params=params(1),
        cost_estimate=cost(1e4 * left.size, 8 * left.size, 1000),
        name="add_edges",
    )(flags, grads, left, right)


def out_proj_kernel(m_ref, x_ref, w_ref, scale_ref, gain_ref, attn_ref, in_ref):
    attn = dot(m_ref[...], w_ref[...])
    attn_ref[...] = attn.astype(BF16)
    middle = x_ref[...].astype(F32) + scale_ref[...] * attn
    inv = lax.rsqrt(jnp.mean(middle * middle, axis=-1, keepdims=True) + RMS_EPS)
    in_ref[...] = (middle * inv * gain_ref[...]).astype(BF16)


def out_proj(mixed, x, w_output, scale, gain):
    rows, width = x.shape
    block = rows // 2
    row = pl.BlockSpec((block, width), lambda i: (i, 0))
    return pl.pallas_call(
        out_proj_kernel,
        grid=(rows // block,),
        in_specs=[row, row, whole((width, width)), whole((1, width)), whole((1, width))],
        out_specs=[row, row],
        out_shape=[
            jax.ShapeDtypeStruct((rows, width), BF16),
            jax.ShapeDtypeStruct((rows, width), BF16),
        ],
        compiler_params=params(1),
        cost_estimate=cost(2 * rows * width * width, 2 * rows * width * 5 + 2 * width * width),
        name="out_proj",
    )(mixed, x, w_output, scale, gain)


def hidden_grad_kernel(core_ref, own_ref, peer_ref, scale_ref, one_ref, two_ref, low_ref, out_ref):
    rows = own_ref.shape[0]
    block = one_ref.shape[0]

    @pl.when(pl.program_id(0) == 0)
    def _():
        low_ref[0:rows, :] = (own_ref[...].astype(F32) * scale_ref[...]).astype(BF16)
        low_ref[rows:, :] = (peer_ref[...].astype(F32) * scale_ref[...]).astype(BF16)

    out_ref[:, :block] = dot(low_ref[...], one_ref[...], NT).astype(BF16)
    out_ref[:, block:] = dot(low_ref[...], two_ref[...], NT).astype(BF16)


def hidden_grad(core, own, peer, scale, w_down, block):
    rows, width = own.shape
    count = w_down.shape[0] // block // 4
    half = w_down.shape[0] // 2
    return pl.pallas_call(
        hidden_grad_kernel,
        grid_spec=pltpu.PrefetchScalarGridSpec(
            num_scalar_prefetch=1,
            grid=(count,),
            in_specs=[
                whole((rows, width)),
                whole((rows, width)),
                whole((1, width)),
                pl.BlockSpec((block, width), lambda j, c: (4 * j + c[0], 0)),
                pl.BlockSpec((block, width), lambda j, c: (4 * j + 2 + c[0], 0)),
            ],
            out_specs=[
                whole((2 * rows, width)),
                pl.BlockSpec((2 * rows, 2 * block), lambda j, c: (0, j)),
            ],
        ),
        out_shape=[
            jax.ShapeDtypeStruct((2 * rows, width), BF16),
            jax.ShapeDtypeStruct((2 * rows, half), BF16),
        ],
        compiler_params=params(1),
        cost_estimate=cost(
            4 * rows * width * half, 2 * (4 * rows * width + half * (width + 2 * rows))
        ),
        name="hidden_grad",
    )(core, own, peer, scale, w_down, w_down)


def halves_of(value, bit, inner):
    rows, columns = value.shape
    both = value.reshape(rows // (2 * inner), 2, inner, columns)
    zero, one = both[:, 0], both[:, 1]
    out = jnp.where(bit == 0, one, zero).reshape(rows // 2, columns)
    stay = jnp.where(bit == 0, zero, one).reshape(rows // 2, columns)
    return out, stay


def feed_kernel(inners, core_ref, xo_ref, xp_ref, gh_ref, wg_ref, wu_ref, *refs):
    hid_own_ref, hid_peer_ref, gg_ref, gu_ref, *outs, x_all = refs[-9:]
    rows = xo_ref.shape[0]

    @pl.when(pl.program_id(0) == 0)
    def _():
        x_all[0:rows, :] = xo_ref[...]
        x_all[rows:, :] = xp_ref[...]

    for at in (0, rows):
        part = slice(at, at + rows)
        gate = dot(x_all[part, :], wg_ref[...])
        up = dot(x_all[part, :], wu_ref[...])
        grad = gh_ref[part, :].astype(F32)
        sig = 1.0 / (1.0 + jnp.exp(-gate))
        act = gate * sig
        (hid_peer_ref if at else hid_own_ref)[...] = (act * up).astype(BF16)
        gg_ref[part, :] = (grad * up * sig * (1.0 + gate * (1.0 - sig))).astype(BF16)
        gu_ref[part, :] = (grad * act).astype(BF16)
    for i, src in enumerate((gg_ref, gu_ref)):
        out, stay = halves_of(dot(x_all[...], src[...], TN), core_ref[1 + i], inners[i])
        outs[2 * i][...] = out.astype(BF16)
        outs[2 * i + 1][...] = stay.astype(BF16)


def feed(core, x_own, x_peer, grad_hidden, w_gate, w_up, block, first, count, before, inners):
    rows, width = x_own.shape
    half = grad_hidden.shape[1]
    wide = pl.BlockSpec((2 * rows, block), lambda j, c: (0, j + first))
    weight = pl.BlockSpec((width, block), lambda j, c: (0, 2 * (j + first) + c[0]))
    tall = pl.BlockSpec((rows, block), lambda j, c: (0, j + first))
    kept = pltpu.HBM((2 * rows, half), BF16)
    single = pltpu.HBM((rows, half), BF16)
    grads = pltpu.HBM((width // 2, count * block), BF16)
    any_spec = pl.BlockSpec(memory_space=pl.ANY)
    return pl.pallas_call(
        functools.partial(feed_kernel, inners),
        grid_spec=pltpu.PrefetchScalarGridSpec(
            num_scalar_prefetch=1,
            grid=(count,),
            in_specs=[whole((rows, width)), whole((rows, width)), wide, weight, weight]
            + [any_spec] * len(before),
            out_specs=[tall] * 2
            + [wide] * 2
            + [pl.BlockSpec((width // 2, block), lambda j, c: (0, j))] * 4,
            scratch_shapes=[pltpu.VMEM((2 * rows, width), BF16)],
        ),
        out_shape=[single] * 2 + [kept] * 2 + [grads] * 4,
        input_output_aliases={6 + i: i for i in range(len(before))},
        compiler_params=params(1, 46 << 20),
        cost_estimate=cost(
            2 * 2 * rows * width * block * count * 4,
            2 * (4 * rows * width + count * block * (8 * rows + 4 * width)),
        ),
        name="feed",
    )(core, *in_hbm([x_own]), x_peer, *in_hbm([grad_hidden, w_gate, w_up, *before]))


def down_kernel(each, inners, bits_ref, own_ref, peer_ref, low_ref, *refs):
    *outs, both = refs
    both[: own_ref.shape[0], :] = own_ref[...]
    both[own_ref.shape[0] :, :] = peer_ref[...]
    value = dot(both[...], low_ref[...], TN)
    rows, width = value.shape
    value = value.reshape(rows // (2 * each), 2, each, width)
    for i in range(2):
        part = value[:, i].reshape(rows // 2, width)
        out, stay = halves_of(part, bits_ref[1 + i], inners[i])
        outs[2 * i][...] = out.astype(BF16)
        outs[2 * i + 1][...] = stay.astype(BF16)


def down(bits, own, peer, low, each, inners):
    rows, half = own.shape
    width = low.shape[1]
    block = 512
    out = jax.ShapeDtypeStruct((half // 4, width), BF16)
    return pl.pallas_call(
        functools.partial(down_kernel, each, inners),
        grid_spec=pltpu.PrefetchScalarGridSpec(
            num_scalar_prefetch=1,
            grid=(half // block,),
            in_specs=[
                pl.BlockSpec((rows, block), lambda j, c: (0, j)),
                pl.BlockSpec((rows, block), lambda j, c: (0, j)),
                whole((2 * rows, width)),
            ],
            out_specs=[pl.BlockSpec((block // 4, width), lambda j, c: (j, 0))] * 4,
            scratch_shapes=[pltpu.VMEM((2 * rows, block), BF16)],
        ),
        out_shape=[out] * 4,
        compiler_params=params(1),
        cost_estimate=cost(
            4 * rows * half * width, 2 * (2 * rows * half + 2 * rows * width + half * width)
        ),
        name="down_weight",
    )(bits, own, peer, low)


def in_halves(value, refs):
    half = value.shape[1] // 2
    refs[0][...] = value[:, :half]
    refs[1][...] = value[:, half:]


def feed_back_kernel(core_ref, *refs):
    *peer_refs, own_ref, acc = refs[-4:]
    part, step = pl.program_id(0), pl.program_id(1)
    block = refs[2].shape[1]
    total = None
    for i in range(2):
        for half in range(2):
            out = dot(refs[i][:, half * block : (half + 1) * block], refs[2 + 2 * i + half][...], NT)
            total = out if total is None else total + out
    last = pl.num_programs(1) - 1

    @pl.when(step == 0)
    def _():
        acc[...] = total

    @pl.when((step > 0) & (step < last))
    def _():
        acc[...] += total

    @pl.when((step == last) & (part == 0))
    def _():
        in_halves((acc[...] + total).astype(BF16), peer_refs)

    @pl.when((step == last) & (part == 1))
    def _():
        own_ref[...] = (acc[...] + total).astype(BF16)


def feed_back(core, grad_gate, grad_up, w_gate, w_up, block):
    rows, half = grad_gate.shape
    rows = rows // 2
    width = w_gate.shape[0]
    tall = pl.BlockSpec((rows, 2 * block), lambda p, j, c: (1 - p, j))
    one = pl.BlockSpec((width, block), lambda p, j, c: (0, 4 * j + c[0]))
    two = pl.BlockSpec((width, block), lambda p, j, c: (0, 4 * j + 2 + c[0]))
    return pl.pallas_call(
        feed_back_kernel,
        grid_spec=pltpu.PrefetchScalarGridSpec(
            num_scalar_prefetch=1,
            grid=(2, half // block // 2),
            in_specs=[tall, tall, one, two, one, two],
            out_specs=[whole((rows, width // 2))] * 2 + [whole((rows, width))],
            scratch_shapes=[pltpu.VMEM((rows, width), F32)],
        ),
        out_shape=[jax.ShapeDtypeStruct((rows, width // 2), BF16)] * 2
        + [jax.ShapeDtypeStruct((rows, width), BF16)],
        compiler_params=params(2),
        cost_estimate=cost(8 * rows * half * width, 8 * (rows * half + half * width)),
        name="feed_back",
    )(core, grad_gate, grad_up, w_gate, w_gate, w_up, w_up)


def join_kernel(
    x_ref, attn_ref, g_ref, in_ref, got_one_ref, got_two_ref, attn_scale_ref, gain_ref, w_ref,
    grad_attn_ref, grad_mixed_ref, middle_ref, sums_ref,
):
    x = x_ref[...].astype(F32)
    attn = attn_ref[...].astype(F32)
    grad_y = g_ref[...].astype(F32)
    got = jnp.concatenate([got_one_ref[...], got_two_ref[...]], axis=1)
    grad_in = in_ref[...].astype(F32) + got.astype(F32)
    middle = x + attn_scale_ref[...] * attn
    inv = lax.rsqrt(jnp.mean(middle * middle, axis=-1, keepdims=True) + RMS_EPS)
    unit = middle * inv
    scaled = grad_in * gain_ref[...]
    grad_middle = grad_y + inv * (scaled - unit * jnp.mean(scaled * unit, axis=-1, keepdims=True))
    middle_ref[...] = grad_middle.astype(BF16)
    grad_attn = (attn_scale_ref[...] * grad_middle).astype(BF16)
    grad_attn_ref[...] = grad_attn
    grad_mixed_ref[...] = dot(grad_attn, w_ref[...], NT).astype(BF16)

    @pl.when(pl.program_id(0) == 0)
    def _():
        sums_ref[...] = jnp.zeros_like(sums_ref)

    sums_ref[0:1, :] += jnp.sum(grad_middle * attn, axis=0, keepdims=True)
    sums_ref[1:2, :] += jnp.sum(grad_in * unit, axis=0, keepdims=True)


def join(x, attn, grad_y, grad_in, got, attn_scale, gain, w_output):
    rows, width = x.shape
    block = rows // 2
    row = pl.BlockSpec((block, width), lambda i: (i, 0))
    half = pl.BlockSpec((block, width // 2), lambda i: (i, 0))
    vec = whole((1, width))
    low = jax.ShapeDtypeStruct((rows, width), BF16)
    return pl.pallas_call(
        join_kernel,
        grid=(rows // block,),
        in_specs=[row] * 4 + [half] * 2 + [vec] * 2 + [whole((width, width))],
        out_specs=[row] * 3 + [whole((8, width))],
        out_shape=[
            low,
            low,
            low,
            jax.ShapeDtypeStruct((8, width), F32),
        ],
        compiler_params=params(1),
        cost_estimate=cost(2 * rows * width * width, rows * width * 22 + 2 * width * width),
        name="join",
    )(x, attn, grad_y, grad_in, *got, attn_scale, gain, w_output)


def feed_out_kernel(
    core_ref, own_ref, got_ref, w_ref, x_ref, attn_ref, g_ref, attn_scale_ref, mlp_scale_ref,
    layer_ref, sums_ref, hidden, acc,
):
    step, last = pl.program_id(0), pl.num_programs(0) - 1
    block = own_ref.shape[1] // 2
    for i in range(2):
        part = slice(i * block, (i + 1) * block)
        own, got = own_ref[:, part], got_ref[:, part]
        first = core_ref[0] == 0
        hidden[:, 2 * i * block : (2 * i + 1) * block] = jnp.where(first, own, got)
        hidden[:, (2 * i + 1) * block : (2 * i + 2) * block] = jnp.where(first, got, own)
    total = dot(hidden[...], w_ref[...])

    @pl.when(step == 0)
    def _():
        acc[...] = total

    @pl.when((step > 0) & (step < last))
    def _():
        acc[...] += total

    @pl.when(step == last)
    def _():
        down_out = acc[...] + total
        middle = x_ref[...].astype(F32) + attn_scale_ref[...] * attn_ref[...].astype(F32)
        layer_ref[...] = (middle + mlp_scale_ref[...] * down_out).astype(BF16)
        sums_ref[...] = jnp.zeros_like(sums_ref)
        sums_ref[0:1, :] = jnp.sum(g_ref[...].astype(F32) * down_out, axis=0, keepdims=True)


def feed_out(core, own, got, w_down, x, attn, grad_y, attn_scale, mlp_scale, block):
    rows, half = own.shape
    width = w_down.shape[1]
    tall = pl.BlockSpec((rows, 2 * block), lambda j, c: (0, j))
    row, vec = whole((rows, width)), whole((1, width))
    return pl.pallas_call(
        feed_out_kernel,
        grid_spec=pltpu.PrefetchScalarGridSpec(
            num_scalar_prefetch=1,
            grid=(half // block // 2,),
            in_specs=[tall, tall, pl.BlockSpec((4 * block, width), lambda j, c: (j, 0))]
            + [row] * 3
            + [vec] * 2,
            out_specs=[row, whole((8, width))],
            scratch_shapes=[pltpu.VMEM((rows, 4 * block), BF16), pltpu.VMEM((rows, width), F32)],
        ),
        out_shape=[
            jax.ShapeDtypeStruct((rows, width), BF16),
            jax.ShapeDtypeStruct((8, width), F32),
        ],
        compiler_params=params(1),
        cost_estimate=cost(4 * rows * half * width, 4 * (rows * half + half * width), 10),
        name="feed_out",
    )(core, own, got, w_down, x, attn, grad_y, attn_scale, mlp_scale)


def weight_grad_kernel(inner, order, counts, bit_ref, *refs):
    out_ref, stay_ref = refs[-2:]
    step = pl.program_id(0)
    lefts = [refs[i] for i in order]
    rights = refs[max(order) + 1 : -2]
    first = 0
    for left, right, count in zip(lefts, rights, counts):

        @pl.when((step >= first) & (step < first + count))
        def _(left=left, right=right):
            rows = right[...].reshape(right.shape[-2:])
            out, stay = halves_of(dot(left[...], rows, TN), bit_ref[0], inner)
            out_ref[...] = out.astype(BF16)
            stay_ref[...] = stay.astype(BF16)

        first += count


def weight_grad(bit, inner, pairs, name, scale):
    block = 512
    width = pairs[0][0].shape[1]
    lefts = []
    for left, _ in pairs:
        if not any(left is other for other in lefts):
            lefts.append(left)
    order = [[left is other for other in lefts].index(True) for left, _ in pairs]
    counts, specs, rights, first = [], [], [], 0
    for left, right in pairs:
        rows = left.shape[0]
        array, part = right if isinstance(right, tuple) else (right, None)
        count = array.shape[-1] // block
        at = lambda j, first=first, count=count: jnp.clip(j - first, 0, count - 1)
        if part is None:
            specs.append(pl.BlockSpec((rows, block), lambda j, c, at=at: (0, at(j))))
        else:
            specs.append(
                pl.BlockSpec((1, rows, block), lambda j, c, at=at, part=part: (part, 0, at(j)))
            )
        rights.append(array)
        counts.append(count)
        first += count
    out = jax.ShapeDtypeStruct((width // 2, first * block), BF16)
    return pl.pallas_call(
        functools.partial(weight_grad_kernel, inner, order, counts),
        grid_spec=pltpu.PrefetchScalarGridSpec(
            num_scalar_prefetch=1,
            grid=(first,),
            in_specs=[whole(left.shape) for left in lefts] + specs,
            out_specs=[pl.BlockSpec((width // 2, block), lambda j, c: (0, j))] * 2,
        ),
        out_shape=[out, out],
        compiler_params=params(1),
        cost_estimate=cost(
            2 * rows * width * first * block,
            2 * (len(lefts) * rows * width + (rows + width) * first * block),
            scale,
        ),
        name=name,
    )(bit, *lefts, *rights)


def input_grad_kernel(
    x_ref, gq_ref, gk_ref, gv_ref, middle_ref, gain_ref, wq_ref, wk_ref, wv_ref, out_ref, sums_ref
):
    grad = (
        dot(gq_ref[...], wq_ref[...], NT)
        + dot(gk_ref[0], wk_ref[...], NT)
        + dot(gv_ref[0], wv_ref[...], NT)
    )
    x = x_ref[...].astype(F32)
    centered = x - jnp.mean(x, axis=-1, keepdims=True)
    inv = lax.rsqrt(jnp.mean(centered * centered, axis=-1, keepdims=True) + LN_EPS)
    unit = centered * inv
    scaled = grad * gain_ref[...]
    back = inv * (
        scaled
        - jnp.mean(scaled, axis=-1, keepdims=True)
        - unit * jnp.mean(scaled * unit, axis=-1, keepdims=True)
    )
    out_ref[...] = (middle_ref[...].astype(F32) + back).astype(BF16)

    @pl.when(pl.program_id(0) == 0)
    def _():
        sums_ref[...] = jnp.zeros_like(sums_ref)

    sums_ref[0:1, :] += jnp.sum(grad * unit, axis=0, keepdims=True)


def input_grad(x, gq, gkv, grad_middle, gain, w_query, w_key, w_value):
    rows, width = x.shape
    block = rows // 2
    row = pl.BlockSpec((block, width), lambda i: (i, 0))
    square = whole((width, width))
    return pl.pallas_call(
        input_grad_kernel,
        grid=(rows // block,),
        in_specs=[
            row,
            row,
            pl.BlockSpec((1, block, width), lambda i: (0, i, 0)),
            pl.BlockSpec((1, block, width), lambda i: (1, i, 0)),
            row,
            whole((1, width)),
        ]
        + [square] * 3,
        out_specs=[row, whole((8, width))],
        out_shape=[
            jax.ShapeDtypeStruct((rows, width), BF16),
            jax.ShapeDtypeStruct((8, width), F32),
        ],
        compiler_params=params(1),
        cost_estimate=cost(2 * 3 * rows * width * width, rows * width * 14 + 6 * width * width),
        name="input_grad",
    )(x, gq, gkv, gkv, grad_middle, gain, w_query, w_key, w_value)


def log2(n):
    return n.bit_length() - 1


class Places:
    def __init__(self):
        self.n_seq, self.n_sp = lax.axis_size("seq"), lax.axis_size("sp")
        self.sp_bits = log2(self.n_sp)
        self.count = self.sp_bits + log2(self.n_seq)
        self.core = self.sp_bits
        self.me = lax.axis_index("seq") * self.n_sp + lax.axis_index("sp")
        self.down_bits = [b for b in reversed(range(self.count)) if b != self.core]

    def swap(self, value, bit):
        if bit < self.sp_bits:
            axis, size, at = "sp", self.n_sp, bit
        else:
            axis, size, at = "seq", self.n_seq, bit - self.sp_bits
        return lax.ppermute(value, axis, [(i, i ^ (1 << at)) for i in range(size)])

    def send(self, value, flip):
        pairs = [(i, i ^ flip) for i in range(1 << self.count)]
        return lax.ppermute(value, ("seq", "sp"), pairs)

    def own(self, bit):
        return (self.me >> bit) & 1


def round_kernel(has, inners, bits_ref, *refs):
    two, one, new, carry = has
    refs = list(refs)
    take = lambda n: [refs.pop(0) for _ in range(n)]
    second, carried = take(4) if two else (), take(2) if carry else ()
    first = take(4) if one else ()
    fresh = take({"sent": 2, "core": 4, "": 0}[new])
    bufs = take(2) if one or new else ()
    bits = bits_ref[1], bits_ref[2], bits_ref[3]

    def split(keep, got, bit, inner):
        total = keep[...].astype(F32) + got[...].astype(F32)
        return [v.astype(BF16) for v in halves_of(total, bit, inner)]

    if two:
        outs = take(2)
        at = carried[0].shape[0] if carry else 0
        for src, dst in zip(carried, outs):
            dst[0:at, :] = src[...]
        for i in range(2):
            rows = second[i].shape[0] // 2
            for dst, part in zip(outs, split(second[i], second[2 + i], bits[2], inners["two"])):
                dst[at : at + rows, :] = part
            at += rows
    at = [0, 0]
    if new:
        stays = take(2) if new == "core" else ()
        for i in range(2):
            if new == "core":
                out, stays[i][...] = split(fresh[2 * i], fresh[2 * i + 1], bits[i], inners["new"][i])
            else:
                out = fresh[i][...]
            at[i] = out.shape[0]
            bufs[i][0 : at[i], :] = out
    if one:
        stays = take(2)
        for i in range(2):
            out, stays[i][...] = split(first[i], first[2 + i], bits[1 - i], inners["one"][i])
            bufs[1 - i][at[1 - i] :, :] = out


class Rounds:
    def __init__(self, places, x, y, z):
        self.places, self.x, self.y, self.z = places, x, y, z
        self.one = self.two = None
        self.got = []

    def inner(self, group, without, bit):
        bits = [b for b in sorted(group["bits"], reverse=True) if b not in without]
        return group["each"] << (len(bits) - 1 - bits.index(bit))

    def first_inners(self, bits, each):
        group = {"bits": bits, "each": each}
        return [self.inner(group, (), self.x), self.inner(group, (), self.y)]

    def send(self, buf_x, buf_y):
        self.got = [self.places.swap(buf_x, self.x), self.places.swap(buf_y, self.y)]

    def begin(self, parts, bits, each):
        self.one = {"bits": bits, "each": each, "keep": [parts[1], parts[3]]}
        self.send(parts[0], parts[2])

    def set_aside(self):
        group, self.two = self.two, None
        return dict(group, got=self.got)

    def run(self, flags, new="", arrays=(), bits=(), each=0, carry=(), wait=False, aside=None, scale=0.02):
        one = self.one
        two = aside or self.two
        steps = 2
        ins, specs, outs, inners, heights, wide = [], [], [], {}, [0, 0], 0

        def tall(rows, columns, at=0, row=0):
            return pl.BlockSpec((rows, columns // steps), lambda j, b: (row, j + at))

        if two:
            rows, columns = two["keep"][0].shape
            got_x, got_y = two["got"] if aside else self.got
            ins += two["keep"] + [got_y, got_x]
            last = [got_y.shape[0] // rows - 1, got_x.shape[0] // rows - 1]
            specs += [tall(rows, columns)] * 2 + [tall(rows, columns, 0, row) for row in last]
            ins += carry
            specs += [tall(*v.shape) for v in carry]
            outs += [(rows + (carry[0].shape[0] if carry else 0), columns)] * 2
            inners["two"] = self.inner(two, (self.x, self.y), self.z)
        group = {"bits": list(bits), "each": each}
        if one:
            rows, wide = one["keep"][0].shape
            ins += one["keep"] + self.got
            specs += [tall(rows, wide)] * 4
            inners["one"] = self.inner(one, (self.x,), self.y), self.inner(one, (self.y,), self.x)
        if new == "sent":
            ins += [arrays[0], arrays[2]]
            specs += [tall(*arrays[0].shape), tall(*arrays[2].shape)]
            heights, wide = [arrays[0].shape[0], arrays[2].shape[0]], arrays[0].shape[1]
            group["keep"] = [arrays[1], arrays[3]]
        if new == "core":
            keep, got = arrays
            rows, wide = keep.shape[0], keep.shape[1] // 2
            ins += [keep, got, keep, got]
            specs += [tall(rows, wide)] * 2 + [tall(rows, wide, steps)] * 2
            heights = [rows // 2, rows // 2]
            outs += [(rows // 2, wide)] * 2
            inners["new"] = self.first_inners(bits, each)
        if one:
            rows = one["keep"][0].shape[0] // 2
            heights = [h + rows for h in heights]
            outs += [(rows, wide)] * 2
        if one or new:
            outs = [(h, wide) for h in heights] + outs
        size = sum(v.size for v in ins)
        ins = [
            v if any(v is g for g in self.got) else in_hbm([v])[0] for v in ins
        ]
        results = list(
            pl.pallas_call(
                functools.partial(round_kernel, (bool(two), bool(one), new, bool(carry)), inners),
                grid_spec=pltpu.PrefetchScalarGridSpec(
                    num_scalar_prefetch=1,
                    grid=(steps,),
                    in_specs=specs,
                    out_specs=[tall(*shape) for shape in outs],
                ),
                out_shape=[pltpu.HBM(shape, BF16) for shape in outs],
                compiler_params=params(1, 24 << 20),
                cost_estimate=cost(2 * size, 4 * size, scale),
                name="round",
            )(flags, *ins)
        )
        take = lambda n: [results.pop(0) for _ in range(n)]
        buf_x, buf_y = take(2) if one or new else (None, None)
        done = None
        if two:
            done = take(2)
            if not wait:
                piece = Piece(self.places, [b for b in two["bits"] if b not in (self.x, self.y)], two["each"])
                piece.fork(*done, self.z)
                done = piece
        if new == "core":
            group["keep"] = take(2)
        self.two = dict(one, keep=take(2)) if one else None
        self.one = group if new else None
        self.got = []
        if one or new:
            self.send(buf_x, buf_y)
        return done


class Piece:
    def __init__(self, places, bits, each):
        self.places, self.bits, self.each = places, sorted(bits, reverse=True), each
        self.keep = self.got = None
        self.at = 0

    def inner(self, bit):
        return self.each << (len(self.bits) - 1 - self.bits.index(bit))

    def fork(self, out, stay, bit):
        self.bits.remove(bit)
        self.keep, self.got = stay, self.places.swap(out, bit)
        self.at, self.columns = 0, stay.shape[1]

    def split(self, bit):
        rows, columns = self.keep.shape
        inner = self.inner(bit)
        both = self.keep.reshape(rows // (2 * inner), 2, inner, columns)
        at = self.places.own(bit)
        out = lax.dynamic_index_in_dim(both, 1 - at, 1, False).reshape(rows // 2, columns)
        stay = lax.dynamic_index_in_dim(both, at, 1, False).reshape(rows // 2, columns)
        self.fork(out, stay, bit)

    def add(self, low=True):
        cols = slice(self.at * self.columns, (self.at + 1) * self.columns)
        self.keep = self.keep[:, cols].astype(F32) + self.got[:, cols].astype(F32)
        self.at = 0
        if low:
            self.keep = self.keep.astype(BF16)


def share(places, value, bits, group):
    axes = [bits.index(b) for b in group]

    def part(flip):
        out = value
        for b, axis in zip(group, axes):
            out = lax.dynamic_index_in_dim(out, places.own(b) ^ ((flip >> b) & 1), axis, True)
        return lax.squeeze(out, axes)

    flips = [sum(b << g for b, g in zip(f, group)) for f in np.ndindex(*(2,) * len(group))]
    return [part(0)] + [places.send(part(f), f) for f in flips if f]


def hold(small, *arrays):
    small, *arrays = lax.optimization_barrier((small, *arrays))
    return (small, *arrays)


def meet(small, arrays=(), pieces=(), rounds=None):
    many = list(arrays), [p.got for p in pieces], list(rounds.got) if rounds else []
    small, (arrays, gots, round_gots) = lax.optimization_barrier((small, many))
    for p, g in zip(pieces, gots):
        p.got = g
    if rounds:
        rounds.got = round_gots
    return (small, *arrays)


def on_device(
    frames, clip_ids, norm_gain, w_query, w_key, w_value, w_output, attn_scale,
    mlp_gain, w_gate, w_up, w_down, mlp_scale, out_grad,
):
    places = Places()
    seqs, length, width = frames.shape
    total_len = clip_ids.shape[1]
    rows = seqs * length
    n_sp, n_seq = places.n_sp, places.n_seq
    devices = n_sp * n_seq
    feed_width = w_gate.shape[1]
    own_rows = width // devices
    feed_rows = feed_width // devices
    block = feed_rows * n_sp
    core = lax.axis_index("seq") & 1
    sp = lax.axis_index("sp")
    sp_bits = list(reversed(range(places.core)))
    seq_bits = list(range(places.core + 1, places.count))
    x_bit, y_bit, z_bit = sp_bits[0], seq_bits[0], seq_bits[1]
    late = seq_bits[2:] + sp_bits[1:]
    every = list(range(places.count))
    not_core = [b for b in every if b != places.core]
    flags = jnp.stack([places.own(b) for b in (places.core, x_bit, y_bit, z_bit)]).astype(jnp.int32)
    rounds = Rounds(places, x_bit, y_bit, z_bit)

    x = frames.reshape(rows, width)
    grad_y = out_grad.reshape(rows, width)

    def neighbours(last, first):
        if n_sp == 2:
            got = lax.ppermute(jnp.where(sp == 0, last, first), "sp", [(0, 1), (1, 0)])
            return got, got
        return (
            lax.ppermute(last, "sp", [(i, i + 1) for i in range(n_sp - 1)]),
            lax.ppermute(first, "sp", [(i + 1, i) for i in range(n_sp - 1)]),
        )

    has = jnp.stack([sp > 0, sp < n_sp - 1]).astype(jnp.int32)
    from_left, from_right = neighbours(frames[:, length - HALF :], frames[:, :HALF])
    grad_y_peer = places.swap(grad_y, places.core)

    start = sp * length
    near = lax.dynamic_slice_in_dim(
        jnp.pad(clip_ids, ((0, 0), (HALF, HALF))), start, length + 2 * HALF, 1
    )
    ids = jnp.arange(CLIPS + 1, dtype=jnp.int32)
    begins = jnp.sum((clip_ids[:, None, :] < ids[:, None]).astype(jnp.int32), axis=-1)
    is_id = near[:, None, :] == ids[:CLIPS, None]
    first = jnp.sum(jnp.where(is_id, begins[:, :CLIPS, None], 0), axis=1)
    end = jnp.sum(jnp.where(is_id, begins[:, 1:, None], 0), axis=1)
    frame = lax.broadcasted_iota(jnp.int32, near.shape, 1) + (start - HALF)
    place = (frame - first).astype(F32).reshape(-1, 1)
    mid = slice(HALF, HALF + length)
    low = jnp.maximum(frame - HALF, first)[:, mid] - (start - HALF)
    high = jnp.minimum(frame + HALF, end)[:, mid] - (start - HALF)
    padded = -(-length // QB) * QB
    span = jnp.pad(jnp.stack([low, high], axis=1), ((0, 0), (0, 0), (0, padded - length)))

    gain = norm_gain[None]
    joint, normed, normed_own, cos_tab, sin_tab = project(
        x, from_left.reshape(-1, width), from_right.reshape(-1, width), place, gain,
        w_query, w_key, w_value, seqs,
    )
    mixed, probs = attend(span, joint, seqs)

    attn_out, mlp_in = out_proj(mixed, x, w_output, attn_scale[None], mlp_gain[None])
    flags_now, mlp_in = hold(flags, mlp_in)
    mlp_in_peer = places.swap(mlp_in, places.core)
    grad_low, grad_hidden = hidden_grad(
        flags_now, grad_y, grad_y_peer, mlp_scale[None], w_down, block
    )

    blocks = n_seq // 2
    per = blocks // 2

    def onward(piece):
        piece.add()
        piece.split(late[-1 - piece.left])
        piece.left -= 1

    def started(piece):
        piece.left = len(late) - 1
        return piece

    def finished(piece):
        while piece.left >= 0:
            onward(piece)
        piece.add(False)
        return piece.keep

    inners = rounds.first_inners(every, own_rows)
    *kept, a, b, c, d = feed(
        flags, mlp_in, mlp_in_peer, grad_hidden, w_gate, w_up, block, 0, per, (), inners
    )
    rounds.begin((a, b, c, d), every, own_rows)
    *kept, a, b, c, d = feed(
        flags, mlp_in, mlp_in_peer, grad_hidden, w_gate, w_up, block, per, per, kept, inners
    )
    hidden, hidden_peer, grad_gate, grad_up = kept
    hidden_got = places.swap(hidden_peer, places.core)
    flags_now, a = meet(flags, [a], rounds=rounds)
    rounds.run(flags_now, "sent", (a, b, c, d), every, own_rows)

    flags_now, rounds.two["keep"][0] = meet(flags, [rounds.two["keep"][0]])
    *in_peer, in_own = feed_back(flags_now, grad_gate, grad_up, w_gate, w_up, block)
    in_got = [places.swap(v, places.core) for v in in_peer]

    flags_now, in_own = meet(flags, [in_own])
    each = feed_rows // 2
    parts = down(
        flags_now, hidden, hidden_peer, grad_low, each, rounds.first_inners(not_core, each)
    )

    flags_now, *both = meet(flags, [*in_got, *parts], rounds=rounds)
    in_got, parts = both[:2], both[2:]
    carry = rounds.run(flags_now, "sent", parts, not_core, each, wait=True)

    scale_row, rounds.two["keep"][0], hidden_got = meet(
        attn_scale[None], [rounds.two["keep"][0], hidden_got]
    )
    grad_attn, grad_mixed, grad_middle, join_sums = join(
        x, attn_out, grad_y, in_own, in_got, scale_row, mlp_gain[None], w_output
    )
    flip = ((sp == 0) & (n_sp == 2)).astype(jnp.int32).reshape(1)
    grad_query, grad_kv, grad_near, edge, other_edge = attend_back(
        flip, probs, joint, grad_mixed, cos_tab, sin_tab, seqs
    )
    if n_sp == 2:
        to_right = to_left = lax.ppermute(edge, "sp", [(0, 1), (1, 0)])
    else:
        to_left = lax.ppermute(edge, "sp", [(i + 1, i) for i in range(n_sp - 1)])
        to_right = lax.ppermute(other_edge, "sp", [(i, i + 1) for i in range(n_sp - 1)])
    to_right, to_left = [v.reshape(2, seqs, HALF, width) for v in (to_right, to_left)]

    core_inner = Piece(places, every, own_rows).inner(places.core)

    flags_now, grad_query = meet(flags, [grad_query])
    out, stay = weight_grad(
        flags_now,
        core_inner,
        [(mixed, grad_attn), (normed_own, grad_query), (normed, (grad_near, 0)), (normed, (grad_near, 1))],
        "attention_weights",
        0.02,
    )
    from_core = places.swap(out, places.core)

    flags_now, stay, to_right, to_left = meet(flags, [stay, to_right, to_left], [], rounds)
    first = started(rounds.run(flags_now, carry=carry))
    aside = rounds.set_aside()
    has_now, aside["keep"][0] = meet(has, [aside["keep"][0]])
    grad_kv = add_edges(has_now, grad_kv, to_right, to_left)
    flags_now, grad_kv, from_core = meet(flags, [grad_kv, from_core])
    rounds.run(flags_now, "core", (stay, from_core), not_core, own_rows)

    flags_now, rounds.one["keep"][0], *aside["got"] = meet(
        flags, [rounds.one["keep"][0], *aside["got"]]
    )
    layer_out, out_sums = feed_out(
        flags_now, hidden, hidden_got, w_down, x, attn_out, grad_y,
        attn_scale[None], mlp_scale[None], block,
    )
    flags_now, layer_out, join_sums = meet(flags, [layer_out, join_sums], [first])
    onward(first)
    flags_now, first.keep = meet(flags_now, [first.keep], [], rounds)
    third = started(rounds.run(flags_now, aside=aside))
    gain_now, rounds.two["keep"][0] = meet(gain, [rounds.two["keep"][0]])
    frames_grad, norm_sums = input_grad(
        x, grad_query, grad_kv, grad_middle, gain_now, w_query, w_key, w_value
    )
    flags_now, frames_grad = meet(flags, [frames_grad], [third], rounds)
    fourth = started(rounds.run(flags_now))
    onward(third)
    _, fourth.keep, norm_sums = meet(flags, [fourth.keep, norm_sums])
    vectors = jnp.stack([norm_sums[0], join_sums[0], join_sums[1], out_sums[0]], axis=1)
    vectors = vectors.reshape((2,) * places.count + (own_rows, 4))
    left = list(reversed(every))
    groups = [[b] for b in [places.core, x_bit, y_bit, z_bit] + late]
    shares = share(places, vectors, left, groups[0])
    _, *shares = meet(flags, shares, [first])
    feeds = finished(first).reshape(2, 2, 2, own_rows, width)
    mine = lax.dynamic_index_in_dim(feeds, core, 2, False)
    got = places.swap(lax.dynamic_index_in_dim(feeds, 1 - core, 2, False), places.core)
    for done, group in zip(groups, groups[1:]):
        left = [b for b in left if b not in done]
        shares = share(places, sum(shares), left, group)
        if group is groups[-3]:
            _, *shares = meet(flags, shares, [fourth])
            onward(fourth)
    down_grad = finished(third)
    pair = jnp.stack([jnp.where(core == 0, mine, got), jnp.where(core == 0, got, mine)], axis=0)
    pair = pair.reshape(2, 2, 2, own_rows, per, block)
    pair = pair.transpose(2, 3, 1, 4, 0, 5).reshape(2, own_rows, feed_width)
    while fourth.left >= 0:
        onward(fourth)
    _, gate_grad, up_grad, down_grad, *shares = meet(
        flags, [pair[0], pair[1], down_grad, *shares], [fourth]
    )
    vectors = sum(shares).T
    output_grad, query_grad, key_grad, value_grad = [
        fourth.keep[rows, columns].astype(F32) + fourth.got[rows, columns].astype(F32)
        for rows in (slice(0, own_rows), slice(own_rows, 2 * own_rows))
        for columns in (slice(0, width), slice(width, 2 * width))
    ]
    return (
        layer_out.reshape(frames.shape),
        frames_grad.reshape(frames.shape),
        vectors[0],
        query_grad,
        key_grad,
        value_grad,
        output_grad,
        vectors[1],
        vectors[2],
        gate_grad,
        up_grad,
        down_grad,
        vectors[3],
    )


def solution(mesh):
    split = P("seq", "sp", None)
    rows = P(("seq", "sp"), None)
    vec = P(("seq", "sp"))
    return jax.shard_map(
        on_device,
        mesh=mesh,
        in_specs=(split, P("seq", None)) + (P(),) * 11 + (split,),
        out_specs=(
            split, split, vec, rows, rows, rows, rows, vec, vec, rows, rows, rows, vec,
        ),
        check_vma=False,
    )
```

```python
import functools
import math

import jax
import jax.numpy as jnp
import numpy as np
from jax import lax
from jax.experimental import pallas as pl
from jax.experimental.pallas import tpu as pltpu
from jax.sharding import PartitionSpec as P

HEAD_DIM = 64
HALF = 64
LANES = 128
GROUP = 256
GH = GROUP // HEAD_DIM
QB = 128
KB = QB + 2 * HALF
CLIPS = 8
LN_EPS = 1e-05
RMS_EPS = 1e-06
VMEM = 58 << 20
F32 = jnp.float32
BF16 = jnp.bfloat16

NT = (((1,), (1,)), ((), ()))
NN = (((1,), (0,)), ((), ()))
TN = (((0,), (0,)), ((), ()))


def dot(a, b, dims=NN):
    return lax.dot_general(a, b, dims, preferred_element_type=F32)


def params(grid=0, vmem=VMEM):
    kinds = ("arbitrary",) * grid if grid else None
    return pltpu.CompilerParams(vmem_limit_bytes=vmem, dimension_semantics=kinds)


def cost(flops, moved, scale=0.02):
    return pl.CostEstimate(
        flops=int(flops * scale), bytes_accessed=int(moved * scale), transcendentals=0
    )


def in_hbm(values):
    return [pltpu.with_memory_space_constraint(v, pltpu.HBM) for v in values]


def whole(shape):
    return pl.BlockSpec(shape, lambda *_: (0,) * len(shape))


def swap_halves(v):
    lane = lax.broadcasted_iota(jnp.int32, v.shape, 1)
    return jnp.where(lane % HEAD_DIM < HEAD_DIM // 2, pltpu.roll(v, 96, 1), pltpu.roll(v, 32, 1))


def rotated(v, cos_tab, sin_tab, sign):
    pieces = []
    for at in range(0, v.shape[1], LANES):
        part = v[:, at : at + LANES]
        turned = swap_halves(part) * sin_tab
        pieces.append(part * cos_tab + turned if sign > 0 else part * cos_tab - turned)
    return jnp.concatenate(pieces, axis=1)


def project_kernel(
    seqs, x_ref, left_ref, right_ref, place_ref, gain_ref, wv_ref, wk_ref, wq_ref,
    out_ref, normed_ref, own_ref, cos_ref, sin_ref, low, weights, sems,
):
    step = pl.program_id(0)
    rows, width = low.shape
    padded = rows // seqs
    length = padded - 2 * HALF
    fetches = [
        pltpu.make_async_copy(src, weights.at[i], sems.at[i]) for i, src in enumerate((wv_ref, wk_ref, wq_ref))
    ]
    keeps = [pltpu.make_async_copy(low, normed_ref, sems.at[3])] + [
        pltpu.make_async_copy(
            low.at[s * padded + HALF : s * padded + HALF + length, :],
            own_ref.at[s * length : (s + 1) * length, :],
            sems.at[4 + s],
        )
        for s in range(seqs)
    ]

    def products(which, after):
        blocks = [slice(at, at + GROUP) for at in range(0, width, GROUP)]
        ahead = dot(low[...], weights[which, :, blocks[0]])
        for i, columns in enumerate(blocks):
            out = ahead
            if i + 1 < len(blocks):
                ahead = dot(low[...], weights[which, :, blocks[i + 1]])
            out_ref[0, :, columns] = after(out).astype(BF16)

    @pl.when(step == 0)
    def _():
        for copy in fetches:
            copy.start()
        for src, first, step in ((x_ref, HALF, length), (left_ref, 0, HALF), (right_ref, HALF + length, HALF)):
            x = src[...].astype(F32)
            centered = x - jnp.mean(x, axis=-1, keepdims=True)
            inv = lax.rsqrt(jnp.mean(centered * centered, axis=-1, keepdims=True) + LN_EPS)
            normed = (centered * inv * gain_ref[...]).astype(BF16)
            for s in range(seqs):
                at = s * padded + first
                low[at : at + step, :] = normed[s * step : (s + 1) * step]
        for copy in keeps:
            copy.start()
        fetches[0].wait()
        products(0, lambda out: out)
        lane = lax.broadcasted_iota(jnp.int32, (1, LANES), 1)
        exponent = (lane % (HEAD_DIM // 2)).astype(F32) * (2.0 / HEAD_DIM)
        angles = place_ref[...] * jnp.exp(-math.log(10000.0) * exponent)
        cos_ref[...] = jnp.cos(angles)
        sin_ref[...] = jnp.where(lane % HEAD_DIM < HEAD_DIM // 2, -1.0, 1.0) * jnp.sin(angles)

    @pl.when(step == 1)
    def _():
        fetches[1].wait()
        products(1, lambda out: rotated(out, cos_ref[...], sin_ref[...], 1))

    @pl.when(step == 2)
    def _():
        fetches[2].wait()
        scale = 1.0 / math.sqrt(HEAD_DIM)
        products(2, lambda out: rotated(out, cos_ref[...], sin_ref[...], 1) * scale)
        for copy in keeps:
            copy.wait()


def project(x, left, right, place, gain, w_query, w_key, w_value, seqs):
    own, width = x.shape
    rows = own + seqs * 2 * HALF
    edge = whole((seqs * HALF, width))
    hbm = pl.BlockSpec(memory_space=pl.ANY)
    table = jax.ShapeDtypeStruct((rows, LANES), F32)
    return pl.pallas_call(
        functools.partial(project_kernel, seqs),
        grid=(3,),
        in_specs=[whole((own, width)), edge, edge, whole((rows, 1)), whole((1, width))] + [hbm] * 3,
        out_specs=[
            pl.BlockSpec((1, rows, width), lambda j: (j, 0, 0)),
            hbm,
            hbm,
            whole((rows, LANES)),
            whole((rows, LANES)),
        ],
        out_shape=[
            jax.ShapeDtypeStruct((3, rows, width), BF16),
            jax.ShapeDtypeStruct((rows, width), BF16),
            jax.ShapeDtypeStruct((own, width), BF16),
            table,
            table,
        ],
        scratch_shapes=[
            pltpu.VMEM((rows, width), BF16),
            pltpu.VMEM((3, width, width), BF16),
            pltpu.SemaphoreType.DMA((4 + seqs,)),
        ],
        compiler_params=params(1),
        cost_estimate=cost(6 * rows * width * width, 6 * width * width + 10 * rows * width),
        name="project",
    )(x, left, right, place, gain, w_value, w_key, w_query)


def stack_heads(block):
    lane = lax.broadcasted_iota(jnp.int32, block.shape, 1)
    zero = jnp.zeros_like(block)
    return jnp.concatenate(
        [jnp.where(lane // HEAD_DIM == h, block, zero) for h in range(GH)], axis=0
    )


def fill_keys(buf, ref):
    rows = ref.shape[1]
    buf[0:rows, :] = ref[0]
    if buf.shape[0] > rows:
        buf[rows:, :] = jnp.zeros((buf.shape[0] - rows, buf.shape[1]), buf.dtype)


def fill_queries(buf, ref, length):
    buf[0:length, :] = ref[0, HALF : HALF + length, :] if ref.ndim == 3 else ref[...]
    rest = buf.shape[0] - length
    if rest:
        buf[length:, :] = jnp.zeros((rest, buf.shape[1]), buf.dtype)


def attend_kernel(span_ref, q_ref, k_ref, v_ref, o_ref, p_ref, kbuf, vbuf, qbuf, vt, ot):
    length = o_ref.shape[0]
    padded = qbuf.shape[0]
    fill_keys(kbuf, k_ref)
    fill_keys(vbuf, v_ref)
    fill_queries(qbuf, q_ref, length)
    blocks = padded // QB

    def scores_of(b):
        return dot(kbuf[b * QB : b * QB + KB, :], stack_heads(qbuf[b * QB : (b + 1) * QB, :]), NT)

    def mix(b, probs):
        for h in range(GH):
            rows = slice(h * HEAD_DIM, (h + 1) * HEAD_DIM)
            ot[rows, b * QB : (b + 1) * QB] = dot(vt[rows, b * QB : b * QB + KB], probs[h]).astype(BF16)

    ahead = scores_of(0)
    vt[...] = vbuf[...].T
    before = None
    for b in range(blocks):
        scores = ahead
        if b + 1 < blocks:
            ahead = scores_of(b + 1)
        if before is not None:
            mix(b - 1, before)
        place = lax.broadcasted_iota(jnp.int32, (KB, QB), 0) + b * QB
        low = span_ref[0, 0:1, b * QB : (b + 1) * QB]
        high = span_ref[0, 1:2, b * QB : (b + 1) * QB]
        seen = (place >= low) & (place < high)
        before = []
        for h in range(GH):
            masked = jnp.where(seen, scores[:, h * QB : (h + 1) * QB], -1e30)
            terms = jnp.exp(masked - jnp.max(masked, axis=0, keepdims=True))
            total = jnp.sum(terms, axis=0, keepdims=True)
            probs = (terms * (1.0 / total)).astype(BF16)
            p_ref[:, b * GH * QB + h * QB : b * GH * QB + (h + 1) * QB] = probs
            before.append(probs)
    mix(blocks - 1, before)
    o_ref[...] = ot[...].T[0:length, :]


def attend(span, joint, seqs):
    _, rows, width = joint.shape
    length = rows // seqs - 2 * HALF
    rows = seqs * length
    padded = span.shape[2]
    groups = width // GROUP
    keys = padded + 2 * HALF
    own = pl.BlockSpec((length, GROUP), lambda s, g: (s, g))
    near = [pl.BlockSpec((1, length + 2 * HALF, GROUP), lambda s, g, i=i: (i, s, g)) for i in range(3)]
    return pl.pallas_call(
        attend_kernel,
        grid=(seqs, groups),
        in_specs=[
            pl.BlockSpec((1, 2, padded), lambda s, g: (s, 0, 0)),
            near[2],
            near[1],
            near[0],
        ],
        out_specs=[
            own,
            pl.BlockSpec((KB, GH * padded), lambda s, g: (s, g)),
        ],
        out_shape=[
            jax.ShapeDtypeStruct((rows, width), BF16),
            jax.ShapeDtypeStruct((seqs * KB, groups * GH * padded), BF16),
        ],
        scratch_shapes=[
            pltpu.VMEM((keys, GROUP), BF16),
            pltpu.VMEM((keys, GROUP), BF16),
            pltpu.VMEM((padded, GROUP), BF16),
            pltpu.VMEM((GROUP, keys), BF16),
            pltpu.VMEM((GROUP, padded), BF16),
        ],
        compiler_params=params(2),
        cost_estimate=cost(
            2 * 2 * seqs * width * padded * KB * 4, 2 * width * (4 * rows + KB * seqs * padded // 64)
        ),
        name="attend",
    )(span, joint, joint, joint)


def attend_back_kernel(
    flip_ref, p_ref, q_ref, k_ref, v_ref, g_ref, cos_ref, sin_ref,
    dq_ref, dkv_ref, near_ref, edge_ref, other_ref,
    kbuf, vbuf, qbuf, gbuf, kt, dqt, dkb, dvb,
):
    length = g_ref.shape[0]
    padded = qbuf.shape[0]
    fill_keys(kbuf, k_ref)
    fill_keys(vbuf, v_ref)
    fill_queries(qbuf, q_ref, length)
    fill_queries(gbuf, g_ref, length)
    blocks = padded // QB

    def probs_grads(b):
        g4 = stack_heads(gbuf[b * QB : (b + 1) * QB, :])
        return g4, dot(vbuf[b * QB : b * QB + KB, :], g4, NT)

    def spread(b, g4, probs, lows):
        at, keys = slice(b * QB, (b + 1) * QB), slice(b * QB, b * QB + KB)
        for h in range(GH):
            rows = slice(h * HEAD_DIM, (h + 1) * HEAD_DIM)
            dqt[rows, at] = dot(kt[rows, keys], lows[h])
        q4 = stack_heads(qbuf[at, :])
        grads = (dkb, dot(jnp.concatenate(lows, axis=1), q4)), (dvb, dot(probs, g4))
        for buf, grad in grads:
            if b:
                buf[at, :] += grad[:QB]
            else:
                buf[at, :] = grad[:QB]
            buf[(b + 1) * QB : b * QB + KB, :] = grad[QB:]

    ahead = probs_grads(0)
    kt[...] = kbuf[...].T
    before = None
    for b in range(blocks):
        g4, grads = ahead
        if b + 1 < blocks:
            ahead = probs_grads(b + 1)
        if before is not None:
            spread(b - 1, *before)
        probs = p_ref[:, b * GH * QB : (b + 1) * GH * QB]
        lows = []
        for h in range(GH):
            part = probs[:, h * QB : (h + 1) * QB].astype(F32)
            grad = grads[:, h * QB : (h + 1) * QB]
            delta = jnp.sum(part * grad, axis=0, keepdims=True)
            lows.append((part * (grad - delta)).astype(BF16))
        before = g4, probs, lows
    spread(blocks - 1, *before)
    cos_tab, sin_tab = cos_ref[...], sin_ref[...]
    middle = slice(HALF, HALF + length)
    dq = dqt[...].T[0:length, :] * (1.0 / math.sqrt(HEAD_DIM))
    dq_ref[...] = rotated(dq, cos_tab[middle], sin_tab[middle], -1).astype(BF16)
    span = length + 2 * HALF
    dk = rotated(dkb[0:span, :], cos_tab, sin_tab, -1).astype(BF16)
    dv = dvb[0:span, :].astype(BF16)
    for i, grad in enumerate((dk, dv)):
        dkv_ref[i] = grad[middle]
        near_ref[i] = grad
        ends = grad[0:HALF], grad[span - HALF :]
        edge_ref[i] = jnp.where(flip_ref[0] == 1, ends[1], ends[0])
        other_ref[i] = jnp.where(flip_ref[0] == 1, ends[0], ends[1])


def attend_back(flip, probs, joint, grad, cos_tab, sin_tab, seqs):
    rows, width = grad.shape
    length = rows // seqs
    padded = -(-length // QB) * QB
    groups = width // GROUP
    keys = padded + 2 * HALF
    own = pl.BlockSpec((length, GROUP), lambda s, g, f: (s, g))
    both = pl.BlockSpec((2, length, GROUP), lambda s, g, f: (0, s, g))
    both_near = pl.BlockSpec((2, length + 2 * HALF, GROUP), lambda s, g, f: (0, s, g))
    near = [pl.BlockSpec((1, length + 2 * HALF, GROUP), lambda s, g, f, i=i: (i, s, g)) for i in range(3)]
    table = pl.BlockSpec((length + 2 * HALF, LANES), lambda s, g, f: (s, 0))
    edge = pl.BlockSpec((2, HALF, GROUP), lambda s, g, f: (0, s, g))
    out_edge = jax.ShapeDtypeStruct((2, seqs * HALF, width), BF16)
    out = jax.ShapeDtypeStruct((rows, width), BF16)
    out_both = jax.ShapeDtypeStruct((2, rows, width), BF16)
    out_near = jax.ShapeDtypeStruct((2, rows + seqs * 2 * HALF, width), BF16)
    return pl.pallas_call(
        attend_back_kernel,
        grid_spec=pltpu.PrefetchScalarGridSpec(
            num_scalar_prefetch=1,
            grid=(seqs, groups),
        in_specs=[
            pl.BlockSpec((KB, GH * padded), lambda s, g, f: (s, g)),
            near[2],
            near[1],
            near[0],
            own,
            table,
            table,
        ],
        out_specs=[own, both, both_near, edge, edge],
        scratch_shapes=[
            pltpu.VMEM((keys, GROUP), BF16),
            pltpu.VMEM((keys, GROUP), BF16),
            pltpu.VMEM((padded, GROUP), BF16),
            pltpu.VMEM((padded, GROUP), BF16),
            pltpu.VMEM((GROUP, keys), BF16),
            pltpu.VMEM((GROUP, padded), F32),
            pltpu.VMEM((keys, GROUP), F32),
            pltpu.VMEM((keys, GROUP), F32),
        ],
        ),
        out_shape=[out, out_both, out_near, out_edge, out_edge],
        compiler_params=params(2),
        cost_estimate=cost(
            2 * 4 * seqs * width * padded * KB * 4, 2 * width * (8 * rows + KB * seqs * padded // 64)
        ),
        name="attend_back",
    )(flip, probs, joint, joint, joint, grad, cos_tab, sin_tab)


def edges_kernel(seqs, flags_ref, from_ref, left_ref, right_ref, to_ref, buf, sems):
    length = from_ref.shape[1] // seqs
    places = [
        (i, s, e, pl.ds(s * length + e * (length - HALF), HALF))
        for i in range(2)
        for s in range(seqs)
        for e in range(2)
    ]
    copies = [
        (from_ref.at[i, rows, :], to_ref.at[i, rows, :], buf.at[at]) for at, (i, _, _, rows) in enumerate(places)
    ]
    for at, (src, _, mid) in enumerate(copies):
        pltpu.make_async_copy(src, mid, sems.at[0, at]).start()
    for at, (src, _, mid) in enumerate(copies):
        pltpu.make_async_copy(src, mid, sems.at[0, at]).wait()
    for at, (i, s, e, _) in enumerate(places):
        got = (right_ref if e else left_ref)[i, s].astype(F32) * flags_ref[e].astype(F32)
        buf[at] = (buf[at].astype(F32) + got).astype(BF16)
    for at, (_, dst, mid) in enumerate(copies):
        pltpu.make_async_copy(mid, dst, sems.at[1, at]).start()
    for at, (_, dst, mid) in enumerate(copies):
        pltpu.make_async_copy(mid, dst, sems.at[1, at]).wait()


def add_edges(flags, grads, left, right):
    seqs = left.shape[1]
    hbm = pl.BlockSpec(memory_space=pl.ANY)
    return pl.pallas_call(
        functools.partial(edges_kernel, seqs),
        grid_spec=pltpu.PrefetchScalarGridSpec(
            num_scalar_prefetch=1,
            grid=(1,),
            in_specs=[hbm, whole(left.shape), whole(right.shape)],
            out_specs=hbm,
            scratch_shapes=[
                pltpu.VMEM((4 * seqs, HALF, grads.shape[2]), BF16),
                pltpu.SemaphoreType.DMA((2, 4 * seqs)),
            ],
        ),
        out_shape=jax.ShapeDtypeStruct(grads.shape, BF16),
        input_output_aliases={1: 0},
        compiler_params=params(1),
        cost_estimate=cost(1e4 * left.size, 8 * left.size, 1000),
        name="add_edges",
    )(flags, grads, left, right)


def out_proj_kernel(m_ref, x_ref, w_ref, scale_ref, gain_ref, attn_ref, in_ref):
    attn = dot(m_ref[...], w_ref[...])
    attn_ref[...] = attn.astype(BF16)
    middle = x_ref[...].astype(F32) + scale_ref[...] * attn
    inv = lax.rsqrt(jnp.mean(middle * middle, axis=-1, keepdims=True) + RMS_EPS)
    in_ref[...] = (middle * inv * gain_ref[...]).astype(BF16)


def out_proj(mixed, x, w_output, scale, gain):
    rows, width = x.shape
    block = rows // 2
    row = pl.BlockSpec((block, width), lambda i: (i, 0))
    return pl.pallas_call(
        out_proj_kernel,
        grid=(rows // block,),
        in_specs=[row, row, whole((width, width)), whole((1, width)), whole((1, width))],
        out_specs=[row, row],
        out_shape=[
            jax.ShapeDtypeStruct((rows, width), BF16),
            jax.ShapeDtypeStruct((rows, width), BF16),
        ],
        compiler_params=params(1),
        cost_estimate=cost(2 * rows * width * width, 2 * rows * width * 5 + 2 * width * width),
        name="out_proj",
    )(mixed, x, w_output, scale, gain)


def hidden_grad_kernel(core_ref, own_ref, peer_ref, scale_ref, one_ref, two_ref, low_ref, out_ref):
    rows = own_ref.shape[0]
    block = one_ref.shape[0]

    @pl.when(pl.program_id(0) == 0)
    def _():
        low_ref[0:rows, :] = (own_ref[...].astype(F32) * scale_ref[...]).astype(BF16)
        low_ref[rows:, :] = (peer_ref[...].astype(F32) * scale_ref[...]).astype(BF16)

    out_ref[:, :block] = dot(low_ref[...], one_ref[...], NT).astype(BF16)
    out_ref[:, block:] = dot(low_ref[...], two_ref[...], NT).astype(BF16)


def hidden_grad(core, own, peer, scale, w_down, block):
    rows, width = own.shape
    count = w_down.shape[0] // block // 4
    half = w_down.shape[0] // 2
    return pl.pallas_call(
        hidden_grad_kernel,
        grid_spec=pltpu.PrefetchScalarGridSpec(
            num_scalar_prefetch=1,
            grid=(count,),
            in_specs=[
                whole((rows, width)),
                whole((rows, width)),
                whole((1, width)),
                pl.BlockSpec((block, width), lambda j, c: (4 * j + c[0], 0)),
                pl.BlockSpec((block, width), lambda j, c: (4 * j + 2 + c[0], 0)),
            ],
            out_specs=[
                whole((2 * rows, width)),
                pl.BlockSpec((2 * rows, 2 * block), lambda j, c: (0, j)),
            ],
        ),
        out_shape=[
            jax.ShapeDtypeStruct((2 * rows, width), BF16),
            jax.ShapeDtypeStruct((2 * rows, half), BF16),
        ],
        compiler_params=params(1),
        cost_estimate=cost(
            4 * rows * width * half, 2 * (4 * rows * width + half * (width + 2 * rows))
        ),
        name="hidden_grad",
    )(core, own, peer, scale, w_down, w_down)


def halves_of(value, bit, inner):
    rows, columns = value.shape
    both = value.reshape(rows // (2 * inner), 2, inner, columns)
    zero, one = both[:, 0], both[:, 1]
    out = jnp.where(bit == 0, one, zero).reshape(rows // 2, columns)
    stay = jnp.where(bit == 0, zero, one).reshape(rows // 2, columns)
    return out, stay


def feed_kernel(inners, core_ref, xo_ref, xp_ref, gh_ref, wg_ref, wu_ref, *refs):
    hid_own_ref, hid_peer_ref, gg_ref, gu_ref, *outs, x_all = refs[-9:]
    rows = xo_ref.shape[0]

    @pl.when(pl.program_id(0) == 0)
    def _():
        x_all[0:rows, :] = xo_ref[...]
        x_all[rows:, :] = xp_ref[...]

    for at in (0, rows):
        part = slice(at, at + rows)
        gate = dot(x_all[part, :], wg_ref[...])
        up = dot(x_all[part, :], wu_ref[...])
        grad = gh_ref[part, :].astype(F32)
        sig = 1.0 / (1.0 + jnp.exp(-gate))
        act = gate * sig
        (hid_peer_ref if at else hid_own_ref)[...] = (act * up).astype(BF16)
        gg_ref[part, :] = (grad * up * sig * (1.0 + gate * (1.0 - sig))).astype(BF16)
        gu_ref[part, :] = (grad * act).astype(BF16)
    for i, src in enumerate((gg_ref, gu_ref)):
        out, stay = halves_of(dot(x_all[...], src[...], TN), core_ref[1 + i], inners[i])
        outs[2 * i][...] = out.astype(BF16)
        outs[2 * i + 1][...] = stay.astype(BF16)


def feed(core, x_own, x_peer, grad_hidden, w_gate, w_up, block, first, count, before, inners):
    rows, width = x_own.shape
    half = grad_hidden.shape[1]
    wide = pl.BlockSpec((2 * rows, block), lambda j, c: (0, j + first))
    weight = pl.BlockSpec((width, block), lambda j, c: (0, 2 * (j + first) + c[0]))
    tall = pl.BlockSpec((rows, block), lambda j, c: (0, j + first))
    kept = pltpu.HBM((2 * rows, half), BF16)
    single = pltpu.HBM((rows, half), BF16)
    grads = pltpu.HBM((width // 2, count * block), BF16)
    any_spec = pl.BlockSpec(memory_space=pl.ANY)
    return pl.pallas_call(
        functools.partial(feed_kernel, inners),
        grid_spec=pltpu.PrefetchScalarGridSpec(
            num_scalar_prefetch=1,
            grid=(count,),
            in_specs=[whole((rows, width)), whole((rows, width)), wide, weight, weight]
            + [any_spec] * len(before),
            out_specs=[tall] * 2
            + [wide] * 2
            + [pl.BlockSpec((width // 2, block), lambda j, c: (0, j))] * 4,
            scratch_shapes=[pltpu.VMEM((2 * rows, width), BF16)],
        ),
        out_shape=[single] * 2 + [kept] * 2 + [grads] * 4,
        input_output_aliases={6 + i: i for i in range(len(before))},
        compiler_params=params(1, 46 << 20),
        cost_estimate=cost(
            2 * 2 * rows * width * block * count * 4,
            2 * (4 * rows * width + count * block * (8 * rows + 4 * width)),
        ),
        name="feed",
    )(core, *in_hbm([x_own]), x_peer, *in_hbm([grad_hidden, w_gate, w_up, *before]))


def down_kernel(each, inners, bits_ref, own_ref, peer_ref, low_ref, *refs):
    *outs, both = refs
    both[: own_ref.shape[0], :] = own_ref[...]
    both[own_ref.shape[0] :, :] = peer_ref[...]
    value = dot(both[...], low_ref[...], TN)
    rows, width = value.shape
    value = value.reshape(rows // (2 * each), 2, each, width)
    for i in range(2):
        part = value[:, i].reshape(rows // 2, width)
        out, stay = halves_of(part, bits_ref[1 + i], inners[i])
        outs[2 * i][...] = out.astype(BF16)
        outs[2 * i + 1][...] = stay.astype(BF16)


def down(bits, own, peer, low, each, inners):
    rows, half = own.shape
    width = low.shape[1]
    block = 512
    out = jax.ShapeDtypeStruct((half // 4, width), BF16)
    return pl.pallas_call(
        functools.partial(down_kernel, each, inners),
        grid_spec=pltpu.PrefetchScalarGridSpec(
            num_scalar_prefetch=1,
            grid=(half // block,),
            in_specs=[
                pl.BlockSpec((rows, block), lambda j, c: (0, j)),
                pl.BlockSpec((rows, block), lambda j, c: (0, j)),
                whole((2 * rows, width)),
            ],
            out_specs=[pl.BlockSpec((block // 4, width), lambda j, c: (j, 0))] * 4,
            scratch_shapes=[pltpu.VMEM((2 * rows, block), BF16)],
        ),
        out_shape=[out] * 4,
        compiler_params=params(1),
        cost_estimate=cost(
            4 * rows * half * width, 2 * (2 * rows * half + 2 * rows * width + half * width)
        ),
        name="down_weight",
    )(bits, own, peer, low)


def in_halves(value, refs):
    half = value.shape[1] // 2
    refs[0][...] = value[:, :half]
    refs[1][...] = value[:, half:]


def feed_back_kernel(core_ref, *refs):
    *peer_refs, own_ref, acc = refs[-4:]
    part, step = pl.program_id(0), pl.program_id(1)
    block = refs[2].shape[1]
    total = None
    for i in range(2):
        for half in range(2):
            out = dot(refs[i][:, half * block : (half + 1) * block], refs[2 + 2 * i + half][...], NT)
            total = out if total is None else total + out
    last = pl.num_programs(1) - 1

    @pl.when(step == 0)
    def _():
        acc[...] = total

    @pl.when((step > 0) & (step < last))
    def _():
        acc[...] += total

    @pl.when((step == last) & (part == 0))
    def _():
        in_halves((acc[...] + total).astype(BF16), peer_refs)

    @pl.when((step == last) & (part == 1))
    def _():
        own_ref[...] = (acc[...] + total).astype(BF16)


def feed_back(core, grad_gate, grad_up, w_gate, w_up, block):
    rows, half = grad_gate.shape
    rows = rows // 2
    width = w_gate.shape[0]
    tall = pl.BlockSpec((rows, 2 * block), lambda p, j, c: (1 - p, j))
    one = pl.BlockSpec((width, block), lambda p, j, c: (0, 4 * j + c[0]))
    two = pl.BlockSpec((width, block), lambda p, j, c: (0, 4 * j + 2 + c[0]))
    return pl.pallas_call(
        feed_back_kernel,
        grid_spec=pltpu.PrefetchScalarGridSpec(
            num_scalar_prefetch=1,
            grid=(2, half // block // 2),
            in_specs=[tall, tall, one, two, one, two],
            out_specs=[whole((rows, width // 2))] * 2 + [whole((rows, width))],
            scratch_shapes=[pltpu.VMEM((rows, width), F32)],
        ),
        out_shape=[jax.ShapeDtypeStruct((rows, width // 2), BF16)] * 2
        + [jax.ShapeDtypeStruct((rows, width), BF16)],
        compiler_params=params(2),
        cost_estimate=cost(8 * rows * half * width, 8 * (rows * half + half * width)),
        name="feed_back",
    )(core, grad_gate, grad_up, w_gate, w_gate, w_up, w_up)


def join_kernel(
    x_ref, attn_ref, g_ref, in_ref, got_one_ref, got_two_ref, attn_scale_ref, gain_ref, w_ref,
    grad_attn_ref, grad_mixed_ref, middle_ref, sums_ref,
):
    x = x_ref[...].astype(F32)
    attn = attn_ref[...].astype(F32)
    grad_y = g_ref[...].astype(F32)
    got = jnp.concatenate([got_one_ref[...], got_two_ref[...]], axis=1)
    grad_in = in_ref[...].astype(F32) + got.astype(F32)
    middle = x + attn_scale_ref[...] * attn
    inv = lax.rsqrt(jnp.mean(middle * middle, axis=-1, keepdims=True) + RMS_EPS)
    unit = middle * inv
    scaled = grad_in * gain_ref[...]
    grad_middle = grad_y + inv * (scaled - unit * jnp.mean(scaled * unit, axis=-1, keepdims=True))
    middle_ref[...] = grad_middle.astype(BF16)
    grad_attn = (attn_scale_ref[...] * grad_middle).astype(BF16)
    grad_attn_ref[...] = grad_attn
    grad_mixed_ref[...] = dot(grad_attn, w_ref[...], NT).astype(BF16)

    @pl.when(pl.program_id(0) == 0)
    def _():
        sums_ref[...] = jnp.zeros_like(sums_ref)

    sums_ref[0:1, :] += jnp.sum(grad_middle * attn, axis=0, keepdims=True)
    sums_ref[1:2, :] += jnp.sum(grad_in * unit, axis=0, keepdims=True)


def join(x, attn, grad_y, grad_in, got, attn_scale, gain, w_output):
    rows, width = x.shape
    block = rows // 2
    row = pl.BlockSpec((block, width), lambda i: (i, 0))
    half = pl.BlockSpec((block, width // 2), lambda i: (i, 0))
    vec = whole((1, width))
    low = jax.ShapeDtypeStruct((rows, width), BF16)
    return pl.pallas_call(
        join_kernel,
        grid=(rows // block,),
        in_specs=[row] * 4 + [half] * 2 + [vec] * 2 + [whole((width, width))],
        out_specs=[row] * 3 + [whole((8, width))],
        out_shape=[
            low,
            low,
            low,
            jax.ShapeDtypeStruct((8, width), F32),
        ],
        compiler_params=params(1),
        cost_estimate=cost(2 * rows * width * width, rows * width * 22 + 2 * width * width),
        name="join",
    )(x, attn, grad_y, grad_in, *got, attn_scale, gain, w_output)


def feed_out_kernel(
    core_ref, own_ref, got_ref, w_ref, x_ref, attn_ref, g_ref, attn_scale_ref, mlp_scale_ref,
    layer_ref, sums_ref, hidden, acc,
):
    step, last = pl.program_id(0), pl.num_programs(0) - 1
    block = own_ref.shape[1] // 2
    for i in range(2):
        part = slice(i * block, (i + 1) * block)
        own, got = own_ref[:, part], got_ref[:, part]
        first = core_ref[0] == 0
        hidden[:, 2 * i * block : (2 * i + 1) * block] = jnp.where(first, own, got)
        hidden[:, (2 * i + 1) * block : (2 * i + 2) * block] = jnp.where(first, got, own)
    total = dot(hidden[...], w_ref[...])

    @pl.when(step == 0)
    def _():
        acc[...] = total

    @pl.when((step > 0) & (step < last))
    def _():
        acc[...] += total

    @pl.when(step == last)
    def _():
        down_out = acc[...] + total
        middle = x_ref[...].astype(F32) + attn_scale_ref[...] * attn_ref[...].astype(F32)
        layer_ref[...] = (middle + mlp_scale_ref[...] * down_out).astype(BF16)
        sums_ref[...] = jnp.zeros_like(sums_ref)
        sums_ref[0:1, :] = jnp.sum(g_ref[...].astype(F32) * down_out, axis=0, keepdims=True)


def feed_out(core, own, got, w_down, x, attn, grad_y, attn_scale, mlp_scale, block):
    rows, half = own.shape
    width = w_down.shape[1]
    tall = pl.BlockSpec((rows, 2 * block), lambda j, c: (0, j))
    row, vec = whole((rows, width)), whole((1, width))
    return pl.pallas_call(
        feed_out_kernel,
        grid_spec=pltpu.PrefetchScalarGridSpec(
            num_scalar_prefetch=1,
            grid=(half // block // 2,),
            in_specs=[tall, tall, pl.BlockSpec((4 * block, width), lambda j, c: (j, 0))]
            + [row] * 3
            + [vec] * 2,
            out_specs=[row, whole((8, width))],
            scratch_shapes=[pltpu.VMEM((rows, 4 * block), BF16), pltpu.VMEM((rows, width), F32)],
        ),
        out_shape=[
            jax.ShapeDtypeStruct((rows, width), BF16),
            jax.ShapeDtypeStruct((8, width), F32),
        ],
        compiler_params=params(1),
        cost_estimate=cost(4 * rows * half * width, 4 * (rows * half + half * width), 10),
        name="feed_out",
    )(core, own, got, w_down, x, attn, grad_y, attn_scale, mlp_scale)


def weight_grad_kernel(inner, order, counts, bit_ref, *refs):
    out_ref, stay_ref = refs[-2:]
    step = pl.program_id(0)
    lefts = [refs[i] for i in order]
    rights = refs[max(order) + 1 : -2]
    first = 0
    for left, right, count in zip(lefts, rights, counts):

        @pl.when((step >= first) & (step < first + count))
        def _(left=left, right=right):
            rows = right[...].reshape(right.shape[-2:])
            out, stay = halves_of(dot(left[...], rows, TN), bit_ref[0], inner)
            out_ref[...] = out.astype(BF16)
            stay_ref[...] = stay.astype(BF16)

        first += count


def weight_grad(bit, inner, pairs, name, scale):
    block = 512
    width = pairs[0][0].shape[1]
    lefts = []
    for left, _ in pairs:
        if not any(left is other for other in lefts):
            lefts.append(left)
    order = [[left is other for other in lefts].index(True) for left, _ in pairs]
    counts, specs, rights, first = [], [], [], 0
    for left, right in pairs:
        rows = left.shape[0]
        array, part = right if isinstance(right, tuple) else (right, None)
        count = array.shape[-1] // block
        at = lambda j, first=first, count=count: jnp.clip(j - first, 0, count - 1)
        if part is None:
            specs.append(pl.BlockSpec((rows, block), lambda j, c, at=at: (0, at(j))))
        else:
            specs.append(
                pl.BlockSpec((1, rows, block), lambda j, c, at=at, part=part: (part, 0, at(j)))
            )
        rights.append(array)
        counts.append(count)
        first += count
    out = jax.ShapeDtypeStruct((width // 2, first * block), BF16)
    return pl.pallas_call(
        functools.partial(weight_grad_kernel, inner, order, counts),
        grid_spec=pltpu.PrefetchScalarGridSpec(
            num_scalar_prefetch=1,
            grid=(first,),
            in_specs=[whole(left.shape) for left in lefts] + specs,
            out_specs=[pl.BlockSpec((width // 2, block), lambda j, c: (0, j))] * 2,
        ),
        out_shape=[out, out],
        compiler_params=params(1),
        cost_estimate=cost(
            2 * rows * width * first * block,
            2 * (len(lefts) * rows * width + (rows + width) * first * block),
            scale,
        ),
        name=name,
    )(bit, *lefts, *rights)


def input_grad_kernel(
    x_ref, gq_ref, gk_ref, gv_ref, middle_ref, gain_ref, wq_ref, wk_ref, wv_ref, out_ref, sums_ref
):
    grad = (
        dot(gq_ref[...], wq_ref[...], NT)
        + dot(gk_ref[0], wk_ref[...], NT)
        + dot(gv_ref[0], wv_ref[...], NT)
    )
    x = x_ref[...].astype(F32)
    centered = x - jnp.mean(x, axis=-1, keepdims=True)
    inv = lax.rsqrt(jnp.mean(centered * centered, axis=-1, keepdims=True) + LN_EPS)
    unit = centered * inv
    scaled = grad * gain_ref[...]
    back = inv * (
        scaled
        - jnp.mean(scaled, axis=-1, keepdims=True)
        - unit * jnp.mean(scaled * unit, axis=-1, keepdims=True)
    )
    out_ref[...] = (middle_ref[...].astype(F32) + back).astype(BF16)

    @pl.when(pl.program_id(0) == 0)
    def _():
        sums_ref[...] = jnp.zeros_like(sums_ref)

    sums_ref[0:1, :] += jnp.sum(grad * unit, axis=0, keepdims=True)


def input_grad(x, gq, gkv, grad_middle, gain, w_query, w_key, w_value):
    rows, width = x.shape
    block = rows // 2
    row = pl.BlockSpec((block, width), lambda i: (i, 0))
    square = whole((width, width))
    return pl.pallas_call(
        input_grad_kernel,
        grid=(rows // block,),
        in_specs=[
            row,
            row,
            pl.BlockSpec((1, block, width), lambda i: (0, i, 0)),
            pl.BlockSpec((1, block, width), lambda i: (1, i, 0)),
            row,
            whole((1, width)),
        ]
        + [square] * 3,
        out_specs=[row, whole((8, width))],
        out_shape=[
            jax.ShapeDtypeStruct((rows, width), BF16),
            jax.ShapeDtypeStruct((8, width), F32),
        ],
        compiler_params=params(1),
        cost_estimate=cost(2 * 3 * rows * width * width, rows * width * 14 + 6 * width * width),
        name="input_grad",
    )(x, gq, gkv, gkv, grad_middle, gain, w_query, w_key, w_value)


def log2(n):
    return n.bit_length() - 1


class Places:
    def __init__(self):
        self.n_seq, self.n_sp = lax.axis_size("seq"), lax.axis_size("sp")
        self.sp_bits = log2(self.n_sp)
        self.count = self.sp_bits + log2(self.n_seq)
        self.core = self.sp_bits
        self.me = lax.axis_index("seq") * self.n_sp + lax.axis_index("sp")
        self.down_bits = [b for b in reversed(range(self.count)) if b != self.core]

    def swap(self, value, bit):
        if bit < self.sp_bits:
            axis, size, at = "sp", self.n_sp, bit
        else:
            axis, size, at = "seq", self.n_seq, bit - self.sp_bits
        return lax.ppermute(value, axis, [(i, i ^ (1 << at)) for i in range(size)])

    def send(self, value, flip):
        pairs = [(i, i ^ flip) for i in range(1 << self.count)]
        return lax.ppermute(value, ("seq", "sp"), pairs)

    def own(self, bit):
        return (self.me >> bit) & 1


def round_kernel(has, inners, bits_ref, *refs):
    two, one, new, carry = has
    refs = list(refs)
    take = lambda n: [refs.pop(0) for _ in range(n)]
    second, carried = take(4) if two else (), take(2) if carry else ()
    first = take(4) if one else ()
    fresh = take({"sent": 2, "core": 4, "": 0}[new])
    bufs = take(2) if one or new else ()
    bits = bits_ref[1], bits_ref[2], bits_ref[3]

    def split(keep, got, bit, inner):
        total = keep[...].astype(F32) + got[...].astype(F32)
        return [v.astype(BF16) for v in halves_of(total, bit, inner)]

    if two:
        outs = take(2)
        at = carried[0].shape[0] if carry else 0
        for src, dst in zip(carried, outs):
            dst[0:at, :] = src[...]
        for i in range(2):
            rows = second[i].shape[0] // 2
            for dst, part in zip(outs, split(second[i], second[2 + i], bits[2], inners["two"])):
                dst[at : at + rows, :] = part
            at += rows
    at = [0, 0]
    if new:
        stays = take(2) if new == "core" else ()
        for i in range(2):
            if new == "core":
                out, stays[i][...] = split(fresh[2 * i], fresh[2 * i + 1], bits[i], inners["new"][i])
            else:
                out = fresh[i][...]
            at[i] = out.shape[0]
            bufs[i][0 : at[i], :] = out
    if one:
        stays = take(2)
        for i in range(2):
            out, stays[i][...] = split(first[i], first[2 + i], bits[1 - i], inners["one"][i])
            bufs[1 - i][at[1 - i] :, :] = out


class Rounds:
    def __init__(self, places, x, y, z):
        self.places, self.x, self.y, self.z = places, x, y, z
        self.one = self.two = None
        self.got = []

    def inner(self, group, without, bit):
        bits = [b for b in sorted(group["bits"], reverse=True) if b not in without]
        return group["each"] << (len(bits) - 1 - bits.index(bit))

    def first_inners(self, bits, each):
        group = {"bits": bits, "each": each}
        return [self.inner(group, (), self.x), self.inner(group, (), self.y)]

    def send(self, buf_x, buf_y):
        self.got = [self.places.swap(buf_x, self.x), self.places.swap(buf_y, self.y)]

    def begin(self, parts, bits, each):
        self.one = {"bits": bits, "each": each, "keep": [parts[1], parts[3]]}
        self.send(parts[0], parts[2])

    def set_aside(self):
        group, self.two = self.two, None
        return dict(group, got=self.got)

    def run_aside(self, flags, aside):
        kept = self.one, self.two, self.got
        self.one, self.two, self.got = None, None, aside["got"]
        done = self.run(flags, aside=aside)
        self.one, self.two, self.got = kept
        return done

    def run(self, flags, new="", arrays=(), bits=(), each=0, carry=(), wait=False, aside=None, scale=0.02):
        one = self.one
        two = aside or self.two
        steps = 2
        ins, specs, outs, inners, heights, wide = [], [], [], {}, [0, 0], 0

        def tall(rows, columns, at=0, row=0):
            return pl.BlockSpec((rows, columns // steps), lambda j, b: (row, j + at))

        if two:
            rows, columns = two["keep"][0].shape
            got_x, got_y = two["got"] if aside else self.got
            ins += two["keep"] + [got_y, got_x]
            last = [got_y.shape[0] // rows - 1, got_x.shape[0] // rows - 1]
            specs += [tall(rows, columns)] * 2 + [tall(rows, columns, 0, row) for row in last]
            ins += carry
            specs += [tall(*v.shape) for v in carry]
            outs += [(rows + (carry[0].shape[0] if carry else 0), columns)] * 2
            inners["two"] = self.inner(two, (self.x, self.y), self.z)
        group = {"bits": list(bits), "each": each}
        if one:
            rows, wide = one["keep"][0].shape
            ins += one["keep"] + self.got
            specs += [tall(rows, wide)] * 4
            inners["one"] = self.inner(one, (self.x,), self.y), self.inner(one, (self.y,), self.x)
        if new == "sent":
            ins += [arrays[0], arrays[2]]
            specs += [tall(*arrays[0].shape), tall(*arrays[2].shape)]
            heights, wide = [arrays[0].shape[0], arrays[2].shape[0]], arrays[0].shape[1]
            group["keep"] = [arrays[1], arrays[3]]
        if new == "core":
            keep, got = arrays
            rows, wide = keep.shape[0], keep.shape[1] // 2
            ins += [keep, got, keep, got]
            specs += [tall(rows, wide)] * 2 + [tall(rows, wide, steps)] * 2
            heights = [rows // 2, rows // 2]
            outs += [(rows // 2, wide)] * 2
            inners["new"] = self.first_inners(bits, each)
        if one:
            rows = one["keep"][0].shape[0] // 2
            heights = [h + rows for h in heights]
            outs += [(rows, wide)] * 2
        if one or new:
            outs = [(h, wide) for h in heights] + outs
        size = sum(v.size for v in ins)
        ins = [
            v if any(v is g for g in self.got) else in_hbm([v])[0] for v in ins
        ]
        results = list(
            pl.pallas_call(
                functools.partial(round_kernel, (bool(two), bool(one), new, bool(carry)), inners),
                grid_spec=pltpu.PrefetchScalarGridSpec(
                    num_scalar_prefetch=1,
                    grid=(steps,),
                    in_specs=specs,
                    out_specs=[tall(*shape) for shape in outs],
                ),
                out_shape=[pltpu.HBM(shape, BF16) for shape in outs],
                compiler_params=params(1, 24 << 20),
                cost_estimate=cost(2 * size, 4 * size, scale),
                name="round",
            )(flags, *ins)
        )
        take = lambda n: [results.pop(0) for _ in range(n)]
        buf_x, buf_y = take(2) if one or new else (None, None)
        done = None
        if two:
            done = take(2)
            if not wait:
                piece = Piece(self.places, [b for b in two["bits"] if b not in (self.x, self.y)], two["each"])
                piece.fork(*done, self.z)
                done = piece
        if new == "core":
            group["keep"] = take(2)
        self.two = dict(one, keep=take(2)) if one else None
        self.one = group if new else None
        self.got = []
        if one or new:
            self.send(buf_x, buf_y)
        return done


class Piece:
    def __init__(self, places, bits, each):
        self.places, self.bits, self.each = places, sorted(bits, reverse=True), each
        self.keep = self.got = None
        self.at = 0

    def inner(self, bit):
        return self.each << (len(self.bits) - 1 - self.bits.index(bit))

    def fork(self, out, stay, bit):
        self.bits.remove(bit)
        self.keep, self.got = stay, self.places.swap(out, bit)
        self.at, self.columns = 0, stay.shape[1]

    def split(self, bit):
        rows, columns = self.keep.shape
        inner = self.inner(bit)
        both = self.keep.reshape(rows // (2 * inner), 2, inner, columns)
        at = self.places.own(bit)
        out = lax.dynamic_index_in_dim(both, 1 - at, 1, False).reshape(rows // 2, columns)
        stay = lax.dynamic_index_in_dim(both, at, 1, False).reshape(rows // 2, columns)
        self.fork(out, stay, bit)

    def add(self, low=True):
        cols = slice(self.at * self.columns, (self.at + 1) * self.columns)
        self.keep = self.keep[:, cols].astype(F32) + self.got[:, cols].astype(F32)
        self.at = 0
        if low:
            self.keep = self.keep.astype(BF16)


def share(places, value, bits, group):
    axes = [bits.index(b) for b in group]

    def part(flip):
        out = value
        for b, axis in zip(group, axes):
            out = lax.dynamic_index_in_dim(out, places.own(b) ^ ((flip >> b) & 1), axis, True)
        return lax.squeeze(out, axes)

    flips = [sum(b << g for b, g in zip(f, group)) for f in np.ndindex(*(2,) * len(group))]
    return [part(0)] + [places.send(part(f), f) for f in flips if f]


def hold(small, *arrays):
    small, *arrays = lax.optimization_barrier((small, *arrays))
    return (small, *arrays)


def meet(small, arrays=(), pieces=(), rounds=None):
    many = list(arrays), [p.got for p in pieces], list(rounds.got) if rounds else []
    small, (arrays, gots, round_gots) = lax.optimization_barrier((small, many))
    for p, g in zip(pieces, gots):
        p.got = g
    if rounds:
        rounds.got = round_gots
    return (small, *arrays)


def on_device(
    frames, clip_ids, norm_gain, w_query, w_key, w_value, w_output, attn_scale,
    mlp_gain, w_gate, w_up, w_down, mlp_scale, out_grad,
):
    places = Places()
    seqs, length, width = frames.shape
    total_len = clip_ids.shape[1]
    rows = seqs * length
    n_sp, n_seq = places.n_sp, places.n_seq
    devices = n_sp * n_seq
    feed_width = w_gate.shape[1]
    own_rows = width // devices
    feed_rows = feed_width // devices
    block = feed_rows * n_sp
    core = lax.axis_index("seq") & 1
    sp = lax.axis_index("sp")
    sp_bits = list(reversed(range(places.core)))
    seq_bits = list(range(places.core + 1, places.count))
    x_bit, y_bit, z_bit = sp_bits[0], seq_bits[0], seq_bits[1]
    late = seq_bits[2:] + sp_bits[1:]
    every = list(range(places.count))
    not_core = [b for b in every if b != places.core]
    flags = jnp.stack([places.own(b) for b in (places.core, x_bit, y_bit, z_bit)]).astype(jnp.int32)
    rounds = Rounds(places, x_bit, y_bit, z_bit)

    x = frames.reshape(rows, width)
    grad_y = out_grad.reshape(rows, width)

    def neighbours(last, first):
        if n_sp == 2:
            got = lax.ppermute(jnp.where(sp == 0, last, first), "sp", [(0, 1), (1, 0)])
            return got, got
        return (
            lax.ppermute(last, "sp", [(i, i + 1) for i in range(n_sp - 1)]),
            lax.ppermute(first, "sp", [(i + 1, i) for i in range(n_sp - 1)]),
        )

    has = jnp.stack([sp > 0, sp < n_sp - 1]).astype(jnp.int32)
    from_left, from_right = neighbours(frames[:, length - HALF :], frames[:, :HALF])
    grad_y_peer = places.swap(grad_y, places.core)

    start = sp * length
    near = lax.dynamic_slice_in_dim(
        jnp.pad(clip_ids, ((0, 0), (HALF, HALF))), start, length + 2 * HALF, 1
    )
    ids = jnp.arange(CLIPS + 1, dtype=jnp.int32)
    begins = jnp.sum((clip_ids[:, None, :] < ids[:, None]).astype(jnp.int32), axis=-1)
    is_id = near[:, None, :] == ids[:CLIPS, None]
    first = jnp.sum(jnp.where(is_id, begins[:, :CLIPS, None], 0), axis=1)
    end = jnp.sum(jnp.where(is_id, begins[:, 1:, None], 0), axis=1)
    frame = lax.broadcasted_iota(jnp.int32, near.shape, 1) + (start - HALF)
    place = (frame - first).astype(F32).reshape(-1, 1)
    mid = slice(HALF, HALF + length)
    low = jnp.maximum(frame - HALF, first)[:, mid] - (start - HALF)
    high = jnp.minimum(frame + HALF, end)[:, mid] - (start - HALF)
    padded = -(-length // QB) * QB
    span = jnp.pad(jnp.stack([low, high], axis=1), ((0, 0), (0, 0), (0, padded - length)))

    gain = norm_gain[None]
    joint, normed, normed_own, cos_tab, sin_tab = project(
        x, from_left.reshape(-1, width), from_right.reshape(-1, width), place, gain,
        w_query, w_key, w_value, seqs,
    )
    mixed, probs = attend(span, joint, seqs)

    attn_out, mlp_in = out_proj(mixed, x, w_output, attn_scale[None], mlp_gain[None])
    flags_now, mlp_in = hold(flags, mlp_in)
    mlp_in_peer = places.swap(mlp_in, places.core)
    grad_low, grad_hidden = hidden_grad(
        flags_now, grad_y, grad_y_peer, mlp_scale[None], w_down, block
    )

    blocks = n_seq // 2
    per = blocks // 2

    def onward(piece):
        piece.add()
        piece.split(late[-1 - piece.left])
        piece.left -= 1

    def started(piece):
        piece.left = len(late) - 1
        return piece

    def finished(piece):
        while piece.left >= 0:
            onward(piece)
        piece.add(False)
        return piece.keep

    inners = rounds.first_inners(every, own_rows)
    *kept, a, b, c, d = feed(
        flags, mlp_in, mlp_in_peer, grad_hidden, w_gate, w_up, block, 0, per, (), inners
    )
    rounds.begin((a, b, c, d), every, own_rows)
    *kept, a, b, c, d = feed(
        flags, mlp_in, mlp_in_peer, grad_hidden, w_gate, w_up, block, per, per, kept, inners
    )
    hidden, hidden_peer, grad_gate, grad_up = kept
    hidden_got = places.swap(hidden_peer, places.core)
    flags_now, a = meet(flags, [a], rounds=rounds)
    rounds.run(flags_now, "sent", (a, b, c, d), every, own_rows)

    flags_now, rounds.two["keep"][0] = meet(flags, [rounds.two["keep"][0]])
    *in_peer, in_own = feed_back(flags_now, grad_gate, grad_up, w_gate, w_up, block)
    in_got = [places.swap(v, places.core) for v in in_peer]

    flags_now, in_own = meet(flags, [in_own])
    each = feed_rows // 2
    parts = down(
        flags_now, hidden, hidden_peer, grad_low, each, rounds.first_inners(not_core, each)
    )

    flags_now, *both = meet(flags, [*in_got, *parts], rounds=rounds)
    in_got, parts = both[:2], both[2:]
    carry = rounds.run(flags_now, "sent", parts, not_core, each, wait=True)

    scale_row, rounds.two["keep"][0], hidden_got = meet(
        attn_scale[None], [rounds.two["keep"][0], hidden_got]
    )
    grad_attn, grad_mixed, grad_middle, join_sums = join(
        x, attn_out, grad_y, in_own, in_got, scale_row, mlp_gain[None], w_output
    )
    flip = ((sp == 0) & (n_sp == 2)).astype(jnp.int32).reshape(1)
    grad_query, grad_kv, grad_near, edge, other_edge = attend_back(
        flip, probs, joint, grad_mixed, cos_tab, sin_tab, seqs
    )
    if n_sp == 2:
        to_right = to_left = lax.ppermute(edge, "sp", [(0, 1), (1, 0)])
    else:
        to_left = lax.ppermute(edge, "sp", [(i + 1, i) for i in range(n_sp - 1)])
        to_right = lax.ppermute(other_edge, "sp", [(i, i + 1) for i in range(n_sp - 1)])
    to_right, to_left = [v.reshape(2, seqs, HALF, width) for v in (to_right, to_left)]

    core_inner = Piece(places, every, own_rows).inner(places.core)

    flags_now, grad_query = meet(flags, [grad_query])
    out, stay = weight_grad(
        flags_now,
        core_inner,
        [(mixed, grad_attn), (normed_own, grad_query), (normed, (grad_near, 0)), (normed, (grad_near, 1))],
        "attention_weights",
        0.02,
    )
    from_core = places.swap(out, places.core)

    flags_now, stay, to_right, to_left = meet(flags, [stay, to_right, to_left], [], rounds)
    first = started(rounds.run(flags_now, carry=carry))
    aside = rounds.set_aside()
    has_now, aside["keep"][0] = meet(has, [aside["keep"][0]])
    grad_kv = add_edges(has_now, grad_kv, to_right, to_left)
    flags_now, grad_kv, from_core = meet(flags, [grad_kv, from_core])
    rounds.run(flags_now, "core", (stay, from_core), not_core, own_rows)

    flags_now, rounds.one["keep"][0], *aside["got"] = meet(
        flags, [rounds.one["keep"][0], *aside["got"]]
    )
    layer_out, out_sums = feed_out(
        flags_now, hidden, hidden_got, w_down, x, attn_out, grad_y,
        attn_scale[None], mlp_scale[None], block,
    )
    flags_now, layer_out, join_sums = meet(flags, [layer_out, join_sums], [first])
    third = started(rounds.run_aside(flags_now, aside))
    onward(first)
    flags_now, first.keep, third.keep = meet(flags, [first.keep, third.keep], [], rounds)
    rounds.run(flags_now)
    gain_now, rounds.two["keep"][0] = meet(gain, [rounds.two["keep"][0]])
    frames_grad, norm_sums = input_grad(
        x, grad_query, grad_kv, grad_middle, gain_now, w_query, w_key, w_value
    )
    flags_now, frames_grad = meet(flags, [frames_grad], [third], rounds)
    fourth = started(rounds.run(flags_now))
    onward(third)
    _, fourth.keep, norm_sums = meet(flags, [fourth.keep, norm_sums])
    norm_sums, join_sums, out_sums = lax.optimization_barrier((norm_sums, join_sums, out_sums))
    vectors = jnp.stack([norm_sums[0], join_sums[0], join_sums[1], out_sums[0]], axis=1)
    vectors = vectors.reshape((2,) * places.count + (own_rows, 4))
    left = list(reversed(every))
    groups = [[b] for b in [places.core, x_bit, y_bit, z_bit] + late]
    shares = share(places, vectors, left, groups[0])
    _, *shares = meet(flags, shares, [first])
    feeds = finished(first).reshape(2, 2, 2, own_rows, width)
    mine = lax.dynamic_index_in_dim(feeds, core, 2, False)
    got = places.swap(lax.dynamic_index_in_dim(feeds, 1 - core, 2, False), places.core)
    for done, group in zip(groups, groups[1:]):
        left = [b for b in left if b not in done]
        shares = share(places, sum(shares), left, group)
        if group is groups[-3]:
            _, *shares = meet(flags, shares, [fourth])
            onward(fourth)
    down_grad = finished(third)
    pair = jnp.stack([jnp.where(core == 0, mine, got), jnp.where(core == 0, got, mine)], axis=0)
    pair = pair.reshape(2, 2, 2, own_rows, per, block)
    pair = pair.transpose(2, 3, 1, 4, 0, 5).reshape(2, own_rows, feed_width)
    while fourth.left >= 0:
        onward(fourth)
    _, gate_grad, up_grad, down_grad, *shares = meet(
        flags, [pair[0], pair[1], down_grad, *shares], [fourth]
    )
    vectors = sum(shares).T
    output_grad, query_grad, key_grad, value_grad = [
        fourth.keep[rows, columns].astype(F32) + fourth.got[rows, columns].astype(F32)
        for rows in (slice(0, own_rows), slice(own_rows, 2 * own_rows))
        for columns in (slice(0, width), slice(width, 2 * width))
    ]
    return (
        layer_out.reshape(frames.shape),
        frames_grad.reshape(frames.shape),
        vectors[0],
        query_grad,
        key_grad,
        value_grad,
        output_grad,
        vectors[1],
        vectors[2],
        gate_grad,
        up_grad,
        down_grad,
        vectors[3],
    )


def solution(mesh):
    split = P("seq", "sp", None)
    rows = P(("seq", "sp"), None)
    vec = P(("seq", "sp"))
    return jax.shard_map(
        on_device,
        mesh=mesh,
        in_specs=(split, P("seq", None)) + (P(),) * 11 + (split,),
        out_specs=(
            split, split, vec, rows, rows, rows, rows, vec, vec, rows, rows, rows, vec,
        ),
        check_vma=False,
    )
```

```python
import functools
import math

import jax
import jax.numpy as jnp
import numpy as np
from jax import lax
from jax.experimental import pallas as pl
from jax.experimental.pallas import tpu as pltpu
from jax.sharding import PartitionSpec as P

HEAD_DIM = 64
HALF = 64
LANES = 128
GROUP = 256
GH = GROUP // HEAD_DIM
QB = 128
KB = QB + 2 * HALF
CLIPS = 8
LN_EPS = 1e-05
RMS_EPS = 1e-06
VMEM = 58 << 20
F32 = jnp.float32
BF16 = jnp.bfloat16

NT = (((1,), (1,)), ((), ()))
NN = (((1,), (0,)), ((), ()))
TN = (((0,), (0,)), ((), ()))


def dot(a, b, dims=NN):
    return lax.dot_general(a, b, dims, preferred_element_type=F32)


def params(grid=0, vmem=VMEM):
    kinds = ("arbitrary",) * grid if grid else None
    return pltpu.CompilerParams(vmem_limit_bytes=vmem, dimension_semantics=kinds)


def cost(flops, moved, scale=0.02):
    return pl.CostEstimate(
        flops=int(flops * scale), bytes_accessed=int(moved * scale), transcendentals=0
    )


def in_hbm(values):
    return [pltpu.with_memory_space_constraint(v, pltpu.HBM) for v in values]


def whole(shape):
    return pl.BlockSpec(shape, lambda *_: (0,) * len(shape))


def swap_halves(v):
    lane = lax.broadcasted_iota(jnp.int32, v.shape, 1)
    return jnp.where(lane % HEAD_DIM < HEAD_DIM // 2, pltpu.roll(v, 96, 1), pltpu.roll(v, 32, 1))


def rotated(v, cos_tab, sin_tab, sign):
    pieces = []
    for at in range(0, v.shape[1], LANES):
        part = v[:, at : at + LANES]
        turned = swap_halves(part) * sin_tab
        pieces.append(part * cos_tab + turned if sign > 0 else part * cos_tab - turned)
    return jnp.concatenate(pieces, axis=1)


def project_kernel(
    seqs, x_ref, left_ref, right_ref, place_ref, gain_ref, wv_ref, wk_ref, wq_ref,
    out_ref, normed_ref, own_ref, cos_ref, sin_ref, low, weights, sems,
):
    step = pl.program_id(0)
    rows, width = low.shape
    padded = rows // seqs
    length = padded - 2 * HALF
    fetches = [
        pltpu.make_async_copy(src, weights.at[i], sems.at[i]) for i, src in enumerate((wv_ref, wk_ref, wq_ref))
    ]
    keeps = [pltpu.make_async_copy(low, normed_ref, sems.at[3])] + [
        pltpu.make_async_copy(
            low.at[s * padded + HALF : s * padded + HALF + length, :],
            own_ref.at[s * length : (s + 1) * length, :],
            sems.at[4 + s],
        )
        for s in range(seqs)
    ]

    def products(which, after):
        blocks = [slice(at, at + GROUP) for at in range(0, width, GROUP)]
        ahead = dot(low[...], weights[which, :, blocks[0]])
        for i, columns in enumerate(blocks):
            out = ahead
            if i + 1 < len(blocks):
                ahead = dot(low[...], weights[which, :, blocks[i + 1]])
            out_ref[0, :, columns] = after(out).astype(BF16)

    @pl.when(step == 0)
    def _():
        for copy in fetches:
            copy.start()
        for src, first, step in ((x_ref, HALF, length), (left_ref, 0, HALF), (right_ref, HALF + length, HALF)):
            x = src[...].astype(F32)
            centered = x - jnp.mean(x, axis=-1, keepdims=True)
            inv = lax.rsqrt(jnp.mean(centered * centered, axis=-1, keepdims=True) + LN_EPS)
            normed = (centered * inv * gain_ref[...]).astype(BF16)
            for s in range(seqs):
                at = s * padded + first
                low[at : at + step, :] = normed[s * step : (s + 1) * step]
        for copy in keeps:
            copy.start()
        fetches[0].wait()
        products(0, lambda out: out)
        lane = lax.broadcasted_iota(jnp.int32, (1, LANES), 1)
        exponent = (lane % (HEAD_DIM // 2)).astype(F32) * (2.0 / HEAD_DIM)
        angles = place_ref[...] * jnp.exp(-math.log(10000.0) * exponent)
        cos_ref[...] = jnp.cos(angles)
        sin_ref[...] = jnp.where(lane % HEAD_DIM < HEAD_DIM // 2, -1.0, 1.0) * jnp.sin(angles)

    @pl.when(step == 1)
    def _():
        fetches[1].wait()
        products(1, lambda out: rotated(out, cos_ref[...], sin_ref[...], 1))

    @pl.when(step == 2)
    def _():
        fetches[2].wait()
        scale = 1.0 / math.sqrt(HEAD_DIM)
        products(2, lambda out: rotated(out, cos_ref[...], sin_ref[...], 1) * scale)
        for copy in keeps:
            copy.wait()


def project(x, left, right, place, gain, w_query, w_key, w_value, seqs):
    own, width = x.shape
    rows = own + seqs * 2 * HALF
    edge = whole((seqs * HALF, width))
    hbm = pl.BlockSpec(memory_space=pl.ANY)
    table = jax.ShapeDtypeStruct((rows, LANES), F32)
    return pl.pallas_call(
        functools.partial(project_kernel, seqs),
        grid=(3,),
        in_specs=[whole((own, width)), edge, edge, whole((rows, 1)), whole((1, width))] + [hbm] * 3,
        out_specs=[
            pl.BlockSpec((1, rows, width), lambda j: (j, 0, 0)),
            hbm,
            hbm,
            whole((rows, LANES)),
            whole((rows, LANES)),
        ],
        out_shape=[
            jax.ShapeDtypeStruct((3, rows, width), BF16),
            jax.ShapeDtypeStruct((rows, width), BF16),
            jax.ShapeDtypeStruct((own, width), BF16),
            table,
            table,
        ],
        scratch_shapes=[
            pltpu.VMEM((rows, width), BF16),
            pltpu.VMEM((3, width, width), BF16),
            pltpu.SemaphoreType.DMA((4 + seqs,)),
        ],
        compiler_params=params(1),
        cost_estimate=cost(6 * rows * width * width, 6 * width * width + 10 * rows * width),
        name="project",
    )(x, left, right, place, gain, w_value, w_key, w_query)


def stack_heads(block):
    lane = lax.broadcasted_iota(jnp.int32, block.shape, 1)
    zero = jnp.zeros_like(block)
    return jnp.concatenate(
        [jnp.where(lane // HEAD_DIM == h, block, zero) for h in range(GH)], axis=0
    )


def fill_keys(buf, ref):
    rows = ref.shape[1]
    buf[0:rows, :] = ref[0]
    if buf.shape[0] > rows:
        buf[rows:, :] = jnp.zeros((buf.shape[0] - rows, buf.shape[1]), buf.dtype)


def fill_queries(buf, ref, length):
    buf[0:length, :] = ref[0, HALF : HALF + length, :] if ref.ndim == 3 else ref[...]
    rest = buf.shape[0] - length
    if rest:
        buf[length:, :] = jnp.zeros((rest, buf.shape[1]), buf.dtype)


def attend_kernel(span_ref, q_ref, k_ref, v_ref, o_ref, p_ref, kbuf, vbuf, qbuf, vt, ot):
    length = o_ref.shape[0]
    padded = qbuf.shape[0]
    fill_keys(kbuf, k_ref)
    fill_keys(vbuf, v_ref)
    fill_queries(qbuf, q_ref, length)
    blocks = padded // QB

    def scores_of(b):
        return dot(kbuf[b * QB : b * QB + KB, :], stack_heads(qbuf[b * QB : (b + 1) * QB, :]), NT)

    def mix(b, probs):
        for h in range(GH):
            rows = slice(h * HEAD_DIM, (h + 1) * HEAD_DIM)
            ot[rows, b * QB : (b + 1) * QB] = dot(vt[rows, b * QB : b * QB + KB], probs[h]).astype(BF16)

    ahead = scores_of(0)
    vt[...] = vbuf[...].T
    before = None
    for b in range(blocks):
        scores = ahead
        if b + 1 < blocks:
            ahead = scores_of(b + 1)
        if before is not None:
            mix(b - 1, before)
        place = lax.broadcasted_iota(jnp.int32, (KB, QB), 0) + b * QB
        low = span_ref[0, 0:1, b * QB : (b + 1) * QB]
        high = span_ref[0, 1:2, b * QB : (b + 1) * QB]
        seen = (place >= low) & (place < high)
        before = []
        for h in range(GH):
            masked = jnp.where(seen, scores[:, h * QB : (h + 1) * QB], -1e30)
            terms = jnp.exp(masked - jnp.max(masked, axis=0, keepdims=True))
            total = jnp.sum(terms, axis=0, keepdims=True)
            probs = (terms * (1.0 / total)).astype(BF16)
            p_ref[:, b * GH * QB + h * QB : b * GH * QB + (h + 1) * QB] = probs
            before.append(probs)
    mix(blocks - 1, before)
    o_ref[...] = ot[...].T[0:length, :]


def attend(span, joint, seqs):
    _, rows, width = joint.shape
    length = rows // seqs - 2 * HALF
    rows = seqs * length
    padded = span.shape[2]
    groups = width // GROUP
    keys = padded + 2 * HALF
    own = pl.BlockSpec((length, GROUP), lambda s, g: (s, g))
    near = [pl.BlockSpec((1, length + 2 * HALF, GROUP), lambda s, g, i=i: (i, s, g)) for i in range(3)]
    return pl.pallas_call(
        attend_kernel,
        grid=(seqs, groups),
        in_specs=[
            pl.BlockSpec((1, 2, padded), lambda s, g: (s, 0, 0)),
            near[2],
            near[1],
            near[0],
        ],
        out_specs=[
            own,
            pl.BlockSpec((KB, GH * padded), lambda s, g: (s, g)),
        ],
        out_shape=[
            jax.ShapeDtypeStruct((rows, width), BF16),
            jax.ShapeDtypeStruct((seqs * KB, groups * GH * padded), BF16),
        ],
        scratch_shapes=[
            pltpu.VMEM((keys, GROUP), BF16),
            pltpu.VMEM((keys, GROUP), BF16),
            pltpu.VMEM((padded, GROUP), BF16),
            pltpu.VMEM((GROUP, keys), BF16),
            pltpu.VMEM((GROUP, padded), BF16),
        ],
        compiler_params=params(2),
        cost_estimate=cost(
            2 * 2 * seqs * width * padded * KB * 4, 2 * width * (4 * rows + KB * seqs * padded // 64)
        ),
        name="attend",
    )(span, joint, joint, joint)


def attend_back_kernel(
    flip_ref, p_ref, q_ref, k_ref, v_ref, g_ref, cos_ref, sin_ref,
    dq_ref, dkv_ref, near_ref, edge_ref, other_ref,
    kbuf, vbuf, qbuf, gbuf, kt, dqt, dkb, dvb,
):
    length = g_ref.shape[0]
    padded = qbuf.shape[0]
    fill_keys(kbuf, k_ref)
    fill_keys(vbuf, v_ref)
    fill_queries(qbuf, q_ref, length)
    fill_queries(gbuf, g_ref, length)
    blocks = padded // QB

    def probs_grads(b):
        g4 = stack_heads(gbuf[b * QB : (b + 1) * QB, :])
        return g4, dot(vbuf[b * QB : b * QB + KB, :], g4, NT)

    def spread(b, g4, probs, lows):
        at, keys = slice(b * QB, (b + 1) * QB), slice(b * QB, b * QB + KB)
        for h in range(GH):
            rows = slice(h * HEAD_DIM, (h + 1) * HEAD_DIM)
            dqt[rows, at] = dot(kt[rows, keys], lows[h])
        q4 = stack_heads(qbuf[at, :])
        grads = (dkb, dot(jnp.concatenate(lows, axis=1), q4)), (dvb, dot(probs, g4))
        for buf, grad in grads:
            if b:
                buf[at, :] += grad[:QB]
            else:
                buf[at, :] = grad[:QB]
            buf[(b + 1) * QB : b * QB + KB, :] = grad[QB:]

    ahead = probs_grads(0)
    kt[...] = kbuf[...].T
    before = None
    for b in range(blocks):
        g4, grads = ahead
        if b + 1 < blocks:
            ahead = probs_grads(b + 1)
        if before is not None:
            spread(b - 1, *before)
        probs = p_ref[:, b * GH * QB : (b + 1) * GH * QB]
        lows = []
        for h in range(GH):
            part = probs[:, h * QB : (h + 1) * QB].astype(F32)
            grad = grads[:, h * QB : (h + 1) * QB]
            delta = jnp.sum(part * grad, axis=0, keepdims=True)
            lows.append((part * (grad - delta)).astype(BF16))
        before = g4, probs, lows
    spread(blocks - 1, *before)
    cos_tab, sin_tab = cos_ref[...], sin_ref[...]
    middle = slice(HALF, HALF + length)
    dq = dqt[...].T[0:length, :] * (1.0 / math.sqrt(HEAD_DIM))
    dq_ref[...] = rotated(dq, cos_tab[middle], sin_tab[middle], -1).astype(BF16)
    span = length + 2 * HALF
    dk = rotated(dkb[0:span, :], cos_tab, sin_tab, -1).astype(BF16)
    dv = dvb[0:span, :].astype(BF16)
    for i, grad in enumerate((dk, dv)):
        dkv_ref[i] = grad[middle]
        near_ref[i] = grad
        ends = grad[0:HALF], grad[span - HALF :]
        edge_ref[i] = jnp.where(flip_ref[0] == 1, ends[1], ends[0])
        other_ref[i] = jnp.where(flip_ref[0] == 1, ends[0], ends[1])


def attend_back(flip, probs, joint, grad, cos_tab, sin_tab, seqs):
    rows, width = grad.shape
    length = rows // seqs
    padded = -(-length // QB) * QB
    groups = width // GROUP
    keys = padded + 2 * HALF
    own = pl.BlockSpec((length, GROUP), lambda s, g, f: (s, g))
    both = pl.BlockSpec((2, length, GROUP), lambda s, g, f: (0, s, g))
    both_near = pl.BlockSpec((2, length + 2 * HALF, GROUP), lambda s, g, f: (0, s, g))
    near = [pl.BlockSpec((1, length + 2 * HALF, GROUP), lambda s, g, f, i=i: (i, s, g)) for i in range(3)]
    table = pl.BlockSpec((length + 2 * HALF, LANES), lambda s, g, f: (s, 0))
    edge = pl.BlockSpec((2, HALF, GROUP), lambda s, g, f: (0, s, g))
    out_edge = jax.ShapeDtypeStruct((2, seqs * HALF, width), BF16)
    out = jax.ShapeDtypeStruct((rows, width), BF16)
    out_both = jax.ShapeDtypeStruct((2, rows, width), BF16)
    out_near = jax.ShapeDtypeStruct((2, rows + seqs * 2 * HALF, width), BF16)
    return pl.pallas_call(
        attend_back_kernel,
        grid_spec=pltpu.PrefetchScalarGridSpec(
            num_scalar_prefetch=1,
            grid=(seqs, groups),
        in_specs=[
            pl.BlockSpec((KB, GH * padded), lambda s, g, f: (s, g)),
            near[2],
            near[1],
            near[0],
            own,
            table,
            table,
        ],
        out_specs=[own, both, both_near, edge, edge],
        scratch_shapes=[
            pltpu.VMEM((keys, GROUP), BF16),
            pltpu.VMEM((keys, GROUP), BF16),
            pltpu.VMEM((padded, GROUP), BF16),
            pltpu.VMEM((padded, GROUP), BF16),
            pltpu.VMEM((GROUP, keys), BF16),
            pltpu.VMEM((GROUP, padded), F32),
            pltpu.VMEM((keys, GROUP), F32),
            pltpu.VMEM((keys, GROUP), F32),
        ],
        ),
        out_shape=[out, out_both, out_near, out_edge, out_edge],
        compiler_params=params(2),
        cost_estimate=cost(
            2 * 4 * seqs * width * padded * KB * 4, 2 * width * (8 * rows + KB * seqs * padded // 64)
        ),
        name="attend_back",
    )(flip, probs, joint, joint, joint, grad, cos_tab, sin_tab)


def edges_kernel(seqs, flags_ref, from_ref, left_ref, right_ref, to_ref, buf, sems):
    length = from_ref.shape[1] // seqs
    places = [
        (i, s, e, pl.ds(s * length + e * (length - HALF), HALF))
        for i in range(2)
        for s in range(seqs)
        for e in range(2)
    ]
    copies = [
        (from_ref.at[i, rows, :], to_ref.at[i, rows, :], buf.at[at]) for at, (i, _, _, rows) in enumerate(places)
    ]
    for at, (src, _, mid) in enumerate(copies):
        pltpu.make_async_copy(src, mid, sems.at[0, at]).start()
    for at, (src, _, mid) in enumerate(copies):
        pltpu.make_async_copy(src, mid, sems.at[0, at]).wait()
    for at, (i, s, e, _) in enumerate(places):
        got = (right_ref if e else left_ref)[i, s].astype(F32) * flags_ref[e].astype(F32)
        buf[at] = (buf[at].astype(F32) + got).astype(BF16)
    for at, (_, dst, mid) in enumerate(copies):
        pltpu.make_async_copy(mid, dst, sems.at[1, at]).start()
    for at, (_, dst, mid) in enumerate(copies):
        pltpu.make_async_copy(mid, dst, sems.at[1, at]).wait()


def add_edges(flags, grads, left, right):
    seqs = left.shape[1]
    hbm = pl.BlockSpec(memory_space=pl.ANY)
    return pl.pallas_call(
        functools.partial(edges_kernel, seqs),
        grid_spec=pltpu.PrefetchScalarGridSpec(
            num_scalar_prefetch=1,
            grid=(1,),
            in_specs=[hbm, whole(left.shape), whole(right.shape)],
            out_specs=hbm,
            scratch_shapes=[
                pltpu.VMEM((4 * seqs, HALF, grads.shape[2]), BF16),
                pltpu.SemaphoreType.DMA((2, 4 * seqs)),
            ],
        ),
        out_shape=jax.ShapeDtypeStruct(grads.shape, BF16),
        input_output_aliases={1: 0},
        compiler_params=params(1),
        cost_estimate=cost(1e4 * left.size, 8 * left.size, 1000),
        name="add_edges",
    )(flags, grads, left, right)


def out_proj_kernel(m_ref, x_ref, w_ref, scale_ref, gain_ref, attn_ref, in_ref):
    attn = dot(m_ref[...], w_ref[...])
    attn_ref[...] = attn.astype(BF16)
    middle = x_ref[...].astype(F32) + scale_ref[...] * attn
    inv = lax.rsqrt(jnp.mean(middle * middle, axis=-1, keepdims=True) + RMS_EPS)
    in_ref[...] = (middle * inv * gain_ref[...]).astype(BF16)


def out_proj(mixed, x, w_output, scale, gain):
    rows, width = x.shape
    block = rows // 2
    row = pl.BlockSpec((block, width), lambda i: (i, 0))
    return pl.pallas_call(
        out_proj_kernel,
        grid=(rows // block,),
        in_specs=[row, row, whole((width, width)), whole((1, width)), whole((1, width))],
        out_specs=[row, row],
        out_shape=[
            jax.ShapeDtypeStruct((rows, width), BF16),
            jax.ShapeDtypeStruct((rows, width), BF16),
        ],
        compiler_params=params(1),
        cost_estimate=cost(2 * rows * width * width, 2 * rows * width * 5 + 2 * width * width),
        name="out_proj",
    )(mixed, x, w_output, scale, gain)


def hidden_grad_kernel(core_ref, own_ref, peer_ref, scale_ref, one_ref, two_ref, low_ref, out_ref):
    rows = own_ref.shape[0]
    block = one_ref.shape[0]

    @pl.when(pl.program_id(0) == 0)
    def _():
        low_ref[0:rows, :] = (own_ref[...].astype(F32) * scale_ref[...]).astype(BF16)
        low_ref[rows:, :] = (peer_ref[...].astype(F32) * scale_ref[...]).astype(BF16)

    out_ref[:, :block] = dot(low_ref[...], one_ref[...], NT).astype(BF16)
    out_ref[:, block:] = dot(low_ref[...], two_ref[...], NT).astype(BF16)


def hidden_grad(core, own, peer, scale, w_down, block):
    rows, width = own.shape
    count = w_down.shape[0] // block // 4
    half = w_down.shape[0] // 2
    return pl.pallas_call(
        hidden_grad_kernel,
        grid_spec=pltpu.PrefetchScalarGridSpec(
            num_scalar_prefetch=1,
            grid=(count,),
            in_specs=[
                whole((rows, width)),
                whole((rows, width)),
                whole((1, width)),
                pl.BlockSpec((block, width), lambda j, c: (4 * j + c[0], 0)),
                pl.BlockSpec((block, width), lambda j, c: (4 * j + 2 + c[0], 0)),
            ],
            out_specs=[
                whole((2 * rows, width)),
                pl.BlockSpec((2 * rows, 2 * block), lambda j, c: (0, j)),
            ],
        ),
        out_shape=[
            jax.ShapeDtypeStruct((2 * rows, width), BF16),
            jax.ShapeDtypeStruct((2 * rows, half), BF16),
        ],
        compiler_params=params(1),
        cost_estimate=cost(
            4 * rows * width * half, 2 * (4 * rows * width + half * (width + 2 * rows))
        ),
        name="hidden_grad",
    )(core, own, peer, scale, w_down, w_down)


def halves_of(value, bit, inner):
    rows, columns = value.shape
    both = value.reshape(rows // (2 * inner), 2, inner, columns)
    zero, one = both[:, 0], both[:, 1]
    out = jnp.where(bit == 0, one, zero).reshape(rows // 2, columns)
    stay = jnp.where(bit == 0, zero, one).reshape(rows // 2, columns)
    return out, stay


def feed_kernel(inners, core_ref, xo_ref, xp_ref, gh_ref, wg_ref, wu_ref, *refs):
    hid_own_ref, hid_peer_ref, gg_ref, gu_ref, *outs, x_all = refs[-9:]
    rows = xo_ref.shape[0]

    @pl.when(pl.program_id(0) == 0)
    def _():
        x_all[0:rows, :] = xo_ref[...]
        x_all[rows:, :] = xp_ref[...]

    for at in (0, rows):
        part = slice(at, at + rows)
        gate = dot(x_all[part, :], wg_ref[...])
        up = dot(x_all[part, :], wu_ref[...])
        grad = gh_ref[part, :].astype(F32)
        sig = 1.0 / (1.0 + jnp.exp(-gate))
        act = gate * sig
        (hid_peer_ref if at else hid_own_ref)[...] = (act * up).astype(BF16)
        gg_ref[part, :] = (grad * up * sig * (1.0 + gate * (1.0 - sig))).astype(BF16)
        gu_ref[part, :] = (grad * act).astype(BF16)
    for i, src in enumerate((gg_ref, gu_ref)):
        out, stay = halves_of(dot(x_all[...], src[...], TN), core_ref[1 + i], inners[i])
        outs[2 * i][...] = out.astype(BF16)
        outs[2 * i + 1][...] = stay.astype(BF16)


def feed(core, x_own, x_peer, grad_hidden, w_gate, w_up, block, first, count, before, inners, room=0):
    rows, width = x_own.shape
    half = grad_hidden.shape[1]
    wide = pl.BlockSpec((2 * rows, block), lambda j, c: (0, j + first))
    weight = pl.BlockSpec((width, block), lambda j, c: (0, 2 * (j + first) + c[0]))
    tall = pl.BlockSpec((rows, block), lambda j, c: (0, j + first))
    kept = pltpu.HBM((2 * rows, half), BF16)
    single = pltpu.HBM((rows, half), BF16)
    grads = [pltpu.HBM((width // 2 + more, count * block), BF16) for more in (room, 0, room, 0)]
    any_spec = pl.BlockSpec(memory_space=pl.ANY)
    return pl.pallas_call(
        functools.partial(feed_kernel, inners),
        grid_spec=pltpu.PrefetchScalarGridSpec(
            num_scalar_prefetch=1,
            grid=(count,),
            in_specs=[whole((rows, width)), whole((rows, width)), wide, weight, weight]
            + [any_spec] * len(before),
            out_specs=[tall] * 2
            + [wide] * 2
            + [pl.BlockSpec((width // 2, block), lambda j, c: (0, j))] * 4,
            scratch_shapes=[pltpu.VMEM((2 * rows, width), BF16)],
        ),
        out_shape=[single] * 2 + [kept] * 2 + grads,
        input_output_aliases={6 + i: i for i in range(len(before))},
        compiler_params=params(1, 46 << 20),
        cost_estimate=cost(
            2 * 2 * rows * width * block * count * 4,
            2 * (4 * rows * width + count * block * (8 * rows + 4 * width)),
        ),
        name="feed",
    )(core, *in_hbm([x_own]), x_peer, *in_hbm([grad_hidden, w_gate, w_up, *before]))


def down_kernel(each, inners, bits_ref, own_ref, peer_ref, low_ref, *refs):
    *outs, both = refs
    both[: own_ref.shape[0], :] = own_ref[...]
    both[own_ref.shape[0] :, :] = peer_ref[...]
    value = dot(both[...], low_ref[...], TN)
    rows, width = value.shape
    value = value.reshape(rows // (2 * each), 2, each, width)
    for i in range(2):
        part = value[:, i].reshape(rows // 2, width)
        out, stay = halves_of(part, bits_ref[1 + i], inners[i])
        outs[2 * i][...] = out.astype(BF16)
        outs[2 * i + 1][...] = stay.astype(BF16)


def down(bits, own, peer, low, each, inners, room):
    rows, half = own.shape
    width = low.shape[1]
    block = 512
    return pl.pallas_call(
        functools.partial(down_kernel, each, inners),
        grid_spec=pltpu.PrefetchScalarGridSpec(
            num_scalar_prefetch=1,
            grid=(half // block,),
            in_specs=[
                pl.BlockSpec((rows, block), lambda j, c: (0, j)),
                pl.BlockSpec((rows, block), lambda j, c: (0, j)),
                whole((2 * rows, width)),
            ],
            out_specs=[pl.BlockSpec((block // 4, width), lambda j, c: (j, 0))] * 4,
            scratch_shapes=[pltpu.VMEM((2 * rows, block), BF16)],
        ),
        out_shape=[jax.ShapeDtypeStruct((half // 4 + more, width), BF16) for more in (room, 0, room, 0)],
        compiler_params=params(1),
        cost_estimate=cost(
            4 * rows * half * width, 2 * (2 * rows * half + 2 * rows * width + half * width)
        ),
        name="down_weight",
    )(bits, own, peer, low)


def in_halves(value, refs):
    half = value.shape[1] // 2
    refs[0][...] = value[:, :half]
    refs[1][...] = value[:, half:]


def feed_back_kernel(core_ref, *refs):
    *peer_refs, own_ref, acc = refs[-4:]
    part, step = pl.program_id(0), pl.program_id(1)
    block = refs[2].shape[1]
    total = None
    for i in range(2):
        for half in range(2):
            out = dot(refs[i][:, half * block : (half + 1) * block], refs[2 + 2 * i + half][...], NT)
            total = out if total is None else total + out
    last = pl.num_programs(1) - 1

    @pl.when(step == 0)
    def _():
        acc[...] = total

    @pl.when((step > 0) & (step < last))
    def _():
        acc[...] += total

    @pl.when((step == last) & (part == 0))
    def _():
        in_halves((acc[...] + total).astype(BF16), peer_refs)

    @pl.when((step == last) & (part == 1))
    def _():
        own_ref[...] = (acc[...] + total).astype(BF16)


def feed_back(core, grad_gate, grad_up, w_gate, w_up, block):
    rows, half = grad_gate.shape
    rows = rows // 2
    width = w_gate.shape[0]
    tall = pl.BlockSpec((rows, 2 * block), lambda p, j, c: (1 - p, j))
    one = pl.BlockSpec((width, block), lambda p, j, c: (0, 4 * j + c[0]))
    two = pl.BlockSpec((width, block), lambda p, j, c: (0, 4 * j + 2 + c[0]))
    return pl.pallas_call(
        feed_back_kernel,
        grid_spec=pltpu.PrefetchScalarGridSpec(
            num_scalar_prefetch=1,
            grid=(2, half // block // 2),
            in_specs=[tall, tall, one, two, one, two],
            out_specs=[whole((rows, width // 2))] * 2 + [whole((rows, width))],
            scratch_shapes=[pltpu.VMEM((rows, width), F32)],
        ),
        out_shape=[jax.ShapeDtypeStruct((rows, width // 2), BF16)] * 2
        + [jax.ShapeDtypeStruct((rows, width), BF16)],
        compiler_params=params(2),
        cost_estimate=cost(8 * rows * half * width, 8 * (rows * half + half * width)),
        name="feed_back",
    )(core, grad_gate, grad_up, w_gate, w_gate, w_up, w_up)


def join_kernel(
    x_ref, attn_ref, g_ref, in_ref, got_one_ref, got_two_ref, attn_scale_ref, gain_ref, w_ref,
    grad_attn_ref, grad_mixed_ref, middle_ref, sums_ref,
):
    x = x_ref[...].astype(F32)
    attn = attn_ref[...].astype(F32)
    grad_y = g_ref[...].astype(F32)
    got = jnp.concatenate([got_one_ref[...], got_two_ref[...]], axis=1)
    grad_in = in_ref[...].astype(F32) + got.astype(F32)
    middle = x + attn_scale_ref[...] * attn
    inv = lax.rsqrt(jnp.mean(middle * middle, axis=-1, keepdims=True) + RMS_EPS)
    unit = middle * inv
    scaled = grad_in * gain_ref[...]
    grad_middle = grad_y + inv * (scaled - unit * jnp.mean(scaled * unit, axis=-1, keepdims=True))
    middle_ref[...] = grad_middle.astype(BF16)
    grad_attn = (attn_scale_ref[...] * grad_middle).astype(BF16)
    grad_attn_ref[...] = grad_attn
    grad_mixed_ref[...] = dot(grad_attn, w_ref[...], NT).astype(BF16)

    @pl.when(pl.program_id(0) == 0)
    def _():
        sums_ref[...] = jnp.zeros_like(sums_ref)

    sums_ref[0:1, :] += jnp.sum(grad_middle * attn, axis=0, keepdims=True)
    sums_ref[1:2, :] += jnp.sum(grad_in * unit, axis=0, keepdims=True)


def join(x, attn, grad_y, grad_in, got, attn_scale, gain, w_output):
    rows, width = x.shape
    block = rows // 2
    row = pl.BlockSpec((block, width), lambda i: (i, 0))
    half = pl.BlockSpec((block, width // 2), lambda i: (i, 0))
    vec = whole((1, width))
    low = jax.ShapeDtypeStruct((rows, width), BF16)
    return pl.pallas_call(
        join_kernel,
        grid=(rows // block,),
        in_specs=[row] * 4 + [half] * 2 + [vec] * 2 + [whole((width, width))],
        out_specs=[row] * 3 + [whole((8, width))],
        out_shape=[
            low,
            low,
            low,
            jax.ShapeDtypeStruct((8, width), F32),
        ],
        compiler_params=params(1),
        cost_estimate=cost(2 * rows * width * width, rows * width * 22 + 2 * width * width),
        name="join",
    )(x, attn, grad_y, grad_in, *got, attn_scale, gain, w_output)


def feed_out_kernel(
    core_ref, own_ref, got_ref, w_ref, x_ref, attn_ref, g_ref, attn_scale_ref, mlp_scale_ref,
    layer_ref, sums_ref, hidden, acc,
):
    step, last = pl.program_id(0), pl.num_programs(0) - 1
    block = own_ref.shape[1] // 2
    for i in range(2):
        part = slice(i * block, (i + 1) * block)
        own, got = own_ref[:, part], got_ref[:, part]
        first = core_ref[0] == 0
        hidden[:, 2 * i * block : (2 * i + 1) * block] = jnp.where(first, own, got)
        hidden[:, (2 * i + 1) * block : (2 * i + 2) * block] = jnp.where(first, got, own)
    total = dot(hidden[...], w_ref[...])

    @pl.when(step == 0)
    def _():
        acc[...] = total

    @pl.when((step > 0) & (step < last))
    def _():
        acc[...] += total

    @pl.when(step == last)
    def _():
        down_out = acc[...] + total
        middle = x_ref[...].astype(F32) + attn_scale_ref[...] * attn_ref[...].astype(F32)
        layer_ref[...] = (middle + mlp_scale_ref[...] * down_out).astype(BF16)
        sums_ref[...] = jnp.zeros_like(sums_ref)
        sums_ref[0:1, :] = jnp.sum(g_ref[...].astype(F32) * down_out, axis=0, keepdims=True)


def feed_out(core, own, got, w_down, x, attn, grad_y, attn_scale, mlp_scale, block):
    rows, half = own.shape
    width = w_down.shape[1]
    tall = pl.BlockSpec((rows, 2 * block), lambda j, c: (0, j))
    row, vec = whole((rows, width)), whole((1, width))
    return pl.pallas_call(
        feed_out_kernel,
        grid_spec=pltpu.PrefetchScalarGridSpec(
            num_scalar_prefetch=1,
            grid=(half // block // 2,),
            in_specs=[tall, tall, pl.BlockSpec((4 * block, width), lambda j, c: (j, 0))]
            + [row] * 3
            + [vec] * 2,
            out_specs=[row, whole((8, width))],
            scratch_shapes=[pltpu.VMEM((rows, 4 * block), BF16), pltpu.VMEM((rows, width), F32)],
        ),
        out_shape=[
            jax.ShapeDtypeStruct((rows, width), BF16),
            jax.ShapeDtypeStruct((8, width), F32),
        ],
        compiler_params=params(1),
        cost_estimate=cost(4 * rows * half * width, 4 * (rows * half + half * width), 10),
        name="feed_out",
    )(core, own, got, w_down, x, attn, grad_y, attn_scale, mlp_scale)


def weight_grad_kernel(inner, order, counts, bit_ref, *refs):
    out_ref, stay_ref = refs[-2:]
    step = pl.program_id(0)
    lefts = [refs[i] for i in order]
    rights = refs[max(order) + 1 : -2]
    first = 0
    for left, right, count in zip(lefts, rights, counts):

        @pl.when((step >= first) & (step < first + count))
        def _(left=left, right=right):
            rows = right[...].reshape(right.shape[-2:])
            out, stay = halves_of(dot(left[...], rows, TN), bit_ref[0], inner)
            out_ref[...] = out.astype(BF16)
            stay_ref[...] = stay.astype(BF16)

        first += count


def weight_grad(bit, inner, pairs, name, scale):
    block = 512
    width = pairs[0][0].shape[1]
    lefts = []
    for left, _ in pairs:
        if not any(left is other for other in lefts):
            lefts.append(left)
    order = [[left is other for other in lefts].index(True) for left, _ in pairs]
    counts, specs, rights, first = [], [], [], 0
    for left, right in pairs:
        rows = left.shape[0]
        array, part = right if isinstance(right, tuple) else (right, None)
        count = array.shape[-1] // block
        at = lambda j, first=first, count=count: jnp.clip(j - first, 0, count - 1)
        if part is None:
            specs.append(pl.BlockSpec((rows, block), lambda j, c, at=at: (0, at(j))))
        else:
            specs.append(
                pl.BlockSpec((1, rows, block), lambda j, c, at=at, part=part: (part, 0, at(j)))
            )
        rights.append(array)
        counts.append(count)
        first += count
    out = jax.ShapeDtypeStruct((width // 2, first * block), BF16)
    return pl.pallas_call(
        functools.partial(weight_grad_kernel, inner, order, counts),
        grid_spec=pltpu.PrefetchScalarGridSpec(
            num_scalar_prefetch=1,
            grid=(first,),
            in_specs=[whole(left.shape) for left in lefts] + specs,
            out_specs=[pl.BlockSpec((width // 2, block), lambda j, c: (0, j))] * 2,
        ),
        out_shape=[out, out],
        compiler_params=params(1),
        cost_estimate=cost(
            2 * rows * width * first * block,
            2 * (len(lefts) * rows * width + (rows + width) * first * block),
            scale,
        ),
        name=name,
    )(bit, *lefts, *rights)


def input_grad_kernel(
    x_ref, gq_ref, gk_ref, gv_ref, middle_ref, gain_ref, wq_ref, wk_ref, wv_ref, out_ref, sums_ref
):
    grad = (
        dot(gq_ref[...], wq_ref[...], NT)
        + dot(gk_ref[0], wk_ref[...], NT)
        + dot(gv_ref[0], wv_ref[...], NT)
    )
    x = x_ref[...].astype(F32)
    centered = x - jnp.mean(x, axis=-1, keepdims=True)
    inv = lax.rsqrt(jnp.mean(centered * centered, axis=-1, keepdims=True) + LN_EPS)
    unit = centered * inv
    scaled = grad * gain_ref[...]
    back = inv * (
        scaled
        - jnp.mean(scaled, axis=-1, keepdims=True)
        - unit * jnp.mean(scaled * unit, axis=-1, keepdims=True)
    )
    out_ref[...] = (middle_ref[...].astype(F32) + back).astype(BF16)

    @pl.when(pl.program_id(0) == 0)
    def _():
        sums_ref[...] = jnp.zeros_like(sums_ref)

    sums_ref[0:1, :] += jnp.sum(grad * unit, axis=0, keepdims=True)


def input_grad(x, gq, gkv, grad_middle, gain, w_query, w_key, w_value):
    rows, width = x.shape
    block = rows // 2
    row = pl.BlockSpec((block, width), lambda i: (i, 0))
    square = whole((width, width))
    return pl.pallas_call(
        input_grad_kernel,
        grid=(rows // block,),
        in_specs=[
            row,
            row,
            pl.BlockSpec((1, block, width), lambda i: (0, i, 0)),
            pl.BlockSpec((1, block, width), lambda i: (1, i, 0)),
            row,
            whole((1, width)),
        ]
        + [square] * 3,
        out_specs=[row, whole((8, width))],
        out_shape=[
            jax.ShapeDtypeStruct((rows, width), BF16),
            jax.ShapeDtypeStruct((8, width), F32),
        ],
        compiler_params=params(1),
        cost_estimate=cost(2 * 3 * rows * width * width, rows * width * 14 + 6 * width * width),
        name="input_grad",
    )(x, gq, gkv, gkv, grad_middle, gain, w_query, w_key, w_value)


def log2(n):
    return n.bit_length() - 1


class Places:
    def __init__(self):
        self.n_seq, self.n_sp = lax.axis_size("seq"), lax.axis_size("sp")
        self.sp_bits = log2(self.n_sp)
        self.count = self.sp_bits + log2(self.n_seq)
        self.core = self.sp_bits
        self.me = lax.axis_index("seq") * self.n_sp + lax.axis_index("sp")
        self.down_bits = [b for b in reversed(range(self.count)) if b != self.core]

    def swap(self, value, bit):
        if bit < self.sp_bits:
            axis, size, at = "sp", self.n_sp, bit
        else:
            axis, size, at = "seq", self.n_seq, bit - self.sp_bits
        return lax.ppermute(value, axis, [(i, i ^ (1 << at)) for i in range(size)])

    def send(self, value, flip):
        pairs = [(i, i ^ flip) for i in range(1 << self.count)]
        return lax.ppermute(value, ("seq", "sp"), pairs)

    def own(self, bit):
        return (self.me >> bit) & 1


def round_kernel(has, inners, bits_ref, *refs):
    two, one, new, carry = has
    refs = list(refs)
    take = lambda n: [refs.pop(0) for _ in range(n)]
    second, carried = take(4) if two else (), take(2) if carry else ()
    first = take(4) if one else ()
    fresh = take({"sent": 2, "core": 4, "": 0}[new])
    bufs = take(2) if one or new else ()
    bits = bits_ref[1], bits_ref[2], bits_ref[3]

    def split(keep, got, bit, inner):
        total = keep[...].astype(F32) + got[...].astype(F32)
        return [v.astype(BF16) for v in halves_of(total, bit, inner)]

    if two:
        outs = take(2)
        at = carried[0].shape[0] if carry else 0
        for src, dst in zip(carried, outs):
            dst[0:at, :] = src[...]
        for i in range(2):
            rows = second[i].shape[0] // 2
            for dst, part in zip(outs, split(second[i], second[2 + i], bits[2], inners["two"])):
                dst[at : at + rows, :] = part
            at += rows
    at = [0, 0]
    if new == "core":
        stays = take(2)
        for i in range(2):
            out, stays[i][...] = split(fresh[2 * i], fresh[2 * i + 1], bits[i], inners["new"][i])
            at[i] = out.shape[0]
            bufs[i][0 : at[i], :] = out
    if one:
        stays = take(2)
        for i in range(2):
            out, stays[i][...] = split(first[i], first[2 + i], bits[1 - i], inners["one"][i])
            bufs[1 - i][at[1 - i] :, :] = out


class Rounds:
    def __init__(self, places, x, y, z):
        self.places, self.x, self.y, self.z = places, x, y, z
        self.one = self.two = None
        self.got = []

    def inner(self, group, without, bit):
        bits = [b for b in sorted(group["bits"], reverse=True) if b not in without]
        return group["each"] << (len(bits) - 1 - bits.index(bit))

    def first_inners(self, bits, each):
        group = {"bits": bits, "each": each}
        return [self.inner(group, (), self.x), self.inner(group, (), self.y)]

    def send(self, buf_x, buf_y):
        self.got = [self.places.swap(buf_x, self.x), self.places.swap(buf_y, self.y)]

    def begin(self, parts, bits, each):
        self.one = {"bits": bits, "each": each, "keep": [parts[1], parts[3]]}
        self.send(parts[0], parts[2])

    def set_aside(self):
        group, self.two = self.two, None
        return dict(group, got=self.got)

    def run_aside(self, flags, aside):
        kept = self.one, self.two, self.got
        self.one, self.two, self.got = None, None, aside["got"]
        done = self.run(flags, aside=aside)
        self.one, self.two, self.got = kept
        return done

    def run(self, flags, new="", arrays=(), bits=(), each=0, carry=(), wait=False, aside=None, scale=0.02):
        one = self.one
        two = aside or self.two
        steps = 2
        ins, specs, outs, inners, heights, wide = [], [], [], {}, [0, 0], 0

        def tall(rows, columns, at=0, row=0):
            return pl.BlockSpec((rows, columns // steps), lambda j, b: (row, j + at))

        if two:
            rows, columns = two["keep"][0].shape
            got_x, got_y = two["got"] if aside else self.got
            ins += two["keep"] + [got_y, got_x]
            last = [got_y.shape[0] // rows - 1, got_x.shape[0] // rows - 1]
            specs += [tall(rows, columns)] * 2 + [tall(rows, columns, 0, row) for row in last]
            ins += carry
            specs += [tall(*v.shape) for v in carry]
            outs += [(rows + (carry[0].shape[0] if carry else 0), columns)] * 2
            inners["two"] = self.inner(two, (self.x, self.y), self.z)
        group, aliases = {"bits": list(bits), "each": each}, {}
        if one:
            rows, wide = one["keep"][0].shape
            ins += one["keep"] + self.got
            specs += [tall(rows, wide)] * 4
            inners["one"] = self.inner(one, (self.x,), self.y), self.inner(one, (self.y,), self.x)
        if new == "sent":
            aliases = {1 + len(ins) + i: i for i in range(2)}
            ins += [arrays[0], arrays[2]]
            specs += [pl.BlockSpec(memory_space=pl.ANY)] * 2
            group["keep"] = [arrays[1], arrays[3]]
        if new == "core":
            keep, got = arrays
            rows, wide = keep.shape[0], keep.shape[1] // 2
            ins += [keep, got, keep, got]
            specs += [tall(rows, wide)] * 2 + [tall(rows, wide, steps)] * 2
            heights = [rows // 2, rows // 2]
            outs += [(rows // 2, wide)] * 2
            inners["new"] = self.first_inners(bits, each)
        if one:
            rows = one["keep"][0].shape[0] // 2
            heights = [h + rows for h in heights]
            outs += [(rows, wide)] * 2
        out_specs = [tall(*shape) for shape in outs]
        if new == "sent":
            rows = one["keep"][0].shape[0] // 2
            outs = [arrays[0].shape, arrays[2].shape] + outs
            out_specs = [tall(rows, wide, 0, arrays[0].shape[0] // rows - 1)] * 2 + out_specs
        elif one or new:
            outs = [(h, wide) for h in heights] + outs
            out_specs = [tall(*shape) for shape in outs[:2]] + out_specs
        size = sum(v.size for v in ins)
        ins = [
            v if any(v is g for g in self.got) else in_hbm([v])[0] for v in ins
        ]
        results = list(
            pl.pallas_call(
                functools.partial(round_kernel, (bool(two), bool(one), new, bool(carry)), inners),
                grid_spec=pltpu.PrefetchScalarGridSpec(
                    num_scalar_prefetch=1,
                    grid=(steps,),
                    in_specs=specs,
                    out_specs=out_specs,
                ),
                out_shape=[pltpu.HBM(shape, BF16) for shape in outs],
                input_output_aliases=aliases,
                compiler_params=params(1, 24 << 20),
                cost_estimate=cost(2 * size, 4 * size, scale),
                name="round",
            )(flags, *ins)
        )
        take = lambda n: [results.pop(0) for _ in range(n)]
        buf_x, buf_y = take(2) if one or new else (None, None)
        done = None
        if two:
            done = take(2)
            if not wait:
                piece = Piece(self.places, [b for b in two["bits"] if b not in (self.x, self.y)], two["each"])
                piece.fork(*done, self.z)
                done = piece
        if new == "core":
            group["keep"] = take(2)
        self.two = dict(one, keep=take(2)) if one else None
        self.one = group if new else None
        self.got = []
        if one or new:
            self.send(buf_x, buf_y)
        return done


class Piece:
    def __init__(self, places, bits, each):
        self.places, self.bits, self.each = places, sorted(bits, reverse=True), each
        self.keep = self.got = None
        self.at = 0

    def inner(self, bit):
        return self.each << (len(self.bits) - 1 - self.bits.index(bit))

    def fork(self, out, stay, bit):
        self.bits.remove(bit)
        self.keep, self.got = stay, self.places.swap(out, bit)
        self.at, self.columns = 0, stay.shape[1]

    def split(self, bit):
        rows, columns = self.keep.shape
        inner = self.inner(bit)
        both = self.keep.reshape(rows // (2 * inner), 2, inner, columns)
        at = self.places.own(bit)
        out = lax.dynamic_index_in_dim(both, 1 - at, 1, False).reshape(rows // 2, columns)
        stay = lax.dynamic_index_in_dim(both, at, 1, False).reshape(rows // 2, columns)
        self.fork(out, stay, bit)

    def add(self, low=True):
        cols = slice(self.at * self.columns, (self.at + 1) * self.columns)
        self.keep = self.keep[:, cols].astype(F32) + self.got[:, cols].astype(F32)
        self.at = 0
        if low:
            self.keep = self.keep.astype(BF16)


def share(places, value, bits, group):
    axes = [bits.index(b) for b in group]

    def part(flip):
        out = value
        for b, axis in zip(group, axes):
            out = lax.dynamic_index_in_dim(out, places.own(b) ^ ((flip >> b) & 1), axis, True)
        return lax.squeeze(out, axes)

    flips = [sum(b << g for b, g in zip(f, group)) for f in np.ndindex(*(2,) * len(group))]
    return [part(0)] + [places.send(part(f), f) for f in flips if f]


def hold(small, *arrays):
    small, *arrays = lax.optimization_barrier((small, *arrays))
    return (small, *arrays)


def meet(small, arrays=(), pieces=(), rounds=None):
    many = list(arrays), [p.got for p in pieces], list(rounds.got) if rounds else []
    small, (arrays, gots, round_gots) = lax.optimization_barrier((small, many))
    for p, g in zip(pieces, gots):
        p.got = g
    if rounds:
        rounds.got = round_gots
    return (small, *arrays)


def on_device(
    frames, clip_ids, norm_gain, w_query, w_key, w_value, w_output, attn_scale,
    mlp_gain, w_gate, w_up, w_down, mlp_scale, out_grad,
):
    places = Places()
    seqs, length, width = frames.shape
    total_len = clip_ids.shape[1]
    rows = seqs * length
    n_sp, n_seq = places.n_sp, places.n_seq
    devices = n_sp * n_seq
    feed_width = w_gate.shape[1]
    own_rows = width // devices
    feed_rows = feed_width // devices
    block = feed_rows * n_sp
    core = lax.axis_index("seq") & 1
    sp = lax.axis_index("sp")
    sp_bits = list(reversed(range(places.core)))
    seq_bits = list(range(places.core + 1, places.count))
    x_bit, y_bit, z_bit = sp_bits[0], seq_bits[0], seq_bits[1]
    late = seq_bits[2:] + sp_bits[1:]
    every = list(range(places.count))
    not_core = [b for b in every if b != places.core]
    flags = jnp.stack([places.own(b) for b in (places.core, x_bit, y_bit, z_bit)]).astype(jnp.int32)
    rounds = Rounds(places, x_bit, y_bit, z_bit)

    x = frames.reshape(rows, width)
    grad_y = out_grad.reshape(rows, width)

    def neighbours(last, first):
        if n_sp == 2:
            got = lax.ppermute(jnp.where(sp == 0, last, first), "sp", [(0, 1), (1, 0)])
            return got, got
        return (
            lax.ppermute(last, "sp", [(i, i + 1) for i in range(n_sp - 1)]),
            lax.ppermute(first, "sp", [(i + 1, i) for i in range(n_sp - 1)]),
        )

    has = jnp.stack([sp > 0, sp < n_sp - 1]).astype(jnp.int32)
    from_left, from_right = neighbours(frames[:, length - HALF :], frames[:, :HALF])
    grad_y_peer = places.swap(grad_y, places.core)

    start = sp * length
    near = lax.dynamic_slice_in_dim(
        jnp.pad(clip_ids, ((0, 0), (HALF, HALF))), start, length + 2 * HALF, 1
    )
    ids = jnp.arange(CLIPS + 1, dtype=jnp.int32)
    begins = jnp.sum((clip_ids[:, None, :] < ids[:, None]).astype(jnp.int32), axis=-1)
    is_id = near[:, None, :] == ids[:CLIPS, None]
    first = jnp.sum(jnp.where(is_id, begins[:, :CLIPS, None], 0), axis=1)
    end = jnp.sum(jnp.where(is_id, begins[:, 1:, None], 0), axis=1)
    frame = lax.broadcasted_iota(jnp.int32, near.shape, 1) + (start - HALF)
    place = (frame - first).astype(F32).reshape(-1, 1)
    mid = slice(HALF, HALF + length)
    low = jnp.maximum(frame - HALF, first)[:, mid] - (start - HALF)
    high = jnp.minimum(frame + HALF, end)[:, mid] - (start - HALF)
    padded = -(-length // QB) * QB
    span = jnp.pad(jnp.stack([low, high], axis=1), ((0, 0), (0, 0), (0, padded - length)))

    gain = norm_gain[None]
    joint, normed, normed_own, cos_tab, sin_tab = project(
        x, from_left.reshape(-1, width), from_right.reshape(-1, width), place, gain,
        w_query, w_key, w_value, seqs,
    )
    mixed, probs = attend(span, joint, seqs)

    attn_out, mlp_in = out_proj(mixed, x, w_output, attn_scale[None], mlp_gain[None])
    flags_now, mlp_in = hold(flags, mlp_in)
    mlp_in_peer = places.swap(mlp_in, places.core)
    grad_low, grad_hidden = hidden_grad(
        flags_now, grad_y, grad_y_peer, mlp_scale[None], w_down, block
    )

    blocks = n_seq // 2
    per = blocks // 2

    def onward(piece):
        piece.add()
        piece.split(late[-1 - piece.left])
        piece.left -= 1

    def started(piece):
        piece.left = len(late) - 1
        return piece

    def finished(piece):
        while piece.left >= 0:
            onward(piece)
        piece.add(False)
        return piece.keep

    inners = rounds.first_inners(every, own_rows)
    *kept, a, b, c, d = feed(
        flags, mlp_in, mlp_in_peer, grad_hidden, w_gate, w_up, block, 0, per, (), inners
    )
    rounds.begin((a, b, c, d), every, own_rows)
    *kept, a, b, c, d = feed(
        flags, mlp_in, mlp_in_peer, grad_hidden, w_gate, w_up, block, per, per, kept, inners, width // 4
    )
    hidden, hidden_peer, grad_gate, grad_up = kept
    hidden_got = places.swap(hidden_peer, places.core)
    flags_now, a = meet(flags, [a], rounds=rounds)
    rounds.run(flags_now, "sent", (a, b, c, d), every, own_rows)

    flags_now, rounds.two["keep"][0] = meet(flags, [rounds.two["keep"][0]])
    *in_peer, in_own = feed_back(flags_now, grad_gate, grad_up, w_gate, w_up, block)
    in_got = [places.swap(v, places.core) for v in in_peer]

    flags_now, in_own = meet(flags, [in_own])
    each = feed_rows // 2
    parts = down(
        flags_now, hidden, hidden_peer, grad_low, each, rounds.first_inners(not_core, each), width // 4
    )

    flags_now, *both = meet(flags, [*in_got, *parts], rounds=rounds)
    in_got, parts = both[:2], both[2:]
    carry = rounds.run(flags_now, "sent", parts, not_core, each, wait=True)

    scale_row, rounds.two["keep"][0], hidden_got = meet(
        attn_scale[None], [rounds.two["keep"][0], hidden_got]
    )
    grad_attn, grad_mixed, grad_middle, join_sums = join(
        x, attn_out, grad_y, in_own, in_got, scale_row, mlp_gain[None], w_output
    )
    flip = ((sp == 0) & (n_sp == 2)).astype(jnp.int32).reshape(1)
    grad_query, grad_kv, grad_near, edge, other_edge = attend_back(
        flip, probs, joint, grad_mixed, cos_tab, sin_tab, seqs
    )
    if n_sp == 2:
        to_right = to_left = lax.ppermute(edge, "sp", [(0, 1), (1, 0)])
    else:
        to_left = lax.ppermute(edge, "sp", [(i + 1, i) for i in range(n_sp - 1)])
        to_right = lax.ppermute(other_edge, "sp", [(i, i + 1) for i in range(n_sp - 1)])
    to_right, to_left = [v.reshape(2, seqs, HALF, width) for v in (to_right, to_left)]

    core_inner = Piece(places, every, own_rows).inner(places.core)

    flags_now, grad_query = meet(flags, [grad_query])
    out, stay = weight_grad(
        flags_now,
        core_inner,
        [(mixed, grad_attn), (normed_own, grad_query), (normed, (grad_near, 0)), (normed, (grad_near, 1))],
        "attention_weights",
        0.02,
    )
    from_core = places.swap(out, places.core)

    flags_now, stay, to_right, to_left = meet(flags, [stay, to_right, to_left], [], rounds)
    first = started(rounds.run(flags_now, carry=carry))
    aside = rounds.set_aside()
    has_now, aside["keep"][0] = meet(has, [aside["keep"][0]])
    grad_kv = add_edges(has_now, grad_kv, to_right, to_left)
    flags_now, grad_kv, from_core = meet(flags, [grad_kv, from_core])
    rounds.run(flags_now, "core", (stay, from_core), not_core, own_rows)

    flags_now, rounds.one["keep"][0], *aside["got"] = meet(
        flags, [rounds.one["keep"][0], *aside["got"]]
    )
    layer_out, out_sums = feed_out(
        flags_now, hidden, hidden_got, w_down, x, attn_out, grad_y,
        attn_scale[None], mlp_scale[None], block,
    )
    flags_now, layer_out, join_sums = meet(flags, [layer_out, join_sums], [first])
    third = started(rounds.run_aside(flags_now, aside))
    onward(first)
    flags_now, first.keep, third.keep = meet(flags, [first.keep, third.keep], [], rounds)
    rounds.run(flags_now)
    gain_now, rounds.two["keep"][0] = meet(gain, [rounds.two["keep"][0]])
    frames_grad, norm_sums = input_grad(
        x, grad_query, grad_kv, grad_middle, gain_now, w_query, w_key, w_value
    )
    flags_now, frames_grad = meet(flags, [frames_grad], [third], rounds)
    fourth = started(rounds.run(flags_now))
    onward(third)
    _, fourth.keep, norm_sums = meet(flags, [fourth.keep, norm_sums])
    norm_sums, join_sums, out_sums = lax.optimization_barrier((norm_sums, join_sums, out_sums))
    vectors = jnp.stack([norm_sums[0], join_sums[0], join_sums[1], out_sums[0]], axis=1)
    vectors = vectors.reshape((2,) * places.count + (own_rows, 4))
    left = list(reversed(every))
    groups = [[b] for b in [places.core, x_bit, y_bit, z_bit] + late]
    shares = share(places, vectors, left, groups[0])
    _, *shares = meet(flags, shares, [first])
    feeds = finished(first).reshape(2, 2, 2, own_rows, width)
    mine = lax.dynamic_index_in_dim(feeds, core, 2, False)
    got = places.swap(lax.dynamic_index_in_dim(feeds, 1 - core, 2, False), places.core)
    for done, group in zip(groups, groups[1:]):
        left = [b for b in left if b not in done]
        shares = share(places, sum(shares), left, group)
        if group is groups[-3]:
            _, *shares = meet(flags, shares, [fourth])
            onward(fourth)
    down_grad = finished(third)
    pair = jnp.stack([jnp.where(core == 0, mine, got), jnp.where(core == 0, got, mine)], axis=0)
    pair = pair.reshape(2, 2, 2, own_rows, per, block)
    pair = pair.transpose(2, 3, 1, 4, 0, 5).reshape(2, own_rows, feed_width)
    while fourth.left >= 0:
        onward(fourth)
    _, gate_grad, up_grad, down_grad, *shares = meet(
        flags, [pair[0], pair[1], down_grad, *shares], [fourth]
    )
    vectors = sum(shares).T
    output_grad, query_grad, key_grad, value_grad = [
        fourth.keep[rows, columns].astype(F32) + fourth.got[rows, columns].astype(F32)
        for rows in (slice(0, own_rows), slice(own_rows, 2 * own_rows))
        for columns in (slice(0, width), slice(width, 2 * width))
    ]
    return (
        layer_out.reshape(frames.shape),
        frames_grad.reshape(frames.shape),
        vectors[0],
        query_grad,
        key_grad,
        value_grad,
        output_grad,
        vectors[1],
        vectors[2],
        gate_grad,
        up_grad,
        down_grad,
        vectors[3],
    )


def solution(mesh):
    split = P("seq", "sp", None)
    rows = P(("seq", "sp"), None)
    vec = P(("seq", "sp"))
    return jax.shard_map(
        on_device,
        mesh=mesh,
        in_specs=(split, P("seq", None)) + (P(),) * 11 + (split,),
        out_specs=(
            split, split, vec, rows, rows, rows, rows, vec, vec, rows, rows, rows, vec,
        ),
        check_vma=False,
    )
```

```python
import functools
import math

import jax
import jax.numpy as jnp
import numpy as np
from jax import lax
from jax.experimental import pallas as pl
from jax.experimental.pallas import tpu as pltpu
from jax.sharding import PartitionSpec as P

HEAD_DIM = 64
HALF = 64
LANES = 128
GROUP = 256
GH = GROUP // HEAD_DIM
QB = 128
KB = QB + 2 * HALF
CLIPS = 8
LN_EPS = 1e-05
RMS_EPS = 1e-06
VMEM = 58 << 20
F32 = jnp.float32
BF16 = jnp.bfloat16

NT = (((1,), (1,)), ((), ()))
NN = (((1,), (0,)), ((), ()))
TN = (((0,), (0,)), ((), ()))


def dot(a, b, dims=NN):
    return lax.dot_general(a, b, dims, preferred_element_type=F32)


def params(grid=0, vmem=VMEM):
    kinds = ("arbitrary",) * grid if grid else None
    return pltpu.CompilerParams(vmem_limit_bytes=vmem, dimension_semantics=kinds)


def cost(flops, moved, scale=0.02):
    return pl.CostEstimate(
        flops=int(flops * scale), bytes_accessed=int(moved * scale), transcendentals=0
    )


def in_hbm(values):
    return [pltpu.with_memory_space_constraint(v, pltpu.HBM) for v in values]


def whole(shape):
    return pl.BlockSpec(shape, lambda *_: (0,) * len(shape))


def swap_halves(v):
    lane = lax.broadcasted_iota(jnp.int32, v.shape, 1)
    return jnp.where(lane % HEAD_DIM < HEAD_DIM // 2, pltpu.roll(v, 96, 1), pltpu.roll(v, 32, 1))


def rotated(v, cos_tab, sin_tab, sign):
    pieces = []
    for at in range(0, v.shape[1], LANES):
        part = v[:, at : at + LANES]
        turned = swap_halves(part) * sin_tab
        pieces.append(part * cos_tab + turned if sign > 0 else part * cos_tab - turned)
    return jnp.concatenate(pieces, axis=1)


def project_kernel(
    seqs, x_ref, left_ref, right_ref, place_ref, gain_ref, wv_ref, wk_ref, wq_ref,
    out_ref, normed_ref, own_ref, cos_ref, sin_ref, low, weights, sems,
):
    step = pl.program_id(0)
    rows, width = low.shape
    padded = rows // seqs
    length = padded - 2 * HALF
    fetches = [
        pltpu.make_async_copy(src, weights.at[i], sems.at[i]) for i, src in enumerate((wv_ref, wk_ref, wq_ref))
    ]
    keeps = [pltpu.make_async_copy(low, normed_ref, sems.at[3])] + [
        pltpu.make_async_copy(
            low.at[s * padded + HALF : s * padded + HALF + length, :],
            own_ref.at[s * length : (s + 1) * length, :],
            sems.at[4 + s],
        )
        for s in range(seqs)
    ]

    def products(which, after):
        blocks = [slice(at, at + GROUP) for at in range(0, width, GROUP)]
        ahead = dot(low[...], weights[which, :, blocks[0]])
        for i, columns in enumerate(blocks):
            out = ahead
            if i + 1 < len(blocks):
                ahead = dot(low[...], weights[which, :, blocks[i + 1]])
            out_ref[0, :, columns] = after(out).astype(BF16)

    @pl.when(step == 0)
    def _():
        for copy in fetches:
            copy.start()
        for src, first, step in ((x_ref, HALF, length), (left_ref, 0, HALF), (right_ref, HALF + length, HALF)):
            x = src[...].astype(F32)
            centered = x - jnp.mean(x, axis=-1, keepdims=True)
            inv = lax.rsqrt(jnp.mean(centered * centered, axis=-1, keepdims=True) + LN_EPS)
            normed = (centered * inv * gain_ref[...]).astype(BF16)
            for s in range(seqs):
                at = s * padded + first
                low[at : at + step, :] = normed[s * step : (s + 1) * step]
        for copy in keeps:
            copy.start()
        fetches[0].wait()
        products(0, lambda out: out)
        lane = lax.broadcasted_iota(jnp.int32, (1, LANES), 1)
        exponent = (lane % (HEAD_DIM // 2)).astype(F32) * (2.0 / HEAD_DIM)
        angles = place_ref[...] * jnp.exp(-math.log(10000.0) * exponent)
        cos_ref[...] = jnp.cos(angles)
        sin_ref[...] = jnp.where(lane % HEAD_DIM < HEAD_DIM // 2, -1.0, 1.0) * jnp.sin(angles)

    @pl.when(step == 1)
    def _():
        fetches[1].wait()
        products(1, lambda out: rotated(out, cos_ref[...], sin_ref[...], 1))

    @pl.when(step == 2)
    def _():
        fetches[2].wait()
        scale = 1.0 / math.sqrt(HEAD_DIM)
        products(2, lambda out: rotated(out, cos_ref[...], sin_ref[...], 1) * scale)
        for copy in keeps:
            copy.wait()


def project(x, left, right, place, gain, w_query, w_key, w_value, seqs):
    own, width = x.shape
    rows = own + seqs * 2 * HALF
    edge = whole((seqs * HALF, width))
    hbm = pl.BlockSpec(memory_space=pl.ANY)
    table = jax.ShapeDtypeStruct((rows, LANES), F32)
    return pl.pallas_call(
        functools.partial(project_kernel, seqs),
        grid=(3,),
        in_specs=[whole((own, width)), edge, edge, whole((rows, 1)), whole((1, width))] + [hbm] * 3,
        out_specs=[
            pl.BlockSpec((1, rows, width), lambda j: (j, 0, 0)),
            hbm,
            hbm,
            whole((rows, LANES)),
            whole((rows, LANES)),
        ],
        out_shape=[
            jax.ShapeDtypeStruct((3, rows, width), BF16),
            jax.ShapeDtypeStruct((rows, width), BF16),
            jax.ShapeDtypeStruct((own, width), BF16),
            table,
            table,
        ],
        scratch_shapes=[
            pltpu.VMEM((rows, width), BF16),
            pltpu.VMEM((3, width, width), BF16),
            pltpu.SemaphoreType.DMA((4 + seqs,)),
        ],
        compiler_params=params(1),
        cost_estimate=cost(6 * rows * width * width, 6 * width * width + 10 * rows * width),
        name="project",
    )(x, left, right, place, gain, w_value, w_key, w_query)


def stack_heads(block):
    lane = lax.broadcasted_iota(jnp.int32, block.shape, 1)
    zero = jnp.zeros_like(block)
    return jnp.concatenate(
        [jnp.where(lane // HEAD_DIM == h, block, zero) for h in range(GH)], axis=0
    )


def fill_keys(buf, ref):
    rows = ref.shape[1]
    buf[0:rows, :] = ref[0]
    if buf.shape[0] > rows:
        buf[rows:, :] = jnp.zeros((buf.shape[0] - rows, buf.shape[1]), buf.dtype)


def fill_queries(buf, ref, length):
    buf[0:length, :] = ref[0, HALF : HALF + length, :] if ref.ndim == 3 else ref[...]
    rest = buf.shape[0] - length
    if rest:
        buf[length:, :] = jnp.zeros((rest, buf.shape[1]), buf.dtype)


def attend_kernel(span_ref, q_ref, k_ref, v_ref, o_ref, p_ref, kbuf, vbuf, qbuf, vt, ot):
    length = o_ref.shape[0]
    padded = qbuf.shape[0]
    fill_keys(kbuf, k_ref)
    fill_keys(vbuf, v_ref)
    fill_queries(qbuf, q_ref, length)
    blocks = padded // QB

    def scores_of(b):
        return dot(kbuf[b * QB : b * QB + KB, :], stack_heads(qbuf[b * QB : (b + 1) * QB, :]), NT)

    def mix(b, probs):
        for h in range(GH):
            rows = slice(h * HEAD_DIM, (h + 1) * HEAD_DIM)
            ot[rows, b * QB : (b + 1) * QB] = dot(vt[rows, b * QB : b * QB + KB], probs[h]).astype(BF16)

    ahead = scores_of(0)
    vt[...] = vbuf[...].T
    before = None
    for b in range(blocks):
        scores = ahead
        if b + 1 < blocks:
            ahead = scores_of(b + 1)
        if before is not None:
            mix(b - 1, before)
        place = lax.broadcasted_iota(jnp.int32, (KB, QB), 0) + b * QB
        low = span_ref[0, 0:1, b * QB : (b + 1) * QB]
        high = span_ref[0, 1:2, b * QB : (b + 1) * QB]
        seen = (place >= low) & (place < high)
        before = []
        for h in range(GH):
            masked = jnp.where(seen, scores[:, h * QB : (h + 1) * QB], -1e30)
            terms = jnp.exp(masked - jnp.max(masked, axis=0, keepdims=True))
            total = jnp.sum(terms, axis=0, keepdims=True)
            probs = (terms * (1.0 / total)).astype(BF16)
            p_ref[:, b * GH * QB + h * QB : b * GH * QB + (h + 1) * QB] = probs
            before.append(probs)
    mix(blocks - 1, before)
    o_ref[...] = ot[...].T[0:length, :]


def attend(span, joint, seqs):
    _, rows, width = joint.shape
    length = rows // seqs - 2 * HALF
    rows = seqs * length
    padded = span.shape[2]
    groups = width // GROUP
    keys = padded + 2 * HALF
    own = pl.BlockSpec((length, GROUP), lambda s, g: (s, g))
    near = [pl.BlockSpec((1, length + 2 * HALF, GROUP), lambda s, g, i=i: (i, s, g)) for i in range(3)]
    return pl.pallas_call(
        attend_kernel,
        grid=(seqs, groups),
        in_specs=[
            pl.BlockSpec((1, 2, padded), lambda s, g: (s, 0, 0)),
            near[2],
            near[1],
            near[0],
        ],
        out_specs=[
            own,
            pl.BlockSpec((KB, GH * padded), lambda s, g: (s, g)),
        ],
        out_shape=[
            jax.ShapeDtypeStruct((rows, width), BF16),
            jax.ShapeDtypeStruct((seqs * KB, groups * GH * padded), BF16),
        ],
        scratch_shapes=[
            pltpu.VMEM((keys, GROUP), BF16),
            pltpu.VMEM((keys, GROUP), BF16),
            pltpu.VMEM((padded, GROUP), BF16),
            pltpu.VMEM((GROUP, keys), BF16),
            pltpu.VMEM((GROUP, padded), BF16),
        ],
        compiler_params=params(2),
        cost_estimate=cost(
            2 * 2 * seqs * width * padded * KB * 4, 2 * width * (4 * rows + KB * seqs * padded // 64)
        ),
        name="attend",
    )(span, joint, joint, joint)


def attend_back_kernel(
    flip_ref, p_ref, q_ref, k_ref, v_ref, g_ref, cos_ref, sin_ref,
    dq_ref, dkv_ref, near_ref, edge_ref, other_ref,
    kbuf, vbuf, qbuf, gbuf, kt, dqt, dkb, dvb,
):
    length = g_ref.shape[0]
    padded = qbuf.shape[0]
    fill_keys(kbuf, k_ref)
    fill_keys(vbuf, v_ref)
    fill_queries(qbuf, q_ref, length)
    fill_queries(gbuf, g_ref, length)
    blocks = padded // QB

    def probs_grads(b):
        g4 = stack_heads(gbuf[b * QB : (b + 1) * QB, :])
        return g4, dot(vbuf[b * QB : b * QB + KB, :], g4, NT)

    def spread(b, g4, probs, lows):
        at, keys = slice(b * QB, (b + 1) * QB), slice(b * QB, b * QB + KB)
        for h in range(GH):
            rows = slice(h * HEAD_DIM, (h + 1) * HEAD_DIM)
            dqt[rows, at] = dot(kt[rows, keys], lows[h])
        q4 = stack_heads(qbuf[at, :])
        grads = (dkb, dot(jnp.concatenate(lows, axis=1), q4)), (dvb, dot(probs, g4))
        for buf, grad in grads:
            if b:
                buf[at, :] += grad[:QB]
            else:
                buf[at, :] = grad[:QB]
            buf[(b + 1) * QB : b * QB + KB, :] = grad[QB:]

    ahead = probs_grads(0)
    kt[...] = kbuf[...].T
    before = None
    for b in range(blocks):
        g4, grads = ahead
        if b + 1 < blocks:
            ahead = probs_grads(b + 1)
        if before is not None:
            spread(b - 1, *before)
        probs = p_ref[:, b * GH * QB : (b + 1) * GH * QB]
        lows = []
        for h in range(GH):
            part = probs[:, h * QB : (h + 1) * QB].astype(F32)
            grad = grads[:, h * QB : (h + 1) * QB]
            delta = jnp.sum(part * grad, axis=0, keepdims=True)
            lows.append((part * (grad - delta)).astype(BF16))
        before = g4, probs, lows
    spread(blocks - 1, *before)
    cos_tab, sin_tab = cos_ref[...], sin_ref[...]
    middle = slice(HALF, HALF + length)
    dq = dqt[...].T[0:length, :] * (1.0 / math.sqrt(HEAD_DIM))
    dq_ref[...] = rotated(dq, cos_tab[middle], sin_tab[middle], -1).astype(BF16)
    span = length + 2 * HALF
    dk = rotated(dkb[0:span, :], cos_tab, sin_tab, -1).astype(BF16)
    dv = dvb[0:span, :].astype(BF16)
    for i, grad in enumerate((dk, dv)):
        dkv_ref[i] = grad[middle]
        near_ref[i] = grad
        ends = grad[0:HALF], grad[span - HALF :]
        edge_ref[i] = jnp.where(flip_ref[0] == 1, ends[1], ends[0])
        other_ref[i] = jnp.where(flip_ref[0] == 1, ends[0], ends[1])


def attend_back(flip, probs, joint, grad, cos_tab, sin_tab, seqs):
    rows, width = grad.shape
    length = rows // seqs
    padded = -(-length // QB) * QB
    groups = width // GROUP
    keys = padded + 2 * HALF
    own = pl.BlockSpec((length, GROUP), lambda s, g, f: (s, g))
    both = pl.BlockSpec((2, length, GROUP), lambda s, g, f: (0, s, g))
    both_near = pl.BlockSpec((2, length + 2 * HALF, GROUP), lambda s, g, f: (0, s, g))
    near = [pl.BlockSpec((1, length + 2 * HALF, GROUP), lambda s, g, f, i=i: (i, s, g)) for i in range(3)]
    table = pl.BlockSpec((length + 2 * HALF, LANES), lambda s, g, f: (s, 0))
    edge = pl.BlockSpec((2, HALF, GROUP), lambda s, g, f: (0, s, g))
    out_edge = jax.ShapeDtypeStruct((2, seqs * HALF, width), BF16)
    out = jax.ShapeDtypeStruct((rows, width), BF16)
    out_both = jax.ShapeDtypeStruct((2, rows, width), BF16)
    out_near = jax.ShapeDtypeStruct((2, rows + seqs * 2 * HALF, width), BF16)
    return pl.pallas_call(
        attend_back_kernel,
        grid_spec=pltpu.PrefetchScalarGridSpec(
            num_scalar_prefetch=1,
            grid=(seqs, groups),
        in_specs=[
            pl.BlockSpec((KB, GH * padded), lambda s, g, f: (s, g)),
            near[2],
            near[1],
            near[0],
            own,
            table,
            table,
        ],
        out_specs=[own, both, both_near, edge, edge],
        scratch_shapes=[
            pltpu.VMEM((keys, GROUP), BF16),
            pltpu.VMEM((keys, GROUP), BF16),
            pltpu.VMEM((padded, GROUP), BF16),
            pltpu.VMEM((padded, GROUP), BF16),
            pltpu.VMEM((GROUP, keys), BF16),
            pltpu.VMEM((GROUP, padded), F32),
            pltpu.VMEM((keys, GROUP), F32),
            pltpu.VMEM((keys, GROUP), F32),
        ],
        ),
        out_shape=[out, out_both, out_near, out_edge, out_edge],
        compiler_params=params(2),
        cost_estimate=cost(
            2 * 4 * seqs * width * padded * KB * 4, 2 * width * (8 * rows + KB * seqs * padded // 64)
        ),
        name="attend_back",
    )(flip, probs, joint, joint, joint, grad, cos_tab, sin_tab)


def edges_kernel(seqs, flags_ref, from_ref, left_ref, right_ref, to_ref, buf, sems):
    length = from_ref.shape[1] // seqs
    places = [
        (i, s, e, pl.ds(s * length + e * (length - HALF), HALF))
        for i in range(2)
        for s in range(seqs)
        for e in range(2)
    ]
    copies = [
        (from_ref.at[i, rows, :], to_ref.at[i, rows, :], buf.at[at]) for at, (i, _, _, rows) in enumerate(places)
    ]
    for at, (src, _, mid) in enumerate(copies):
        pltpu.make_async_copy(src, mid, sems.at[0, at]).start()
    for at, (src, _, mid) in enumerate(copies):
        pltpu.make_async_copy(src, mid, sems.at[0, at]).wait()
    for at, (i, s, e, _) in enumerate(places):
        got = (right_ref if e else left_ref)[i, s].astype(F32) * flags_ref[e].astype(F32)
        buf[at] = (buf[at].astype(F32) + got).astype(BF16)
    for at, (_, dst, mid) in enumerate(copies):
        pltpu.make_async_copy(mid, dst, sems.at[1, at]).start()
    for at, (_, dst, mid) in enumerate(copies):
        pltpu.make_async_copy(mid, dst, sems.at[1, at]).wait()


def add_edges(flags, grads, left, right):
    seqs = left.shape[1]
    hbm = pl.BlockSpec(memory_space=pl.ANY)
    return pl.pallas_call(
        functools.partial(edges_kernel, seqs),
        grid_spec=pltpu.PrefetchScalarGridSpec(
            num_scalar_prefetch=1,
            grid=(1,),
            in_specs=[hbm, whole(left.shape), whole(right.shape)],
            out_specs=hbm,
            scratch_shapes=[
                pltpu.VMEM((4 * seqs, HALF, grads.shape[2]), BF16),
                pltpu.SemaphoreType.DMA((2, 4 * seqs)),
            ],
        ),
        out_shape=jax.ShapeDtypeStruct(grads.shape, BF16),
        input_output_aliases={1: 0},
        compiler_params=params(1),
        cost_estimate=cost(1e4 * left.size, 8 * left.size, 1000),
        name="add_edges",
    )(flags, grads, left, right)


def out_proj_kernel(m_ref, x_ref, w_ref, scale_ref, gain_ref, attn_ref, in_ref):
    attn = dot(m_ref[...], w_ref[...])
    attn_ref[...] = attn.astype(BF16)
    middle = x_ref[...].astype(F32) + scale_ref[...] * attn
    inv = lax.rsqrt(jnp.mean(middle * middle, axis=-1, keepdims=True) + RMS_EPS)
    in_ref[...] = (middle * inv * gain_ref[...]).astype(BF16)


def out_proj(mixed, x, w_output, scale, gain):
    rows, width = x.shape
    block = rows // 2
    row = pl.BlockSpec((block, width), lambda i: (i, 0))
    return pl.pallas_call(
        out_proj_kernel,
        grid=(rows // block,),
        in_specs=[row, row, whole((width, width)), whole((1, width)), whole((1, width))],
        out_specs=[row, row],
        out_shape=[
            jax.ShapeDtypeStruct((rows, width), BF16),
            jax.ShapeDtypeStruct((rows, width), BF16),
        ],
        compiler_params=params(1),
        cost_estimate=cost(2 * rows * width * width, 2 * rows * width * 5 + 2 * width * width),
        name="out_proj",
    )(mixed, x, w_output, scale, gain)


def hidden_grad_kernel(core_ref, own_ref, peer_ref, scale_ref, one_ref, two_ref, low_ref, out_ref):
    rows = own_ref.shape[0]
    block = one_ref.shape[0]

    @pl.when(pl.program_id(0) == 0)
    def _():
        low_ref[0:rows, :] = (own_ref[...].astype(F32) * scale_ref[...]).astype(BF16)
        low_ref[rows:, :] = (peer_ref[...].astype(F32) * scale_ref[...]).astype(BF16)

    out_ref[:, :block] = dot(low_ref[...], one_ref[...], NT).astype(BF16)
    out_ref[:, block:] = dot(low_ref[...], two_ref[...], NT).astype(BF16)


def hidden_grad(core, own, peer, scale, w_down, block):
    rows, width = own.shape
    count = w_down.shape[0] // block // 4
    half = w_down.shape[0] // 2
    return pl.pallas_call(
        hidden_grad_kernel,
        grid_spec=pltpu.PrefetchScalarGridSpec(
            num_scalar_prefetch=1,
            grid=(count,),
            in_specs=[
                whole((rows, width)),
                whole((rows, width)),
                whole((1, width)),
                pl.BlockSpec((block, width), lambda j, c: (4 * j + c[0], 0)),
                pl.BlockSpec((block, width), lambda j, c: (4 * j + 2 + c[0], 0)),
            ],
            out_specs=[
                whole((2 * rows, width)),
                pl.BlockSpec((2 * rows, 2 * block), lambda j, c: (0, j)),
            ],
        ),
        out_shape=[
            jax.ShapeDtypeStruct((2 * rows, width), BF16),
            jax.ShapeDtypeStruct((2 * rows, half), BF16),
        ],
        compiler_params=params(1),
        cost_estimate=cost(
            4 * rows * width * half, 2 * (4 * rows * width + half * (width + 2 * rows))
        ),
        name="hidden_grad",
    )(core, own, peer, scale, w_down, w_down)


def halves_of(value, bit, inner):
    rows, columns = value.shape
    both = value.reshape(rows // (2 * inner), 2, inner, columns)
    zero, one = both[:, 0], both[:, 1]
    out = jnp.where(bit == 0, one, zero).reshape(rows // 2, columns)
    stay = jnp.where(bit == 0, zero, one).reshape(rows // 2, columns)
    return out, stay


def feed_kernel(inners, core_ref, xo_ref, xp_ref, gh_ref, wg_ref, wu_ref, *refs):
    hid_own_ref, hid_peer_ref, gg_ref, gu_ref, *outs, x_all = refs[-9:]
    rows = xo_ref.shape[0]

    @pl.when(pl.program_id(0) == 0)
    def _():
        x_all[0:rows, :] = xo_ref[...]
        x_all[rows:, :] = xp_ref[...]

    for at in (0, rows):
        part = slice(at, at + rows)
        gate = dot(x_all[part, :], wg_ref[...])
        up = dot(x_all[part, :], wu_ref[...])
        grad = gh_ref[part, :].astype(F32)
        sig = 1.0 / (1.0 + jnp.exp(-gate))
        act = gate * sig
        (hid_peer_ref if at else hid_own_ref)[...] = (act * up).astype(BF16)
        gg_ref[part, :] = (grad * up * sig * (1.0 + gate * (1.0 - sig))).astype(BF16)
        gu_ref[part, :] = (grad * act).astype(BF16)
    for i, src in enumerate((gg_ref, gu_ref)):
        out, stay = halves_of(dot(x_all[...], src[...], TN), core_ref[1 + i], inners[i])
        outs[2 * i][...] = out.astype(BF16)
        outs[2 * i + 1][...] = stay.astype(BF16)


def feed(core, x_own, x_peer, grad_hidden, w_gate, w_up, block, first, count, before, inners, room=0):
    rows, width = x_own.shape
    half = grad_hidden.shape[1]
    wide = pl.BlockSpec((2 * rows, block), lambda j, c: (0, j + first))
    weight = pl.BlockSpec((width, block), lambda j, c: (0, 2 * (j + first) + c[0]))
    tall = pl.BlockSpec((rows, block), lambda j, c: (0, j + first))
    kept = pltpu.HBM((2 * rows, half), BF16)
    single = pltpu.HBM((rows, half), BF16)
    grads = [pltpu.HBM((width // 2 + more, count * block), BF16) for more in (room, 0, room, 0)]
    any_spec = pl.BlockSpec(memory_space=pl.ANY)
    return pl.pallas_call(
        functools.partial(feed_kernel, inners),
        grid_spec=pltpu.PrefetchScalarGridSpec(
            num_scalar_prefetch=1,
            grid=(count,),
            in_specs=[whole((rows, width)), whole((rows, width)), wide, weight, weight]
            + [any_spec] * len(before),
            out_specs=[tall] * 2
            + [wide] * 2
            + [pl.BlockSpec((width // 2, block), lambda j, c: (0, j))] * 4,
            scratch_shapes=[pltpu.VMEM((2 * rows, width), BF16)],
        ),
        out_shape=[single] * 2 + [kept] * 2 + grads,
        input_output_aliases={6 + i: i for i in range(len(before))},
        compiler_params=params(1, 46 << 20),
        cost_estimate=cost(
            2 * 2 * rows * width * block * count * 4,
            2 * (4 * rows * width + count * block * (8 * rows + 4 * width)),
        ),
        name="feed",
    )(core, *in_hbm([x_own]), x_peer, *in_hbm([grad_hidden, w_gate, w_up, *before]))


def down_kernel(each, inners, bits_ref, own_ref, peer_ref, low_ref, *refs):
    *outs, both = refs
    both[: own_ref.shape[0], :] = own_ref[...]
    both[own_ref.shape[0] :, :] = peer_ref[...]
    value = dot(both[...], low_ref[...], TN)
    rows, width = value.shape
    value = value.reshape(rows // (2 * each), 2, each, width)
    for i in range(2):
        part = value[:, i].reshape(rows // 2, width)
        out, stay = halves_of(part, bits_ref[1 + i], inners[i])
        outs[2 * i][...] = out.astype(BF16)
        outs[2 * i + 1][...] = stay.astype(BF16)


def down(bits, own, peer, low, each, inners, room):
    rows, half = own.shape
    width = low.shape[1]
    block = 512
    return pl.pallas_call(
        functools.partial(down_kernel, each, inners),
        grid_spec=pltpu.PrefetchScalarGridSpec(
            num_scalar_prefetch=1,
            grid=(half // block,),
            in_specs=[
                pl.BlockSpec((rows, block), lambda j, c: (0, j)),
                pl.BlockSpec((rows, block), lambda j, c: (0, j)),
                whole((2 * rows, width)),
            ],
            out_specs=[pl.BlockSpec((block // 4, width), lambda j, c: (j, 0))] * 4,
            scratch_shapes=[pltpu.VMEM((2 * rows, block), BF16)],
        ),
        out_shape=[jax.ShapeDtypeStruct((half // 4 + more, width), BF16) for more in (room, 0, room, 0)],
        compiler_params=params(1),
        cost_estimate=cost(
            4 * rows * half * width, 2 * (2 * rows * half + 2 * rows * width + half * width)
        ),
        name="down_weight",
    )(bits, own, peer, low)


def in_halves(value, refs):
    half = value.shape[1] // 2
    refs[0][...] = value[:, :half]
    refs[1][...] = value[:, half:]


def feed_back_kernel(core_ref, *refs):
    *peer_refs, own_ref, acc = refs[-4:]
    part, step = pl.program_id(0), pl.program_id(1)
    block = refs[2].shape[1]
    total = None
    for i in range(2):
        for half in range(2):
            out = dot(refs[i][:, half * block : (half + 1) * block], refs[2 + 2 * i + half][...], NT)
            total = out if total is None else total + out
    last = pl.num_programs(1) - 1

    @pl.when(step == 0)
    def _():
        acc[...] = total

    @pl.when((step > 0) & (step < last))
    def _():
        acc[...] += total

    @pl.when((step == last) & (part == 0))
    def _():
        in_halves((acc[...] + total).astype(BF16), peer_refs)

    @pl.when((step == last) & (part == 1))
    def _():
        own_ref[...] = (acc[...] + total).astype(BF16)


def feed_back(core, grad_gate, grad_up, w_gate, w_up, block):
    rows, half = grad_gate.shape
    rows = rows // 2
    width = w_gate.shape[0]
    tall = pl.BlockSpec((rows, 2 * block), lambda p, j, c: (1 - p, j))
    one = pl.BlockSpec((width, block), lambda p, j, c: (0, 4 * j + c[0]))
    two = pl.BlockSpec((width, block), lambda p, j, c: (0, 4 * j + 2 + c[0]))
    return pl.pallas_call(
        feed_back_kernel,
        grid_spec=pltpu.PrefetchScalarGridSpec(
            num_scalar_prefetch=1,
            grid=(2, half // block // 2),
            in_specs=[tall, tall, one, two, one, two],
            out_specs=[whole((rows, width // 2))] * 2 + [whole((rows, width))],
            scratch_shapes=[pltpu.VMEM((rows, width), F32)],
        ),
        out_shape=[jax.ShapeDtypeStruct((rows, width // 2), BF16)] * 2
        + [jax.ShapeDtypeStruct((rows, width), BF16)],
        compiler_params=params(2),
        cost_estimate=cost(8 * rows * half * width, 8 * (rows * half + half * width)),
        name="feed_back",
    )(core, grad_gate, grad_up, w_gate, w_gate, w_up, w_up)


def join_kernel(
    x_ref, attn_ref, g_ref, in_ref, got_one_ref, got_two_ref, attn_scale_ref, gain_ref, w_ref,
    grad_attn_ref, grad_mixed_ref, middle_ref, sums_ref,
):
    x = x_ref[...].astype(F32)
    attn = attn_ref[...].astype(F32)
    grad_y = g_ref[...].astype(F32)
    got = jnp.concatenate([got_one_ref[...], got_two_ref[...]], axis=1)
    grad_in = in_ref[...].astype(F32) + got.astype(F32)
    middle = x + attn_scale_ref[...] * attn
    inv = lax.rsqrt(jnp.mean(middle * middle, axis=-1, keepdims=True) + RMS_EPS)
    unit = middle * inv
    scaled = grad_in * gain_ref[...]
    grad_middle = grad_y + inv * (scaled - unit * jnp.mean(scaled * unit, axis=-1, keepdims=True))
    middle_ref[...] = grad_middle.astype(BF16)
    grad_attn = (attn_scale_ref[...] * grad_middle).astype(BF16)
    grad_attn_ref[...] = grad_attn
    grad_mixed_ref[...] = dot(grad_attn, w_ref[...], NT).astype(BF16)

    @pl.when(pl.program_id(0) == 0)
    def _():
        sums_ref[...] = jnp.zeros_like(sums_ref)

    sums_ref[0:1, :] += jnp.sum(grad_middle * attn, axis=0, keepdims=True)
    sums_ref[1:2, :] += jnp.sum(grad_in * unit, axis=0, keepdims=True)


def join(x, attn, grad_y, grad_in, got, attn_scale, gain, w_output):
    rows, width = x.shape
    block = rows // 2
    row = pl.BlockSpec((block, width), lambda i: (i, 0))
    half = pl.BlockSpec((block, width // 2), lambda i: (i, 0))
    vec = whole((1, width))
    low = jax.ShapeDtypeStruct((rows, width), BF16)
    return pl.pallas_call(
        join_kernel,
        grid=(rows // block,),
        in_specs=[row] * 4 + [half] * 2 + [vec] * 2 + [whole((width, width))],
        out_specs=[row] * 3 + [whole((8, width))],
        out_shape=[
            low,
            low,
            low,
            jax.ShapeDtypeStruct((8, width), F32),
        ],
        compiler_params=params(1),
        cost_estimate=cost(2 * rows * width * width, rows * width * 22 + 2 * width * width),
        name="join",
    )(x, attn, grad_y, grad_in, *got, attn_scale, gain, w_output)


def feed_out_kernel(
    core_ref, own_ref, got_ref, w_ref, x_ref, attn_ref, g_ref, attn_scale_ref, mlp_scale_ref,
    layer_ref, sums_ref, hidden, acc,
):
    step, last = pl.program_id(0), pl.num_programs(0) - 1
    block = own_ref.shape[1] // 2
    for i in range(2):
        part = slice(i * block, (i + 1) * block)
        own, got = own_ref[:, part], got_ref[:, part]
        first = core_ref[0] == 0
        hidden[:, 2 * i * block : (2 * i + 1) * block] = jnp.where(first, own, got)
        hidden[:, (2 * i + 1) * block : (2 * i + 2) * block] = jnp.where(first, got, own)
    total = dot(hidden[...], w_ref[...])

    @pl.when(step == 0)
    def _():
        acc[...] = total

    @pl.when((step > 0) & (step < last))
    def _():
        acc[...] += total

    @pl.when(step == last)
    def _():
        down_out = acc[...] + total
        middle = x_ref[...].astype(F32) + attn_scale_ref[...] * attn_ref[...].astype(F32)
        layer_ref[...] = (middle + mlp_scale_ref[...] * down_out).astype(BF16)
        sums_ref[...] = jnp.zeros_like(sums_ref)
        sums_ref[0:1, :] = jnp.sum(g_ref[...].astype(F32) * down_out, axis=0, keepdims=True)


def feed_out(core, own, got, w_down, x, attn, grad_y, attn_scale, mlp_scale, block):
    rows, half = own.shape
    width = w_down.shape[1]
    tall = pl.BlockSpec((rows, 2 * block), lambda j, c: (0, j))
    row, vec = whole((rows, width)), whole((1, width))
    return pl.pallas_call(
        feed_out_kernel,
        grid_spec=pltpu.PrefetchScalarGridSpec(
            num_scalar_prefetch=1,
            grid=(half // block // 2,),
            in_specs=[tall, tall, pl.BlockSpec((4 * block, width), lambda j, c: (j, 0))]
            + [row] * 3
            + [vec] * 2,
            out_specs=[row, whole((8, width))],
            scratch_shapes=[pltpu.VMEM((rows, 4 * block), BF16), pltpu.VMEM((rows, width), F32)],
        ),
        out_shape=[
            jax.ShapeDtypeStruct((rows, width), BF16),
            jax.ShapeDtypeStruct((8, width), F32),
        ],
        compiler_params=params(1),
        cost_estimate=cost(4 * rows * half * width, 4 * (rows * half + half * width), 10),
        name="feed_out",
    )(core, own, got, w_down, x, attn, grad_y, attn_scale, mlp_scale)


def weight_grad_kernel(inner, order, counts, bit_ref, *refs):
    out_ref, stay_ref = refs[-2:]
    step = pl.program_id(0)
    lefts = [refs[i] for i in order]
    rights = refs[max(order) + 1 : -2]
    first = 0
    for left, right, count in zip(lefts, rights, counts):

        @pl.when((step >= first) & (step < first + count))
        def _(left=left, right=right):
            rows = right[...].reshape(right.shape[-2:])
            out, stay = halves_of(dot(left[...], rows, TN), bit_ref[0], inner)
            out_ref[...] = out.astype(BF16)
            stay_ref[...] = stay.astype(BF16)

        first += count


def weight_grad(bit, inner, pairs, name, scale):
    block = 512
    width = pairs[0][0].shape[1]
    lefts = []
    for left, _ in pairs:
        if not any(left is other for other in lefts):
            lefts.append(left)
    order = [[left is other for other in lefts].index(True) for left, _ in pairs]
    counts, specs, rights, first = [], [], [], 0
    for left, right in pairs:
        rows = left.shape[0]
        array, part = right if isinstance(right, tuple) else (right, None)
        count = array.shape[-1] // block
        at = lambda j, first=first, count=count: jnp.clip(j - first, 0, count - 1)
        if part is None:
            specs.append(pl.BlockSpec((rows, block), lambda j, c, at=at: (0, at(j))))
        else:
            specs.append(
                pl.BlockSpec((1, rows, block), lambda j, c, at=at, part=part: (part, 0, at(j)))
            )
        rights.append(array)
        counts.append(count)
        first += count
    out = jax.ShapeDtypeStruct((width // 2, first * block), BF16)
    return pl.pallas_call(
        functools.partial(weight_grad_kernel, inner, order, counts),
        grid_spec=pltpu.PrefetchScalarGridSpec(
            num_scalar_prefetch=1,
            grid=(first,),
            in_specs=[whole(left.shape) for left in lefts] + specs,
            out_specs=[pl.BlockSpec((width // 2, block), lambda j, c: (0, j))] * 2,
        ),
        out_shape=[out, out],
        compiler_params=params(1),
        cost_estimate=cost(
            2 * rows * width * first * block,
            2 * (len(lefts) * rows * width + (rows + width) * first * block),
            scale,
        ),
        name=name,
    )(bit, *lefts, *rights)


def input_grad_kernel(
    x_ref, gq_ref, gk_ref, gv_ref, middle_ref, gain_ref, wq_ref, wk_ref, wv_ref, out_ref, sums_ref
):
    grad = (
        dot(gq_ref[...], wq_ref[...], NT)
        + dot(gk_ref[0], wk_ref[...], NT)
        + dot(gv_ref[0], wv_ref[...], NT)
    )
    x = x_ref[...].astype(F32)
    centered = x - jnp.mean(x, axis=-1, keepdims=True)
    inv = lax.rsqrt(jnp.mean(centered * centered, axis=-1, keepdims=True) + LN_EPS)
    unit = centered * inv
    scaled = grad * gain_ref[...]
    back = inv * (
        scaled
        - jnp.mean(scaled, axis=-1, keepdims=True)
        - unit * jnp.mean(scaled * unit, axis=-1, keepdims=True)
    )
    out_ref[...] = (middle_ref[...].astype(F32) + back).astype(BF16)

    @pl.when(pl.program_id(0) == 0)
    def _():
        sums_ref[...] = jnp.zeros_like(sums_ref)

    sums_ref[0:1, :] += jnp.sum(grad * unit, axis=0, keepdims=True)


def input_grad(x, gq, gkv, grad_middle, gain, w_query, w_key, w_value):
    rows, width = x.shape
    block = rows // 2
    row = pl.BlockSpec((block, width), lambda i: (i, 0))
    square = whole((width, width))
    return pl.pallas_call(
        input_grad_kernel,
        grid=(rows // block,),
        in_specs=[
            row,
            row,
            pl.BlockSpec((1, block, width), lambda i: (0, i, 0)),
            pl.BlockSpec((1, block, width), lambda i: (1, i, 0)),
            row,
            whole((1, width)),
        ]
        + [square] * 3,
        out_specs=[row, whole((8, width))],
        out_shape=[
            jax.ShapeDtypeStruct((rows, width), BF16),
            jax.ShapeDtypeStruct((8, width), F32),
        ],
        compiler_params=params(1),
        cost_estimate=cost(2 * 3 * rows * width * width, rows * width * 14 + 6 * width * width),
        name="input_grad",
    )(x, gq, gkv, gkv, grad_middle, gain, w_query, w_key, w_value)


def log2(n):
    return n.bit_length() - 1


class Places:
    def __init__(self):
        self.n_seq, self.n_sp = lax.axis_size("seq"), lax.axis_size("sp")
        self.sp_bits = log2(self.n_sp)
        self.count = self.sp_bits + log2(self.n_seq)
        self.core = self.sp_bits
        self.me = lax.axis_index("seq") * self.n_sp + lax.axis_index("sp")
        self.down_bits = [b for b in reversed(range(self.count)) if b != self.core]

    def swap(self, value, bit):
        if bit < self.sp_bits:
            axis, size, at = "sp", self.n_sp, bit
        else:
            axis, size, at = "seq", self.n_seq, bit - self.sp_bits
        return lax.ppermute(value, axis, [(i, i ^ (1 << at)) for i in range(size)])

    def send(self, value, flip):
        pairs = [(i, i ^ flip) for i in range(1 << self.count)]
        return lax.ppermute(value, ("seq", "sp"), pairs)

    def own(self, bit):
        return (self.me >> bit) & 1


def round_kernel(has, inners, bits_ref, *refs):
    two, one, new, carry = has
    refs = list(refs)
    take = lambda n: [refs.pop(0) for _ in range(n)]
    second, carried = take(4) if two else (), take(2) if carry else ()
    first = take(4) if one else ()
    fresh = take({"sent": 2, "core": 4, "": 0}[new])
    bufs = take(2) if one or new else ()
    bits = bits_ref[1], bits_ref[2], bits_ref[3]

    def split(keep, got, bit, inner):
        total = keep[...].astype(F32) + got[...].astype(F32)
        return [v.astype(BF16) for v in halves_of(total, bit, inner)]

    if two:
        outs = take(2)
        at = carried[0].shape[0] if carry else 0
        for src, dst in zip(carried, outs):
            dst[0:at, :] = src[...]
        for i in range(2):
            rows = second[i].shape[0] // 2
            for dst, part in zip(outs, split(second[i], second[2 + i], bits[2], inners["two"])):
                dst[at : at + rows, :] = part
            at += rows
    at = [0, 0]
    if new == "core":
        stays = take(2)
        for i in range(2):
            out, stays[i][...] = split(fresh[2 * i], fresh[2 * i + 1], bits[i], inners["new"][i])
            at[i] = out.shape[0]
            bufs[i][0 : at[i], :] = out
    if one:
        stays = take(2)
        for i in range(2):
            out, stays[i][...] = split(first[i], first[2 + i], bits[1 - i], inners["one"][i])
            bufs[1 - i][at[1 - i] :, :] = out


class Rounds:
    def __init__(self, places, x, y, z):
        self.places, self.x, self.y, self.z = places, x, y, z
        self.one = self.two = None
        self.got = []

    def inner(self, group, without, bit):
        bits = [b for b in sorted(group["bits"], reverse=True) if b not in without]
        return group["each"] << (len(bits) - 1 - bits.index(bit))

    def first_inners(self, bits, each):
        group = {"bits": bits, "each": each}
        return [self.inner(group, (), self.x), self.inner(group, (), self.y)]

    def send(self, buf_x, buf_y):
        self.got = [self.places.swap(buf_x, self.x), self.places.swap(buf_y, self.y)]

    def begin(self, parts, bits, each):
        self.one = {"bits": bits, "each": each, "keep": [parts[1], parts[3]]}
        self.send(parts[0], parts[2])

    def set_aside(self):
        group, self.two = self.two, None
        return dict(group, got=self.got)

    def run_aside(self, flags, aside):
        kept = self.one, self.two, self.got
        self.one, self.two, self.got = None, None, aside["got"]
        done = self.run(flags, aside=aside)
        self.one, self.two, self.got = kept
        return done

    def run(self, flags, new="", arrays=(), bits=(), each=0, carry=(), wait=False, aside=None, scale=0.02):
        one = self.one
        two = aside or self.two
        steps = 2
        ins, specs, outs, inners, heights, wide = [], [], [], {}, [0, 0], 0

        def tall(rows, columns, at=0, row=0):
            return pl.BlockSpec((rows, columns // steps), lambda j, b: (row, j + at))

        if two:
            rows, columns = two["keep"][0].shape
            got_x, got_y = two["got"] if aside else self.got
            ins += two["keep"] + [got_y, got_x]
            last = [got_y.shape[0] // rows - 1, got_x.shape[0] // rows - 1]
            specs += [tall(rows, columns)] * 2 + [tall(rows, columns, 0, row) for row in last]
            ins += carry
            specs += [tall(*v.shape) for v in carry]
            outs += [(rows + (carry[0].shape[0] if carry else 0), columns)] * 2
            inners["two"] = self.inner(two, (self.x, self.y), self.z)
        group, aliases = {"bits": list(bits), "each": each}, {}
        if one:
            rows, wide = one["keep"][0].shape
            ins += one["keep"] + self.got
            specs += [tall(rows, wide)] * 4
            inners["one"] = self.inner(one, (self.x,), self.y), self.inner(one, (self.y,), self.x)
        if new == "sent":
            aliases = {1 + len(ins) + i: i for i in range(2)}
            ins += [arrays[0], arrays[2]]
            specs += [pl.BlockSpec(memory_space=pl.ANY)] * 2
            group["keep"] = [arrays[1], arrays[3]]
        if new == "core":
            keep, got = arrays
            rows, wide = keep.shape[0], keep.shape[1] // 2
            ins += [keep, got, keep, got]
            specs += [tall(rows, wide)] * 2 + [tall(rows, wide, steps)] * 2
            heights = [rows // 2, rows // 2]
            outs += [(rows // 2, wide)] * 2
            inners["new"] = self.first_inners(bits, each)
        if one:
            rows = one["keep"][0].shape[0] // 2
            heights = [h + rows for h in heights]
            outs += [(rows, wide)] * 2
        out_specs = [tall(*shape) for shape in outs]
        if new == "sent":
            rows = one["keep"][0].shape[0] // 2
            outs = [arrays[0].shape, arrays[2].shape] + outs
            out_specs = [tall(rows, wide, 0, arrays[0].shape[0] // rows - 1)] * 2 + out_specs
        elif one or new:
            outs = [(h, wide) for h in heights] + outs
            out_specs = [tall(*shape) for shape in outs[:2]] + out_specs
        size = sum(v.size for v in ins)
        ins = [
            v if any(v is g for g in self.got) else in_hbm([v])[0] for v in ins
        ]
        results = list(
            pl.pallas_call(
                functools.partial(round_kernel, (bool(two), bool(one), new, bool(carry)), inners),
                grid_spec=pltpu.PrefetchScalarGridSpec(
                    num_scalar_prefetch=1,
                    grid=(steps,),
                    in_specs=specs,
                    out_specs=out_specs,
                ),
                out_shape=[pltpu.HBM(shape, BF16) for shape in outs],
                input_output_aliases=aliases,
                compiler_params=params(1, 24 << 20),
                cost_estimate=cost(2 * size, 4 * size, scale),
                name="round",
            )(flags, *ins)
        )
        take = lambda n: [results.pop(0) for _ in range(n)]
        buf_x, buf_y = take(2) if one or new else (None, None)
        done = None
        if two:
            done = take(2)
            if not wait:
                piece = Piece(self.places, [b for b in two["bits"] if b not in (self.x, self.y)], two["each"])
                piece.fork(*done, self.z)
                done = piece
        if new == "core":
            group["keep"] = take(2)
        self.two = dict(one, keep=take(2)) if one else None
        self.one = group if new else None
        self.got = []
        if one or new:
            self.send(buf_x, buf_y)
        return done


class Piece:
    def __init__(self, places, bits, each):
        self.places, self.bits, self.each = places, sorted(bits, reverse=True), each
        self.keep = self.got = None
        self.at = 0

    def inner(self, bit):
        return self.each << (len(self.bits) - 1 - self.bits.index(bit))

    def fork(self, out, stay, bit):
        self.bits.remove(bit)
        self.keep, self.got = stay, self.places.swap(out, bit)
        self.at, self.columns = 0, stay.shape[1]

    def split(self, bit):
        rows, columns = self.keep.shape
        inner = self.inner(bit)
        both = self.keep.reshape(rows // (2 * inner), 2, inner, columns)
        at = self.places.own(bit)
        out = lax.dynamic_index_in_dim(both, 1 - at, 1, False).reshape(rows // 2, columns)
        stay = lax.dynamic_index_in_dim(both, at, 1, False).reshape(rows // 2, columns)
        self.fork(out, stay, bit)

    def add(self, low=True):
        cols = slice(self.at * self.columns, (self.at + 1) * self.columns)
        self.keep = self.keep[:, cols].astype(F32) + self.got[:, cols].astype(F32)
        self.at = 0
        if low:
            self.keep = self.keep.astype(BF16)


def share(places, value, bits, group):
    axes = [bits.index(b) for b in group]

    def part(flip):
        out = value
        for b, axis in zip(group, axes):
            out = lax.dynamic_index_in_dim(out, places.own(b) ^ ((flip >> b) & 1), axis, True)
        return lax.squeeze(out, axes)

    flips = [sum(b << g for b, g in zip(f, group)) for f in np.ndindex(*(2,) * len(group))]
    return [part(0)] + [places.send(part(f), f) for f in flips if f]


def hold(small, *arrays):
    small, *arrays = lax.optimization_barrier((small, *arrays))
    return (small, *arrays)


def meet(small, arrays=(), pieces=(), rounds=None):
    many = list(arrays), [p.got for p in pieces], list(rounds.got) if rounds else []
    small, (arrays, gots, round_gots) = lax.optimization_barrier((small, many))
    for p, g in zip(pieces, gots):
        p.got = g
    if rounds:
        rounds.got = round_gots
    return (small, *arrays)


def on_device(
    frames, clip_ids, norm_gain, w_query, w_key, w_value, w_output, attn_scale,
    mlp_gain, w_gate, w_up, w_down, mlp_scale, out_grad,
):
    places = Places()
    seqs, length, width = frames.shape
    total_len = clip_ids.shape[1]
    rows = seqs * length
    n_sp, n_seq = places.n_sp, places.n_seq
    devices = n_sp * n_seq
    feed_width = w_gate.shape[1]
    own_rows = width // devices
    feed_rows = feed_width // devices
    block = feed_rows * n_sp
    core = lax.axis_index("seq") & 1
    sp = lax.axis_index("sp")
    sp_bits = list(reversed(range(places.core)))
    seq_bits = list(range(places.core + 1, places.count))
    x_bit, y_bit, z_bit = sp_bits[0], seq_bits[0], seq_bits[1]
    late = seq_bits[2:] + sp_bits[1:]
    every = list(range(places.count))
    not_core = [b for b in every if b != places.core]
    flags = jnp.stack([places.own(b) for b in (places.core, x_bit, y_bit, z_bit)]).astype(jnp.int32)
    rounds = Rounds(places, x_bit, y_bit, z_bit)

    x = frames.reshape(rows, width)
    grad_y = out_grad.reshape(rows, width)

    def neighbours(last, first):
        if n_sp == 2:
            got = lax.ppermute(jnp.where(sp == 0, last, first), "sp", [(0, 1), (1, 0)])
            return got, got
        return (
            lax.ppermute(last, "sp", [(i, i + 1) for i in range(n_sp - 1)]),
            lax.ppermute(first, "sp", [(i + 1, i) for i in range(n_sp - 1)]),
        )

    has = jnp.stack([sp > 0, sp < n_sp - 1]).astype(jnp.int32)
    from_left, from_right = neighbours(frames[:, length - HALF :], frames[:, :HALF])
    grad_y_peer = places.swap(grad_y, places.core)

    start = sp * length
    near = lax.dynamic_slice_in_dim(
        jnp.pad(clip_ids, ((0, 0), (HALF, HALF))), start, length + 2 * HALF, 1
    )
    ids = jnp.arange(CLIPS + 1, dtype=jnp.int32)
    begins = jnp.sum((clip_ids[:, None, :] < ids[:, None]).astype(jnp.int32), axis=-1)
    is_id = near[:, None, :] == ids[:CLIPS, None]
    first = jnp.sum(jnp.where(is_id, begins[:, :CLIPS, None], 0), axis=1)
    end = jnp.sum(jnp.where(is_id, begins[:, 1:, None], 0), axis=1)
    frame = lax.broadcasted_iota(jnp.int32, near.shape, 1) + (start - HALF)
    place = (frame - first).astype(F32).reshape(-1, 1)
    mid = slice(HALF, HALF + length)
    low = jnp.maximum(frame - HALF, first)[:, mid] - (start - HALF)
    high = jnp.minimum(frame + HALF, end)[:, mid] - (start - HALF)
    padded = -(-length // QB) * QB
    span = jnp.pad(jnp.stack([low, high], axis=1), ((0, 0), (0, 0), (0, padded - length)))

    gain = norm_gain[None]
    joint, normed, normed_own, cos_tab, sin_tab = project(
        x, from_left.reshape(-1, width), from_right.reshape(-1, width), place, gain,
        w_query, w_key, w_value, seqs,
    )
    mixed, probs = attend(span, joint, seqs)

    attn_out, mlp_in = out_proj(mixed, x, w_output, attn_scale[None], mlp_gain[None])
    flags_now, mlp_in, has = hold(flags, mlp_in, has)
    mlp_in_peer = places.swap(mlp_in, places.core)
    grad_low, grad_hidden = hidden_grad(
        flags_now, grad_y, grad_y_peer, mlp_scale[None], w_down, block
    )

    blocks = n_seq // 2
    per = blocks // 2

    def onward(piece):
        piece.add()
        piece.split(late[-1 - piece.left])
        piece.left -= 1

    def started(piece):
        piece.left = len(late) - 1
        return piece

    def finished(piece):
        while piece.left >= 0:
            onward(piece)
        piece.add(False)
        return piece.keep

    inners = rounds.first_inners(every, own_rows)
    *kept, a, b, c, d = feed(
        flags, mlp_in, mlp_in_peer, grad_hidden, w_gate, w_up, block, 0, per, (), inners
    )
    rounds.begin((a, b, c, d), every, own_rows)
    *kept, a, b, c, d = feed(
        flags, mlp_in, mlp_in_peer, grad_hidden, w_gate, w_up, block, per, per, kept, inners, width // 4
    )
    hidden, hidden_peer, grad_gate, grad_up = kept
    hidden_got = places.swap(hidden_peer, places.core)
    flags_now, a = meet(flags, [a], rounds=rounds)
    rounds.run(flags_now, "sent", (a, b, c, d), every, own_rows)

    flags_now, rounds.two["keep"][0] = meet(flags, [rounds.two["keep"][0]])
    *in_peer, in_own = feed_back(flags_now, grad_gate, grad_up, w_gate, w_up, block)
    in_got = [places.swap(v, places.core) for v in in_peer]

    flags_now, in_own = meet(flags, [in_own])
    each = feed_rows // 2
    parts = down(
        flags_now, hidden, hidden_peer, grad_low, each, rounds.first_inners(not_core, each), width // 4
    )

    flags_now, *both = meet(flags, [*in_got, *parts], rounds=rounds)
    in_got, parts = both[:2], both[2:]
    carry = rounds.run(flags_now, "sent", parts, not_core, each, wait=True)

    scale_row, rounds.two["keep"][0], hidden_got = meet(
        attn_scale[None], [rounds.two["keep"][0], hidden_got]
    )
    grad_attn, grad_mixed, grad_middle, join_sums = join(
        x, attn_out, grad_y, in_own, in_got, scale_row, mlp_gain[None], w_output
    )
    flip = ((sp == 0) & (n_sp == 2)).astype(jnp.int32).reshape(1)
    grad_query, grad_kv, grad_near, edge, other_edge = attend_back(
        flip, probs, joint, grad_mixed, cos_tab, sin_tab, seqs
    )
    if n_sp == 2:
        to_right = to_left = lax.ppermute(edge, "sp", [(0, 1), (1, 0)])
    else:
        to_left = lax.ppermute(edge, "sp", [(i + 1, i) for i in range(n_sp - 1)])
        to_right = lax.ppermute(other_edge, "sp", [(i, i + 1) for i in range(n_sp - 1)])
    to_right, to_left = [v.reshape(2, seqs, HALF, width) for v in (to_right, to_left)]

    core_inner = Piece(places, every, own_rows).inner(places.core)

    flags_now, grad_query = meet(flags, [grad_query])
    out, stay = weight_grad(
        flags_now,
        core_inner,
        [(mixed, grad_attn), (normed_own, grad_query), (normed, (grad_near, 0)), (normed, (grad_near, 1))],
        "attention_weights",
        0.02,
    )
    from_core = places.swap(out, places.core)

    flags_now, stay, to_right, to_left = meet(flags, [stay, to_right, to_left], [], rounds)
    first = started(rounds.run(flags_now, carry=carry))
    aside = rounds.set_aside()
    has_now, aside["keep"][0] = meet(has, [aside["keep"][0]])
    grad_kv = add_edges(has_now, grad_kv, to_right, to_left)
    flags_now, grad_kv, from_core = meet(flags, [grad_kv, from_core])
    rounds.run(flags_now, "core", (stay, from_core), not_core, own_rows)

    flags_now, rounds.one["keep"][0], *aside["got"] = meet(
        flags, [rounds.one["keep"][0], *aside["got"]]
    )
    layer_out, out_sums = feed_out(
        flags_now, hidden, hidden_got, w_down, x, attn_out, grad_y,
        attn_scale[None], mlp_scale[None], block,
    )
    flags_now, layer_out, join_sums = meet(flags, [layer_out, join_sums], [first])
    third = started(rounds.run_aside(flags_now, aside))
    onward(first)
    flags_now, first.keep, third.keep = meet(flags, [first.keep, third.keep], [], rounds)
    rounds.run(flags_now)
    gain_now, rounds.two["keep"][0] = meet(gain, [rounds.two["keep"][0]])
    frames_grad, norm_sums = input_grad(
        x, grad_query, grad_kv, grad_middle, gain_now, w_query, w_key, w_value
    )
    flags_now, frames_grad = meet(flags, [frames_grad], [third], rounds)
    fourth = started(rounds.run(flags_now))
    onward(third)
    _, fourth.keep, norm_sums = meet(flags, [fourth.keep, norm_sums])
    norm_sums, join_sums, out_sums = lax.optimization_barrier((norm_sums, join_sums, out_sums))
    vectors = jnp.stack([norm_sums[0], join_sums[0], join_sums[1], out_sums[0]], axis=1)
    vectors = vectors.reshape((2,) * places.count + (own_rows, 4))
    left = list(reversed(every))
    groups = [[b] for b in [places.core, x_bit, y_bit, z_bit] + late]
    shares = share(places, vectors, left, groups[0])
    _, *shares = meet(flags, shares, [first])
    feeds = finished(first).reshape(2, 2, 2, own_rows, width)
    mine = lax.dynamic_index_in_dim(feeds, core, 2, False)
    got = places.swap(lax.dynamic_index_in_dim(feeds, 1 - core, 2, False), places.core)
    for done, group in zip(groups, groups[1:]):
        left = [b for b in left if b not in done]
        shares = share(places, sum(shares), left, group)
        if group is groups[-3]:
            _, *shares = meet(flags, shares, [fourth])
            onward(fourth)
    down_grad = finished(third)
    pair = jnp.stack([jnp.where(core == 0, mine, got), jnp.where(core == 0, got, mine)], axis=0)
    pair = pair.reshape(2, 2, 2, own_rows, per, block)
    pair = pair.transpose(2, 3, 1, 4, 0, 5).reshape(2, own_rows, feed_width)
    while fourth.left >= 0:
        onward(fourth)
    _, gate_grad, up_grad, down_grad, *shares = meet(
        flags, [pair[0], pair[1], down_grad, *shares], [fourth]
    )
    vectors = sum(shares).T
    output_grad, query_grad, key_grad, value_grad = [
        fourth.keep[rows, columns].astype(F32) + fourth.got[rows, columns].astype(F32)
        for rows in (slice(0, own_rows), slice(own_rows, 2 * own_rows))
        for columns in (slice(0, width), slice(width, 2 * width))
    ]
    return (
        layer_out.reshape(frames.shape),
        frames_grad.reshape(frames.shape),
        vectors[0],
        query_grad,
        key_grad,
        value_grad,
        output_grad,
        vectors[1],
        vectors[2],
        gate_grad,
        up_grad,
        down_grad,
        vectors[3],
    )


def solution(mesh):
    split = P("seq", "sp", None)
    rows = P(("seq", "sp"), None)
    vec = P(("seq", "sp"))
    return jax.shard_map(
        on_device,
        mesh=mesh,
        in_specs=(split, P("seq", None)) + (P(),) * 11 + (split,),
        out_specs=(
            split, split, vec, rows, rows, rows, rows, vec, vec, rows, rows, rows, vec,
        ),
        check_vma=False,
    )
```

```python
import functools
import math

import jax
import jax.numpy as jnp
import numpy as np
from jax import lax
from jax.experimental import pallas as pl
from jax.experimental.pallas import tpu as pltpu
from jax.sharding import PartitionSpec as P

HEAD_DIM = 64
HALF = 64
LANES = 128
GROUP = 256
GH = GROUP // HEAD_DIM
QB = 128
KB = QB + 2 * HALF
CLIPS = 8
LN_EPS = 1e-05
RMS_EPS = 1e-06
VMEM = 58 << 20
F32 = jnp.float32
BF16 = jnp.bfloat16

NT = (((1,), (1,)), ((), ()))
NN = (((1,), (0,)), ((), ()))
TN = (((0,), (0,)), ((), ()))


def dot(a, b, dims=NN):
    return lax.dot_general(a, b, dims, preferred_element_type=F32)


def params(grid=0, vmem=VMEM):
    kinds = ("arbitrary",) * grid if grid else None
    return pltpu.CompilerParams(vmem_limit_bytes=vmem, dimension_semantics=kinds)


def cost(flops, moved, scale=0.02):
    return pl.CostEstimate(
        flops=int(flops * scale), bytes_accessed=int(moved * scale), transcendentals=0
    )


def in_hbm(values):
    return [pltpu.with_memory_space_constraint(v, pltpu.HBM) for v in values]


def whole(shape):
    return pl.BlockSpec(shape, lambda *_: (0,) * len(shape))


def swap_halves(v):
    lane = lax.broadcasted_iota(jnp.int32, v.shape, 1)
    return jnp.where(lane % HEAD_DIM < HEAD_DIM // 2, pltpu.roll(v, 96, 1), pltpu.roll(v, 32, 1))


def rotated(v, cos_tab, sin_tab, sign):
    pieces = []
    for at in range(0, v.shape[1], LANES):
        part = v[:, at : at + LANES]
        turned = swap_halves(part) * sin_tab
        pieces.append(part * cos_tab + turned if sign > 0 else part * cos_tab - turned)
    return jnp.concatenate(pieces, axis=1)


def project_kernel(
    seqs, x_ref, left_ref, right_ref, place_ref, gain_ref, wv_ref, wk_ref, wq_ref,
    out_ref, normed_ref, own_ref, cos_ref, sin_ref, low, weights, sems,
):
    step = pl.program_id(0)
    rows, width = low.shape
    padded = rows // seqs
    length = padded - 2 * HALF
    fetches = [
        pltpu.make_async_copy(src, weights.at[i], sems.at[i]) for i, src in enumerate((wv_ref, wk_ref, wq_ref))
    ]
    keeps = [pltpu.make_async_copy(low, normed_ref, sems.at[3])] + [
        pltpu.make_async_copy(
            low.at[s * padded + HALF : s * padded + HALF + length, :],
            own_ref.at[s * length : (s + 1) * length, :],
            sems.at[4 + s],
        )
        for s in range(seqs)
    ]

    def products(which, after):
        blocks = [slice(at, at + GROUP) for at in range(0, width, GROUP)]
        ahead = dot(low[...], weights[which, :, blocks[0]])
        for i, columns in enumerate(blocks):
            out = ahead
            if i + 1 < len(blocks):
                ahead = dot(low[...], weights[which, :, blocks[i + 1]])
            out_ref[0, :, columns] = after(out).astype(BF16)

    @pl.when(step == 0)
    def _():
        for copy in fetches:
            copy.start()
        for src, first, step in ((x_ref, HALF, length), (left_ref, 0, HALF), (right_ref, HALF + length, HALF)):
            x = src[...].astype(F32)
            centered = x - jnp.mean(x, axis=-1, keepdims=True)
            inv = lax.rsqrt(jnp.mean(centered * centered, axis=-1, keepdims=True) + LN_EPS)
            normed = (centered * inv * gain_ref[...]).astype(BF16)
            for s in range(seqs):
                at = s * padded + first
                low[at : at + step, :] = normed[s * step : (s + 1) * step]
        for copy in keeps:
            copy.start()
        fetches[0].wait()
        products(0, lambda out: out)
        lane = lax.broadcasted_iota(jnp.int32, (1, LANES), 1)
        exponent = (lane % (HEAD_DIM // 2)).astype(F32) * (2.0 / HEAD_DIM)
        angles = place_ref[...] * jnp.exp(-math.log(10000.0) * exponent)
        cos_ref[...] = jnp.cos(angles)
        sin_ref[...] = jnp.where(lane % HEAD_DIM < HEAD_DIM // 2, -1.0, 1.0) * jnp.sin(angles)

    @pl.when(step == 1)
    def _():
        fetches[1].wait()
        products(1, lambda out: rotated(out, cos_ref[...], sin_ref[...], 1))

    @pl.when(step == 2)
    def _():
        fetches[2].wait()
        scale = 1.0 / math.sqrt(HEAD_DIM)
        products(2, lambda out: rotated(out, cos_ref[...], sin_ref[...], 1) * scale)
        for copy in keeps:
            copy.wait()


def project(x, left, right, place, gain, w_query, w_key, w_value, seqs):
    own, width = x.shape
    rows = own + seqs * 2 * HALF
    edge = whole((seqs * HALF, width))
    hbm = pl.BlockSpec(memory_space=pl.ANY)
    table = jax.ShapeDtypeStruct((rows, LANES), F32)
    return pl.pallas_call(
        functools.partial(project_kernel, seqs),
        grid=(3,),
        in_specs=[whole((own, width)), edge, edge, whole((rows, 1)), whole((1, width))] + [hbm] * 3,
        out_specs=[
            pl.BlockSpec((1, rows, width), lambda j: (j, 0, 0)),
            hbm,
            hbm,
            whole((rows, LANES)),
            whole((rows, LANES)),
        ],
        out_shape=[
            jax.ShapeDtypeStruct((3, rows, width), BF16),
            jax.ShapeDtypeStruct((rows, width), BF16),
            jax.ShapeDtypeStruct((own, width), BF16),
            table,
            table,
        ],
        scratch_shapes=[
            pltpu.VMEM((rows, width), BF16),
            pltpu.VMEM((3, width, width), BF16),
            pltpu.SemaphoreType.DMA((4 + seqs,)),
        ],
        compiler_params=params(1),
        cost_estimate=cost(6 * rows * width * width, 6 * width * width + 10 * rows * width),
        name="project",
    )(x, left, right, place, gain, w_value, w_key, w_query)


def stack_heads(block):
    lane = lax.broadcasted_iota(jnp.int32, block.shape, 1)
    zero = jnp.zeros_like(block)
    return jnp.concatenate(
        [jnp.where(lane // HEAD_DIM == h, block, zero) for h in range(GH)], axis=0
    )


def fill_keys(buf, ref):
    rows = ref.shape[1]
    buf[0:rows, :] = ref[0]
    if buf.shape[0] > rows:
        buf[rows:, :] = jnp.zeros((buf.shape[0] - rows, buf.shape[1]), buf.dtype)


def fill_queries(buf, ref, length):
    buf[0:length, :] = ref[0, HALF : HALF + length, :] if ref.ndim == 3 else ref[...]
    rest = buf.shape[0] - length
    if rest:
        buf[length:, :] = jnp.zeros((rest, buf.shape[1]), buf.dtype)


def attend_kernel(span_ref, q_ref, k_ref, v_ref, o_ref, p_ref, kbuf, vbuf, qbuf, vt, ot):
    length = o_ref.shape[0]
    padded = qbuf.shape[0]
    fill_keys(kbuf, k_ref)
    fill_keys(vbuf, v_ref)
    fill_queries(qbuf, q_ref, length)
    blocks = padded // QB

    def scores_of(b):
        return dot(kbuf[b * QB : b * QB + KB, :], stack_heads(qbuf[b * QB : (b + 1) * QB, :]), NT)

    def mix(b, probs):
        for h in range(GH):
            rows = slice(h * HEAD_DIM, (h + 1) * HEAD_DIM)
            ot[rows, b * QB : (b + 1) * QB] = dot(vt[rows, b * QB : b * QB + KB], probs[h]).astype(BF16)

    ahead = scores_of(0)
    vt[...] = vbuf[...].T
    before = None
    for b in range(blocks):
        scores = ahead
        if b + 1 < blocks:
            ahead = scores_of(b + 1)
        if before is not None:
            mix(b - 1, before)
        place = lax.broadcasted_iota(jnp.int32, (KB, QB), 0) + b * QB
        low = span_ref[0, 0:1, b * QB : (b + 1) * QB]
        high = span_ref[0, 1:2, b * QB : (b + 1) * QB]
        seen = (place >= low) & (place < high)
        before = []
        for h in range(GH):
            masked = jnp.where(seen, scores[:, h * QB : (h + 1) * QB], -1e30)
            terms = jnp.exp(masked - jnp.max(masked, axis=0, keepdims=True))
            total = jnp.sum(terms, axis=0, keepdims=True)
            probs = (terms * (1.0 / total)).astype(BF16)
            p_ref[:, b * GH * QB + h * QB : b * GH * QB + (h + 1) * QB] = probs
            before.append(probs)
    mix(blocks - 1, before)
    o_ref[...] = ot[...].T[0:length, :]


def attend(span, joint, seqs):
    _, rows, width = joint.shape
    length = rows // seqs - 2 * HALF
    rows = seqs * length
    padded = span.shape[2]
    groups = width // GROUP
    keys = padded + 2 * HALF
    own = pl.BlockSpec((length, GROUP), lambda s, g: (s, g))
    near = [pl.BlockSpec((1, length + 2 * HALF, GROUP), lambda s, g, i=i: (i, s, g)) for i in range(3)]
    return pl.pallas_call(
        attend_kernel,
        grid=(seqs, groups),
        in_specs=[
            pl.BlockSpec((1, 2, padded), lambda s, g: (s, 0, 0)),
            near[2],
            near[1],
            near[0],
        ],
        out_specs=[
            own,
            pl.BlockSpec((KB, GH * padded), lambda s, g: (s, g)),
        ],
        out_shape=[
            jax.ShapeDtypeStruct((rows, width), BF16),
            jax.ShapeDtypeStruct((seqs * KB, groups * GH * padded), BF16),
        ],
        scratch_shapes=[
            pltpu.VMEM((keys, GROUP), BF16),
            pltpu.VMEM((keys, GROUP), BF16),
            pltpu.VMEM((padded, GROUP), BF16),
            pltpu.VMEM((GROUP, keys), BF16),
            pltpu.VMEM((GROUP, padded), BF16),
        ],
        compiler_params=params(2),
        cost_estimate=cost(
            2 * 2 * seqs * width * padded * KB * 4, 2 * width * (4 * rows + KB * seqs * padded // 64)
        ),
        name="attend",
    )(span, joint, joint, joint)


def attend_back_kernel(
    flip_ref, p_ref, q_ref, k_ref, v_ref, g_ref, cos_ref, sin_ref,
    dq_ref, dkv_ref, near_ref, edge_ref, other_ref,
    kbuf, vbuf, qbuf, gbuf, kt, dqt, dkb, dvb,
):
    length = g_ref.shape[0]
    padded = qbuf.shape[0]
    fill_keys(kbuf, k_ref)
    fill_keys(vbuf, v_ref)
    fill_queries(qbuf, q_ref, length)
    fill_queries(gbuf, g_ref, length)
    blocks = padded // QB

    def probs_grads(b):
        g4 = stack_heads(gbuf[b * QB : (b + 1) * QB, :])
        return g4, dot(vbuf[b * QB : b * QB + KB, :], g4, NT)

    def spread(b, g4, probs, lows):
        at, keys = slice(b * QB, (b + 1) * QB), slice(b * QB, b * QB + KB)
        for h in range(GH):
            rows = slice(h * HEAD_DIM, (h + 1) * HEAD_DIM)
            dqt[rows, at] = dot(kt[rows, keys], lows[h])
        q4 = stack_heads(qbuf[at, :])
        grads = (dkb, dot(jnp.concatenate(lows, axis=1), q4)), (dvb, dot(probs, g4))
        for buf, grad in grads:
            if b:
                buf[at, :] += grad[:QB]
            else:
                buf[at, :] = grad[:QB]
            buf[(b + 1) * QB : b * QB + KB, :] = grad[QB:]

    ahead = probs_grads(0)
    kt[...] = kbuf[...].T
    before = None
    for b in range(blocks):
        g4, grads = ahead
        if b + 1 < blocks:
            ahead = probs_grads(b + 1)
        if before is not None:
            spread(b - 1, *before)
        probs = p_ref[:, b * GH * QB : (b + 1) * GH * QB]
        lows = []
        for h in range(GH):
            part = probs[:, h * QB : (h + 1) * QB].astype(F32)
            grad = grads[:, h * QB : (h + 1) * QB]
            delta = jnp.sum(part * grad, axis=0, keepdims=True)
            lows.append((part * (grad - delta)).astype(BF16))
        before = g4, probs, lows
    spread(blocks - 1, *before)
    cos_tab, sin_tab = cos_ref[...], sin_ref[...]
    middle = slice(HALF, HALF + length)
    dq = dqt[...].T[0:length, :] * (1.0 / math.sqrt(HEAD_DIM))
    dq_ref[...] = rotated(dq, cos_tab[middle], sin_tab[middle], -1).astype(BF16)
    span = length + 2 * HALF
    dk = rotated(dkb[0:span, :], cos_tab, sin_tab, -1).astype(BF16)
    dv = dvb[0:span, :].astype(BF16)
    for i, grad in enumerate((dk, dv)):
        dkv_ref[i] = grad[middle]
        near_ref[i] = grad
        ends = grad[0:HALF], grad[span - HALF :]
        edge_ref[i] = jnp.where(flip_ref[0] == 1, ends[1], ends[0])
        other_ref[i] = jnp.where(flip_ref[0] == 1, ends[0], ends[1])


def attend_back(flip, probs, joint, grad, cos_tab, sin_tab, seqs):
    rows, width = grad.shape
    length = rows // seqs
    padded = -(-length // QB) * QB
    groups = width // GROUP
    keys = padded + 2 * HALF
    own = pl.BlockSpec((length, GROUP), lambda s, g, f: (s, g))
    both = pl.BlockSpec((2, length, GROUP), lambda s, g, f: (0, s, g))
    both_near = pl.BlockSpec((2, length + 2 * HALF, GROUP), lambda s, g, f: (0, s, g))
    near = [pl.BlockSpec((1, length + 2 * HALF, GROUP), lambda s, g, f, i=i: (i, s, g)) for i in range(3)]
    table = pl.BlockSpec((length + 2 * HALF, LANES), lambda s, g, f: (s, 0))
    edge = pl.BlockSpec((2, HALF, GROUP), lambda s, g, f: (0, s, g))
    out_edge = jax.ShapeDtypeStruct((2, seqs * HALF, width), BF16)
    out = jax.ShapeDtypeStruct((rows, width), BF16)
    out_both = jax.ShapeDtypeStruct((2, rows, width), BF16)
    out_near = jax.ShapeDtypeStruct((2, rows + seqs * 2 * HALF, width), BF16)
    return pl.pallas_call(
        attend_back_kernel,
        grid_spec=pltpu.PrefetchScalarGridSpec(
            num_scalar_prefetch=1,
            grid=(seqs, groups),
        in_specs=[
            pl.BlockSpec((KB, GH * padded), lambda s, g, f: (s, g)),
            near[2],
            near[1],
            near[0],
            own,
            table,
            table,
        ],
        out_specs=[own, both, both_near, edge, edge],
        scratch_shapes=[
            pltpu.VMEM((keys, GROUP), BF16),
            pltpu.VMEM((keys, GROUP), BF16),
            pltpu.VMEM((padded, GROUP), BF16),
            pltpu.VMEM((padded, GROUP), BF16),
            pltpu.VMEM((GROUP, keys), BF16),
            pltpu.VMEM((GROUP, padded), F32),
            pltpu.VMEM((keys, GROUP), F32),
            pltpu.VMEM((keys, GROUP), F32),
        ],
        ),
        out_shape=[out, out_both, out_near, out_edge, out_edge],
        compiler_params=params(2),
        cost_estimate=cost(
            2 * 4 * seqs * width * padded * KB * 4, 2 * width * (8 * rows + KB * seqs * padded // 64)
        ),
        name="attend_back",
    )(flip, probs, joint, joint, joint, grad, cos_tab, sin_tab)


def edges_kernel(seqs, flags_ref, from_ref, left_ref, right_ref, to_ref, buf, sems):
    length = from_ref.shape[1] // seqs
    places = [
        (i, s, e, pl.ds(s * length + e * (length - HALF), HALF))
        for i in range(2)
        for s in range(seqs)
        for e in range(2)
    ]
    copies = [
        (from_ref.at[i, rows, :], to_ref.at[i, rows, :], buf.at[at]) for at, (i, _, _, rows) in enumerate(places)
    ]
    for at, (src, _, mid) in enumerate(copies):
        pltpu.make_async_copy(src, mid, sems.at[0, at]).start()
    for at, (src, _, mid) in enumerate(copies):
        pltpu.make_async_copy(src, mid, sems.at[0, at]).wait()
    for at, (i, s, e, _) in enumerate(places):
        got = (right_ref if e else left_ref)[i, s].astype(F32) * flags_ref[e].astype(F32)
        buf[at] = (buf[at].astype(F32) + got).astype(BF16)
    for at, (_, dst, mid) in enumerate(copies):
        pltpu.make_async_copy(mid, dst, sems.at[1, at]).start()
    for at, (_, dst, mid) in enumerate(copies):
        pltpu.make_async_copy(mid, dst, sems.at[1, at]).wait()


def add_edges(flags, grads, left, right):
    seqs = left.shape[1]
    hbm = pl.BlockSpec(memory_space=pl.ANY)
    return pl.pallas_call(
        functools.partial(edges_kernel, seqs),
        grid_spec=pltpu.PrefetchScalarGridSpec(
            num_scalar_prefetch=1,
            grid=(1,),
            in_specs=[hbm, whole(left.shape), whole(right.shape)],
            out_specs=hbm,
            scratch_shapes=[
                pltpu.VMEM((4 * seqs, HALF, grads.shape[2]), BF16),
                pltpu.SemaphoreType.DMA((2, 4 * seqs)),
            ],
        ),
        out_shape=jax.ShapeDtypeStruct(grads.shape, BF16),
        input_output_aliases={1: 0},
        compiler_params=params(1),
        cost_estimate=cost(1e4 * left.size, 8 * left.size, 1000),
        name="add_edges",
    )(flags, grads, left, right)


def out_proj_kernel(m_ref, x_ref, w_ref, scale_ref, gain_ref, attn_ref, in_ref):
    attn = dot(m_ref[...], w_ref[...])
    attn_ref[...] = attn.astype(BF16)
    middle = x_ref[...].astype(F32) + scale_ref[...] * attn
    inv = lax.rsqrt(jnp.mean(middle * middle, axis=-1, keepdims=True) + RMS_EPS)
    in_ref[...] = (middle * inv * gain_ref[...]).astype(BF16)


def out_proj(mixed, x, w_output, scale, gain):
    rows, width = x.shape
    block = rows // 2
    row = pl.BlockSpec((block, width), lambda i: (i, 0))
    return pl.pallas_call(
        out_proj_kernel,
        grid=(rows // block,),
        in_specs=[row, row, whole((width, width)), whole((1, width)), whole((1, width))],
        out_specs=[row, row],
        out_shape=[
            jax.ShapeDtypeStruct((rows, width), BF16),
            jax.ShapeDtypeStruct((rows, width), BF16),
        ],
        compiler_params=params(1),
        cost_estimate=cost(2 * rows * width * width, 2 * rows * width * 5 + 2 * width * width),
        name="out_proj",
    )(mixed, x, w_output, scale, gain)


def hidden_grad_kernel(core_ref, own_ref, peer_ref, scale_ref, one_ref, two_ref, low_ref, out_ref):
    rows = own_ref.shape[0]
    block = one_ref.shape[0]

    @pl.when(pl.program_id(0) == 0)
    def _():
        low_ref[0:rows, :] = (own_ref[...].astype(F32) * scale_ref[...]).astype(BF16)
        low_ref[rows:, :] = (peer_ref[...].astype(F32) * scale_ref[...]).astype(BF16)

    out_ref[:, :block] = dot(low_ref[...], one_ref[...], NT).astype(BF16)
    out_ref[:, block:] = dot(low_ref[...], two_ref[...], NT).astype(BF16)


def hidden_grad(core, own, peer, scale, w_down, block):
    rows, width = own.shape
    count = w_down.shape[0] // block // 4
    half = w_down.shape[0] // 2
    return pl.pallas_call(
        hidden_grad_kernel,
        grid_spec=pltpu.PrefetchScalarGridSpec(
            num_scalar_prefetch=1,
            grid=(count,),
            in_specs=[
                whole((rows, width)),
                whole((rows, width)),
                whole((1, width)),
                pl.BlockSpec((block, width), lambda j, c: (4 * j + c[0], 0)),
                pl.BlockSpec((block, width), lambda j, c: (4 * j + 2 + c[0], 0)),
            ],
            out_specs=[
                whole((2 * rows, width)),
                pl.BlockSpec((2 * rows, 2 * block), lambda j, c: (0, j)),
            ],
        ),
        out_shape=[
            jax.ShapeDtypeStruct((2 * rows, width), BF16),
            jax.ShapeDtypeStruct((2 * rows, half), BF16),
        ],
        compiler_params=params(1),
        cost_estimate=cost(
            4 * rows * width * half, 2 * (4 * rows * width + half * (width + 2 * rows))
        ),
        name="hidden_grad",
    )(core, own, peer, scale, w_down, w_down)


def halves_of(value, bit, inner):
    rows, columns = value.shape
    both = value.reshape(rows // (2 * inner), 2, inner, columns)
    zero, one = both[:, 0], both[:, 1]
    out = jnp.where(bit == 0, one, zero).reshape(rows // 2, columns)
    stay = jnp.where(bit == 0, zero, one).reshape(rows // 2, columns)
    return out, stay


def feed_kernel(inners, core_ref, xo_ref, xp_ref, gh_ref, wg_ref, wu_ref, *refs):
    hid_own_ref, hid_peer_ref, gg_ref, gu_ref, *outs, x_all, sem = refs[-10:]
    rows = xo_ref.shape[0]
    first = pl.program_id(0) == 0
    fetch = pltpu.make_async_copy(xo_ref, x_all.at[0:rows, :], sem)

    @pl.when(first)
    def _():
        fetch.start()
        x_all[rows:, :] = xp_ref[...]

    for at in (rows, 0):
        part = slice(at, at + rows)
        if not at:
            pl.when(first)(fetch.wait)
        gate = dot(x_all[part, :], wg_ref[...])
        up = dot(x_all[part, :], wu_ref[...])
        grad = gh_ref[part, :].astype(F32)
        sig = 1.0 / (1.0 + jnp.exp(-gate))
        act = gate * sig
        (hid_peer_ref if at else hid_own_ref)[...] = (act * up).astype(BF16)
        gg_ref[part, :] = (grad * up * sig * (1.0 + gate * (1.0 - sig))).astype(BF16)
        gu_ref[part, :] = (grad * act).astype(BF16)
    for i, src in enumerate((gg_ref, gu_ref)):
        out, stay = halves_of(dot(x_all[...], src[...], TN), core_ref[1 + i], inners[i])
        outs[2 * i][...] = out.astype(BF16)
        outs[2 * i + 1][...] = stay.astype(BF16)


def feed(core, x_own, x_peer, grad_hidden, w_gate, w_up, block, first, count, before, inners, room=0):
    rows, width = x_own.shape
    half = grad_hidden.shape[1]
    wide = pl.BlockSpec((2 * rows, block), lambda j, c: (0, j + first))
    weight = pl.BlockSpec((width, block), lambda j, c: (0, 2 * (j + first) + c[0]))
    tall = pl.BlockSpec((rows, block), lambda j, c: (0, j + first))
    kept = pltpu.HBM((2 * rows, half), BF16)
    single = pltpu.HBM((rows, half), BF16)
    grads = [pltpu.HBM((width // 2 + more, count * block), BF16) for more in (room, 0, room, 0)]
    any_spec = pl.BlockSpec(memory_space=pl.ANY)
    return pl.pallas_call(
        functools.partial(feed_kernel, inners),
        grid_spec=pltpu.PrefetchScalarGridSpec(
            num_scalar_prefetch=1,
            grid=(count,),
            in_specs=[any_spec, whole((rows, width)), wide, weight, weight]
            + [any_spec] * len(before),
            out_specs=[tall] * 2
            + [wide] * 2
            + [pl.BlockSpec((width // 2, block), lambda j, c: (0, j))] * 4,
            scratch_shapes=[pltpu.VMEM((2 * rows, width), BF16), pltpu.SemaphoreType.DMA],
        ),
        out_shape=[single] * 2 + [kept] * 2 + grads,
        input_output_aliases={6 + i: i for i in range(len(before))},
        compiler_params=params(1, 46 << 20),
        cost_estimate=cost(
            2 * 2 * rows * width * block * count * 4,
            2 * (4 * rows * width + count * block * (8 * rows + 4 * width)),
        ),
        name="feed",
    )(core, *in_hbm([x_own]), x_peer, *in_hbm([grad_hidden, w_gate, w_up, *before]))


def down_kernel(each, inners, bits_ref, own_ref, peer_ref, low_ref, *refs):
    *outs, both = refs
    both[: own_ref.shape[0], :] = own_ref[...]
    both[own_ref.shape[0] :, :] = peer_ref[...]
    value = dot(both[...], low_ref[...], TN)
    rows, width = value.shape
    value = value.reshape(rows // (2 * each), 2, each, width)
    for i in range(2):
        part = value[:, i].reshape(rows // 2, width)
        out, stay = halves_of(part, bits_ref[1 + i], inners[i])
        outs[2 * i][...] = out.astype(BF16)
        outs[2 * i + 1][...] = stay.astype(BF16)


def down(bits, own, peer, low, each, inners, room):
    rows, half = own.shape
    width = low.shape[1]
    block = 512
    return pl.pallas_call(
        functools.partial(down_kernel, each, inners),
        grid_spec=pltpu.PrefetchScalarGridSpec(
            num_scalar_prefetch=1,
            grid=(half // block,),
            in_specs=[
                pl.BlockSpec((rows, block), lambda j, c: (0, j)),
                pl.BlockSpec((rows, block), lambda j, c: (0, j)),
                whole((2 * rows, width)),
            ],
            out_specs=[pl.BlockSpec((block // 4, width), lambda j, c: (j, 0))] * 4,
            scratch_shapes=[pltpu.VMEM((2 * rows, block), BF16)],
        ),
        out_shape=[jax.ShapeDtypeStruct((half // 4 + more, width), BF16) for more in (room, 0, room, 0)],
        compiler_params=params(1),
        cost_estimate=cost(
            4 * rows * half * width, 2 * (2 * rows * half + 2 * rows * width + half * width)
        ),
        name="down_weight",
    )(bits, own, peer, low)


def in_halves(value, refs):
    half = value.shape[1] // 2
    refs[0][...] = value[:, :half]
    refs[1][...] = value[:, half:]


def feed_back_kernel(core_ref, *refs):
    *peer_refs, own_ref, acc = refs[-4:]
    part, step = pl.program_id(0), pl.program_id(1)
    block = refs[2].shape[1]
    total = None
    for i in range(2):
        for half in range(2):
            out = dot(refs[i][:, half * block : (half + 1) * block], refs[2 + 2 * i + half][...], NT)
            total = out if total is None else total + out
    last = pl.num_programs(1) - 1

    @pl.when(step == 0)
    def _():
        acc[...] = total

    @pl.when((step > 0) & (step < last))
    def _():
        acc[...] += total

    @pl.when((step == last) & (part == 0))
    def _():
        in_halves((acc[...] + total).astype(BF16), peer_refs)

    @pl.when((step == last) & (part == 1))
    def _():
        own_ref[...] = (acc[...] + total).astype(BF16)


def feed_back(core, grad_gate, grad_up, w_gate, w_up, block):
    rows, half = grad_gate.shape
    rows = rows // 2
    width = w_gate.shape[0]
    tall = pl.BlockSpec((rows, 2 * block), lambda p, j, c: (1 - p, j))
    one = pl.BlockSpec((width, block), lambda p, j, c: (0, 4 * j + c[0]))
    two = pl.BlockSpec((width, block), lambda p, j, c: (0, 4 * j + 2 + c[0]))
    return pl.pallas_call(
        feed_back_kernel,
        grid_spec=pltpu.PrefetchScalarGridSpec(
            num_scalar_prefetch=1,
            grid=(2, half // block // 2),
            in_specs=[tall, tall, one, two, one, two],
            out_specs=[whole((rows, width // 2))] * 2 + [whole((rows, width))],
            scratch_shapes=[pltpu.VMEM((rows, width), F32)],
        ),
        out_shape=[jax.ShapeDtypeStruct((rows, width // 2), BF16)] * 2
        + [jax.ShapeDtypeStruct((rows, width), BF16)],
        compiler_params=params(2),
        cost_estimate=cost(8 * rows * half * width, 8 * (rows * half + half * width)),
        name="feed_back",
    )(core, grad_gate, grad_up, w_gate, w_gate, w_up, w_up)


def join_kernel(
    x_ref, attn_ref, g_ref, in_ref, got_one_ref, got_two_ref, attn_scale_ref, gain_ref, w_ref,
    grad_attn_ref, grad_mixed_ref, middle_ref, sums_ref,
):
    x = x_ref[...].astype(F32)
    attn = attn_ref[...].astype(F32)
    grad_y = g_ref[...].astype(F32)
    got = jnp.concatenate([got_one_ref[...], got_two_ref[...]], axis=1)
    grad_in = in_ref[...].astype(F32) + got.astype(F32)
    middle = x + attn_scale_ref[...] * attn
    inv = lax.rsqrt(jnp.mean(middle * middle, axis=-1, keepdims=True) + RMS_EPS)
    unit = middle * inv
    scaled = grad_in * gain_ref[...]
    grad_middle = grad_y + inv * (scaled - unit * jnp.mean(scaled * unit, axis=-1, keepdims=True))
    middle_ref[...] = grad_middle.astype(BF16)
    grad_attn = (attn_scale_ref[...] * grad_middle).astype(BF16)
    grad_attn_ref[...] = grad_attn
    grad_mixed_ref[...] = dot(grad_attn, w_ref[...], NT).astype(BF16)

    @pl.when(pl.program_id(0) == 0)
    def _():
        sums_ref[...] = jnp.zeros_like(sums_ref)

    sums_ref[0:1, :] += jnp.sum(grad_middle * attn, axis=0, keepdims=True)
    sums_ref[1:2, :] += jnp.sum(grad_in * unit, axis=0, keepdims=True)


def join(x, attn, grad_y, grad_in, got, attn_scale, gain, w_output):
    rows, width = x.shape
    block = rows // 2
    row = pl.BlockSpec((block, width), lambda i: (i, 0))
    half = pl.BlockSpec((block, width // 2), lambda i: (i, 0))
    vec = whole((1, width))
    low = jax.ShapeDtypeStruct((rows, width), BF16)
    return pl.pallas_call(
        join_kernel,
        grid=(rows // block,),
        in_specs=[row] * 4 + [half] * 2 + [vec] * 2 + [whole((width, width))],
        out_specs=[row] * 3 + [whole((8, width))],
        out_shape=[
            low,
            low,
            low,
            jax.ShapeDtypeStruct((8, width), F32),
        ],
        compiler_params=params(1),
        cost_estimate=cost(2 * rows * width * width, rows * width * 22 + 2 * width * width),
        name="join",
    )(x, attn, grad_y, grad_in, *got, attn_scale, gain, w_output)


def feed_out_kernel(
    core_ref, own_ref, got_ref, w_ref, x_ref, attn_ref, g_ref, attn_scale_ref, mlp_scale_ref,
    layer_ref, sums_ref, hidden, acc,
):
    step, last = pl.program_id(0), pl.num_programs(0) - 1
    block = own_ref.shape[1] // 2
    for i in range(2):
        part = slice(i * block, (i + 1) * block)
        own, got = own_ref[:, part], got_ref[:, part]
        first = core_ref[0] == 0
        hidden[:, 2 * i * block : (2 * i + 1) * block] = jnp.where(first, own, got)
        hidden[:, (2 * i + 1) * block : (2 * i + 2) * block] = jnp.where(first, got, own)
    total = dot(hidden[...], w_ref[...])

    @pl.when(step == 0)
    def _():
        acc[...] = total

    @pl.when((step > 0) & (step < last))
    def _():
        acc[...] += total

    @pl.when(step == last)
    def _():
        down_out = acc[...] + total
        middle = x_ref[...].astype(F32) + attn_scale_ref[...] * attn_ref[...].astype(F32)
        layer_ref[...] = (middle + mlp_scale_ref[...] * down_out).astype(BF16)
        sums_ref[...] = jnp.zeros_like(sums_ref)
        sums_ref[0:1, :] = jnp.sum(g_ref[...].astype(F32) * down_out, axis=0, keepdims=True)


def feed_out(core, own, got, w_down, x, attn, grad_y, attn_scale, mlp_scale, block):
    rows, half = own.shape
    width = w_down.shape[1]
    tall = pl.BlockSpec((rows, 2 * block), lambda j, c: (0, j))
    row, vec = whole((rows, width)), whole((1, width))
    return pl.pallas_call(
        feed_out_kernel,
        grid_spec=pltpu.PrefetchScalarGridSpec(
            num_scalar_prefetch=1,
            grid=(half // block // 2,),
            in_specs=[tall, tall, pl.BlockSpec((4 * block, width), lambda j, c: (j, 0))]
            + [row] * 3
            + [vec] * 2,
            out_specs=[row, whole((8, width))],
            scratch_shapes=[pltpu.VMEM((rows, 4 * block), BF16), pltpu.VMEM((rows, width), F32)],
        ),
        out_shape=[
            jax.ShapeDtypeStruct((rows, width), BF16),
            jax.ShapeDtypeStruct((8, width), F32),
        ],
        compiler_params=params(1),
        cost_estimate=cost(4 * rows * half * width, 4 * (rows * half + half * width), 10),
        name="feed_out",
    )(core, own, got, w_down, x, attn, grad_y, attn_scale, mlp_scale)


def weight_grad_kernel(inner, order, counts, bit_ref, *refs):
    total = max(order) + 1
    sources, rights = refs[:total], refs[total : total + len(order)]
    out_ref, stay_ref, *bufs, sems = refs[total + len(order) :]
    step = pl.program_id(0)
    fetches = [pltpu.make_async_copy(sources[i], bufs[i], sems.at[i]) for i in range(total)]

    @pl.when(step == 0)
    def _():
        for copy in fetches:
            copy.start()

    first = 0
    for k, (right, count) in enumerate(zip(rights, counts)):
        left = bufs[order[k]]
        if order[k] not in order[:k]:
            pl.when(step == first)(fetches[order[k]].wait)

        @pl.when((step >= first) & (step < first + count))
        def _(left=left, right=right):
            rows = right[...].reshape(right.shape[-2:])
            out, stay = halves_of(dot(left[...], rows, TN), bit_ref[0], inner)
            out_ref[...] = out.astype(BF16)
            stay_ref[...] = stay.astype(BF16)

        first += count


def weight_grad(bit, inner, pairs, name, scale):
    block = 512
    width = pairs[0][0].shape[1]
    lefts = []
    for left, _ in pairs:
        if not any(left is other for other in lefts):
            lefts.append(left)
    order = [[left is other for other in lefts].index(True) for left, _ in pairs]
    counts, specs, rights, first = [], [], [], 0
    for left, right in pairs:
        rows = left.shape[0]
        array, part = right if isinstance(right, tuple) else (right, None)
        count = array.shape[-1] // block
        at = lambda j, first=first, count=count: jnp.clip(j - first, 0, count - 1)
        if part is None:
            specs.append(pl.BlockSpec((rows, block), lambda j, c, at=at: (0, at(j))))
        else:
            specs.append(
                pl.BlockSpec((1, rows, block), lambda j, c, at=at, part=part: (part, 0, at(j)))
            )
        rights.append(array)
        counts.append(count)
        first += count
    out = jax.ShapeDtypeStruct((width // 2, first * block), BF16)
    return pl.pallas_call(
        functools.partial(weight_grad_kernel, inner, order, counts),
        grid_spec=pltpu.PrefetchScalarGridSpec(
            num_scalar_prefetch=1,
            grid=(first,),
            in_specs=[pl.BlockSpec(memory_space=pl.ANY)] * len(lefts) + specs,
            out_specs=[pl.BlockSpec((width // 2, block), lambda j, c: (0, j))] * 2,
            scratch_shapes=[pltpu.VMEM(left.shape, BF16) for left in lefts]
            + [pltpu.SemaphoreType.DMA((len(lefts),))],
        ),
        out_shape=[out, out],
        compiler_params=params(1),
        cost_estimate=cost(
            2 * rows * width * first * block,
            2 * (len(lefts) * rows * width + (rows + width) * first * block),
            scale,
        ),
        name=name,
    )(bit, *lefts, *rights)


def input_grad_kernel(
    x_ref, gq_ref, gk_ref, gv_ref, middle_ref, gain_ref, wq_ref, wk_ref, wv_ref, out_ref, sums_ref
):
    grad = (
        dot(gq_ref[...], wq_ref[...], NT)
        + dot(gk_ref[0], wk_ref[...], NT)
        + dot(gv_ref[0], wv_ref[...], NT)
    )
    x = x_ref[...].astype(F32)
    centered = x - jnp.mean(x, axis=-1, keepdims=True)
    inv = lax.rsqrt(jnp.mean(centered * centered, axis=-1, keepdims=True) + LN_EPS)
    unit = centered * inv
    scaled = grad * gain_ref[...]
    back = inv * (
        scaled
        - jnp.mean(scaled, axis=-1, keepdims=True)
        - unit * jnp.mean(scaled * unit, axis=-1, keepdims=True)
    )
    out_ref[...] = (middle_ref[...].astype(F32) + back).astype(BF16)

    @pl.when(pl.program_id(0) == 0)
    def _():
        sums_ref[...] = jnp.zeros_like(sums_ref)

    sums_ref[0:1, :] += jnp.sum(grad * unit, axis=0, keepdims=True)


def input_grad(x, gq, gkv, grad_middle, gain, w_query, w_key, w_value):
    rows, width = x.shape
    block = rows // 2
    row = pl.BlockSpec((block, width), lambda i: (i, 0))
    square = whole((width, width))
    return pl.pallas_call(
        input_grad_kernel,
        grid=(rows // block,),
        in_specs=[
            row,
            row,
            pl.BlockSpec((1, block, width), lambda i: (0, i, 0)),
            pl.BlockSpec((1, block, width), lambda i: (1, i, 0)),
            row,
            whole((1, width)),
        ]
        + [square] * 3,
        out_specs=[row, whole((8, width))],
        out_shape=[
            jax.ShapeDtypeStruct((rows, width), BF16),
            jax.ShapeDtypeStruct((8, width), F32),
        ],
        compiler_params=params(1),
        cost_estimate=cost(2 * 3 * rows * width * width, rows * width * 14 + 6 * width * width),
        name="input_grad",
    )(x, gq, gkv, gkv, grad_middle, gain, w_query, w_key, w_value)


def log2(n):
    return n.bit_length() - 1


class Places:
    def __init__(self):
        self.n_seq, self.n_sp = lax.axis_size("seq"), lax.axis_size("sp")
        self.sp_bits = log2(self.n_sp)
        self.count = self.sp_bits + log2(self.n_seq)
        self.core = self.sp_bits
        self.me = lax.axis_index("seq") * self.n_sp + lax.axis_index("sp")
        self.down_bits = [b for b in reversed(range(self.count)) if b != self.core]

    def swap(self, value, bit):
        if bit < self.sp_bits:
            axis, size, at = "sp", self.n_sp, bit
        else:
            axis, size, at = "seq", self.n_seq, bit - self.sp_bits
        return lax.ppermute(value, axis, [(i, i ^ (1 << at)) for i in range(size)])

    def send(self, value, flip):
        pairs = [(i, i ^ flip) for i in range(1 << self.count)]
        return lax.ppermute(value, ("seq", "sp"), pairs)

    def own(self, bit):
        return (self.me >> bit) & 1


def round_kernel(has, inners, bits_ref, *refs):
    two, one, new, carry = has
    refs = list(refs)
    take = lambda n: [refs.pop(0) for _ in range(n)]
    second, carried = take(4) if two else (), take(2) if carry else ()
    first = take(4) if one else ()
    fresh = take({"sent": 2, "core": 4, "": 0}[new])
    bufs = take(2) if one or new else ()
    bits = bits_ref[1], bits_ref[2], bits_ref[3]

    def split(keep, got, bit, inner):
        total = keep[...].astype(F32) + got[...].astype(F32)
        return [v.astype(BF16) for v in halves_of(total, bit, inner)]

    if two:
        outs = take(2)
        at = carried[0].shape[0] if carry else 0
        for src, dst in zip(carried, outs):
            dst[0:at, :] = src[...]
        for i in range(2):
            rows = second[i].shape[0] // 2
            for dst, part in zip(outs, split(second[i], second[2 + i], bits[2], inners["two"])):
                dst[at : at + rows, :] = part
            at += rows
    at = [0, 0]
    if new == "core":
        stays = take(2)
        for i in range(2):
            out, stays[i][...] = split(fresh[2 * i], fresh[2 * i + 1], bits[i], inners["new"][i])
            at[i] = out.shape[0]
            bufs[i][0 : at[i], :] = out
    if one:
        stays = take(2)
        for i in range(2):
            out, stays[i][...] = split(first[i], first[2 + i], bits[1 - i], inners["one"][i])
            bufs[1 - i][at[1 - i] :, :] = out


class Rounds:
    def __init__(self, places, x, y, z):
        self.places, self.x, self.y, self.z = places, x, y, z
        self.one = self.two = None
        self.got = []

    def inner(self, group, without, bit):
        bits = [b for b in sorted(group["bits"], reverse=True) if b not in without]
        return group["each"] << (len(bits) - 1 - bits.index(bit))

    def first_inners(self, bits, each):
        group = {"bits": bits, "each": each}
        return [self.inner(group, (), self.x), self.inner(group, (), self.y)]

    def send(self, buf_x, buf_y):
        self.got = [self.places.swap(buf_x, self.x), self.places.swap(buf_y, self.y)]

    def begin(self, parts, bits, each):
        self.one = {"bits": bits, "each": each, "keep": [parts[1], parts[3]]}
        self.send(parts[0], parts[2])

    def set_aside(self):
        group, self.two = self.two, None
        return dict(group, got=self.got)

    def run_aside(self, flags, aside):
        kept = self.one, self.two, self.got
        self.one, self.two, self.got = None, None, aside["got"]
        done = self.run(flags, aside=aside)
        self.one, self.two, self.got = kept
        return done

    def run(self, flags, new="", arrays=(), bits=(), each=0, carry=(), wait=False, aside=None, scale=0.02):
        one = self.one
        two = aside or self.two
        steps = 2
        ins, specs, outs, inners, heights, wide = [], [], [], {}, [0, 0], 0

        def tall(rows, columns, at=0, row=0):
            return pl.BlockSpec((rows, columns // steps), lambda j, b: (row, j + at))

        if two:
            rows, columns = two["keep"][0].shape
            got_x, got_y = two["got"] if aside else self.got
            ins += two["keep"] + [got_y, got_x]
            last = [got_y.shape[0] // rows - 1, got_x.shape[0] // rows - 1]
            specs += [tall(rows, columns)] * 2 + [tall(rows, columns, 0, row) for row in last]
            ins += carry
            specs += [tall(*v.shape) for v in carry]
            outs += [(rows + (carry[0].shape[0] if carry else 0), columns)] * 2
            inners["two"] = self.inner(two, (self.x, self.y), self.z)
        group, aliases = {"bits": list(bits), "each": each}, {}
        if one:
            rows, wide = one["keep"][0].shape
            ins += one["keep"] + self.got
            specs += [tall(rows, wide)] * 4
            inners["one"] = self.inner(one, (self.x,), self.y), self.inner(one, (self.y,), self.x)
        if new == "sent":
            aliases = {1 + len(ins) + i: i for i in range(2)}
            ins += [arrays[0], arrays[2]]
            specs += [pl.BlockSpec(memory_space=pl.ANY)] * 2
            group["keep"] = [arrays[1], arrays[3]]
        if new == "core":
            keep, got = arrays
            rows, wide = keep.shape[0], keep.shape[1] // 2
            ins += [keep, got, keep, got]
            specs += [tall(rows, wide)] * 2 + [tall(rows, wide, steps)] * 2
            heights = [rows // 2, rows // 2]
            outs += [(rows // 2, wide)] * 2
            inners["new"] = self.first_inners(bits, each)
        if one:
            rows = one["keep"][0].shape[0] // 2
            heights = [h + rows for h in heights]
            outs += [(rows, wide)] * 2
        out_specs = [tall(*shape) for shape in outs]
        if new == "sent":
            rows = one["keep"][0].shape[0] // 2
            outs = [arrays[0].shape, arrays[2].shape] + outs
            out_specs = [tall(rows, wide, 0, arrays[0].shape[0] // rows - 1)] * 2 + out_specs
        elif one or new:
            outs = [(h, wide) for h in heights] + outs
            out_specs = [tall(*shape) for shape in outs[:2]] + out_specs
        size = sum(v.size for v in ins)
        ins = [
            v if any(v is g for g in self.got) else in_hbm([v])[0] for v in ins
        ]
        results = list(
            pl.pallas_call(
                functools.partial(round_kernel, (bool(two), bool(one), new, bool(carry)), inners),
                grid_spec=pltpu.PrefetchScalarGridSpec(
                    num_scalar_prefetch=1,
                    grid=(steps,),
                    in_specs=specs,
                    out_specs=out_specs,
                ),
                out_shape=[pltpu.HBM(shape, BF16) for shape in outs],
                input_output_aliases=aliases,
                compiler_params=params(1, 24 << 20),
                cost_estimate=cost(2 * size, 4 * size, scale),
                name="round",
            )(flags, *ins)
        )
        take = lambda n: [results.pop(0) for _ in range(n)]
        buf_x, buf_y = take(2) if one or new else (None, None)
        done = None
        if two:
            done = take(2)
            if not wait:
                piece = Piece(self.places, [b for b in two["bits"] if b not in (self.x, self.y)], two["each"])
                piece.fork(*done, self.z)
                done = piece
        if new == "core":
            group["keep"] = take(2)
        self.two = dict(one, keep=take(2)) if one else None
        self.one = group if new else None
        self.got = []
        if one or new:
            self.send(buf_x, buf_y)
        return done


class Piece:
    def __init__(self, places, bits, each):
        self.places, self.bits, self.each = places, sorted(bits, reverse=True), each
        self.keep = self.got = None
        self.at = 0

    def inner(self, bit):
        return self.each << (len(self.bits) - 1 - self.bits.index(bit))

    def fork(self, out, stay, bit):
        self.bits.remove(bit)
        self.keep, self.got = stay, self.places.swap(out, bit)
        self.at, self.columns = 0, stay.shape[1]

    def split(self, bit):
        rows, columns = self.keep.shape
        inner = self.inner(bit)
        both = self.keep.reshape(rows // (2 * inner), 2, inner, columns)
        at = self.places.own(bit)
        out = lax.dynamic_index_in_dim(both, 1 - at, 1, False).reshape(rows // 2, columns)
        stay = lax.dynamic_index_in_dim(both, at, 1, False).reshape(rows // 2, columns)
        self.fork(out, stay, bit)

    def add(self, low=True):
        cols = slice(self.at * self.columns, (self.at + 1) * self.columns)
        self.keep = self.keep[:, cols].astype(F32) + self.got[:, cols].astype(F32)
        self.at = 0
        if low:
            self.keep = self.keep.astype(BF16)


def share(places, value, bits, group):
    axes = [bits.index(b) for b in group]

    def part(flip):
        out = value
        for b, axis in zip(group, axes):
            out = lax.dynamic_index_in_dim(out, places.own(b) ^ ((flip >> b) & 1), axis, True)
        return lax.squeeze(out, axes)

    flips = [sum(b << g for b, g in zip(f, group)) for f in np.ndindex(*(2,) * len(group))]
    return [part(0)] + [places.send(part(f), f) for f in flips if f]


def hold(small, *arrays):
    small, *arrays = lax.optimization_barrier((small, *arrays))
    return (small, *arrays)


def meet(small, arrays=(), pieces=(), rounds=None):
    many = list(arrays), [p.got for p in pieces], list(rounds.got) if rounds else []
    small, (arrays, gots, round_gots) = lax.optimization_barrier((small, many))
    for p, g in zip(pieces, gots):
        p.got = g
    if rounds:
        rounds.got = round_gots
    return (small, *arrays)


def on_device(
    frames, clip_ids, norm_gain, w_query, w_key, w_value, w_output, attn_scale,
    mlp_gain, w_gate, w_up, w_down, mlp_scale, out_grad,
):
    places = Places()
    seqs, length, width = frames.shape
    total_len = clip_ids.shape[1]
    rows = seqs * length
    n_sp, n_seq = places.n_sp, places.n_seq
    devices = n_sp * n_seq
    feed_width = w_gate.shape[1]
    own_rows = width // devices
    feed_rows = feed_width // devices
    block = feed_rows * n_sp
    core = lax.axis_index("seq") & 1
    sp = lax.axis_index("sp")
    sp_bits = list(reversed(range(places.core)))
    seq_bits = list(range(places.core + 1, places.count))
    x_bit, y_bit, z_bit = sp_bits[0], seq_bits[0], seq_bits[1]
    late = seq_bits[2:] + sp_bits[1:]
    every = list(range(places.count))
    not_core = [b for b in every if b != places.core]
    flags = jnp.stack([places.own(b) for b in (places.core, x_bit, y_bit, z_bit)]).astype(jnp.int32)
    rounds = Rounds(places, x_bit, y_bit, z_bit)

    x = frames.reshape(rows, width)
    grad_y = out_grad.reshape(rows, width)

    def neighbours(last, first):
        if n_sp == 2:
            got = lax.ppermute(jnp.where(sp == 0, last, first), "sp", [(0, 1), (1, 0)])
            return got, got
        return (
            lax.ppermute(last, "sp", [(i, i + 1) for i in range(n_sp - 1)]),
            lax.ppermute(first, "sp", [(i + 1, i) for i in range(n_sp - 1)]),
        )

    has = jnp.stack([sp > 0, sp < n_sp - 1]).astype(jnp.int32)
    from_left, from_right = neighbours(frames[:, length - HALF :], frames[:, :HALF])
    grad_y_peer = places.swap(grad_y, places.core)

    start = sp * length
    near = lax.dynamic_slice_in_dim(
        jnp.pad(clip_ids, ((0, 0), (HALF, HALF))), start, length + 2 * HALF, 1
    )
    ids = jnp.arange(CLIPS + 1, dtype=jnp.int32)
    begins = jnp.sum((clip_ids[:, None, :] < ids[:, None]).astype(jnp.int32), axis=-1)
    is_id = near[:, None, :] == ids[:CLIPS, None]
    first = jnp.sum(jnp.where(is_id, begins[:, :CLIPS, None], 0), axis=1)
    end = jnp.sum(jnp.where(is_id, begins[:, 1:, None], 0), axis=1)
    frame = lax.broadcasted_iota(jnp.int32, near.shape, 1) + (start - HALF)
    place = (frame - first).astype(F32).reshape(-1, 1)
    mid = slice(HALF, HALF + length)
    low = jnp.maximum(frame - HALF, first)[:, mid] - (start - HALF)
    high = jnp.minimum(frame + HALF, end)[:, mid] - (start - HALF)
    padded = -(-length // QB) * QB
    span = jnp.pad(jnp.stack([low, high], axis=1), ((0, 0), (0, 0), (0, padded - length)))

    gain = norm_gain[None]
    joint, normed, normed_own, cos_tab, sin_tab = project(
        x, from_left.reshape(-1, width), from_right.reshape(-1, width), place, gain,
        w_query, w_key, w_value, seqs,
    )
    mixed, probs = attend(span, joint, seqs)

    attn_out, mlp_in = out_proj(mixed, x, w_output, attn_scale[None], mlp_gain[None])
    flags_now, mlp_in, has = hold(flags, mlp_in, has)
    mlp_in_peer = places.swap(mlp_in, places.core)
    grad_low, grad_hidden = hidden_grad(
        flags_now, grad_y, grad_y_peer, mlp_scale[None], w_down, block
    )

    blocks = n_seq // 2
    per = blocks // 2

    def onward(piece):
        piece.add()
        piece.split(late[-1 - piece.left])
        piece.left -= 1

    def started(piece):
        piece.left = len(late) - 1
        return piece

    def finished(piece):
        while piece.left >= 0:
            onward(piece)
        piece.add(False)
        return piece.keep

    inners = rounds.first_inners(every, own_rows)
    *kept, a, b, c, d = feed(
        flags, mlp_in, mlp_in_peer, grad_hidden, w_gate, w_up, block, 0, per, (), inners
    )
    rounds.begin((a, b, c, d), every, own_rows)
    *kept, a, b, c, d = feed(
        flags, mlp_in, mlp_in_peer, grad_hidden, w_gate, w_up, block, per, per, kept, inners, width // 4
    )
    hidden, hidden_peer, grad_gate, grad_up = kept
    hidden_got = places.swap(hidden_peer, places.core)
    flags_now, a = meet(flags, [a], rounds=rounds)
    rounds.run(flags_now, "sent", (a, b, c, d), every, own_rows)

    flags_now, rounds.two["keep"][0] = meet(flags, [rounds.two["keep"][0]])
    *in_peer, in_own = feed_back(flags_now, grad_gate, grad_up, w_gate, w_up, block)
    in_got = [places.swap(v, places.core) for v in in_peer]

    flags_now, in_own = meet(flags, [in_own])
    each = feed_rows // 2
    parts = down(
        flags_now, hidden, hidden_peer, grad_low, each, rounds.first_inners(not_core, each), width // 4
    )

    flags_now, *both = meet(flags, [*in_got, *parts], rounds=rounds)
    in_got, parts = both[:2], both[2:]
    carry = rounds.run(flags_now, "sent", parts, not_core, each, wait=True)

    scale_row, rounds.two["keep"][0], hidden_got = meet(
        attn_scale[None], [rounds.two["keep"][0], hidden_got]
    )
    grad_attn, grad_mixed, grad_middle, join_sums = join(
        x, attn_out, grad_y, in_own, in_got, scale_row, mlp_gain[None], w_output
    )
    flip = ((sp == 0) & (n_sp == 2)).astype(jnp.int32).reshape(1)
    grad_query, grad_kv, grad_near, edge, other_edge = attend_back(
        flip, probs, joint, grad_mixed, cos_tab, sin_tab, seqs
    )
    if n_sp == 2:
        to_right = to_left = lax.ppermute(edge, "sp", [(0, 1), (1, 0)])
    else:
        to_left = lax.ppermute(edge, "sp", [(i + 1, i) for i in range(n_sp - 1)])
        to_right = lax.ppermute(other_edge, "sp", [(i, i + 1) for i in range(n_sp - 1)])
    to_right, to_left = [v.reshape(2, seqs, HALF, width) for v in (to_right, to_left)]

    core_inner = Piece(places, every, own_rows).inner(places.core)

    flags_now, grad_query = meet(flags, [grad_query])
    out, stay = weight_grad(
        flags_now,
        core_inner,
        [(mixed, grad_attn), (normed_own, grad_query), (normed, (grad_near, 0)), (normed, (grad_near, 1))],
        "attention_weights",
        0.02,
    )
    from_core = places.swap(out, places.core)

    flags_now, stay, to_right, to_left = meet(flags, [stay, to_right, to_left], [], rounds)
    first = started(rounds.run(flags_now, carry=carry))
    aside = rounds.set_aside()
    has_now, aside["keep"][0] = meet(has, [aside["keep"][0]])
    grad_kv = add_edges(has_now, grad_kv, to_right, to_left)
    flags_now, grad_kv, from_core = meet(flags, [grad_kv, from_core])
    rounds.run(flags_now, "core", (stay, from_core), not_core, own_rows)

    flags_now, rounds.one["keep"][0], *aside["got"] = meet(
        flags, [rounds.one["keep"][0], *aside["got"]]
    )
    layer_out, out_sums = feed_out(
        flags_now, hidden, hidden_got, w_down, x, attn_out, grad_y,
        attn_scale[None], mlp_scale[None], block,
    )
    flags_now, layer_out, join_sums = meet(flags, [layer_out, join_sums], [first])
    third = started(rounds.run_aside(flags_now, aside))
    onward(first)
    flags_now, first.keep, third.keep = meet(flags, [first.keep, third.keep], [], rounds)
    rounds.run(flags_now)
    gain_now, rounds.two["keep"][0] = meet(gain, [rounds.two["keep"][0]])
    frames_grad, norm_sums = input_grad(
        x, grad_query, grad_kv, grad_middle, gain_now, w_query, w_key, w_value
    )
    flags_now, frames_grad = meet(flags, [frames_grad], [third], rounds)
    fourth = started(rounds.run(flags_now))
    onward(third)
    _, fourth.keep, norm_sums = meet(flags, [fourth.keep, norm_sums])
    norm_sums, join_sums, out_sums = lax.optimization_barrier((norm_sums, join_sums, out_sums))
    vectors = jnp.stack([norm_sums[0], join_sums[0], join_sums[1], out_sums[0]], axis=1)
    vectors = vectors.reshape((2,) * places.count + (own_rows, 4))
    left = list(reversed(every))
    groups = [[b] for b in [places.core, x_bit, y_bit, z_bit] + late]
    shares = share(places, vectors, left, groups[0])
    _, *shares = meet(flags, shares, [first])
    feeds = finished(first).reshape(2, 2, 2, own_rows, width)
    mine = lax.dynamic_index_in_dim(feeds, core, 2, False)
    got = places.swap(lax.dynamic_index_in_dim(feeds, 1 - core, 2, False), places.core)
    for done, group in zip(groups, groups[1:]):
        left = [b for b in left if b not in done]
        shares = share(places, sum(shares), left, group)
        if group is groups[-3]:
            _, *shares = meet(flags, shares, [fourth])
            onward(fourth)
    down_grad = finished(third)
    pair = jnp.stack([jnp.where(core == 0, mine, got), jnp.where(core == 0, got, mine)], axis=0)
    pair = pair.reshape(2, 2, 2, own_rows, per, block)
    pair = pair.transpose(2, 3, 1, 4, 0, 5).reshape(2, own_rows, feed_width)
    while fourth.left >= 0:
        onward(fourth)
    _, gate_grad, up_grad, down_grad, *shares = meet(
        flags, [pair[0], pair[1], down_grad, *shares], [fourth]
    )
    vectors = sum(shares).T
    output_grad, query_grad, key_grad, value_grad = [
        fourth.keep[rows, columns].astype(F32) + fourth.got[rows, columns].astype(F32)
        for rows in (slice(0, own_rows), slice(own_rows, 2 * own_rows))
        for columns in (slice(0, width), slice(width, 2 * width))
    ]
    return (
        layer_out.reshape(frames.shape),
        frames_grad.reshape(frames.shape),
        vectors[0],
        query_grad,
        key_grad,
        value_grad,
        output_grad,
        vectors[1],
        vectors[2],
        gate_grad,
        up_grad,
        down_grad,
        vectors[3],
    )


def solution(mesh):
    split = P("seq", "sp", None)
    rows = P(("seq", "sp"), None)
    vec = P(("seq", "sp"))
    return jax.shard_map(
        on_device,
        mesh=mesh,
        in_specs=(split, P("seq", None)) + (P(),) * 11 + (split,),
        out_specs=(
            split, split, vec, rows, rows, rows, rows, vec, vec, rows, rows, rows, vec,
        ),
        check_vma=False,
    )
```
